32 devices in a mesh: groups: 2 (over x), elec: 16 (over z, y, core).
Axes of the slice: x: 2, y: 2, z: 4, core: 2. Of those that a mesh axis runs over, the one named last changes fastest.
Arguments:
- features: bfloat16 [131072, 256], P(('groups', 'elec')), parts along dimension 0, may hold values from -6 to 6
- assignment: int32 [131072], P(('groups', 'elec')), parts along dimension 0, may hold values from 0 to 65535, as said below
- pairs: int32 [2048, 3], P(('groups', 'elec')), parts along dimension 0, may hold values from 0 to 1023, as said below
- w_query: bfloat16 [256, 256], replicated
- w_key: bfloat16 [256, 256], replicated
- w_value: bfloat16 [256, 256], replicated, may hold values from -0.375 to 0.375
- w_out: bfloat16 [256, 256], replicated, may hold values from -0.375 to 0.375
- w_mix: bfloat16 [256, 256], replicated, may hold values from -0.375 to 0.375
Outputs:
- mixed: bfloat16 [131072, 256], P(('groups', 'elec')), parts along dimension 0
The draws below stay inside these ranges and needn't reach their ends.
There are 2 independent parts, one for each index of `groups`. The reference program is written for one: setup_inputs(seed, part) draws one part's arguments, and reference() takes and returns one part's arrays. A program takes and returns all parts, laid end to end along the dimension named above; an argument that names none is the same for every part. Nothing has to cross between parts.
Inputs may be any that keep to these rules, and one draw needn't show every extreme that they name: assignment is a permutation of the rows; each group of 512 rows of one walker on one device is filled from electrons of that same group. pairs[b, :] name blocks of block b's own walker (its blocks lie on the 8 devices whose index has the same remainder modulo 1024 // 512 as block b's device, 8 on each). Over the 64 reader blocks of one device, at most 25 of the listed key blocks lie on any one device (blocks d * 64 to (d + 1) * 64 - 1 lie on device d), and exactly 25 on some device.
All inputs are finite; a program needn't handle non-finite values.
Results may differ from the reference program's by a relative error of at most 0.0078.
Values may be sent and summed in bfloat16 or wider, within the bound.
No kernel may reach another device: no remote copies, remote signals or barrier semaphores. Data moves between devices by JAX's collectives and lax.ppermute only.
A program may use at most 128 MiB of HBM per device.

```python
import jax
import jax.numpy as jnp
from jax import lax

D = 256
HEADS = 16
HEAD_DIM = 16
CLUSTER = 64
PAIRS = 3
SPAN = 8
SUB = 8
BLK_DEV = 64
BLOCKS = 1024
ROWS = 65536
CAP = 25


def draw_assignment(key, part):
    group_count = ROWS // (SUB * CLUSTER)
    rows_each = SUB * CLUSTER
    orders = jax.vmap(lambda k: jax.random.permutation(k, rows_each))(jax.random.split(key, group_count))
    offsets = jnp.arange(group_count, dtype=jnp.int32)[:, None] * rows_each
    return (orders.astype(jnp.int32) + offsets).reshape(-1).astype(jnp.int32)


def draw_pairs(key, part):
    shard_count = BLOCKS // BLK_DEV
    stride = shard_count // SPAN
    wanted = BLK_DEV * PAIRS
    rest_count = wanted - SPAN
    rest_cap = CAP - 1
    rest_slots = SPAN * rest_cap

    def one_device(k, device):
        k_perm, k_full, k_shuffle, k_local, k_owner = jax.random.split(k, 5)
        position = device // stride
        group_first = device % stride
        first_owner = jax.random.permutation(k_owner, SPAN).astype(jnp.int32)
        offset = (position - first_owner) % SPAN
        lowbit = jnp.where(offset == 0, SPAN, offset & -offset)
        first_within = (position // lowbit % 2).astype(jnp.int32)
        order_scores = jax.random.permutation(k_perm, rest_slots).astype(jnp.int32)
        full_owner = jax.random.randint(k_full, (), 0, SPAN)
        slot_ids = jnp.arange(rest_slots, dtype=jnp.int32)
        ranked = order_scores - jnp.where(slot_ids // rest_cap == full_owner, rest_slots, 0)
        order = jnp.argsort(ranked, stable=True)
        chosen = order[:rest_count]
        shuffle = jax.random.permutation(k_shuffle, rest_count)
        rest_owner = (chosen[shuffle] // rest_cap).astype(jnp.int32)
        rest_within = jax.random.randint(k_local, (rest_count,), 0, SUB).astype(jnp.int32)
        owner_pos = jnp.concatenate([first_owner, rest_owner])
        within = jnp.concatenate([first_within, rest_within])
        entry = jnp.arange(wanted, dtype=jnp.int32)
        walker_slot = entry // PAIRS // SUB
        listed = (group_first + owner_pos * stride) * BLK_DEV + walker_slot * SUB + within
        return listed.reshape(BLK_DEV, PAIRS)
    devices = jnp.arange(shard_count, dtype=jnp.int32)
    result = jax.vmap(one_device)(jax.random.split(key, shard_count), devices)
    return result.reshape(BLOCKS, PAIRS).astype(jnp.int32)


def projection_pair(key):
    k_one, k_two = jax.random.split(jax.random.fold_in(key, 7), 2)
    first = jax.random.normal(k_one, (D, D), jnp.float32) / D ** 0.5
    second = jax.random.normal(k_two, (D, D), jnp.float32) / D ** 0.5
    return (first, second)


def draw_w_query(key, part):
    return projection_pair(key)[0].astype(jnp.bfloat16)


def draw_w_key(key, part):
    return projection_pair(key)[1].astype(jnp.bfloat16)


def levels(own_key, dims, shards, least, top_value):
    level = 1.0
    for dim, parts in shards:
        draws = jax.random.uniform(jax.random.fold_in(jax.random.fold_in(own_key, 6), dim), (parts,), jnp.float32, least / len(shards), top_value / len(shards))
        level = level * jnp.repeat(jnp.exp(draws), dims[dim] // parts).reshape((-1,) + (1,) * (len(dims) - 1 - dim))
    return level


def noise(stream_key, shape, spread, bound, pieces=(), held_as=jnp.bfloat16):
    values = spread * jax.random.normal(stream_key, shape, jnp.float32)
    if pieces:
        values = values * levels(stream_key, shape, pieces, -0.22, 0.18)
    return jnp.clip(values, -bound, bound).astype(held_as)


def setup_inputs(seed: int = 0, part: int = 0) -> dict:
    streams_of = jax.random.split(jax.random.key(seed), 9)
    part_splits = jax.random.split(jax.random.fold_in(streams_of[8], part), 9)
    return {
        "features": noise(part_splits[0], (ROWS, D), 1.0, 6.0, ((0, 16),)),
        "assignment": draw_assignment(jax.random.fold_in(jax.random.fold_in(streams_of[8], part), 71), part),
        "pairs": draw_pairs(jax.random.fold_in(jax.random.fold_in(streams_of[8], part), 71), part),
        "w_query": draw_w_query(jax.random.fold_in(streams_of[8], 71), part),
        "w_key": draw_w_key(jax.random.fold_in(streams_of[8], 71), part),
        "w_value": noise(streams_of[5], (D, D), D ** -0.5, 0.375),
        "w_out": noise(streams_of[6], (D, D), D ** -0.5, 0.375),
        "w_mix": noise(streams_of[7], (D, D), D ** -0.5, 0.375),
    }


def layer_norm(rows):
    mean = lax.optimization_barrier(jnp.mean(rows, axis=-1, keepdims=True))
    centred = rows - mean
    variance = lax.optimization_barrier(jnp.mean(centred * centred, axis=-1, keepdims=True))
    return centred * lax.rsqrt(variance + 1e-05)

def reference(features, assignment, pairs, w_query, w_key, w_value, w_out, w_mix):
    placed = jnp.take(features, assignment, axis=0)
    normed = layer_norm(placed.astype(jnp.float32)).astype(jnp.bfloat16)
    query = jnp.dot(normed, w_query, preferred_element_type=jnp.float32).astype(jnp.bfloat16)
    keys = jnp.dot(normed, w_key, preferred_element_type=jnp.float32).astype(jnp.bfloat16)
    values = jnp.dot(normed, w_value, preferred_element_type=jnp.float32).astype(jnp.bfloat16)
    query_blocks = query.reshape(BLOCKS, CLUSTER, D)
    key_blocks = keys.reshape(BLOCKS, CLUSTER, D)
    value_blocks = values.reshape(BLOCKS, CLUSTER, D)
    scale = 1.0 / HEAD_DIM ** 0.5

    def attend(args):
        block_query, block_index, listed = args
        chosen = jnp.concatenate([block_index[None], listed]).astype(jnp.int32)
        set_keys = jnp.take(key_blocks, chosen, axis=0).reshape(-1, HEADS, HEAD_DIM).astype(jnp.float32)
        set_values = jnp.take(value_blocks, chosen, axis=0).reshape(-1, HEADS, HEAD_DIM).astype(jnp.float32)
        heads_query = block_query.reshape(CLUSTER, HEADS, HEAD_DIM).astype(jnp.float32)
        scores = jnp.einsum('qhd,khd->hqk', heads_query, set_keys) * scale
        weights = jax.nn.softmax(scores, axis=-1).astype(jnp.bfloat16)
        result = jnp.einsum('hqk,khd->qhd', weights.astype(jnp.float32), set_values)
        return result.astype(jnp.bfloat16).reshape(CLUSTER, D)
    attended = lax.map(attend, (query_blocks, jnp.arange(BLOCKS, dtype=jnp.int32), pairs), batch_size=64)
    attended = attended.reshape(ROWS, D)
    middle = (placed.astype(jnp.float32) + jnp.dot(attended, w_out, preferred_element_type=jnp.float32)).astype(jnp.bfloat16)
    second = layer_norm(middle.astype(jnp.float32)).astype(jnp.bfloat16)
    mixed = middle.astype(jnp.float32) + jnp.tanh(jnp.dot(second, w_mix, preferred_element_type=jnp.float32))
    return mixed.astype(jnp.bfloat16)
```

```python
import functools

import jax
import jax.numpy as jnp
from jax import lax
from jax.experimental import pallas as pl
from jax.experimental.pallas import tpu as pltpu
from jax.sharding import PartitionSpec as P

HEADS = 16
SPAN = 8
SUB = 8
CHUNKS = 4
VMEM_BYTES = 48 * 1024 * 1024

NT = (((1,), (1,)), ((), ()))


def layer_norm(rows):
    mean = jnp.mean(rows, axis=-1, keepdims=True)
    centred = rows - mean
    variance = jnp.mean(centred * centred, axis=-1, keepdims=True)
    return centred * lax.rsqrt(variance + 1e-05)


def place_kernel(features_ref, assignment_ref, placed_ref, normed_ref):
    rows = features_ref.shape[0]
    lane = 128
    features = features_ref[...]
    columns = lax.broadcasted_iota(jnp.int32, (lane, rows), 1)
    for part in range(rows // lane):
        chosen = assignment_ref[0, :, part * lane : (part + 1) * lane] & (rows - 1)
        chosen = jnp.broadcast_to(chosen, (lane, lane)).T
        chosen = jnp.concatenate([chosen] * (rows // lane), axis=1)
        one_hot = jnp.where(chosen == columns, 1.0, 0.0).astype(jnp.bfloat16)
        placed = jnp.dot(one_hot, features, preferred_element_type=jnp.float32)
        placed_ref[pl.ds(part * lane, lane), :] = placed.astype(jnp.bfloat16)
        normed_ref[pl.ds(part * lane, lane), :] = layer_norm(placed).astype(jnp.bfloat16)


def place(features, assignment, first, count, rows):
    width = features.shape[1]
    out = jax.ShapeDtypeStruct((count * rows, width), jnp.bfloat16)
    return pl.pallas_call(
        place_kernel,
        grid=(count,),
        in_specs=[
            pl.BlockSpec((rows, width), lambda i: (first + i, 0)),
            pl.BlockSpec((1, 1, rows), lambda i: (first + i, 0, 0)),
        ],
        out_specs=[pl.BlockSpec((rows, width), lambda i: (i, 0))] * 2,
        out_shape=[out, out],
        cost_estimate=pl.CostEstimate(
            flops=2 * count * rows * rows * width,
            bytes_accessed=6 * count * rows * width,
            transcendentals=0,
        ),
        compiler_params=pltpu.CompilerParams(vmem_limit_bytes=VMEM_BYTES),
        name="place_rows",
    )(features, assignment)


def attend_kernel(
    table_ref,
    source_ref,
    normed_ref,
    placed_ref,
    query_ref,
    key_ref,
    value_ref,
    out_w_ref,
    mix_ref,
    *rest,
    pair_count,
):
    mixed_ref, attended_ref = rest[-2:]
    walker = pl.program_id(0)
    rows, width = normed_ref.shape
    cluster = rows // SUB
    head_width = width // HEADS
    group = 4
    span = group * head_width
    tile = group * cluster
    row_head = lax.broadcasted_iota(jnp.int32, (width, tile), 0) // head_width % group
    lane_head = lax.broadcasted_iota(jnp.int32, (width, tile), 1) // cluster
    diagonal = row_head == lane_head
    fold_row = lax.broadcasted_iota(jnp.int32, (cluster, tile), 0)
    fold_lane = lax.broadcasted_iota(jnp.int32, (cluster, tile), 1) % cluster
    fold = jnp.where(fold_row == fold_lane, 1.0, 0.0).astype(jnp.bfloat16)

    def one_block(block, carry):
        own = normed_ref[pl.ds(pl.multiple_of(block * cluster, cluster), cluster), :]
        base = (walker * SUB + block) * pair_count
        listed = [source_ref[table_ref[base + j]] for j in range(pair_count)]
        members = jnp.concatenate([own] + listed, axis=0)
        keys = jnp.dot(members, key_ref[...], preferred_element_type=jnp.float32)
        keys = keys.astype(jnp.bfloat16)
        values = lax.dot_general(value_ref[...], members, NT, preferred_element_type=jnp.float32)
        values = values.astype(jnp.bfloat16)
        own_tiled = jnp.concatenate([own] * group, axis=0)
        query = lax.dot_general(query_ref[...], own_tiled, NT, preferred_element_type=jnp.float32)
        query = query.astype(jnp.bfloat16) * jnp.bfloat16(1.0 / head_width**0.5)
        query = jnp.where(diagonal, query, jnp.bfloat16(0.0))
        pieces = []
        for t in range(HEADS // group):
            lo = t * span // 128 * 128
            zeros = jnp.zeros((span, tile), jnp.bfloat16)
            picked = query[t * span : (t + 1) * span]
            ahead, behind = t * span - lo, lo + 128 - (t + 1) * span
            stack = [zeros] * (ahead // span) + [picked] + [zeros] * (behind // span)
            scores = jnp.dot(
                keys[:, lo : lo + 128],
                jnp.concatenate(stack, axis=0),
                preferred_element_type=jnp.float32,
            )
            top = jnp.max(scores, axis=0, keepdims=True)
            weights = jnp.exp(scores - top)
            total = jnp.sum(weights, axis=0, keepdims=True)
            result = jnp.dot(
                values[t * span : (t + 1) * span],
                weights.astype(jnp.bfloat16),
                preferred_element_type=jnp.float32,
            )
            result = result * (1.0 / total)
            pieces.append(jnp.where(diagonal[:span], result, 0.0).astype(jnp.bfloat16))
        stacked = jnp.concatenate(pieces, axis=0)
        attended = lax.dot_general(fold, stacked, NT, preferred_element_type=jnp.float32)
        attended_ref[pl.ds(pl.multiple_of(block * cluster, cluster), cluster), :] = attended.astype(
            jnp.bfloat16
        )
        return carry

    lax.fori_loop(0, SUB, one_block, 0)
    middle = placed_ref[...].astype(jnp.float32) + jnp.dot(
        attended_ref[...], out_w_ref[...], preferred_element_type=jnp.float32
    )
    middle = middle.astype(jnp.bfloat16).astype(jnp.float32)
    second = layer_norm(middle).astype(jnp.bfloat16)
    mixed = middle + jnp.tanh(jnp.dot(second, mix_ref[...], preferred_element_type=jnp.float32))
    mixed_ref[...] = mixed.astype(jnp.bfloat16)


def attend(table, source, normed, placed, weights, so_far, first, total_rows, pair_count):
    rows_here, width = normed.shape
    cluster = source.shape[-2]
    rows = SUB * cluster
    count = rows_here // rows
    whole = pl.BlockSpec((width, width), lambda i, t: (0, 0))
    local = pl.BlockSpec((rows, width), lambda i, t: (i, 0))
    in_specs = [
        pl.BlockSpec(source.shape, lambda i, t: (0, 0, 0)),
        local,
        local,
    ] + [whole] * 5
    operands = [source, normed, placed, *weights]
    aliases = {}
    if so_far is not None:
        in_specs.append(pl.BlockSpec(memory_space=pl.ANY))
        operands.append(so_far)
        aliases = {len(operands): 0}
    return pl.pallas_call(
        functools.partial(attend_kernel, pair_count=pair_count),
        grid_spec=pltpu.PrefetchScalarGridSpec(
            num_scalar_prefetch=1,
            grid=(count,),
            in_specs=in_specs,
            out_specs=pl.BlockSpec((rows, width), lambda i, t: (first + i, 0)),
            scratch_shapes=[pltpu.VMEM((rows, width), jnp.bfloat16)],
        ),
        out_shape=jax.ShapeDtypeStruct((total_rows, width), jnp.bfloat16),
        input_output_aliases=aliases,
        cost_estimate=pl.CostEstimate(
            flops=count * SUB * 4 * 1024 * 1024 * 1024 // 4,
            bytes_accessed=source.size * 2 + 6 * rows_here * width,
            transcendentals=rows_here * HEADS * (pair_count + 1) * cluster,
        ),
        compiler_params=pltpu.CompilerParams(vmem_limit_bytes=VMEM_BYTES),
        name="attend_walkers",
    )(table, *operands)


def body(features, assignment, pairs, w_query, w_key, w_value, w_out, w_mix):
    rows_dev, width = features.shape
    block_count, pair_count = pairs.shape
    cluster = rows_dev // block_count
    walkers = block_count // SUB
    rows = SUB * cluster
    stride = lax.axis_size("elec") // SPAN
    groups = [[rest + place_ * stride for place_ in range(SPAN)] for rest in range(stride)]
    assignment = assignment.reshape(walkers, 1, rows)
    weights = (w_query.T, w_key, w_value.T, w_out, w_mix)
    each = walkers // CHUNKS
    owner = pairs // block_count // stride
    within = pairs % block_count % (each * SUB)
    table = (owner * (each * SUB) + within).reshape(CHUNKS, -1)
    mixed = None
    local = [place(features, assignment, c * each, each, rows) for c in range(CHUNKS)]
    gathered = [
        lax.all_gather(normed, "elec", axis_index_groups=groups, axis=0, tiled=True)
        for _, normed in local
    ]
    for c in range(CHUNKS):
        placed, normed = local[c]
        source = gathered[c].reshape(SPAN * each * SUB, cluster, width)
        mixed = attend(
            table[c], source, normed, placed, weights, mixed, c * each, rows_dev, pair_count
        )
    return mixed


def solution(mesh):
    placed = (
        P(("groups", "elec"), None),
        P(("groups", "elec")),
        P(("groups", "elec"), None),
        P(),
        P(),
        P(),
        P(),
        P(),
    )
    return jax.shard_map(
        body, mesh=mesh, in_specs=placed, out_specs=P(("groups", "elec"), None), check_vma=False
    )
```

```python
import functools

import jax
import jax.numpy as jnp
from jax import lax
from jax.experimental import pallas as pl
from jax.experimental.pallas import tpu as pltpu
from jax.sharding import PartitionSpec as P

HEADS = 16
SPAN = 8
SUB = 8
GROUP = 4
STEP = 4
VMEM_BYTES = 48 * 1024 * 1024

NT = (((1,), (1,)), ((), ()))


def kernel_params():
    return pltpu.CompilerParams(vmem_limit_bytes=VMEM_BYTES)


def layer_norm(rows):
    mean = jnp.mean(rows, axis=-1, keepdims=True)
    centred = rows - mean
    variance = jnp.mean(centred * centred, axis=-1, keepdims=True)
    return centred * lax.rsqrt(variance + 1e-05)


def head_mask(shape, head_width, cluster):
    row_head = lax.broadcasted_iota(jnp.int32, shape, 0) // head_width % GROUP
    lane_head = lax.broadcasted_iota(jnp.int32, shape, 1) // cluster
    return row_head == lane_head


def place_kernel(features_ref, assignment_ref, placed_ref, normed_ref):
    rows = features_ref.shape[0]
    lane = 128
    features = features_ref[...]
    columns = lax.broadcasted_iota(jnp.int32, (lane, rows), 1)
    for part in range(rows // lane):
        chosen = assignment_ref[0, :, part * lane : (part + 1) * lane] & (rows - 1)
        chosen = jnp.broadcast_to(chosen, (lane, lane)).T
        chosen = jnp.concatenate([chosen] * (rows // lane), axis=1)
        one_hot = jnp.where(chosen == columns, 1.0, 0.0).astype(jnp.bfloat16)
        placed = jnp.dot(one_hot, features, preferred_element_type=jnp.float32)
        placed_ref[pl.ds(part * lane, lane), :] = placed.astype(jnp.bfloat16)
        normed_ref[pl.ds(part * lane, lane), :] = layer_norm(placed).astype(jnp.bfloat16)


def place(features, assignment):
    width = features.shape[1]
    walkers, _, rows = assignment.shape
    local = pl.BlockSpec((rows, width), lambda i: (i, 0))
    out = jax.ShapeDtypeStruct(features.shape, jnp.bfloat16)
    return pl.pallas_call(
        place_kernel,
        grid=(walkers,),
        in_specs=[local, pl.BlockSpec((1, 1, rows), lambda i: (i, 0, 0))],
        out_specs=[local] * 2,
        out_shape=[out, out],
        cost_estimate=pl.CostEstimate(
            flops=2 * walkers * rows * rows * width,
            bytes_accessed=6 * walkers * rows * width,
            transcendentals=0,
        ),
        compiler_params=kernel_params(),
        name="place_rows",
    )(features, assignment)


def pick_kernel(position_ref, demanded_ref, blocks_ref, *out_refs):
    for step, out_ref in enumerate(out_refs):
        reader = (position_ref[0] + step + 1) % SPAN

        def one_slot(slot, carry, reader=reader, out_ref=out_ref):
            out_ref[slot] = blocks_ref[demanded_ref[reader, slot]]
            return carry

        lax.fori_loop(0, out_ref.shape[0], one_slot, 0)


def pick(position, demanded, blocks):
    capacity = demanded.shape[1]
    piece = jax.ShapeDtypeStruct((capacity,) + blocks.shape[1:], blocks.dtype)
    smem = pl.BlockSpec(memory_space=pltpu.SMEM)
    vmem = pl.BlockSpec(memory_space=pltpu.VMEM)
    return pl.pallas_call(
        pick_kernel,
        in_specs=[smem, smem, vmem],
        out_specs=[vmem] * (SPAN - 1),
        out_shape=[piece] * (SPAN - 1),
        cost_estimate=pl.CostEstimate(
            flops=0, bytes_accessed=4 * (SPAN - 1) * piece.size, transcendentals=0
        ),
        compiler_params=kernel_params(),
        name="pick_blocks",
    )(position, demanded, blocks)


def query_kernel(normed_ref, query_w_ref, query_ref, *, cluster, head_width):
    width = normed_ref.shape[1]
    mask = head_mask((width, GROUP * cluster), head_width, cluster)
    for block in range(query_ref.shape[0]):
        own = normed_ref[pl.ds(block * cluster, cluster), :]
        own = jnp.concatenate([own] * GROUP, axis=0)
        query = lax.dot_general(query_w_ref[...], own, NT, preferred_element_type=jnp.float32)
        query = query.astype(jnp.bfloat16) * jnp.bfloat16(1.0 / head_width**0.5)
        query_ref[block] = jnp.where(mask, query, jnp.bfloat16(0.0))


def project_queries(normed, w_query, cluster):
    rows, width = normed.shape
    blocks = rows // cluster
    return pl.pallas_call(
        functools.partial(query_kernel, cluster=cluster, head_width=width // HEADS),
        grid=(blocks // SUB,),
        in_specs=[
            pl.BlockSpec((SUB * cluster, width), lambda i: (i, 0)),
            pl.BlockSpec((width, width), lambda i: (0, 0)),
        ],
        out_specs=pl.BlockSpec((SUB, width, GROUP * cluster), lambda i: (i, 0, 0)),
        out_shape=jax.ShapeDtypeStruct((blocks, width, GROUP * cluster), jnp.bfloat16),
        cost_estimate=pl.CostEstimate(
            flops=2 * rows * GROUP * width * width,
            bytes_accessed=2 * rows * width * (GROUP + 1),
            transcendentals=0,
        ),
        compiler_params=kernel_params(),
        name="queries",
    )(normed, w_query.T)


def key_value_kernel(rows_ref, w_ref, *rest):
    out_ref = rest[-1]
    blocks, cluster, width = rows_ref.shape
    rows = rows_ref[...].reshape(blocks * cluster, width)
    both = jnp.dot(rows, w_ref[...], preferred_element_type=jnp.float32)
    out_ref[...] = both.astype(jnp.bfloat16).reshape(out_ref.shape)


def project_pairs(piece, w_both, so_far, at, total):
    blocks, cluster, width = piece.shape
    per = 5 if blocks % 5 == 0 else 8
    in_specs = [
        pl.BlockSpec((per, cluster, width), lambda i: (i, 0, 0)),
        pl.BlockSpec((width, 2 * width), lambda i: (0, 0)),
    ]
    operands = [piece, w_both]
    aliases = {}
    if so_far is not None:
        in_specs.append(pl.BlockSpec(memory_space=pl.ANY))
        operands.append(so_far)
        aliases = {2: 0}
    return pl.pallas_call(
        key_value_kernel,
        grid=(blocks // per,),
        in_specs=in_specs,
        out_specs=pl.BlockSpec((per, cluster, 2 * width), lambda i: (at // per + i, 0, 0)),
        out_shape=jax.ShapeDtypeStruct((total, cluster, 2 * width), jnp.bfloat16),
        input_output_aliases=aliases,
        cost_estimate=pl.CostEstimate(
            flops=4 * piece.size * width, bytes_accessed=6 * piece.size, transcendentals=0
        ),
        compiler_params=kernel_params(),
        name="keys_values",
    )(*operands)


def attend_kernel(table_ref, query_ref, own_ref, *rest, pair_count, head_width):
    listed_refs = rest[: STEP * pair_count]
    placed_ref, out_w_ref, mix_ref, mixed_ref = rest[STEP * pair_count :]
    cluster = own_ref.shape[1]
    width = placed_ref.shape[1]
    span = GROUP * head_width
    tile = GROUP * cluster
    diagonal = head_mask((span, tile), head_width, cluster)
    fold_row = lax.broadcasted_iota(jnp.int32, (cluster, tile), 0)
    fold_lane = lax.broadcasted_iota(jnp.int32, (cluster, tile), 1) % cluster
    fold = jnp.where(fold_row == fold_lane, 1.0, 0.0).astype(jnp.bfloat16)
    zeros = jnp.zeros((span, tile), jnp.bfloat16)
    attended = []
    for block in range(STEP):
        members = [own_ref[block]]
        members += [listed_refs[block * pair_count + j][0] for j in range(pair_count)]
        keys = jnp.concatenate([m[:, :width] for m in members], axis=0)
        values = jnp.concatenate([m[:, width:] for m in members], axis=0).T
        pieces = []
        for t in range(HEADS // GROUP):
            lo = t * span // 128 * 128
            picked = query_ref[block, t * span : (t + 1) * span, :]
            ahead, behind = t * span - lo, lo + 128 - (t + 1) * span
            stack = [zeros] * (ahead // span) + [picked] + [zeros] * (behind // span)
            scores = jnp.dot(
                keys[:, lo : lo + 128],
                jnp.concatenate(stack, axis=0),
                preferred_element_type=jnp.float32,
            )
            top = jnp.max(scores, axis=0, keepdims=True)
            weights = jnp.exp(scores - top)
            total = jnp.sum(weights, axis=0, keepdims=True)
            result = jnp.dot(
                values[t * span : (t + 1) * span],
                weights.astype(jnp.bfloat16),
                preferred_element_type=jnp.float32,
            )
            result = result * (1.0 / total)
            pieces.append(jnp.where(diagonal, result, 0.0).astype(jnp.bfloat16))
        stacked = jnp.concatenate(pieces, axis=0)
        folded = lax.dot_general(fold, stacked, NT, preferred_element_type=jnp.float32)
        attended.append(folded.astype(jnp.bfloat16))
    middle = placed_ref[...].astype(jnp.float32) + jnp.dot(
        jnp.concatenate(attended, axis=0), out_w_ref[...], preferred_element_type=jnp.float32
    )
    middle = middle.astype(jnp.bfloat16).astype(jnp.float32)
    second = layer_norm(middle).astype(jnp.bfloat16)
    mixed = middle + jnp.tanh(jnp.dot(second, mix_ref[...], preferred_element_type=jnp.float32))
    mixed_ref[...] = mixed.astype(jnp.bfloat16)


def attend(table, queries, pairs_buffer, own_at, placed, w_out, w_mix, pair_count):
    rows, width = placed.shape
    blocks, _, tile = queries.shape
    cluster = rows // blocks
    whole = pl.BlockSpec((width, width), lambda i, t: (0, 0))
    local = pl.BlockSpec((STEP * cluster, width), lambda i, t: (i, 0))

    def listed(j):
        return pl.BlockSpec(
            (1, cluster, 2 * width), lambda i, t: (t[i * STEP * pair_count + j], 0, 0)
        )

    return pl.pallas_call(
        functools.partial(attend_kernel, pair_count=pair_count, head_width=width // HEADS),
        grid_spec=pltpu.PrefetchScalarGridSpec(
            num_scalar_prefetch=1,
            grid=(blocks // STEP,),
            in_specs=[
                pl.BlockSpec((STEP, width, tile), lambda i, t: (i, 0, 0)),
                pl.BlockSpec((STEP, cluster, 2 * width), lambda i, t: (own_at // STEP + i, 0, 0)),
            ]
            + [listed(j) for j in range(STEP * pair_count)]
            + [local, whole, whole],
            out_specs=local,
        ),
        out_shape=jax.ShapeDtypeStruct((rows, width), jnp.bfloat16),
        cost_estimate=pl.CostEstimate(
            flops=4 * rows * HEADS * width * (pair_count + 1) * cluster,
            bytes_accessed=24 * rows * width,
            transcendentals=rows * HEADS * (pair_count + 1) * cluster,
        ),
        compiler_params=kernel_params(),
        name="attend_blocks",
    )(
        table,
        queries,
        pairs_buffer,
        *[pairs_buffer] * (STEP * pair_count),
        placed,
        w_out,
        w_mix,
    )


def slot_table(owner, within, capacity):
    entries = owner.shape[0]
    alike = owner[:, None] == owner[None, :]
    earlier = jnp.arange(entries)[None, :] < jnp.arange(entries)[:, None]
    ranking = jnp.sum(jnp.where(alike & earlier, 1, 0), axis=1).astype(jnp.int32)
    slots = owner * capacity + ranking
    matches = slots[None, :] == jnp.arange(SPAN * capacity, dtype=jnp.int32)[:, None]
    tables = jnp.sum(jnp.where(matches, within[None, :], 0), axis=1)
    return ranking, tables.reshape(SPAN, capacity)


def body(features, assignment, pairs, w_query, w_key, w_value, w_out, w_mix):
    rows_dev, width = features.shape
    block_count, pair_count = pairs.shape
    cluster = rows_dev // block_count
    peers = lax.axis_size("elec")
    stride = peers // SPAN
    groups = [[rest + place_ * stride for place_ in range(SPAN)] for rest in range(stride)]
    position = lax.axis_index("elec") // stride
    capacity = (block_count * pair_count + SPAN - 1) // SPAN + 1

    listed = pairs.reshape(-1)
    owner = listed // block_count // stride
    within = listed % block_count
    ranking, tables = slot_table(owner, within, capacity)
    demanded = lax.all_to_all(
        tables, "elec", split_axis=0, concat_axis=0, axis_index_groups=groups, tiled=True
    )

    placed, normed = place(
        features, assignment.reshape(block_count // SUB, 1, SUB * cluster)
    )
    blocks = normed.reshape(block_count, cluster, width)
    outgoing = pick(position.reshape(1), demanded, blocks)
    arrived = [
        lax.ppermute(piece, "elec", [(i, (i + (o + 1) * stride) % peers) for i in range(peers)])
        for o, piece in enumerate(outgoing)
    ]

    w_both = jnp.concatenate([w_key, w_value], axis=1)
    own_at = -((1 - SPAN) * capacity // block_count) * block_count
    total = own_at + block_count
    buffer = project_pairs(blocks, w_both, None, own_at, total)
    queries = project_queries(normed, w_query, cluster)
    for o, piece in enumerate(arrived):
        buffer = project_pairs(piece, w_both, buffer, o * capacity, total)
    offset = (position - owner) % SPAN
    table = jnp.where(offset == 0, own_at + within, (offset - 1) * capacity + ranking)
    return attend(table, queries, buffer, own_at, placed, w_out, w_mix, pair_count)


def solution(mesh):
    placed = (
        P(("groups", "elec"), None),
        P(("groups", "elec")),
        P(("groups", "elec"), None),
        P(),
        P(),
        P(),
        P(),
        P(),
    )
    return jax.shard_map(
        body, mesh=mesh, in_specs=placed, out_specs=P(("groups", "elec"), None), check_vma=False
    )
```

```python
import functools

import jax
import jax.numpy as jnp
from jax import lax
from jax.experimental import pallas as pl
from jax.experimental.pallas import tpu as pltpu
from jax.sharding import PartitionSpec as P

HEADS = 16
SPAN = 8
SUB = 8
GROUP = 4
STEP = 4
VMEM_BYTES = 48 * 1024 * 1024

NT = (((1,), (1,)), ((), ()))


def kernel_params():
    return pltpu.CompilerParams(vmem_limit_bytes=VMEM_BYTES)


def layer_norm(rows):
    mean = jnp.mean(rows, axis=-1, keepdims=True)
    centred = rows - mean
    variance = jnp.mean(centred * centred, axis=-1, keepdims=True)
    return centred * lax.rsqrt(variance + 1e-05)


def head_mask(shape, head_width, cluster):
    row_head = lax.broadcasted_iota(jnp.int32, shape, 0) // head_width % GROUP
    lane_head = lax.broadcasted_iota(jnp.int32, shape, 1) // cluster
    return row_head == lane_head


def place_kernel(features_ref, assignment_ref, placed_ref, normed_ref):
    rows = features_ref.shape[0]
    lane = 128
    features = features_ref[...]
    columns = lax.broadcasted_iota(jnp.int32, (lane, rows), 1)
    for part in range(rows // lane):
        chosen = assignment_ref[0, :, part * lane : (part + 1) * lane] & (rows - 1)
        chosen = jnp.broadcast_to(chosen, (lane, lane)).T
        chosen = jnp.concatenate([chosen] * (rows // lane), axis=1)
        one_hot = jnp.where(chosen == columns, 1.0, 0.0).astype(jnp.bfloat16)
        placed = jnp.dot(one_hot, features, preferred_element_type=jnp.float32)
        placed_ref[pl.ds(part * lane, lane), :] = placed.astype(jnp.bfloat16)
        normed_ref[pl.ds(part * lane, lane), :] = layer_norm(placed).astype(jnp.bfloat16)


def place(features, assignment):
    width = features.shape[1]
    walkers, _, rows = assignment.shape
    local = pl.BlockSpec((rows, width), lambda i: (i, 0))
    out = jax.ShapeDtypeStruct(features.shape, jnp.bfloat16)
    return pl.pallas_call(
        place_kernel,
        grid=(walkers,),
        in_specs=[local, pl.BlockSpec((1, 1, rows), lambda i: (i, 0, 0))],
        out_specs=[local] * 2,
        out_shape=[out, out],
        cost_estimate=pl.CostEstimate(
            flops=2 * walkers * rows * rows * width,
            bytes_accessed=6 * walkers * rows * width,
            transcendentals=0,
        ),
        compiler_params=kernel_params(),
        name="place_rows",
    )(features, assignment)


def pick_kernel(position_ref, demanded_ref, blocks_ref, *out_refs):
    for step, out_ref in enumerate(out_refs):
        reader = (position_ref[0] + step + 1) % SPAN

        def one_slot(slot, carry, reader=reader, out_ref=out_ref):
            out_ref[slot] = blocks_ref[demanded_ref[reader, slot]]
            return carry

        lax.fori_loop(0, out_ref.shape[0], one_slot, 0)


def pick(position, demanded, blocks):
    capacity = demanded.shape[1]
    piece = jax.ShapeDtypeStruct((capacity,) + blocks.shape[1:], blocks.dtype)
    smem = pl.BlockSpec(memory_space=pltpu.SMEM)
    vmem = pl.BlockSpec(memory_space=pltpu.VMEM)
    return pl.pallas_call(
        pick_kernel,
        in_specs=[smem, smem, vmem],
        out_specs=[vmem] * (SPAN - 1),
        out_shape=[piece] * (SPAN - 1),
        cost_estimate=pl.CostEstimate(
            flops=0, bytes_accessed=4 * (SPAN - 1) * piece.size, transcendentals=0
        ),
        compiler_params=kernel_params(),
        name="pick_blocks",
    )(position, demanded, blocks)


def query_kernel(normed_ref, query_w_ref, query_ref, *, cluster, head_width):
    width = normed_ref.shape[1]
    mask = head_mask((width, GROUP * cluster), head_width, cluster)
    for block in range(query_ref.shape[0]):
        own = normed_ref[pl.ds(block * cluster, cluster), :]
        own = jnp.concatenate([own] * GROUP, axis=0)
        query = lax.dot_general(query_w_ref[...], own, NT, preferred_element_type=jnp.float32)
        query = query.astype(jnp.bfloat16) * jnp.bfloat16(1.0 / head_width**0.5)
        query_ref[block] = jnp.where(mask, query, jnp.bfloat16(0.0))


def project_queries(normed, w_query, cluster):
    rows, width = normed.shape
    blocks = rows // cluster
    return pl.pallas_call(
        functools.partial(query_kernel, cluster=cluster, head_width=width // HEADS),
        grid=(blocks // SUB,),
        in_specs=[
            pl.BlockSpec((SUB * cluster, width), lambda i: (i, 0)),
            pl.BlockSpec((width, width), lambda i: (0, 0)),
        ],
        out_specs=pl.BlockSpec((SUB, width, GROUP * cluster), lambda i: (i, 0, 0)),
        out_shape=jax.ShapeDtypeStruct((blocks, width, GROUP * cluster), jnp.bfloat16),
        cost_estimate=pl.CostEstimate(
            flops=2 * rows * GROUP * width * width,
            bytes_accessed=2 * rows * width * (GROUP + 1),
            transcendentals=0,
        ),
        compiler_params=kernel_params(),
        name="queries",
    )(normed, w_query.T)


def key_value_kernel(rows_ref, w_ref, *rest):
    out_ref = rest[-1]
    blocks, cluster, width = rows_ref.shape
    rows = rows_ref[...].reshape(blocks * cluster, width)
    both = jnp.dot(rows, w_ref[...], preferred_element_type=jnp.float32)
    out_ref[...] = both.astype(jnp.bfloat16).reshape(out_ref.shape)


def project_pairs(piece, w_both, so_far, at, total):
    blocks, cluster, width = piece.shape
    per = 5 if blocks % 5 == 0 else 8
    in_specs = [
        pl.BlockSpec((per, cluster, width), lambda i: (i, 0, 0)),
        pl.BlockSpec((width, 2 * width), lambda i: (0, 0)),
    ]
    operands = [piece, w_both]
    aliases = {}
    if so_far is not None:
        in_specs.append(pl.BlockSpec(memory_space=pl.ANY))
        operands.append(so_far)
        aliases = {2: 0}
    return pl.pallas_call(
        key_value_kernel,
        grid=(blocks // per,),
        in_specs=in_specs,
        out_specs=pl.BlockSpec((per, cluster, 2 * width), lambda i: (at // per + i, 0, 0)),
        out_shape=jax.ShapeDtypeStruct((total, cluster, 2 * width), jnp.bfloat16),
        input_output_aliases=aliases,
        cost_estimate=pl.CostEstimate(
            flops=4 * piece.size * width, bytes_accessed=6 * piece.size, transcendentals=0
        ),
        compiler_params=kernel_params(),
        name="keys_values",
    )(*operands)


def attend_kernel(table_ref, query_ref, own_ref, *rest, pair_count, head_width):
    listed_refs = rest[: STEP * pair_count]
    placed_ref, out_w_ref, mix_ref, mixed_ref = rest[STEP * pair_count :]
    cluster = own_ref.shape[1]
    width = placed_ref.shape[1]
    span = GROUP * head_width
    tile = GROUP * cluster
    diagonal = head_mask((span, tile), head_width, cluster)
    fold_row = lax.broadcasted_iota(jnp.int32, (cluster, tile), 0)
    fold_lane = lax.broadcasted_iota(jnp.int32, (cluster, tile), 1) % cluster
    fold = jnp.where(fold_row == fold_lane, 1.0, 0.0).astype(jnp.bfloat16)
    zeros = jnp.zeros((span, tile), jnp.bfloat16)
    ones = jnp.ones((16, tile), jnp.bfloat16)
    tiles = HEADS // GROUP
    units = [(block, t) for block in range(STEP) for t in range(tiles)]
    keys, values = {}, {}

    def gather(block):
        members = [own_ref[block]]
        members += [listed_refs[block * pair_count + j][0] for j in range(pair_count)]
        keys[block] = jnp.concatenate([m[:, :width] for m in members], axis=0)
        values[block] = jnp.concatenate([m[:, width:] for m in members], axis=0).T

    def scores_of(block, t):
        if t == 0:
            gather(block)
        lo = t * span // 128 * 128
        picked = query_ref[block, t * span : (t + 1) * span, :]
        ahead, behind = t * span - lo, lo + 128 - (t + 1) * span
        stack = [zeros] * (ahead // span) + [picked] + [zeros] * (behind // span)
        return jnp.dot(
            keys[block][:, lo : lo + 128],
            jnp.concatenate(stack, axis=0),
            preferred_element_type=jnp.float32,
        )

    lead = 2
    scores = [scores_of(*unit) for unit in units[:lead]]
    attended, pieces = [], []
    for at, (block, t) in enumerate(units):
        if at + lead < len(units):
            scores.append(scores_of(*units[at + lead]))
        current = scores[at]
        top = jnp.max(current, axis=0, keepdims=True)
        weights = jnp.exp(current - top).astype(jnp.bfloat16)
        lifted = jnp.concatenate([values[block][t * span : (t + 1) * span], ones], axis=0)
        result = jnp.dot(lifted, weights, preferred_element_type=jnp.float32)
        result = result[:span] * (1.0 / result[span : span + 1])
        pieces.append(jnp.where(diagonal, result, 0.0).astype(jnp.bfloat16))
        if t == tiles - 1:
            stacked = jnp.concatenate(pieces, axis=0)
            folded = lax.dot_general(fold, stacked, NT, preferred_element_type=jnp.float32)
            attended.append(folded.astype(jnp.bfloat16))
            pieces = []
    middle = placed_ref[...].astype(jnp.float32) + jnp.dot(
        jnp.concatenate(attended, axis=0), out_w_ref[...], preferred_element_type=jnp.float32
    )
    middle = middle.astype(jnp.bfloat16).astype(jnp.float32)
    second = layer_norm(middle).astype(jnp.bfloat16)
    mixed = middle + jnp.tanh(jnp.dot(second, mix_ref[...], preferred_element_type=jnp.float32))
    mixed_ref[...] = mixed.astype(jnp.bfloat16)


def attend(table, queries, pairs_buffer, own_at, placed, w_out, w_mix, pair_count):
    rows, width = placed.shape
    blocks, _, tile = queries.shape
    cluster = rows // blocks
    whole = pl.BlockSpec((width, width), lambda i, t: (0, 0))
    local = pl.BlockSpec((STEP * cluster, width), lambda i, t: (i, 0))

    def listed(j):
        return pl.BlockSpec(
            (1, cluster, 2 * width), lambda i, t: (t[i * STEP * pair_count + j], 0, 0)
        )

    return pl.pallas_call(
        functools.partial(attend_kernel, pair_count=pair_count, head_width=width // HEADS),
        grid_spec=pltpu.PrefetchScalarGridSpec(
            num_scalar_prefetch=1,
            grid=(blocks // STEP,),
            in_specs=[
                pl.BlockSpec((STEP, width, tile), lambda i, t: (i, 0, 0)),
                pl.BlockSpec((STEP, cluster, 2 * width), lambda i, t: (own_at // STEP + i, 0, 0)),
            ]
            + [listed(j) for j in range(STEP * pair_count)]
            + [local, whole, whole],
            out_specs=local,
        ),
        out_shape=jax.ShapeDtypeStruct((rows, width), jnp.bfloat16),
        cost_estimate=pl.CostEstimate(
            flops=4 * rows * HEADS * width * (pair_count + 1) * cluster,
            bytes_accessed=24 * rows * width,
            transcendentals=rows * HEADS * (pair_count + 1) * cluster,
        ),
        compiler_params=kernel_params(),
        name="attend_blocks",
    )(
        table,
        queries,
        pairs_buffer,
        *[pairs_buffer] * (STEP * pair_count),
        placed,
        w_out,
        w_mix,
    )


def slot_table(owner, within, capacity):
    entries = owner.shape[0]
    alike = owner[:, None] == owner[None, :]
    earlier = jnp.arange(entries)[None, :] < jnp.arange(entries)[:, None]
    ranking = jnp.sum(jnp.where(alike & earlier, 1, 0), axis=1).astype(jnp.int32)
    slots = owner * capacity + ranking
    matches = slots[None, :] == jnp.arange(SPAN * capacity, dtype=jnp.int32)[:, None]
    tables = jnp.sum(jnp.where(matches, within[None, :], 0), axis=1)
    return ranking, tables.reshape(SPAN, capacity)


def body(features, assignment, pairs, w_query, w_key, w_value, w_out, w_mix):
    rows_dev, width = features.shape
    block_count, pair_count = pairs.shape
    cluster = rows_dev // block_count
    peers = lax.axis_size("elec")
    stride = peers // SPAN
    groups = [[rest + place_ * stride for place_ in range(SPAN)] for rest in range(stride)]
    position = lax.axis_index("elec") // stride
    capacity = (block_count * pair_count + SPAN - 1) // SPAN + 1

    listed = pairs.reshape(-1)
    owner = listed // block_count // stride
    within = listed % block_count
    ranking, tables = slot_table(owner, within, capacity)
    demanded = lax.all_to_all(
        tables, "elec", split_axis=0, concat_axis=0, axis_index_groups=groups, tiled=True
    )

    placed, normed = place(
        features, assignment.reshape(block_count // SUB, 1, SUB * cluster)
    )
    blocks = normed.reshape(block_count, cluster, width)
    outgoing = pick(position.reshape(1), demanded, blocks)
    arrived = [
        lax.ppermute(piece, "elec", [(i, (i + (o + 1) * stride) % peers) for i in range(peers)])
        for o, piece in enumerate(outgoing)
    ]

    w_both = jnp.concatenate([w_key, w_value], axis=1)
    own_at = -((1 - SPAN) * capacity // block_count) * block_count
    total = own_at + block_count
    buffer = project_pairs(blocks, w_both, None, own_at, total)
    queries = project_queries(normed, w_query, cluster)
    for o, piece in enumerate(arrived):
        buffer = project_pairs(piece, w_both, buffer, o * capacity, total)
    offset = (position - owner) % SPAN
    table = jnp.where(offset == 0, own_at + within, (offset - 1) * capacity + ranking)
    return attend(table, queries, buffer, own_at, placed, w_out, w_mix, pair_count)


def solution(mesh):
    placed = (
        P(("groups", "elec"), None),
        P(("groups", "elec")),
        P(("groups", "elec"), None),
        P(),
        P(),
        P(),
        P(),
        P(),
    )
    return jax.shard_map(
        body, mesh=mesh, in_specs=placed, out_specs=P(("groups", "elec"), None), check_vma=False
    )
```

```python
import functools

import jax
import jax.numpy as jnp
from jax import lax
from jax.experimental import pallas as pl
from jax.experimental.pallas import tpu as pltpu
from jax.sharding import PartitionSpec as P

HEADS = 16
SPAN = 8
SUB = 8
GROUP = 4
STEP = 4
VMEM_BYTES = 48 * 1024 * 1024

NT = (((1,), (1,)), ((), ()))


def kernel_params():
    return pltpu.CompilerParams(vmem_limit_bytes=VMEM_BYTES)


def layer_norm(rows):
    mean = jnp.mean(rows, axis=-1, keepdims=True)
    centred = rows - mean
    variance = jnp.mean(centred * centred, axis=-1, keepdims=True)
    return centred * lax.rsqrt(variance + 1e-05)


def head_mask(shape, head_width, cluster):
    row_head = lax.broadcasted_iota(jnp.int32, shape, 0) // head_width % GROUP
    lane_head = lax.broadcasted_iota(jnp.int32, shape, 1) // cluster
    return row_head == lane_head


def place_kernel(features_ref, assignment_ref, normed_ref, *placed_ref):
    rows = features_ref.shape[0]
    lane = 128
    features = features_ref[...]
    columns = lax.broadcasted_iota(jnp.int32, (lane, rows), 1)
    for part in range(rows // lane):
        chosen = assignment_ref[0, :, part * lane : (part + 1) * lane] & (rows - 1)
        chosen = jnp.broadcast_to(chosen, (lane, lane)).T
        chosen = jnp.concatenate([chosen] * (rows // lane), axis=1)
        one_hot = jnp.where(chosen == columns, 1.0, 0.0).astype(jnp.bfloat16)
        placed = jnp.dot(one_hot, features, preferred_element_type=jnp.float32)
        if placed_ref:
            placed_ref[0][pl.ds(part * lane, lane), :] = placed.astype(jnp.bfloat16)
        normed_ref[pl.ds(part * lane, lane), :] = layer_norm(placed).astype(jnp.bfloat16)


def place(features, assignment, outputs):
    width = features.shape[1]
    walkers, _, rows = assignment.shape
    local = pl.BlockSpec((rows, width), lambda i: (i, 0))
    out = jax.ShapeDtypeStruct(features.shape, jnp.bfloat16)
    return pl.pallas_call(
        place_kernel,
        grid=(walkers,),
        in_specs=[local, pl.BlockSpec((1, 1, rows), lambda i: (i, 0, 0))],
        out_specs=[local] * outputs,
        out_shape=[out] * outputs,
        cost_estimate=pl.CostEstimate(
            flops=2 * walkers * rows * rows * width,
            bytes_accessed=6 * walkers * rows * width,
            transcendentals=0,
        ),
        compiler_params=kernel_params(),
        name="place_rows",
    )(features, assignment)


def choose(index, values):
    result = values[-1]
    for at in range(len(values) - 2, -1, -1):
        result = jnp.where(index == at, values[at], result)
    return result


def pick_kernel(position_ref, wanted_ref, blocks_ref, *out_refs, plan, capacity):
    position = position_ref[0]
    for out_ref, pieces in zip(out_refs, plan, strict=True):
        for at, (reader_of, owner_of) in enumerate(pieces):
            reader, first = reader_of(position), owner_of(position) * capacity

            def one_slot(slot, carry, out_ref=out_ref, at=at, reader=reader, first=first):
                out_ref[at * capacity + slot] = blocks_ref[wanted_ref[reader, first + slot]]
                return carry

            lax.fori_loop(0, capacity, one_slot, 0)


def pick(position, wanted, blocks, plan):
    capacity = wanted.shape[1] // SPAN
    outs = [
        jax.ShapeDtypeStruct((len(pieces) * capacity,) + blocks.shape[1:], blocks.dtype)
        for pieces in plan
    ]
    smem = pl.BlockSpec(memory_space=pltpu.SMEM)
    vmem = pl.BlockSpec(memory_space=pltpu.VMEM)
    return pl.pallas_call(
        functools.partial(pick_kernel, plan=plan, capacity=capacity),
        in_specs=[smem, smem, vmem],
        out_specs=[vmem] * len(outs),
        out_shape=outs,
        cost_estimate=pl.CostEstimate(
            flops=0, bytes_accessed=4 * sum(out.size for out in outs), transcendentals=0
        ),
        compiler_params=kernel_params(),
        name="pick_blocks",
    )(position, wanted, blocks)


def query_kernel(normed_ref, query_w_ref, query_ref, *, cluster, head_width):
    width = normed_ref.shape[1]
    mask = head_mask((width, GROUP * cluster), head_width, cluster)
    for block in range(query_ref.shape[0]):
        own = normed_ref[pl.ds(block * cluster, cluster), :]
        own = jnp.concatenate([own] * GROUP, axis=0)
        query = lax.dot_general(query_w_ref[...], own, NT, preferred_element_type=jnp.float32)
        query = query.astype(jnp.bfloat16) * jnp.bfloat16(1.0 / head_width**0.5)
        query_ref[block] = jnp.where(mask, query, jnp.bfloat16(0.0))


def project_queries(normed, w_query, cluster):
    rows, width = normed.shape
    blocks = rows // cluster
    return pl.pallas_call(
        functools.partial(query_kernel, cluster=cluster, head_width=width // HEADS),
        grid=(blocks // SUB,),
        in_specs=[
            pl.BlockSpec((SUB * cluster, width), lambda i: (i, 0)),
            pl.BlockSpec((width, width), lambda i: (0, 0)),
        ],
        out_specs=pl.BlockSpec((SUB, width, GROUP * cluster), lambda i: (i, 0, 0)),
        out_shape=jax.ShapeDtypeStruct((blocks, width, GROUP * cluster), jnp.bfloat16),
        cost_estimate=pl.CostEstimate(
            flops=2 * rows * GROUP * width * width,
            bytes_accessed=2 * rows * width * (GROUP + 1),
            transcendentals=0,
        ),
        compiler_params=kernel_params(),
        name="queries",
    )(normed, w_query.T)


def key_value_kernel(rows_ref, w_ref, *rest):
    out_ref = rest[-1]
    blocks, cluster, width = rows_ref.shape
    rows = rows_ref[...].reshape(blocks * cluster, width)
    both = jnp.dot(rows, w_ref[...], preferred_element_type=jnp.float32)
    out_ref[...] = both.astype(jnp.bfloat16).reshape(out_ref.shape)


def project_pairs(piece, w_both, so_far, at, total, blocks):
    _, cluster, width = piece.shape
    per = max(n for n in range(1, 9) if blocks % n == 0 and at % n == 0)
    in_specs = [
        pl.BlockSpec((per, cluster, width), lambda i: (i, 0, 0)),
        pl.BlockSpec((width, 2 * width), lambda i: (0, 0)),
    ]
    operands = [piece, w_both]
    aliases = {}
    if so_far is not None:
        in_specs.append(pl.BlockSpec(memory_space=pl.ANY))
        operands.append(so_far)
        aliases = {2: 0}
    return pl.pallas_call(
        key_value_kernel,
        grid=(blocks // per,),
        in_specs=in_specs,
        out_specs=pl.BlockSpec((per, cluster, 2 * width), lambda i: (at // per + i, 0, 0)),
        out_shape=jax.ShapeDtypeStruct((total, cluster, 2 * width), jnp.bfloat16),
        input_output_aliases=aliases,
        cost_estimate=pl.CostEstimate(
            flops=4 * blocks * cluster * width * width,
            bytes_accessed=6 * blocks * cluster * width,
            transcendentals=0,
        ),
        compiler_params=kernel_params(),
        name="keys_values",
    )(*operands)


def attend_kernel(table_ref, query_ref, own_ref, *rest, pair_count, head_width):
    listed_refs = rest[: STEP * pair_count]
    placed_ref, out_w_ref, mix_ref, mixed_ref = rest[STEP * pair_count :]
    cluster = own_ref.shape[1]
    width = placed_ref.shape[1]
    span = GROUP * head_width
    tile = GROUP * cluster
    diagonal = head_mask((span, tile), head_width, cluster)
    fold_row = lax.broadcasted_iota(jnp.int32, (cluster, tile), 0)
    fold_lane = lax.broadcasted_iota(jnp.int32, (cluster, tile), 1) % cluster
    fold = jnp.where(fold_row == fold_lane, 1.0, 0.0).astype(jnp.bfloat16)
    zeros = jnp.zeros((span, tile), jnp.bfloat16)
    ones = jnp.ones((16, tile), jnp.bfloat16)
    tiles = HEADS // GROUP
    units = [(block, t) for block in range(STEP) for t in range(tiles)]
    keys, values = {}, {}

    def gather(block):
        members = [own_ref[block]]
        members += [listed_refs[block * pair_count + j][0] for j in range(pair_count)]
        keys[block] = jnp.concatenate([m[:, :width] for m in members], axis=0)
        values[block] = jnp.concatenate([m[:, width:] for m in members], axis=0).T

    def scores_of(block, t):
        if t == 0:
            gather(block)
        lo = t * span // 128 * 128
        picked = query_ref[block, t * span : (t + 1) * span, :]
        ahead, behind = t * span - lo, lo + 128 - (t + 1) * span
        stack = [zeros] * (ahead // span) + [picked] + [zeros] * (behind // span)
        return jnp.dot(
            keys[block][:, lo : lo + 128],
            jnp.concatenate(stack, axis=0),
            preferred_element_type=jnp.float32,
        )

    lead = 2
    scores = [scores_of(*unit) for unit in units[:lead]]
    attended, pieces = [], []
    for at, (block, t) in enumerate(units):
        if at + lead < len(units):
            scores.append(scores_of(*units[at + lead]))
        current = scores[at]
        top = jnp.max(current, axis=0, keepdims=True)
        weights = jnp.exp(current - top).astype(jnp.bfloat16)
        lifted = jnp.concatenate([values[block][t * span : (t + 1) * span], ones], axis=0)
        result = jnp.dot(lifted, weights, preferred_element_type=jnp.float32)
        result = result[:span] * (1.0 / result[span : span + 1])
        pieces.append(jnp.where(diagonal, result, 0.0).astype(jnp.bfloat16))
        if t == tiles - 1:
            stacked = jnp.concatenate(pieces, axis=0)
            folded = lax.dot_general(fold, stacked, NT, preferred_element_type=jnp.float32)
            attended.append(folded.astype(jnp.bfloat16))
            pieces = []
    middle = placed_ref[...].astype(jnp.float32) + jnp.dot(
        jnp.concatenate(attended, axis=0), out_w_ref[...], preferred_element_type=jnp.float32
    )
    middle = middle.astype(jnp.bfloat16).astype(jnp.float32)
    second = layer_norm(middle).astype(jnp.bfloat16)
    mixed = middle + jnp.tanh(jnp.dot(second, mix_ref[...], preferred_element_type=jnp.float32))
    mixed_ref[...] = mixed.astype(jnp.bfloat16)


def attend(table, queries, pairs_buffer, own_at, placed, w_out, w_mix, pair_count):
    rows, width = placed.shape
    blocks, _, tile = queries.shape
    cluster = rows // blocks
    whole = pl.BlockSpec((width, width), lambda i, t: (0, 0))
    local = pl.BlockSpec((STEP * cluster, width), lambda i, t: (i, 0))

    def listed(j):
        return pl.BlockSpec(
            (1, cluster, 2 * width), lambda i, t: (t[i * STEP * pair_count + j], 0, 0)
        )

    return pl.pallas_call(
        functools.partial(attend_kernel, pair_count=pair_count, head_width=width // HEADS),
        grid_spec=pltpu.PrefetchScalarGridSpec(
            num_scalar_prefetch=1,
            grid=(blocks // STEP,),
            in_specs=[
                pl.BlockSpec((STEP, width, tile), lambda i, t: (i, 0, 0)),
                pl.BlockSpec((STEP, cluster, 2 * width), lambda i, t: (own_at // STEP + i, 0, 0)),
            ]
            + [listed(j) for j in range(STEP * pair_count)]
            + [local, whole, whole],
            out_specs=local,
        ),
        out_shape=jax.ShapeDtypeStruct((rows, width), jnp.bfloat16),
        cost_estimate=pl.CostEstimate(
            flops=4 * rows * HEADS * width * (pair_count + 1) * cluster,
            bytes_accessed=24 * rows * width,
            transcendentals=rows * HEADS * (pair_count + 1) * cluster,
        ),
        compiler_params=kernel_params(),
        name="attend_blocks",
    )(
        table,
        queries,
        pairs_buffer,
        *[pairs_buffer] * (STEP * pair_count),
        placed,
        w_out,
        w_mix,
    )


def slot_table(owner, within, capacity):
    entries = owner.shape[0]
    alike = owner[:, None] == owner[None, :]
    earlier = jnp.arange(entries)[None, :] < jnp.arange(entries)[:, None]
    ranking = jnp.sum(jnp.where(alike & earlier, 1, 0), axis=1).astype(jnp.int32)
    slots = owner * capacity + ranking
    matches = slots[None, :] == jnp.arange(SPAN * capacity, dtype=jnp.int32)[:, None]
    tables = jnp.sum(jnp.where(matches, within[None, :], 0), axis=1)
    return ranking, tables.reshape(SPAN, capacity)


OUT = (2, 0, 3, 1)
FROM = (1, 3, 0, 2)
LEVELS = 4


def position_at(z, y):
    return 2 * z + y


def partner(position):
    return position ^ 1


def onward(position):
    return position_at(choose(position // 2, OUT), position % 2)


def source(position):
    return position_at(choose(position // 2, FROM), position % 2)


def opposite(position):
    return position_at(LEVELS - 1 - position // 2, position % 2)


def itself(position):
    return position


def crossed(route):
    return lambda position: partner(route(position))


OWN_PLAN = (
    ((partner, itself),),
    ((source, itself), (crossed(source), itself)),
    ((opposite, itself), (crossed(opposite), itself)),
)
PASSED_PLAN = (
    ((partner, source), (crossed(onward), source)),
    ((onward, source),),
)


def body(features, assignment, pairs, w_query, w_key, w_value, w_out, w_mix):
    rows_dev, width = features.shape
    block_count, pair_count = pairs.shape
    cluster = rows_dev // block_count
    stride = lax.axis_size("elec") // SPAN
    groups = [[rest + place_ * stride for place_ in range(SPAN)] for rest in range(stride)]
    position = lax.axis_index("elec") // stride
    capacity = (block_count * pair_count + SPAN - 1) // SPAN + 1

    def moved(x, moves):
        pairs_of = [(s * stride + r, d * stride + r) for s, d in moves for r in range(stride)]
        return lax.ppermute(x, "elec", pairs_of)

    def across_z(pairs_of_z):
        return [(position_at(s, y), position_at(d, y)) for s, d in pairs_of_z for y in range(2)]

    swap = [(p, p ^ 1) for p in range(SPAN)]
    first_moves = across_z(enumerate(OUT))
    second_moves = across_z(enumerate(FROM))
    middle_moves = across_z([(1, 2), (2, 1)])
    outward_moves = across_z([(2, 3), (1, 0)])

    raw = moved(features, first_moves)
    raw_assignment = moved(assignment, first_moves)

    listed = pairs.reshape(-1)
    owner = listed // block_count // stride
    within = listed % block_count
    ranking, tables = slot_table(owner, within, capacity)
    wanted = lax.all_to_all(
        jnp.broadcast_to(tables.reshape(1, -1), (SPAN, SPAN * capacity)),
        "elec",
        split_axis=0,
        concat_axis=0,
        axis_index_groups=groups,
        tiled=True,
    )
    at_position = position.reshape(1)

    walker_shape = (block_count // SUB, 1, SUB * cluster)
    block_shape = (block_count, cluster, width)
    normed, placed = place(features, assignment.reshape(walker_shape), 2)
    blocks = normed.reshape(block_shape)
    near, second, middle = pick(at_position, wanted, blocks, OWN_PLAN)
    near = moved(near, swap)
    second = moved(second, second_moves)
    middle = moved(middle, middle_moves)

    (passed,) = place(raw, raw_assignment.reshape(walker_shape), 1)
    passed = passed.reshape(block_shape)
    beside, outward = pick(at_position, wanted, passed, PASSED_PLAN)
    outward = moved(outward, outward_moves)
    beside = moved(beside, swap)
    second_beside = moved(second[capacity:], swap)
    outward_beside = moved(beside[capacity:], outward_moves)
    middle_beside = moved(middle[capacity:], swap)

    w_both = jnp.concatenate([w_key, w_value], axis=1)
    pieces = [near, second, second_beside, beside, middle, outward, middle_beside, outward_beside]
    own_at = len(pieces) * capacity
    passed_at = own_at + block_count
    total = passed_at + block_count
    buffer = project_pairs(blocks, w_both, None, own_at, total, block_count)
    queries = project_queries(normed, w_query, cluster)
    buffer = project_pairs(passed, w_both, buffer, passed_at, total, block_count)
    for at, piece in enumerate(pieces):
        buffer = project_pairs(piece, w_both, buffer, at * capacity, total, capacity)

    z, y = position // 2, position % 2
    is_end = (z == 0) | (z == LEVELS - 1)
    z_owner, same = owner // 2, owner % 2 == y
    from_first = z_owner == choose(z, FROM)
    from_second = z_owner == choose(z, OUT)
    piece_of = jnp.where(
        z_owner == z,
        0,
        jnp.where(
            from_first,
            3,
            jnp.where(
                from_second,
                jnp.where(same, 1, 2),
                jnp.where(is_end, jnp.where(same, 5, 7), jnp.where(same, 4, 6)),
            ),
        ),
    )
    whole_at = jnp.where(z_owner == z, own_at, passed_at)
    whole = same & ((z_owner == z) | from_first)
    table = jnp.where(whole, whole_at + within, piece_of * capacity + ranking)
    return attend(table, queries, buffer, own_at, placed, w_out, w_mix, pair_count)


def solution(mesh):
    placed = (
        P(("groups", "elec"), None),
        P(("groups", "elec")),
        P(("groups", "elec"), None),
        P(),
        P(),
        P(),
        P(),
        P(),
    )
    return jax.shard_map(
        body, mesh=mesh, in_specs=placed, out_specs=P(("groups", "elec"), None), check_vma=False
    )
```

```python
import functools

import jax
import jax.numpy as jnp
from jax import lax
from jax.experimental import pallas as pl
from jax.experimental.pallas import tpu as pltpu
from jax.sharding import PartitionSpec as P

HEADS = 16
SPAN = 8
SUB = 8
GROUP = 4
STEP = 4
HEAD_WALKERS = 3
VMEM_BYTES = 48 * 1024 * 1024

NT = (((1,), (1,)), ((), ()))
SHORT = pl.CostEstimate(flops=0, bytes_accessed=0, transcendentals=0)


def kernel_params():
    return pltpu.CompilerParams(vmem_limit_bytes=VMEM_BYTES)


def layer_norm(rows):
    mean = jnp.mean(rows, axis=-1, keepdims=True)
    centred = rows - mean
    variance = jnp.mean(centred * centred, axis=-1, keepdims=True)
    return centred * lax.rsqrt(variance + 1e-05)


def head_mask(shape, head_width, cluster):
    row_head = lax.broadcasted_iota(jnp.int32, shape, 0) // head_width % GROUP
    lane_head = lax.broadcasted_iota(jnp.int32, shape, 1) // cluster
    return row_head == lane_head


def place_kernel(features_ref, assignment_ref, *rest, outputs):
    normed_ref, *placed_ref = rest[len(rest) - outputs :]
    rows = features_ref.shape[0]
    lane = 128
    features = features_ref[...]
    columns = lax.broadcasted_iota(jnp.int32, (lane, rows), 1)
    for part in range(rows // lane):
        chosen = assignment_ref[0, :, part * lane : (part + 1) * lane] & (rows - 1)
        chosen = jnp.broadcast_to(chosen, (lane, lane)).T
        chosen = jnp.concatenate([chosen] * (rows // lane), axis=1)
        one_hot = jnp.where(chosen == columns, 1.0, 0.0).astype(jnp.bfloat16)
        placed = jnp.dot(one_hot, features, preferred_element_type=jnp.float32)
        if placed_ref:
            placed_ref[0][pl.ds(part * lane, lane), :] = placed.astype(jnp.bfloat16)
        normed_ref[pl.ds(part * lane, lane), :] = layer_norm(placed).astype(jnp.bfloat16)


def place(features, assignment, outputs, first=0, so_far=None, after=()):
    count, width = features.shape
    walkers, _, rows = assignment.shape
    out = jax.ShapeDtypeStruct((walkers * rows, width), jnp.bfloat16)
    extra = [x for x in (so_far,) if x is not None] + list(after)
    return pl.pallas_call(
        functools.partial(place_kernel, outputs=outputs),
        grid=(count // rows,),
        in_specs=[
            pl.BlockSpec((rows, width), lambda i: (i, 0)),
            pl.BlockSpec((1, 1, rows), lambda i: (first + i, 0, 0)),
        ]
        + [pl.BlockSpec(memory_space=pl.ANY)] * len(extra),
        out_specs=[pl.BlockSpec((rows, width), lambda i: (first + i, 0))] * outputs,
        out_shape=[out] * outputs,
        input_output_aliases={} if so_far is None else {2: 0},
        cost_estimate=SHORT,
        compiler_params=kernel_params(),
        name="place_rows",
    )(features, assignment, *extra)


def tail_kernel(features_ref, *rest):
    out_ref = rest[-1]
    out_ref[...] = features_ref[...]


def tail_rows(features, rows, first, after):
    total, width = features.shape
    count = total - first * rows
    return pl.pallas_call(
        tail_kernel,
        grid=(count // rows,),
        in_specs=[pl.BlockSpec((rows, width), lambda i: (first + i, 0))]
        + [pl.BlockSpec(memory_space=pl.ANY)] * len(after),
        out_specs=pl.BlockSpec((rows, width), lambda i: (i, 0)),
        out_shape=jax.ShapeDtypeStruct((count, width), features.dtype),
        cost_estimate=SHORT,
        compiler_params=kernel_params(),
        name="tail_rows",
    )(features, *after)


def choose(index, values):
    result = values[-1]
    for at in range(len(values) - 2, -1, -1):
        result = jnp.where(index == at, values[at], result)
    return result


def pick_kernel(position_ref, wanted_ref, *rest, plan, capacity):
    position = position_ref[0]
    for out_ref, pieces in zip(rest[len(rest) - len(plan) :], plan, strict=True):
        for at, (blocks, reader_of, owner_of) in enumerate(pieces):
            reader, first = reader_of(position), owner_of(position) * capacity

            def one_slot(slot, carry, out_ref=out_ref, at=at, blocks=blocks, reader=reader, first=first):
                out_ref[at * capacity + slot] = rest[blocks][wanted_ref[reader, first + slot]]
                return carry

            lax.fori_loop(0, capacity, one_slot, 0)


def pick(position, wanted, sources, plan, after=()):
    capacity = wanted.shape[1] // SPAN
    block = sources[0].shape[1:]
    outs = [
        jax.ShapeDtypeStruct((len(pieces) * capacity,) + block, sources[0].dtype)
        for pieces in plan
    ]
    smem = pl.BlockSpec(memory_space=pltpu.SMEM)
    vmem = pl.BlockSpec(memory_space=pltpu.VMEM)
    return pl.pallas_call(
        functools.partial(pick_kernel, plan=plan, capacity=capacity),
        in_specs=[smem, smem]
        + [vmem] * len(sources)
        + [pl.BlockSpec(memory_space=pl.ANY)] * len(after),
        out_specs=[vmem] * len(outs),
        out_shape=outs,
        cost_estimate=SHORT,
        compiler_params=kernel_params(),
        name="pick_blocks",
    )(position, wanted, *sources, *after)


def query_kernel(normed_ref, query_w_ref, query_ref, *, cluster, head_width):
    width = normed_ref.shape[1]
    mask = head_mask((width, GROUP * cluster), head_width, cluster)
    for block in range(query_ref.shape[0]):
        own = normed_ref[pl.ds(block * cluster, cluster), :]
        own = jnp.concatenate([own] * GROUP, axis=0)
        query = lax.dot_general(query_w_ref[...], own, NT, preferred_element_type=jnp.float32)
        query = query.astype(jnp.bfloat16) * jnp.bfloat16(1.0 / head_width**0.5)
        query_ref[block] = jnp.where(mask, query, jnp.bfloat16(0.0))


def project_queries(normed, w_query, cluster):
    rows, width = normed.shape
    blocks = rows // cluster
    return pl.pallas_call(
        functools.partial(query_kernel, cluster=cluster, head_width=width // HEADS),
        grid=(blocks // SUB,),
        in_specs=[
            pl.BlockSpec((SUB * cluster, width), lambda i: (i, 0)),
            pl.BlockSpec((width, width), lambda i: (0, 0)),
        ],
        out_specs=pl.BlockSpec((SUB, width, GROUP * cluster), lambda i: (i, 0, 0)),
        out_shape=jax.ShapeDtypeStruct((blocks, width, GROUP * cluster), jnp.bfloat16),
        cost_estimate=SHORT,
        compiler_params=kernel_params(),
        name="queries",
    )(normed, w_query.T)


def key_value_kernel(rows_ref, w_ref, *rest):
    out_ref = rest[-1]
    blocks, cluster, width = rows_ref.shape
    per = max(n for n in range(1, 9) if blocks % n == 0)

    def some(at, carry):
        here = pl.ds(at * per, per)
        rows = rows_ref[here].reshape(per * cluster, width)
        both = jnp.dot(rows, w_ref[...], preferred_element_type=jnp.float32)
        out_ref[here] = both.astype(jnp.bfloat16).reshape((per,) + out_ref.shape[1:])
        return carry

    lax.fori_loop(0, blocks // per, some, 0)


def project_pairs(piece, w_both, so_far, at, total):
    blocks, cluster, width = piece.shape
    per = max(n for n in range(1, 33) if blocks % n == 0 and at % n == 0)
    in_specs = [
        pl.BlockSpec((per, cluster, width), lambda i: (i, 0, 0)),
        pl.BlockSpec((width, 2 * width), lambda i: (0, 0)),
    ]
    operands = [piece, w_both]
    aliases = {}
    if so_far is not None:
        in_specs.append(pl.BlockSpec(memory_space=pl.ANY))
        operands.append(so_far)
        aliases = {2: 0}
    return pl.pallas_call(
        key_value_kernel,
        grid=(blocks // per,),
        in_specs=in_specs,
        out_specs=pl.BlockSpec((per, cluster, 2 * width), lambda i: (at // per + i, 0, 0)),
        out_shape=jax.ShapeDtypeStruct((total, cluster, 2 * width), jnp.bfloat16),
        input_output_aliases=aliases,
        cost_estimate=SHORT,
        compiler_params=kernel_params(),
        name="keys_values",
    )(*operands)


def attend_kernel(table_ref, query_ref, own_ref, *rest, pair_count, head_width):
    listed_refs = rest[: STEP * pair_count]
    placed_ref, out_w_ref, mix_ref, mixed_ref = rest[STEP * pair_count :]
    cluster = own_ref.shape[1]
    width = placed_ref.shape[1]
    span = GROUP * head_width
    tile = GROUP * cluster
    diagonal = head_mask((span, tile), head_width, cluster)
    fold_row = lax.broadcasted_iota(jnp.int32, (cluster, tile), 0)
    fold_lane = lax.broadcasted_iota(jnp.int32, (cluster, tile), 1) % cluster
    fold = jnp.where(fold_row == fold_lane, 1.0, 0.0).astype(jnp.bfloat16)
    zeros = jnp.zeros((span, tile), jnp.bfloat16)
    ones = jnp.ones((16, tile), jnp.bfloat16)
    tiles = HEADS // GROUP
    units = [(block, t) for block in range(STEP) for t in range(tiles)]
    keys, values = {}, {}

    def gather(block):
        members = [own_ref[block]]
        members += [listed_refs[block * pair_count + j][0] for j in range(pair_count)]
        keys[block] = jnp.concatenate([m[:, :width] for m in members], axis=0)
        values[block] = jnp.concatenate([m[:, width:] for m in members], axis=0).T

    def scores_of(block, t):
        if t == 0:
            gather(block)
        lo = t * span // 128 * 128
        picked = query_ref[block, t * span : (t + 1) * span, :]
        ahead, behind = t * span - lo, lo + 128 - (t + 1) * span
        stack = [zeros] * (ahead // span) + [picked] + [zeros] * (behind // span)
        return jnp.dot(
            keys[block][:, lo : lo + 128],
            jnp.concatenate(stack, axis=0),
            preferred_element_type=jnp.float32,
        )

    lead = 2
    scores = [scores_of(*unit) for unit in units[:lead]]
    attended, pieces = [], []
    for at, (block, t) in enumerate(units):
        if at + lead < len(units):
            scores.append(scores_of(*units[at + lead]))
        current = scores[at]
        top = jnp.max(current, axis=0, keepdims=True)
        weights = jnp.exp(current - top).astype(jnp.bfloat16)
        lifted = jnp.concatenate([values[block][t * span : (t + 1) * span], ones], axis=0)
        result = jnp.dot(lifted, weights, preferred_element_type=jnp.float32)
        result = result[:span] * (1.0 / result[span : span + 1])
        pieces.append(jnp.where(diagonal, result, 0.0).astype(jnp.bfloat16))
        if t == tiles - 1:
            stacked = jnp.concatenate(pieces, axis=0)
            folded = lax.dot_general(fold, stacked, NT, preferred_element_type=jnp.float32)
            attended.append(folded.astype(jnp.bfloat16))
            pieces = []
    middle = placed_ref[...].astype(jnp.float32) + jnp.dot(
        jnp.concatenate(attended, axis=0), out_w_ref[...], preferred_element_type=jnp.float32
    )
    middle = middle.astype(jnp.bfloat16).astype(jnp.float32)
    second = layer_norm(middle).astype(jnp.bfloat16)
    mixed = middle + jnp.tanh(jnp.dot(second, mix_ref[...], preferred_element_type=jnp.float32))
    mixed_ref[...] = mixed.astype(jnp.bfloat16)


def attend(table, queries, pairs_buffer, own_at, placed, w_out, w_mix, pair_count):
    rows, width = placed.shape
    blocks, _, tile = queries.shape
    cluster = rows // blocks
    whole = pl.BlockSpec((width, width), lambda i, t: (0, 0))
    local = pl.BlockSpec((STEP * cluster, width), lambda i, t: (i, 0))

    def listed(j):
        return pl.BlockSpec(
            (1, cluster, 2 * width), lambda i, t: (t[i * STEP * pair_count + j], 0, 0)
        )

    return pl.pallas_call(
        functools.partial(attend_kernel, pair_count=pair_count, head_width=width // HEADS),
        grid_spec=pltpu.PrefetchScalarGridSpec(
            num_scalar_prefetch=1,
            grid=(blocks // STEP,),
            in_specs=[
                pl.BlockSpec((STEP, width, tile), lambda i, t: (i, 0, 0)),
                pl.BlockSpec((STEP, cluster, 2 * width), lambda i, t: (own_at // STEP + i, 0, 0)),
            ]
            + [listed(j) for j in range(STEP * pair_count)]
            + [local, whole, whole],
            out_specs=local,
        ),
        out_shape=jax.ShapeDtypeStruct((rows, width), jnp.bfloat16),
        cost_estimate=SHORT,
        compiler_params=kernel_params(),
        name="attend_blocks",
    )(
        table,
        queries,
        pairs_buffer,
        *[pairs_buffer] * (STEP * pair_count),
        placed,
        w_out,
        w_mix,
    )


def slot_table(owner, within, capacity):
    entries = owner.shape[0]
    alike = owner[:, None] == owner[None, :]
    earlier = jnp.arange(entries)[None, :] < jnp.arange(entries)[:, None]
    ranking = jnp.sum(jnp.where(alike & earlier, 1, 0), axis=1).astype(jnp.int32)
    slots = owner * capacity + ranking
    matches = slots[None, :] == jnp.arange(SPAN * capacity, dtype=jnp.int32)[:, None]
    tables = jnp.sum(jnp.where(matches, within[None, :], 0), axis=1)
    return ranking, tables.reshape(SPAN, capacity)


OUT = (2, 0, 3, 1)
FROM = (1, 3, 0, 2)
LEVELS = 4


def position_at(z, y):
    return 2 * z + y


def partner(position):
    return position ^ 1


def onward(position):
    return position_at(choose(position // 2, OUT), position % 2)


def source(position):
    return position_at(choose(position // 2, FROM), position % 2)


def opposite(position):
    return position_at(LEVELS - 1 - position // 2, position % 2)


def itself(position):
    return position


def crossed(route):
    return lambda position: partner(route(position))


FIRST_PLAN = (((0, source, itself),), ((0, crossed(source), itself),))
MIDDLE_PLAN = (((0, opposite, itself),), ((0, crossed(opposite), itself),))
ON_PLAN = (((0, crossed(onward), source),),)
BESIDE_PLAN = (((0, partner, itself), (1, partner, source)),)
OUTWARD_PLAN = (((0, onward, source),),)


def body(features, assignment, pairs, w_query, w_key, w_value, w_out, w_mix):
    rows_dev, width = features.shape
    block_count, pair_count = pairs.shape
    cluster = rows_dev // block_count
    stride = lax.axis_size("elec") // SPAN
    groups = [[rest + place_ * stride for place_ in range(SPAN)] for rest in range(stride)]
    position = lax.axis_index("elec") // stride
    capacity = (block_count * pair_count + SPAN - 1) // SPAN + 1

    def moved(x, moves):
        pairs_of = [(s * stride + r, d * stride + r) for s, d in moves for r in range(stride)]
        return lax.ppermute(x, "elec", pairs_of)

    def across_z(pairs_of_z):
        return [(position_at(s, y), position_at(d, y)) for s, d in pairs_of_z for y in range(2)]

    swap = [(p, p ^ 1) for p in range(SPAN)]
    first_moves = across_z(enumerate(OUT))
    second_moves = across_z(enumerate(FROM))
    middle_moves = across_z([(1, 2), (2, 1)])

    def cross(moves):
        return [(s, d ^ 1) for s, d in moves]

    outward_moves = across_z([(2, 3), (1, 0)])

    rows = SUB * cluster
    raw_head = moved(features[: HEAD_WALKERS * rows], first_moves)
    raw_assignment = moved(assignment, first_moves)

    listed = pairs.reshape(-1)
    owner = listed // block_count // stride
    within = listed % block_count
    ranking, tables = slot_table(owner, within, capacity)
    wanted = lax.all_to_all(
        jnp.broadcast_to(tables.reshape(1, -1), (SPAN, SPAN * capacity)),
        "elec",
        split_axis=0,
        concat_axis=0,
        axis_index_groups=groups,
        tiled=True,
    )
    at_position = position.reshape(1)
    raw_tail = moved(tail_rows(features, rows, HEAD_WALKERS, (wanted, raw_head)), first_moves)

    walker_shape = (block_count // SUB, 1, rows)
    block_shape = (block_count, cluster, width)
    normed, placed = place(features, assignment.reshape(walker_shape), 2)
    blocks = normed.reshape(block_shape)
    raw_assignment = raw_assignment.reshape(walker_shape)
    (passed,) = place(raw_head, raw_assignment, 1)
    second, second_cross = pick(at_position, wanted, (blocks,), FIRST_PLAN, after=(passed,))
    second = moved(second, second_moves)
    second_cross = moved(second_cross, cross(second_moves))

    w_both = jnp.concatenate([w_key, w_value], axis=1)
    own_at = 8 * capacity
    passed_at = own_at + block_count
    total = passed_at + block_count
    buffer = project_pairs(blocks, w_both, None, own_at, total)
    queries = project_queries(normed, w_query, cluster)

    (passed,) = place(
        raw_tail, raw_assignment, 1, first=HEAD_WALKERS, so_far=passed, after=(buffer, queries)
    )
    middle, middle_cross = pick(at_position, wanted, (blocks,), MIDDLE_PLAN, after=(raw_tail,))
    middle = moved(middle, middle_moves)
    middle_cross = moved(middle_cross, cross(middle_moves))
    passed = passed.reshape(block_shape)
    (on,) = pick(at_position, wanted, (passed,), ON_PLAN)
    on = moved(on, swap)
    (beside,) = pick(at_position, wanted, (blocks, passed), BESIDE_PLAN)
    beside = moved(beside, swap)
    (outward,) = pick(at_position, wanted, (passed,), OUTWARD_PLAN)
    outward = moved(outward, outward_moves)
    on = moved(on, outward_moves)

    buffer = project_pairs(passed, w_both, buffer, passed_at, total)
    at = 0
    for piece in (second, second_cross, beside, outward, on, middle, middle_cross):
        buffer = project_pairs(piece, w_both, buffer, at, total)
        at += piece.shape[0]

    z, y = position // 2, position % 2
    is_end = (z == 0) | (z == LEVELS - 1)
    z_owner, same = owner // 2, owner % 2 == y
    from_first = z_owner == choose(z, FROM)
    from_second = z_owner == choose(z, OUT)
    piece_of = jnp.where(
        z_owner == z,
        2,
        jnp.where(
            from_first,
            3,
            jnp.where(
                from_second,
                jnp.where(same, 0, 1),
                jnp.where(is_end, jnp.where(same, 4, 5), jnp.where(same, 6, 7)),
            ),
        ),
    )
    whole_at = jnp.where(z_owner == z, own_at, passed_at)
    whole = same & ((z_owner == z) | from_first)
    table = jnp.where(whole, whole_at + within, piece_of * capacity + ranking)
    return attend(table, queries, buffer, own_at, placed, w_out, w_mix, pair_count)


def solution(mesh):
    placed = (
        P(("groups", "elec"), None),
        P(("groups", "elec")),
        P(("groups", "elec"), None),
        P(),
        P(),
        P(),
        P(),
        P(),
    )
    return jax.shard_map(
        body, mesh=mesh, in_specs=placed, out_specs=P(("groups", "elec"), None), check_vma=False
    )
```

```python
import functools

import jax
import jax.numpy as jnp
from jax import lax
from jax.experimental import pallas as pl
from jax.experimental.pallas import tpu as pltpu
from jax.sharding import PartitionSpec as P

HEADS = 16
SPAN = 8
SUB = 8
GROUP = 4
STEP = 4
VMEM_BYTES = 48 * 1024 * 1024

NT = (((1,), (1,)), ((), ()))


def lasting(us):
    return pl.CostEstimate(flops=int(us * 1.15e9), bytes_accessed=0, transcendentals=0)


def kernel_params():
    return pltpu.CompilerParams(vmem_limit_bytes=VMEM_BYTES)


def layer_norm(rows):
    mean = jnp.mean(rows, axis=-1, keepdims=True)
    centred = rows - mean
    variance = jnp.mean(centred * centred, axis=-1, keepdims=True)
    return centred * lax.rsqrt(variance + 1e-05)


def head_mask(shape, head_width, cluster):
    row_head = lax.broadcasted_iota(jnp.int32, shape, 0) // head_width % GROUP
    lane_head = lax.broadcasted_iota(jnp.int32, shape, 1) // cluster
    return row_head == lane_head


def place_kernel(features_ref, assignment_ref, after_ref, placed_ref, normed_ref):
    rows = features_ref.shape[0]
    lane = 128
    features = features_ref[...]
    columns = lax.broadcasted_iota(jnp.int32, (lane, rows), 1)
    for part in range(rows // lane):
        chosen = assignment_ref[0, :, part * lane : (part + 1) * lane] & (rows - 1)
        chosen = jnp.broadcast_to(chosen, (lane, lane)).T
        chosen = jnp.concatenate([chosen] * (rows // lane), axis=1)
        one_hot = jnp.where(chosen == columns, 1.0, 0.0).astype(jnp.bfloat16)
        placed = jnp.dot(one_hot, features, preferred_element_type=jnp.float32)
        placed_ref[pl.ds(part * lane, lane), :] = placed.astype(jnp.bfloat16)
        normed_ref[pl.ds(part * lane, lane), :] = layer_norm(placed).astype(jnp.bfloat16)


def place(features, assignment, after):
    width = features.shape[1]
    walkers, _, rows = assignment.shape
    local = pl.BlockSpec((rows, width), lambda i: (i, 0))
    out = jax.ShapeDtypeStruct(features.shape, jnp.bfloat16)
    return pl.pallas_call(
        place_kernel,
        grid=(walkers,),
        in_specs=[
            local,
            pl.BlockSpec((1, 1, rows), lambda i: (i, 0, 0)),
            pl.BlockSpec(memory_space=pl.ANY),
        ],
        out_specs=[local] * 2,
        out_shape=[out, out],
        cost_estimate=lasting(7),
        compiler_params=kernel_params(),
        name="place_rows",
    )(features, assignment, after)


def choose(index, values):
    result = values[-1]
    for at in range(len(values) - 2, -1, -1):
        result = jnp.where(index == at, values[at], result)
    return result


def pick_kernel(position_ref, wanted_ref, *rest, plan, capacity):
    position = position_ref[0]
    for out_ref, pieces in zip(rest[len(rest) - len(plan) :], plan, strict=True):
        for at, (blocks, reader_of, owner_of) in enumerate(pieces):
            reader, first = reader_of(position), owner_of(position) * capacity

            def one_slot(slot, carry, out_ref=out_ref, at=at, blocks=blocks, reader=reader, first=first):
                out_ref[at * capacity + slot] = rest[blocks][wanted_ref[reader, first + slot]]
                return carry

            lax.fori_loop(0, capacity, one_slot, 0)


def pick(position, wanted, sources, plan, after=()):
    capacity = wanted.shape[1] // SPAN
    block = sources[0].shape[1:]
    outs = [
        jax.ShapeDtypeStruct((len(pieces) * capacity,) + block, sources[0].dtype)
        for pieces in plan
    ]
    smem = pl.BlockSpec(memory_space=pltpu.SMEM)
    vmem = pl.BlockSpec(memory_space=pltpu.VMEM)
    return pl.pallas_call(
        functools.partial(pick_kernel, plan=plan, capacity=capacity),
        in_specs=[smem, smem]
        + [vmem] * len(sources)
        + [pl.BlockSpec(memory_space=pl.ANY)] * len(after),
        out_specs=[vmem] * len(outs),
        out_shape=outs,
        cost_estimate=lasting(1.5),
        compiler_params=kernel_params(),
        name="pick_blocks",
    )(position, wanted, *sources, *after)


def query_kernel(normed_ref, query_w_ref, query_ref, *, cluster, head_width):
    width = normed_ref.shape[1]
    mask = head_mask((width, GROUP * cluster), head_width, cluster)
    for block in range(query_ref.shape[0]):
        own = normed_ref[pl.ds(block * cluster, cluster), :]
        own = jnp.concatenate([own] * GROUP, axis=0)
        query = lax.dot_general(query_w_ref[...], own, NT, preferred_element_type=jnp.float32)
        query = query.astype(jnp.bfloat16) * jnp.bfloat16(1.0 / head_width**0.5)
        query_ref[block] = jnp.where(mask, query, jnp.bfloat16(0.0))


def project_queries(normed, w_query, cluster):
    rows, width = normed.shape
    blocks = rows // cluster
    return pl.pallas_call(
        functools.partial(query_kernel, cluster=cluster, head_width=width // HEADS),
        grid=(blocks // SUB,),
        in_specs=[
            pl.BlockSpec((SUB * cluster, width), lambda i: (i, 0)),
            pl.BlockSpec((width, width), lambda i: (0, 0)),
        ],
        out_specs=pl.BlockSpec((SUB, width, GROUP * cluster), lambda i: (i, 0, 0)),
        out_shape=jax.ShapeDtypeStruct((blocks, width, GROUP * cluster), jnp.bfloat16),
        cost_estimate=lasting(6.5),
        compiler_params=kernel_params(),
        name="queries",
    )(normed, w_query.T)


def key_value_kernel(rows_ref, w_ref, *rest):
    out_ref = rest[-1]
    blocks, cluster, width = rows_ref.shape
    per = max(n for n in range(1, 9) if blocks % n == 0)

    def some(at, carry):
        here = pl.ds(at * per, per)
        rows = rows_ref[here].reshape(per * cluster, width)
        both = jnp.dot(rows, w_ref[...], preferred_element_type=jnp.float32)
        out_ref[here] = both.astype(jnp.bfloat16).reshape((per,) + out_ref.shape[1:])
        return carry

    lax.fori_loop(0, blocks // per, some, 0)


def project_pairs(piece, w_both, so_far, at, total):
    blocks, cluster, width = piece.shape
    per = max(n for n in range(1, 33) if blocks % n == 0 and at % n == 0)
    in_specs = [
        pl.BlockSpec((per, cluster, width), lambda i: (i, 0, 0)),
        pl.BlockSpec((width, 2 * width), lambda i: (0, 0)),
    ]
    operands = [piece, w_both]
    aliases = {}
    if so_far is not None:
        in_specs.append(pl.BlockSpec(memory_space=pl.ANY))
        operands.append(so_far)
        aliases = {2: 0}
    return pl.pallas_call(
        key_value_kernel,
        grid=(blocks // per,),
        in_specs=in_specs,
        out_specs=pl.BlockSpec((per, cluster, 2 * width), lambda i: (at // per + i, 0, 0)),
        out_shape=jax.ShapeDtypeStruct((total, cluster, 2 * width), jnp.bfloat16),
        input_output_aliases=aliases,
        cost_estimate=lasting(blocks / 12),
        compiler_params=kernel_params(),
        name="keys_values",
    )(*operands)


def attend_kernel(range_ref, order_ref, table_ref, *rest, pair_count, head_width):
    step = pl.program_id(0)
    count = range_ref[1]

    @pl.when(step < count)
    def _():
        attend_step(
            step, range_ref[0], count, order_ref, *rest, pair_count=pair_count, head_width=head_width
        )


def attend_step(step, begin, count, order_ref, *rest, pair_count, head_width):
    query_refs, rest = rest[:STEP], rest[STEP:]
    own_refs, rest = rest[:STEP], rest[STEP:]
    listed_refs, rest = rest[: STEP * pair_count], rest[STEP * pair_count :]
    placed_refs, rest = rest[:STEP], rest[STEP:]
    out_w_ref, mix_ref, *_, mixed_ref, done_ref, sems = rest
    cluster, width = placed_refs[0].shape
    span = GROUP * head_width
    tile = GROUP * cluster
    diagonal = head_mask((span, tile), head_width, cluster)
    fold_row = lax.broadcasted_iota(jnp.int32, (cluster, tile), 0)
    fold_lane = lax.broadcasted_iota(jnp.int32, (cluster, tile), 1) % cluster
    fold = jnp.where(fold_row == fold_lane, 1.0, 0.0).astype(jnp.bfloat16)
    zeros = jnp.zeros((span, tile), jnp.bfloat16)
    ones = jnp.ones((16, tile), jnp.bfloat16)
    tiles = HEADS // GROUP
    units = [(block, t) for block in range(STEP) for t in range(tiles)]
    keys, values = {}, {}

    def gather(block):
        members = [own_refs[block][0]]
        members += [listed_refs[block * pair_count + j][0] for j in range(pair_count)]
        keys[block] = jnp.concatenate([m[:, :width] for m in members], axis=0)
        values[block] = jnp.concatenate([m[:, width:] for m in members], axis=0).T

    def scores_of(block, t):
        if t == 0:
            gather(block)
        lo = t * span // 128 * 128
        picked = query_refs[block][0, t * span : (t + 1) * span, :]
        ahead, behind = t * span - lo, lo + 128 - (t + 1) * span
        stack = [zeros] * (ahead // span) + [picked] + [zeros] * (behind // span)
        return jnp.dot(
            keys[block][:, lo : lo + 128],
            jnp.concatenate(stack, axis=0),
            preferred_element_type=jnp.float32,
        )

    lead = 2
    scores = [scores_of(*unit) for unit in units[:lead]]
    attended, pieces = [], []
    for at, (block, t) in enumerate(units):
        if at + lead < len(units):
            scores.append(scores_of(*units[at + lead]))
        current = scores[at]
        top = jnp.max(current, axis=0, keepdims=True)
        weights = jnp.exp(current - top).astype(jnp.bfloat16)
        lifted = jnp.concatenate([values[block][t * span : (t + 1) * span], ones], axis=0)
        result = jnp.dot(lifted, weights, preferred_element_type=jnp.float32)
        result = result[:span] * (1.0 / result[span : span + 1])
        pieces.append(jnp.where(diagonal, result, 0.0).astype(jnp.bfloat16))
        if t == tiles - 1:
            stacked = jnp.concatenate(pieces, axis=0)
            folded = lax.dot_general(fold, stacked, NT, preferred_element_type=jnp.float32)
            attended.append(folded.astype(jnp.bfloat16))
            pieces = []
    placed = jnp.concatenate([ref[...] for ref in placed_refs], axis=0)
    middle = placed.astype(jnp.float32) + jnp.dot(
        jnp.concatenate(attended, axis=0), out_w_ref[...], preferred_element_type=jnp.float32
    )
    middle = middle.astype(jnp.bfloat16).astype(jnp.float32)
    second = layer_norm(middle).astype(jnp.bfloat16)
    mixed = middle + jnp.tanh(jnp.dot(second, mix_ref[...], preferred_element_type=jnp.float32))

    def copies(of_step):
        for block in range(STEP):
            row = order_ref[(begin + of_step) * STEP + block] * cluster
            yield pltpu.make_async_copy(
                done_ref.at[pl.ds(block * cluster, cluster), :],
                mixed_ref.at[pl.ds(pl.multiple_of(row, cluster), cluster), :],
                sems.at[block],
            )

    @pl.when(step > 0)
    def _():
        for copy in copies(step - 1):
            copy.wait()

    done_ref[...] = mixed.astype(jnp.bfloat16)
    for copy in copies(step):
        copy.start()

    @pl.when(step == count - 1)
    def _():
        for copy in copies(step):
            copy.wait()


def attend(begin, count, order, table, queries, buffer, own_at, placed, w_out, w_mix, so_far=None):
    rows, width = placed.shape
    blocks, _, tile = queries.shape
    cluster = rows // blocks
    pair_count = table.shape[0] // blocks
    whole = pl.BlockSpec((width, width), lambda i, f, o, t: (0, 0))

    def reader(i, j, f, o):
        step = f[0] + jnp.minimum(i, jnp.maximum(f[1] - 1, 0))
        return o[step * STEP + j]

    def listed(j, n):
        return pl.BlockSpec(
            (1, cluster, 2 * width),
            lambda i, f, o, t: (t[reader(i, j, f, o) * pair_count + n], 0, 0),
        )

    each = range(STEP)
    in_specs = [
        pl.BlockSpec((1, width, tile), lambda i, f, o, t, j=j: (reader(i, j, f, o), 0, 0))
        for j in each
    ]
    in_specs += [
        pl.BlockSpec(
            (1, cluster, 2 * width), lambda i, f, o, t, j=j: (own_at + reader(i, j, f, o), 0, 0)
        )
        for j in each
    ]
    in_specs += [listed(j, n) for j in each for n in range(pair_count)]
    in_specs += [
        pl.BlockSpec((cluster, width), lambda i, f, o, t, j=j: (reader(i, j, f, o), 0)) for j in each
    ]
    in_specs += [whole, whole]
    operands = [queries] * STEP + [buffer] * (STEP + STEP * pair_count) + [placed] * STEP
    operands += [w_out, w_mix]
    aliases = {}
    if so_far is not None:
        aliases = {3 + len(operands): 0}
        in_specs.append(pl.BlockSpec(memory_space=pl.ANY))
        operands.append(so_far)
    return pl.pallas_call(
        functools.partial(attend_kernel, pair_count=pair_count, head_width=width // HEADS),
        grid_spec=pltpu.PrefetchScalarGridSpec(
            num_scalar_prefetch=3,
            grid=(blocks // STEP,),
            in_specs=in_specs,
            out_specs=pl.BlockSpec(memory_space=pl.ANY),
            scratch_shapes=[
                pltpu.VMEM((STEP * cluster, width), jnp.bfloat16),
                pltpu.SemaphoreType.DMA((STEP,)),
            ],
        ),
        out_shape=jax.ShapeDtypeStruct((rows, width), jnp.bfloat16),
        input_output_aliases=aliases,
        cost_estimate=lasting(25),
        compiler_params=kernel_params(),
        name="attend_blocks",
    )(jnp.stack([begin, count]).astype(jnp.int32), order, table, *operands)


def slot_tables(owner, within, capacity):
    readers, entries = owner.shape
    alike = owner[:, :, None] == owner[:, None, :]
    earlier = jnp.arange(entries)[None, :] < jnp.arange(entries)[:, None]
    ranking = jnp.sum(jnp.where(alike & earlier, 1, 0), axis=2).astype(jnp.int32)
    slots = owner * capacity + ranking
    every = jnp.arange(SPAN * capacity, dtype=jnp.int32)
    matches = slots[:, None, :] == every[None, :, None]
    return ranking, jnp.sum(jnp.where(matches, within[:, None, :], 0), axis=2).astype(jnp.int32)


def early_first(early):
    count = jnp.sum(early.astype(jnp.int32))
    blocks = jnp.arange(early.shape[0], dtype=jnp.int32)
    before = blocks[None, :] < blocks[:, None]
    ahead = jnp.sum(jnp.where(before & (early[None, :] == early[:, None]), 1, 0), axis=1)
    place_ = jnp.where(early, ahead, count + ahead)
    order = jnp.sum(jnp.where(place_[None, :] == blocks[:, None], blocks[None, :], 0), axis=1)
    return order.astype(jnp.int32), count


OUT = (2, 0, 3, 1)
FROM = (1, 3, 0, 2)
LEVELS = 4


def position_at(z, y):
    return 2 * z + y


def partner(position):
    return position ^ 1


def onward(position):
    return position_at(choose(position // 2, OUT), position % 2)


def source(position):
    return position_at(choose(position // 2, FROM), position % 2)


def opposite(position):
    return position_at(LEVELS - 1 - position // 2, position % 2)


def itself(position):
    return position


def crossed(route):
    return lambda position: partner(route(position))


SECOND_PLAN = (((0, source, itself), (1, source, partner)),)
MIDDLE_PLAN = (((0, opposite, itself), (1, opposite, partner)),)
PASSED_PLAN = (((0, crossed(onward), source),), ((0, partner, source),), ((0, onward, source),))


def body(features, assignment, pairs, w_query, w_key, w_value, w_out, w_mix):
    rows_dev, width = features.shape
    block_count, pair_count = pairs.shape
    cluster = rows_dev // block_count
    stride = lax.axis_size("elec") // SPAN
    groups = [[rest + place_ * stride for place_ in range(SPAN)] for rest in range(stride)]
    position = lax.axis_index("elec") // stride
    at_position = position.reshape(1)
    capacity = (block_count * pair_count + SPAN - 1) // SPAN + 1

    def moved(x, moves):
        pairs_of = [(s * stride + r, d * stride + r) for s, d in moves for r in range(stride)]
        return lax.ppermute(x, "elec", pairs_of)

    def across_z(pairs_of_z):
        return [(position_at(s, y), position_at(d, y)) for s, d in pairs_of_z for y in range(2)]

    swap = [(p, p ^ 1) for p in range(SPAN)]
    first_moves = across_z(enumerate(OUT))
    second_moves = across_z(enumerate(FROM))
    middle_moves = across_z([(1, 2), (2, 1)])
    outward_moves = across_z([(2, 3), (1, 0)])

    all_pairs = lax.all_to_all(
        jnp.broadcast_to(pairs.reshape(1, -1), (SPAN, block_count * pair_count)),
        "elec",
        split_axis=0,
        concat_axis=0,
        axis_index_groups=groups,
        tiled=True,
    )
    shape = (block_count // SUB, 1, SUB * cluster)
    placed, normed = place(features, assignment.reshape(shape), all_pairs)
    blocks = normed.reshape(block_count, cluster, width)
    passed = moved(blocks, first_moves)
    beside = moved(blocks, swap)

    w_both = jnp.concatenate([w_key, w_value], axis=1)
    own_at = 8 * capacity
    passed_at = own_at + block_count
    beside_at = passed_at + block_count
    total = beside_at + block_count
    buffer = project_pairs(blocks, w_both, None, own_at, total)
    queries = project_queries(normed, w_query, cluster)
    _, wanted = slot_tables(
        all_pairs // block_count // stride, all_pairs % block_count, capacity
    )

    (second,) = pick(at_position, wanted, (blocks, beside), SECOND_PLAN)
    second = moved(second, second_moves)
    on, near, outward = pick(at_position, wanted, (passed,), PASSED_PLAN)
    on = moved(on, swap)
    near = moved(near, swap)
    outward = moved(outward, outward_moves)
    (middle,) = pick(at_position, wanted, (blocks, beside), MIDDLE_PLAN, after=(on,))
    on = moved(on, outward_moves)
    middle = moved(middle, middle_moves)

    buffer = project_pairs(beside, w_both, buffer, beside_at, total)
    buffer = project_pairs(passed, w_both, buffer, passed_at, total)
    buffer = project_pairs(near, w_both, buffer, 0, total)
    buffer = project_pairs(second, w_both, buffer, capacity, total)

    listed = pairs.reshape(-1)
    owner = listed // block_count // stride
    within = listed % block_count
    (ranking,), _ = slot_tables(owner[None], within[None], capacity)
    z, y = position // 2, position % 2
    is_end = (z == 0) | (z == LEVELS - 1)
    z_owner, same = owner // 2, owner % 2 == y
    from_first = z_owner == choose(z, FROM)
    late = z_owner == LEVELS - 1 - z
    piece_of = jnp.where(
        from_first,
        0,
        jnp.where(
            late,
            jnp.where(is_end, jnp.where(same, 3, 4), jnp.where(same, 5, 6)),
            jnp.where(same, 1, 2),
        ),
    )
    whole_at = jnp.where(z_owner == z, jnp.where(same, own_at, beside_at), passed_at)
    whole = (z_owner == z) | (from_first & same)
    table = jnp.where(whole, whole_at + within, piece_of * capacity + ranking)

    early = ~jnp.any(late.reshape(block_count, pair_count), axis=1)
    order, early_count = early_first(early)
    steps = block_count // STEP
    early_steps = jnp.minimum(early_count // STEP, steps - 1)
    shared = (order, table, queries)
    rest = (own_at, placed, w_out, w_mix)
    mixed = attend(jnp.zeros_like(early_steps), early_steps, *shared, buffer, *rest)
    for piece, at in ((outward, 3), (on, 4), (middle, 5)):
        buffer = project_pairs(piece, w_both, buffer, at * capacity, total)
    return attend(early_steps, steps - early_steps, *shared, buffer, *rest, so_far=mixed)


def solution(mesh):
    placed = (
        P(("groups", "elec"), None),
        P(("groups", "elec")),
        P(("groups", "elec"), None),
        P(),
        P(),
        P(),
        P(),
        P(),
    )
    return jax.shard_map(
        body, mesh=mesh, in_specs=placed, out_specs=P(("groups", "elec"), None), check_vma=False
    )
```

```python
import functools

import jax
import jax.numpy as jnp
from jax import lax
from jax.experimental import pallas as pl
from jax.experimental.pallas import tpu as pltpu
from jax.sharding import PartitionSpec as P

HEADS = 16
SPAN = 8
SUB = 8
GROUP = 4
STEP = 4
VMEM_BYTES = 48 * 1024 * 1024

NT = (((1,), (1,)), ((), ()))


def lasting(us):
    return pl.CostEstimate(flops=int(us * 1.15e9), bytes_accessed=0, transcendentals=0)


def kernel_params():
    return pltpu.CompilerParams(vmem_limit_bytes=VMEM_BYTES)


def layer_norm(rows):
    mean = jnp.mean(rows, axis=-1, keepdims=True)
    centred = rows - mean
    variance = jnp.mean(centred * centred, axis=-1, keepdims=True)
    return centred * lax.rsqrt(variance + 1e-05)


def head_mask(shape, head_width, cluster):
    row_head = lax.broadcasted_iota(jnp.int32, shape, 0) // head_width % GROUP
    lane_head = lax.broadcasted_iota(jnp.int32, shape, 1) // cluster
    return row_head == lane_head


def place_kernel(features_ref, assignment_ref, placed_ref, normed_ref):
    rows = features_ref.shape[0]
    lane = 128
    features = features_ref[...]
    columns = lax.broadcasted_iota(jnp.int32, (lane, rows), 1)
    for part in range(rows // lane):
        chosen = assignment_ref[0, :, part * lane : (part + 1) * lane] & (rows - 1)
        chosen = jnp.broadcast_to(chosen, (lane, lane)).T
        chosen = jnp.concatenate([chosen] * (rows // lane), axis=1)
        one_hot = jnp.where(chosen == columns, 1.0, 0.0).astype(jnp.bfloat16)
        placed = jnp.dot(one_hot, features, preferred_element_type=jnp.float32)
        placed_ref[pl.ds(part * lane, lane), :] = placed.astype(jnp.bfloat16)
        normed_ref[pl.ds(part * lane, lane), :] = layer_norm(placed).astype(jnp.bfloat16)


def place(features, assignment):
    width = features.shape[1]
    walkers, _, rows = assignment.shape
    local = pl.BlockSpec((rows, width), lambda i: (i, 0))
    out = jax.ShapeDtypeStruct(features.shape, jnp.bfloat16)
    return pl.pallas_call(
        place_kernel,
        grid=(walkers,),
        in_specs=[local, pl.BlockSpec((1, 1, rows), lambda i: (i, 0, 0))],
        out_specs=[local] * 2,
        out_shape=[out, out],
        cost_estimate=lasting(7),
        compiler_params=kernel_params(),
        name="place_rows",
    )(features, assignment)


def choose(index, values):
    result = values[-1]
    for at in range(len(values) - 2, -1, -1):
        result = jnp.where(index == at, values[at], result)
    return result


def pick_kernel(position_ref, wanted_ref, *rest, plan, capacity):
    position = position_ref[0]
    for out_ref, pieces in zip(rest[len(rest) - len(plan) :], plan, strict=True):
        for at, (blocks, reader_of, owner_of) in enumerate(pieces):
            reader, first = reader_of(position), owner_of(position) * capacity

            def one_slot(slot, carry, out_ref=out_ref, at=at, blocks=blocks, reader=reader, first=first):
                out_ref[at * capacity + slot] = rest[blocks][wanted_ref[reader, first + slot]]
                return carry

            lax.fori_loop(0, capacity, one_slot, 0)


def pick(position, wanted, sources, plan, after=()):
    capacity = wanted.shape[1] // SPAN
    block = sources[0].shape[1:]
    outs = [
        jax.ShapeDtypeStruct((len(pieces) * capacity,) + block, sources[0].dtype)
        for pieces in plan
    ]
    smem = pl.BlockSpec(memory_space=pltpu.SMEM)
    vmem = pl.BlockSpec(memory_space=pltpu.VMEM)
    return pl.pallas_call(
        functools.partial(pick_kernel, plan=plan, capacity=capacity),
        in_specs=[smem, smem]
        + [vmem] * len(sources)
        + [pl.BlockSpec(memory_space=pl.ANY)] * len(after),
        out_specs=[vmem] * len(outs),
        out_shape=outs,
        cost_estimate=lasting(1.5),
        compiler_params=kernel_params(),
        name="pick_blocks",
    )(position, wanted, *sources, *after)


def query_kernel(normed_ref, query_w_ref, query_ref, *, cluster, head_width):
    width = normed_ref.shape[1]
    mask = head_mask((width, GROUP * cluster), head_width, cluster)
    for block in range(query_ref.shape[0]):
        own = normed_ref[pl.ds(block * cluster, cluster), :]
        own = jnp.concatenate([own] * GROUP, axis=0)
        query = lax.dot_general(query_w_ref[...], own, NT, preferred_element_type=jnp.float32)
        query = query.astype(jnp.bfloat16) * jnp.bfloat16(1.0 / head_width**0.5)
        query_ref[block] = jnp.where(mask, query, jnp.bfloat16(0.0))


def project_queries(normed, w_query, cluster):
    rows, width = normed.shape
    blocks = rows // cluster
    return pl.pallas_call(
        functools.partial(query_kernel, cluster=cluster, head_width=width // HEADS),
        grid=(blocks // SUB,),
        in_specs=[
            pl.BlockSpec((SUB * cluster, width), lambda i: (i, 0)),
            pl.BlockSpec((width, width), lambda i: (0, 0)),
        ],
        out_specs=pl.BlockSpec((SUB, width, GROUP * cluster), lambda i: (i, 0, 0)),
        out_shape=jax.ShapeDtypeStruct((blocks, width, GROUP * cluster), jnp.bfloat16),
        cost_estimate=lasting(6.5),
        compiler_params=kernel_params(),
        name="queries",
    )(normed, w_query.T)


def key_value_kernel(rows_ref, w_ref, *rest):
    out_ref = rest[-1]
    blocks, cluster, width = rows_ref.shape
    per = max(n for n in range(1, 9) if blocks % n == 0)

    def some(at, carry):
        here = pl.ds(at * per, per)
        rows = rows_ref[here].reshape(per * cluster, width)
        both = jnp.dot(rows, w_ref[...], preferred_element_type=jnp.float32)
        out_ref[here] = both.astype(jnp.bfloat16).reshape((per,) + out_ref.shape[1:])
        return carry

    lax.fori_loop(0, blocks // per, some, 0)


def project_pairs(piece, w_both, so_far, at, total):
    blocks, cluster, width = piece.shape
    per = max(n for n in range(1, 26) if blocks % n == 0 and at % n == 0)
    in_specs = [
        pl.BlockSpec((per, cluster, width), lambda i: (i, 0, 0)),
        pl.BlockSpec((width, 2 * width), lambda i: (0, 0)),
    ]
    operands = [piece, w_both]
    aliases = {}
    if so_far is not None:
        in_specs.append(pl.BlockSpec(memory_space=pl.ANY))
        operands.append(so_far)
        aliases = {2: 0}
    return pl.pallas_call(
        key_value_kernel,
        grid=(blocks // per,),
        in_specs=in_specs,
        out_specs=pl.BlockSpec((per, cluster, 2 * width), lambda i: (at // per + i, 0, 0)),
        out_shape=jax.ShapeDtypeStruct((total, cluster, 2 * width), jnp.bfloat16),
        input_output_aliases=aliases,
        cost_estimate=lasting(blocks / 12),
        compiler_params=kernel_params(),
        name="keys_values",
    )(*operands)


def attend_kernel(
    range_ref,
    order_ref,
    table_ref,
    query_ref,
    buffer_ref,
    placed_ref,
    out_w_ref,
    mix_ref,
    *rest,
    own_at,
    head_width,
):
    mixed_ref, query_buf, pair_buf, placed_buf, done_buf, in_sems, out_sems = rest[-7:]
    begin, count = range_ref[0], range_ref[1]
    pair_count = pair_buf.shape[2] - 1

    def fetches(step, slot):
        for j in range(STEP):
            block = order_ref[step * STEP + j]
            sources = [(query_ref.at[block], query_buf.at[slot, j])]
            sources.append((placed_ref.at[block], placed_buf.at[slot, j]))
            sources.append((buffer_ref.at[own_at + block], pair_buf.at[slot, j, 0]))
            for n in range(pair_count):
                listed = table_ref[block * pair_count + n]
                sources.append((buffer_ref.at[listed], pair_buf.at[slot, j, 1 + n]))
            for n, (source_, target) in enumerate(sources):
                sem = in_sems.at[slot, j * (pair_count + 3) + n]
                yield pltpu.make_async_copy(source_, target, sem)

    def stores(step):
        for j in range(STEP):
            target = mixed_ref.at[order_ref[step * STEP + j]]
            yield pltpu.make_async_copy(done_buf.at[j], target, out_sems.at[j])

    def one_step(i, carry):
        slot = i % 2
        for copy in fetches(begin + jnp.minimum(i + 1, count - 1), 1 - slot):
            copy.start()
        for copy in fetches(begin + i, slot):
            copy.wait()
        mixed = attend_step(
            query_buf.at[slot],
            pair_buf.at[slot],
            placed_buf.at[slot],
            out_w_ref,
            mix_ref,
            head_width,
        )

        @pl.when(i > 0)
        def _():
            for copy in stores(begin + i - 1):
                copy.wait()

        done_buf[...] = mixed.reshape(done_buf.shape)
        for copy in stores(begin + i):
            copy.start()
        return carry

    @pl.when(count > 0)
    def _():
        for copy in fetches(begin, 0):
            copy.start()
        lax.fori_loop(0, count, one_step, 0)
        for copy in fetches(begin + count - 1, count % 2):
            copy.wait()
        for copy in stores(begin + count - 1):
            copy.wait()


def attend_step(query_ref, pair_ref, placed_ref, out_w_ref, mix_ref, head_width):
    _, members_count, cluster, _ = pair_ref.shape
    width = placed_ref.shape[2]
    span = GROUP * head_width
    tile = GROUP * cluster
    diagonal = head_mask((span, tile), head_width, cluster)
    fold_row = lax.broadcasted_iota(jnp.int32, (cluster, tile), 0)
    fold_lane = lax.broadcasted_iota(jnp.int32, (cluster, tile), 1) % cluster
    fold = jnp.where(fold_row == fold_lane, 1.0, 0.0).astype(jnp.bfloat16)
    zeros = jnp.zeros((span, tile), jnp.bfloat16)
    ones = jnp.ones((16, tile), jnp.bfloat16)
    tiles = HEADS // GROUP
    units = [(block, t) for block in range(STEP) for t in range(tiles)]
    keys, values = {}, {}

    def gather(block):
        members = [pair_ref[block, n] for n in range(members_count)]
        keys[block] = jnp.concatenate([m[:, :width] for m in members], axis=0)
        values[block] = jnp.concatenate([m[:, width:] for m in members], axis=0).T

    def scores_of(block, t):
        if t == 0:
            gather(block)
        lo = t * span // 128 * 128
        picked = query_ref[block, t * span : (t + 1) * span, :]
        ahead, behind = t * span - lo, lo + 128 - (t + 1) * span
        stack = [zeros] * (ahead // span) + [picked] + [zeros] * (behind // span)
        return jnp.dot(
            keys[block][:, lo : lo + 128],
            jnp.concatenate(stack, axis=0),
            preferred_element_type=jnp.float32,
        )

    lead = 2
    scores = [scores_of(*unit) for unit in units[:lead]]
    attended, pieces = [], []
    for at, (block, t) in enumerate(units):
        if at + lead < len(units):
            scores.append(scores_of(*units[at + lead]))
        current = scores[at]
        top = jnp.max(current, axis=0, keepdims=True)
        weights = jnp.exp(current - top).astype(jnp.bfloat16)
        lifted = jnp.concatenate([values[block][t * span : (t + 1) * span], ones], axis=0)
        result = jnp.dot(lifted, weights, preferred_element_type=jnp.float32)
        result = result[:span] * (1.0 / result[span : span + 1])
        pieces.append(jnp.where(diagonal, result, 0.0).astype(jnp.bfloat16))
        if t == tiles - 1:
            stacked = jnp.concatenate(pieces, axis=0)
            folded = lax.dot_general(fold, stacked, NT, preferred_element_type=jnp.float32)
            attended.append(folded.astype(jnp.bfloat16))
            pieces = []
    placed = placed_ref[...].reshape(STEP * cluster, width)
    middle = placed.astype(jnp.float32) + jnp.dot(
        jnp.concatenate(attended, axis=0), out_w_ref[...], preferred_element_type=jnp.float32
    )
    middle = middle.astype(jnp.bfloat16).astype(jnp.float32)
    second = layer_norm(middle).astype(jnp.bfloat16)
    mixed = middle + jnp.tanh(jnp.dot(second, mix_ref[...], preferred_element_type=jnp.float32))
    return mixed.astype(jnp.bfloat16)


def attend(begin, count, order, table, queries, buffer, own_at, placed, w_out, w_mix, so_far=None):
    blocks, cluster, width = placed.shape
    pair_count = table.shape[0] // blocks
    smem = pl.BlockSpec(memory_space=pltpu.SMEM)
    vmem = pl.BlockSpec(memory_space=pltpu.VMEM)
    hbm = pl.BlockSpec(memory_space=pl.ANY)
    in_specs = [smem, smem, smem, hbm, hbm, hbm, vmem, vmem]
    operands = [queries, buffer, placed, w_out, w_mix]
    aliases = {}
    if so_far is not None:
        aliases = {len(in_specs): 0}
        in_specs.append(hbm)
        operands.append(so_far)
    return pl.pallas_call(
        functools.partial(attend_kernel, own_at=own_at, head_width=width // HEADS),
        in_specs=in_specs,
        out_specs=hbm,
        out_shape=jax.ShapeDtypeStruct(placed.shape, jnp.bfloat16),
        scratch_shapes=[
            pltpu.VMEM((2, STEP) + queries.shape[1:], jnp.bfloat16),
            pltpu.VMEM((2, STEP, pair_count + 1, cluster, 2 * width), jnp.bfloat16),
            pltpu.VMEM((2, STEP, cluster, width), jnp.bfloat16),
            pltpu.VMEM((STEP, cluster, width), jnp.bfloat16),
            pltpu.SemaphoreType.DMA((2, STEP * (pair_count + 3))),
            pltpu.SemaphoreType.DMA((STEP,)),
        ],
        input_output_aliases=aliases,
        cost_estimate=lasting(20),
        compiler_params=kernel_params(),
        name="attend_blocks",
    )(jnp.stack([begin, count]).astype(jnp.int32), order, table, *operands)


def slot_tables(owner, within, capacity):
    entries = owner.shape[0]
    alike = owner[:, None] == owner[None, :]
    earlier = jnp.arange(entries)[None, :] < jnp.arange(entries)[:, None]
    ranking = jnp.sum(jnp.where(alike & earlier, 1, 0), axis=1).astype(jnp.int32)
    slots = owner * capacity + ranking
    matches = slots[None, :] == jnp.arange(SPAN * capacity, dtype=jnp.int32)[:, None]
    return ranking, jnp.sum(jnp.where(matches, within[None, :], 0), axis=1).astype(jnp.int32)


def by_class(classes, count):
    blocks = jnp.arange(classes.shape[0], dtype=jnp.int32)
    before = (classes[None, :] < classes[:, None]) | (
        (classes[None, :] == classes[:, None]) & (blocks[None, :] < blocks[:, None])
    )
    rank = jnp.sum(jnp.where(before, 1, 0), axis=1)
    order = jnp.sum(jnp.where(rank[None, :] == blocks[:, None], blocks[None, :], 0), axis=1)
    ends = [jnp.sum(jnp.where(classes <= c, 1, 0)).astype(jnp.int32) for c in range(count)]
    return order.astype(jnp.int32), ends


OUT = (2, 0, 3, 1)
FROM = (1, 3, 0, 2)
LEVELS = 4


def position_at(z, y):
    return 2 * z + y


def partner(position):
    return position ^ 1


def onward(position):
    return position_at(choose(position // 2, OUT), position % 2)


def source(position):
    return position_at(choose(position // 2, FROM), position % 2)


def opposite(position):
    return position_at(LEVELS - 1 - position // 2, position % 2)


def itself(position):
    return position


def crossed(route):
    return lambda position: partner(route(position))


SECOND_PLAN = (((0, source, itself), (1, source, partner)),)
MIDDLE_PLAN = (((0, opposite, itself),),)
MIDDLE_CROSS_PLAN = (((0, opposite, partner),),)
ON_PLAN = (((0, crossed(onward), source),), ((0, onward, source),))
NEAR_PLAN = (((0, partner, source),),)


def body(features, assignment, pairs, w_query, w_key, w_value, w_out, w_mix):
    rows_dev, width = features.shape
    block_count, pair_count = pairs.shape
    cluster = rows_dev // block_count
    stride = lax.axis_size("elec") // SPAN
    groups = [[rest + place_ * stride for place_ in range(SPAN)] for rest in range(stride)]
    position = lax.axis_index("elec") // stride
    at_position = position.reshape(1)
    capacity = (block_count * pair_count + SPAN - 1) // SPAN + 1

    def moved(x, moves):
        pairs_of = [(s * stride + r, d * stride + r) for s, d in moves for r in range(stride)]
        return lax.ppermute(x, "elec", pairs_of)

    def across_z(pairs_of_z):
        return [(position_at(s, y), position_at(d, y)) for s, d in pairs_of_z for y in range(2)]

    swap = [(p, p ^ 1) for p in range(SPAN)]
    first_moves = across_z(enumerate(OUT))
    second_moves = across_z(enumerate(FROM))
    middle_moves = across_z([(1, 2), (2, 1)])
    outward_moves = across_z([(2, 3), (1, 0)])

    listed = pairs.reshape(-1)
    owner = listed // block_count // stride
    within = listed % block_count
    ranking, tables = slot_tables(owner, within, capacity)
    wanted = lax.all_to_all(
        jnp.broadcast_to(tables[None], (SPAN, SPAN * capacity)),
        "elec",
        split_axis=0,
        concat_axis=0,
        axis_index_groups=groups,
        tiled=True,
    )

    placed, normed = place(features, assignment.reshape(block_count // SUB, 1, SUB * cluster))
    blocks = normed.reshape(block_count, cluster, width)
    passed = moved(blocks, first_moves)
    beside = moved(blocks, swap)

    w_both = jnp.concatenate([w_key, w_value], axis=1)
    own_at = 8 * capacity
    passed_at = own_at + block_count
    beside_at = passed_at + block_count
    total = beside_at + block_count
    buffer = project_pairs(blocks, w_both, None, own_at, total)
    queries = project_queries(normed, w_query, cluster)

    (second,) = pick(at_position, wanted, (blocks, beside), SECOND_PLAN)
    second = moved(second, second_moves)
    on, outward = pick(at_position, wanted, (passed,), ON_PLAN)
    on = moved(on, swap)
    outward = moved(outward, outward_moves)
    (near,) = pick(at_position, wanted, (passed,), NEAR_PLAN, after=(on,))
    near = moved(near, swap)
    (middle,) = pick(at_position, wanted, (blocks,), MIDDLE_PLAN, after=(on,))
    middle = moved(middle, middle_moves)
    on = moved(on, outward_moves)
    (middle_cross,) = pick(
        at_position, wanted, (beside,), MIDDLE_CROSS_PLAN, after=(second,)
    )
    middle_cross = moved(middle_cross, middle_moves)

    buffer = project_pairs(beside, w_both, buffer, beside_at, total)
    buffer = project_pairs(passed, w_both, buffer, passed_at, total)
    buffer = project_pairs(near, w_both, buffer, 0, total)
    buffer = project_pairs(second, w_both, buffer, capacity, total)

    z, y = position // 2, position % 2
    is_end = (z == 0) | (z == LEVELS - 1)
    z_owner, same = owner // 2, owner % 2 == y
    from_first = z_owner == choose(z, FROM)
    late = z_owner == LEVELS - 1 - z
    piece_of = jnp.where(
        from_first,
        0,
        jnp.where(
            late,
            jnp.where(is_end, jnp.where(same, 3, 4), jnp.where(same, 5, 6)),
            jnp.where(same, 1, 2),
        ),
    )
    whole_at = jnp.where(z_owner == z, jnp.where(same, own_at, beside_at), passed_at)
    whole = (z_owner == z) | (from_first & same)
    table = jnp.where(whole, whole_at + within, piece_of * capacity + ranking)

    arrival = jnp.where(late, jnp.where(same | is_end, 1, 2), 0)
    order, ends = by_class(jnp.max(arrival.reshape(block_count, pair_count), axis=1), 2)
    marks = [0, ends[0] // STEP, ends[1] // STEP, block_count // STEP]
    phases = [(marks[n], marks[n + 1] - marks[n]) for n in range(3)]
    shared = (order, table, queries)
    rest = (own_at, placed.reshape(blocks.shape), w_out, w_mix)
    mixed = attend(*phases[0], *shared, buffer, *rest)
    for piece, at in ((outward, 3), (on, 4), (middle, 5)):
        buffer = project_pairs(piece, w_both, buffer, at * capacity, total)
    mixed = attend(*phases[1], *shared, buffer, *rest, so_far=mixed)
    buffer = project_pairs(middle_cross, w_both, buffer, 6 * capacity, total)
    mixed = attend(*phases[2], *shared, buffer, *rest, so_far=mixed)
    return mixed.reshape(rows_dev, width)


def solution(mesh):
    placed = (
        P(("groups", "elec"), None),
        P(("groups", "elec")),
        P(("groups", "elec"), None),
        P(),
        P(),
        P(),
        P(),
        P(),
    )
    return jax.shard_map(
        body, mesh=mesh, in_specs=placed, out_specs=P(("groups", "elec"), None), check_vma=False
    )
```

```python
import functools
import math

import jax
import jax.numpy as jnp
from jax import lax
from jax.experimental import pallas as pl
from jax.experimental.pallas import tpu as pltpu
from jax.sharding import PartitionSpec as P

HEADS = 16
SPAN = 8
SUB = 8
GROUP = 4
STEP = 4
SCORES_AHEAD, WEIGHTS_AHEAD = 3, 1
VMEM_BYTES = 48 * 1024 * 1024

NT = (((1,), (1,)), ((), ()))


def lasting(us):
    return pl.CostEstimate(flops=int(us * 1.15e9), bytes_accessed=0, transcendentals=0)


def kernel_params():
    return pltpu.CompilerParams(vmem_limit_bytes=VMEM_BYTES)


def layer_norm(rows):
    mean = jnp.mean(rows, axis=-1, keepdims=True)
    centred = rows - mean
    variance = jnp.mean(centred * centred, axis=-1, keepdims=True)
    return centred * lax.rsqrt(variance + 1e-05)


def head_mask(shape, head_width, cluster):
    row_head = lax.broadcasted_iota(jnp.int32, shape, 0) // head_width % GROUP
    lane_head = lax.broadcasted_iota(jnp.int32, shape, 1) // cluster
    return row_head == lane_head


def place_kernel(features_ref, assignment_ref, placed_ref, normed_ref):
    rows = features_ref.shape[0]
    lane = 128
    features = features_ref[...]
    columns = lax.broadcasted_iota(jnp.int32, (lane, rows), 1)
    for part in range(rows // lane):
        chosen = assignment_ref[0, :, part * lane : (part + 1) * lane] & (rows - 1)
        chosen = jnp.broadcast_to(chosen, (lane, lane)).T
        chosen = jnp.concatenate([chosen] * (rows // lane), axis=1)
        one_hot = jnp.where(chosen == columns, 1.0, 0.0).astype(jnp.bfloat16)
        placed = jnp.dot(one_hot, features, preferred_element_type=jnp.float32)
        placed_ref[pl.ds(part * lane, lane), :] = placed.astype(jnp.bfloat16)
        normed_ref[pl.ds(part * lane, lane), :] = layer_norm(placed).astype(jnp.bfloat16)


def place(features, assignment):
    width = features.shape[1]
    walkers, _, rows = assignment.shape
    local = pl.BlockSpec((rows, width), lambda i: (i, 0))
    out = jax.ShapeDtypeStruct(features.shape, jnp.bfloat16)
    return pl.pallas_call(
        place_kernel,
        grid=(walkers,),
        in_specs=[local, pl.BlockSpec((1, 1, rows), lambda i: (i, 0, 0))],
        out_specs=[local] * 2,
        out_shape=[out, out],
        cost_estimate=lasting(7),
        compiler_params=kernel_params(),
        name="place_rows",
    )(features, assignment)


def choose(index, values):
    result = values[-1]
    for at in range(len(values) - 2, -1, -1):
        result = jnp.where(index == at, values[at], result)
    return result


def pick_kernel(position_ref, wanted_ref, *rest, plan, capacity):
    position = position_ref[0]
    for out_ref, pieces in zip(rest[len(rest) - len(plan) :], plan, strict=True):
        for at, (blocks, reader_of, owner_of) in enumerate(pieces):
            reader, first = reader_of(position), owner_of(position) * capacity

            def one_slot(slot, carry, out_ref=out_ref, at=at, blocks=blocks, reader=reader, first=first):
                out_ref[at * capacity + slot] = rest[blocks][wanted_ref[reader, first + slot]]
                return carry

            lax.fori_loop(0, capacity, one_slot, 0)


def pick(position, wanted, sources, plan, after=()):
    capacity = wanted.shape[1] // SPAN
    block = sources[0].shape[1:]
    outs = [
        jax.ShapeDtypeStruct((len(pieces) * capacity,) + block, sources[0].dtype)
        for pieces in plan
    ]
    smem = pl.BlockSpec(memory_space=pltpu.SMEM)
    vmem = pl.BlockSpec(memory_space=pltpu.VMEM)
    return pl.pallas_call(
        functools.partial(pick_kernel, plan=plan, capacity=capacity),
        in_specs=[smem, smem]
        + [vmem] * len(sources)
        + [pl.BlockSpec(memory_space=pl.ANY)] * len(after),
        out_specs=[vmem] * len(outs),
        out_shape=outs,
        cost_estimate=lasting(1.5),
        compiler_params=kernel_params(),
        name="pick_blocks",
    )(position, wanted, *sources, *after)


def query_kernel(normed_ref, query_w_ref, query_ref, *, cluster, head_width):
    width = normed_ref.shape[1]
    mask = head_mask((width, GROUP * cluster), head_width, cluster)
    for block in range(query_ref.shape[0]):
        own = normed_ref[pl.ds(block * cluster, cluster), :]
        own = jnp.concatenate([own] * GROUP, axis=0)
        query = lax.dot_general(query_w_ref[...], own, NT, preferred_element_type=jnp.float32)
        query = query * (math.log2(math.e) / head_width**0.5)
        query_ref[block] = jnp.where(mask, query, 0.0).astype(jnp.bfloat16)


def project_queries(normed, w_query, cluster):
    rows, width = normed.shape
    blocks = rows // cluster
    return pl.pallas_call(
        functools.partial(query_kernel, cluster=cluster, head_width=width // HEADS),
        grid=(blocks // SUB,),
        in_specs=[
            pl.BlockSpec((SUB * cluster, width), lambda i: (i, 0)),
            pl.BlockSpec((width, width), lambda i: (0, 0)),
        ],
        out_specs=pl.BlockSpec((SUB, width, GROUP * cluster), lambda i: (i, 0, 0)),
        out_shape=jax.ShapeDtypeStruct((blocks, width, GROUP * cluster), jnp.bfloat16),
        cost_estimate=lasting(6.5),
        compiler_params=kernel_params(),
        name="queries",
    )(normed, w_query.T)


def key_value_kernel(rows_ref, w_ref, *rest):
    out_ref = rest[-1]
    blocks, cluster, width = rows_ref.shape
    per = max(n for n in range(1, 9) if blocks % n == 0)

    def some(at, carry):
        here = pl.ds(at * per, per)
        rows = rows_ref[here].reshape(per * cluster, width)
        both = jnp.dot(rows, w_ref[...], preferred_element_type=jnp.float32)
        out_ref[here] = both.astype(jnp.bfloat16).reshape((per,) + out_ref.shape[1:])
        return carry

    lax.fori_loop(0, blocks // per, some, 0)


def project_pairs(piece, w_both, so_far, at, total):
    blocks, cluster, width = piece.shape
    per = max(n for n in range(1, 26) if blocks % n == 0 and at % n == 0)
    in_specs = [
        pl.BlockSpec((per, cluster, width), lambda i: (i, 0, 0)),
        pl.BlockSpec((width, 2 * width), lambda i: (0, 0)),
    ]
    operands = [piece, w_both]
    aliases = {}
    if so_far is not None:
        in_specs.append(pl.BlockSpec(memory_space=pl.ANY))
        operands.append(so_far)
        aliases = {2: 0}
    return pl.pallas_call(
        key_value_kernel,
        grid=(blocks // per,),
        in_specs=in_specs,
        out_specs=pl.BlockSpec((per, cluster, 2 * width), lambda i: (at // per + i, 0, 0)),
        out_shape=jax.ShapeDtypeStruct((total, cluster, 2 * width), jnp.bfloat16),
        input_output_aliases=aliases,
        cost_estimate=lasting(blocks / 12),
        compiler_params=kernel_params(),
        name="keys_values",
    )(*operands)


def attend_kernel(
    range_ref,
    order_ref,
    table_ref,
    query_ref,
    buffer_ref,
    placed_ref,
    out_w_ref,
    mix_ref,
    *rest,
    own_at,
    head_width,
):
    mixed_ref, query_buf, pair_buf, placed_buf, done_buf, in_sems, out_sems = rest[-7:]
    begin, count = range_ref[0], range_ref[1]
    pair_count = pair_buf.shape[2] - 1

    def fetches(step, slot):
        for j in range(STEP):
            block = order_ref[step * STEP + j]
            sources = [(query_ref.at[block], query_buf.at[slot, j])]
            sources.append((placed_ref.at[block], placed_buf.at[slot, j]))
            sources.append((buffer_ref.at[own_at + block], pair_buf.at[slot, j, 0]))
            for n in range(pair_count):
                listed = table_ref[block * pair_count + n]
                sources.append((buffer_ref.at[listed], pair_buf.at[slot, j, 1 + n]))
            for n, (source_, target) in enumerate(sources):
                sem = in_sems.at[slot, j * (pair_count + 3) + n]
                yield pltpu.make_async_copy(source_, target, sem)

    def stores(step):
        for j in range(STEP):
            target = mixed_ref.at[order_ref[step * STEP + j]]
            yield pltpu.make_async_copy(done_buf.at[j], target, out_sems.at[j])

    def one_step(i, carry):
        slot = i % 2
        for copy in fetches(begin + jnp.minimum(i + 1, count - 1), 1 - slot):
            copy.start()
        for copy in fetches(begin + i, slot):
            copy.wait()
        mixed = attend_step(
            query_buf.at[slot],
            pair_buf.at[slot],
            placed_buf.at[slot],
            out_w_ref,
            mix_ref,
            head_width,
        )

        @pl.when(i > 0)
        def _():
            for copy in stores(begin + i - 1):
                copy.wait()

        done_buf[...] = mixed.reshape(done_buf.shape)
        for copy in stores(begin + i):
            copy.start()
        return carry

    @pl.when(count > 0)
    def _():
        for copy in fetches(begin, 0):
            copy.start()
        lax.fori_loop(0, count, one_step, 0)
        for copy in fetches(begin + count - 1, count % 2):
            copy.wait()
        for copy in stores(begin + count - 1):
            copy.wait()


def attend_step(query_ref, pair_ref, placed_ref, out_w_ref, mix_ref, head_width):
    _, members_count, cluster, _ = pair_ref.shape
    width = placed_ref.shape[2]
    span = GROUP * head_width
    tile = GROUP * cluster
    diagonal = head_mask((span, tile), head_width, cluster)
    fold_row = lax.broadcasted_iota(jnp.int32, (cluster, tile), 0)
    fold_lane = lax.broadcasted_iota(jnp.int32, (cluster, tile), 1) % cluster
    fold = jnp.where(fold_row == fold_lane, 1.0, 0.0).astype(jnp.bfloat16)
    zeros = jnp.zeros((span, tile), jnp.bfloat16)
    ones = jnp.ones((16, tile), jnp.bfloat16)
    tiles = HEADS // GROUP
    units = [(block, t) for block in range(STEP) for t in range(tiles)]
    keys, values = {}, {}

    def gather(block):
        members = [pair_ref[block, n] for n in range(members_count)]
        keys[block] = jnp.concatenate([m[:, :width] for m in members], axis=0)
        values[block] = jnp.concatenate([m[:, width:] for m in members], axis=0).T

    def scores_of(block, t):
        if t == 0:
            gather(block)
        lo = t * span // 128 * 128
        picked = query_ref[block, t * span : (t + 1) * span, :]
        ahead, behind = t * span - lo, lo + 128 - (t + 1) * span
        stack = [zeros] * (ahead // span) + [picked] + [zeros] * (behind // span)
        return jnp.dot(
            keys[block][:, lo : lo + 128],
            jnp.concatenate(stack, axis=0),
            preferred_element_type=jnp.float32,
        )

    def weights_of(scores):
        top = jnp.max(scores, axis=0, keepdims=True)
        return jnp.exp2(scores - top).astype(jnp.bfloat16)

    def product_of(block, t, weights):
        lifted = jnp.concatenate([values[block][t * span : (t + 1) * span], ones], axis=0)
        return jnp.dot(lifted, weights, preferred_element_type=jnp.float32)

    def scaled(product):
        result = product[:span] * (1.0 / product[span : span + 1])
        return jnp.where(diagonal, result, 0.0).astype(jnp.bfloat16)

    count = len(units)
    scores, weights, products, pieces, attended = {}, {}, {}, [], []
    for at in range(-SCORES_AHEAD, count + 1):
        if at + SCORES_AHEAD < count:
            scores[at + SCORES_AHEAD] = scores_of(*units[at + SCORES_AHEAD])
        if 0 <= at + WEIGHTS_AHEAD < count:
            weights[at + WEIGHTS_AHEAD] = weights_of(scores.pop(at + WEIGHTS_AHEAD))
        if 0 <= at < count:
            products[at] = product_of(*units[at], weights.pop(at))
        if at > 0:
            pieces.append(scaled(products.pop(at - 1)))
            if len(pieces) == tiles:
                stacked = jnp.concatenate(pieces, axis=0)
                folded = lax.dot_general(fold, stacked, NT, preferred_element_type=jnp.float32)
                attended.append(folded.astype(jnp.bfloat16))
                pieces = []
    placed = placed_ref[...].reshape(STEP * cluster, width)
    middle = placed.astype(jnp.float32) + jnp.dot(
        jnp.concatenate(attended, axis=0), out_w_ref[...], preferred_element_type=jnp.float32
    )
    middle = middle.astype(jnp.bfloat16).astype(jnp.float32)
    second = layer_norm(middle).astype(jnp.bfloat16)
    mixed = middle + jnp.tanh(jnp.dot(second, mix_ref[...], preferred_element_type=jnp.float32))
    return mixed.astype(jnp.bfloat16)


def attend(begin, count, order, table, queries, buffer, own_at, placed, w_out, w_mix, so_far=None):
    blocks, cluster, width = placed.shape
    pair_count = table.shape[0] // blocks
    smem = pl.BlockSpec(memory_space=pltpu.SMEM)
    vmem = pl.BlockSpec(memory_space=pltpu.VMEM)
    hbm = pl.BlockSpec(memory_space=pl.ANY)
    in_specs = [smem, smem, smem, hbm, hbm, hbm, vmem, vmem]
    operands = [queries, buffer, placed, w_out, w_mix]
    aliases = {}
    if so_far is not None:
        aliases = {len(in_specs): 0}
        in_specs.append(hbm)
        operands.append(so_far)
    return pl.pallas_call(
        functools.partial(attend_kernel, own_at=own_at, head_width=width // HEADS),
        in_specs=in_specs,
        out_specs=hbm,
        out_shape=jax.ShapeDtypeStruct(placed.shape, jnp.bfloat16),
        scratch_shapes=[
            pltpu.VMEM((2, STEP) + queries.shape[1:], jnp.bfloat16),
            pltpu.VMEM((2, STEP, pair_count + 1, cluster, 2 * width), jnp.bfloat16),
            pltpu.VMEM((2, STEP, cluster, width), jnp.bfloat16),
            pltpu.VMEM((STEP, cluster, width), jnp.bfloat16),
            pltpu.SemaphoreType.DMA((2, STEP * (pair_count + 3))),
            pltpu.SemaphoreType.DMA((STEP,)),
        ],
        input_output_aliases=aliases,
        cost_estimate=lasting(20),
        compiler_params=kernel_params(),
        name="attend_blocks",
    )(jnp.stack([begin, count]).astype(jnp.int32), order, table, *operands)


def slot_tables(owner, within, capacity):
    entries = owner.shape[0]
    alike = owner[:, None] == owner[None, :]
    earlier = jnp.arange(entries)[None, :] < jnp.arange(entries)[:, None]
    ranking = jnp.sum(jnp.where(alike & earlier, 1, 0), axis=1).astype(jnp.int32)
    slots = owner * capacity + ranking
    matches = slots[None, :] == jnp.arange(SPAN * capacity, dtype=jnp.int32)[:, None]
    return ranking, jnp.sum(jnp.where(matches, within[None, :], 0), axis=1).astype(jnp.int32)


def by_class(classes, count):
    blocks = jnp.arange(classes.shape[0], dtype=jnp.int32)
    before = (classes[None, :] < classes[:, None]) | (
        (classes[None, :] == classes[:, None]) & (blocks[None, :] < blocks[:, None])
    )
    rank = jnp.sum(jnp.where(before, 1, 0), axis=1)
    order = jnp.sum(jnp.where(rank[None, :] == blocks[:, None], blocks[None, :], 0), axis=1)
    ends = [jnp.sum(jnp.where(classes <= c, 1, 0)).astype(jnp.int32) for c in range(count)]
    return order.astype(jnp.int32), ends


OUT = (2, 0, 3, 1)
FROM = (1, 3, 0, 2)
LEVELS = 4


def position_at(z, y):
    return 2 * z + y


def partner(position):
    return position ^ 1


def onward(position):
    return position_at(choose(position // 2, OUT), position % 2)


def source(position):
    return position_at(choose(position // 2, FROM), position % 2)


def opposite(position):
    return position_at(LEVELS - 1 - position // 2, position % 2)


def itself(position):
    return position


def crossed(route):
    return lambda position: partner(route(position))


SECOND_PLAN = (((0, source, itself), (1, source, partner)),)
MIDDLE_PLAN = (((0, opposite, itself),),)
MIDDLE_CROSS_PLAN = (((0, opposite, partner),),)
ON_PLAN = (((0, crossed(onward), source),), ((0, onward, source),))
NEAR_PLAN = (((0, partner, source),),)


def body(features, assignment, pairs, w_query, w_key, w_value, w_out, w_mix):
    rows_dev, width = features.shape
    block_count, pair_count = pairs.shape
    cluster = rows_dev // block_count
    stride = lax.axis_size("elec") // SPAN
    groups = [[rest + place_ * stride for place_ in range(SPAN)] for rest in range(stride)]
    position = lax.axis_index("elec") // stride
    at_position = position.reshape(1)
    capacity = (block_count * pair_count + SPAN - 1) // SPAN + 1

    def moved(x, moves):
        pairs_of = [(s * stride + r, d * stride + r) for s, d in moves for r in range(stride)]
        return lax.ppermute(x, "elec", pairs_of)

    def across_z(pairs_of_z):
        return [(position_at(s, y), position_at(d, y)) for s, d in pairs_of_z for y in range(2)]

    swap = [(p, p ^ 1) for p in range(SPAN)]
    first_moves = across_z(enumerate(OUT))
    second_moves = across_z(enumerate(FROM))
    middle_moves = across_z([(1, 2), (2, 1)])
    outward_moves = across_z([(2, 3), (1, 0)])

    listed = pairs.reshape(-1)
    owner = listed // block_count // stride
    within = listed % block_count
    ranking, tables = slot_tables(owner, within, capacity)
    wanted = lax.all_to_all(
        jnp.broadcast_to(tables[None], (SPAN, SPAN * capacity)),
        "elec",
        split_axis=0,
        concat_axis=0,
        axis_index_groups=groups,
        tiled=True,
    )

    placed, normed = place(features, assignment.reshape(block_count // SUB, 1, SUB * cluster))
    blocks = normed.reshape(block_count, cluster, width)
    passed = moved(blocks, first_moves)
    beside = moved(blocks, swap)

    w_both = jnp.concatenate([w_key, w_value], axis=1)
    own_at = 8 * capacity
    passed_at = own_at + block_count
    beside_at = passed_at + block_count
    total = beside_at + block_count
    buffer = project_pairs(blocks, w_both, None, own_at, total)
    queries = project_queries(normed, w_query, cluster)

    (second,) = pick(at_position, wanted, (blocks, beside), SECOND_PLAN)
    second = moved(second, second_moves)
    on, outward = pick(at_position, wanted, (passed,), ON_PLAN)
    on = moved(on, swap)
    outward = moved(outward, outward_moves)
    (near,) = pick(at_position, wanted, (passed,), NEAR_PLAN, after=(on,))
    near = moved(near, swap)
    (middle,) = pick(at_position, wanted, (blocks,), MIDDLE_PLAN, after=(on,))
    middle = moved(middle, middle_moves)
    on = moved(on, outward_moves)
    (middle_cross,) = pick(
        at_position, wanted, (beside,), MIDDLE_CROSS_PLAN, after=(second,)
    )
    middle_cross = moved(middle_cross, middle_moves)

    buffer = project_pairs(beside, w_both, buffer, beside_at, total)
    buffer = project_pairs(passed, w_both, buffer, passed_at, total)
    buffer = project_pairs(near, w_both, buffer, 0, total)
    buffer = project_pairs(second, w_both, buffer, capacity, total)

    z, y = position // 2, position % 2
    is_end = (z == 0) | (z == LEVELS - 1)
    z_owner, same = owner // 2, owner % 2 == y
    from_first = z_owner == choose(z, FROM)
    late = z_owner == LEVELS - 1 - z
    piece_of = jnp.where(
        from_first,
        0,
        jnp.where(
            late,
            jnp.where(is_end, jnp.where(same, 3, 4), jnp.where(same, 5, 6)),
            jnp.where(same, 1, 2),
        ),
    )
    whole_at = jnp.where(z_owner == z, jnp.where(same, own_at, beside_at), passed_at)
    whole = (z_owner == z) | (from_first & same)
    table = jnp.where(whole, whole_at + within, piece_of * capacity + ranking)

    arrival = jnp.where(late, jnp.where(same | is_end, 1, 2), 0)
    order, ends = by_class(jnp.max(arrival.reshape(block_count, pair_count), axis=1), 2)
    marks = [0, ends[0] // STEP, ends[1] // STEP, block_count // STEP]
    phases = [(marks[n], marks[n + 1] - marks[n]) for n in range(3)]
    shared = (order, table, queries)
    rest = (own_at, placed.reshape(blocks.shape), w_out, w_mix)
    mixed = attend(*phases[0], *shared, buffer, *rest)
    for piece, at in ((outward, 3), (on, 4), (middle, 5)):
        buffer = project_pairs(piece, w_both, buffer, at * capacity, total)
    mixed = attend(*phases[1], *shared, buffer, *rest, so_far=mixed)
    buffer = project_pairs(middle_cross, w_both, buffer, 6 * capacity, total)
    mixed = attend(*phases[2], *shared, buffer, *rest, so_far=mixed)
    return mixed.reshape(rows_dev, width)


def solution(mesh):
    placed = (
        P(("groups", "elec"), None),
        P(("groups", "elec")),
        P(("groups", "elec"), None),
        P(),
        P(),
        P(),
        P(),
        P(),
    )
    return jax.shard_map(
        body, mesh=mesh, in_specs=placed, out_specs=P(("groups", "elec"), None), check_vma=False
    )
```

```python
import functools
import math

import jax
import jax.numpy as jnp
from jax import lax
from jax.experimental import pallas as pl
from jax.experimental.pallas import tpu as pltpu
from jax.sharding import PartitionSpec as P

HEADS = 16
SPAN = 8
SUB = 8
GROUP = 4
STEP = 4
SCORES_AHEAD, WEIGHTS_AHEAD = 3, 1
VMEM_BYTES = 48 * 1024 * 1024

NT = (((1,), (1,)), ((), ()))


def lasting(us):
    return pl.CostEstimate(flops=int(us * 1.15e9), bytes_accessed=0, transcendentals=0)


def kernel_params():
    return pltpu.CompilerParams(vmem_limit_bytes=VMEM_BYTES)


def layer_norm(rows):
    mean = jnp.mean(rows, axis=-1, keepdims=True)
    centred = rows - mean
    variance = jnp.mean(centred * centred, axis=-1, keepdims=True)
    return centred * lax.rsqrt(variance + 1e-05)


def head_mask(shape, head_width, cluster):
    row_head = lax.broadcasted_iota(jnp.int32, shape, 0) // head_width % GROUP
    lane_head = lax.broadcasted_iota(jnp.int32, shape, 1) // cluster
    return row_head == lane_head


def place_kernel(features_ref, assignment_ref, placed_ref, normed_ref):
    rows = features_ref.shape[0]
    lane = 128
    features = features_ref[...]
    columns = lax.broadcasted_iota(jnp.int32, (lane, rows), 1)
    for part in range(rows // lane):
        chosen = assignment_ref[0, :, part * lane : (part + 1) * lane] & (rows - 1)
        chosen = jnp.broadcast_to(chosen, (lane, lane)).T
        chosen = jnp.concatenate([chosen] * (rows // lane), axis=1)
        one_hot = jnp.where(chosen == columns, 1.0, 0.0).astype(jnp.bfloat16)
        placed = jnp.dot(one_hot, features, preferred_element_type=jnp.float32)
        placed_ref[pl.ds(part * lane, lane), :] = placed.astype(jnp.bfloat16)
        normed_ref[pl.ds(part * lane, lane), :] = layer_norm(placed).astype(jnp.bfloat16)


def place(features, assignment):
    width = features.shape[1]
    walkers, _, rows = assignment.shape
    local = pl.BlockSpec((rows, width), lambda i: (i, 0))
    out = jax.ShapeDtypeStruct(features.shape, jnp.bfloat16)
    return pl.pallas_call(
        place_kernel,
        grid=(walkers,),
        in_specs=[local, pl.BlockSpec((1, 1, rows), lambda i: (i, 0, 0))],
        out_specs=[local] * 2,
        out_shape=[out, out],
        cost_estimate=lasting(7),
        compiler_params=kernel_params(),
        name="place_rows",
    )(features, assignment)


def choose(index, values):
    result = values[-1]
    for at in range(len(values) - 2, -1, -1):
        result = jnp.where(index == at, values[at], result)
    return result


def pick_kernel(position_ref, wanted_ref, *rest, plan, capacity):
    position = position_ref[0]
    for out_ref, pieces in zip(rest[len(rest) - len(plan) :], plan, strict=True):
        for at, (blocks, reader_of, owner_of) in enumerate(pieces):
            reader, first = reader_of(position), owner_of(position) * capacity

            def one_slot(slot, carry, out_ref=out_ref, at=at, blocks=blocks, reader=reader, first=first):
                out_ref[at * capacity + slot] = rest[blocks][wanted_ref[reader, first + slot]]
                return carry

            lax.fori_loop(0, capacity, one_slot, 0)


def pick(position, wanted, sources, plan, after=()):
    capacity = wanted.shape[1] // SPAN
    block = sources[0].shape[1:]
    outs = [
        jax.ShapeDtypeStruct((len(pieces) * capacity,) + block, sources[0].dtype)
        for pieces in plan
    ]
    smem = pl.BlockSpec(memory_space=pltpu.SMEM)
    vmem = pl.BlockSpec(memory_space=pltpu.VMEM)
    return pl.pallas_call(
        functools.partial(pick_kernel, plan=plan, capacity=capacity),
        in_specs=[smem, smem]
        + [vmem] * len(sources)
        + [pl.BlockSpec(memory_space=pl.ANY)] * len(after),
        out_specs=[vmem] * len(outs),
        out_shape=outs,
        cost_estimate=lasting(1.5),
        compiler_params=kernel_params(),
        name="pick_blocks",
    )(position, wanted, *sources, *after)


def query_kernel(normed_ref, query_w_ref, query_ref, *, cluster, head_width):
    width = normed_ref.shape[1]
    mask = head_mask((width, GROUP * cluster), head_width, cluster)
    for block in range(query_ref.shape[0]):
        own = normed_ref[pl.ds(block * cluster, cluster), :]
        own = jnp.concatenate([own] * GROUP, axis=0)
        query = lax.dot_general(query_w_ref[...], own, NT, preferred_element_type=jnp.float32)
        query = query * (math.log2(math.e) / head_width**0.5)
        query_ref[block] = jnp.where(mask, query, 0.0).astype(jnp.bfloat16)


def project_queries(normed, w_query, cluster):
    rows, width = normed.shape
    blocks = rows // cluster
    return pl.pallas_call(
        functools.partial(query_kernel, cluster=cluster, head_width=width // HEADS),
        grid=(blocks // SUB,),
        in_specs=[
            pl.BlockSpec((SUB * cluster, width), lambda i: (i, 0)),
            pl.BlockSpec((width, width), lambda i: (0, 0)),
        ],
        out_specs=pl.BlockSpec((SUB, width, GROUP * cluster), lambda i: (i, 0, 0)),
        out_shape=jax.ShapeDtypeStruct((blocks, width, GROUP * cluster), jnp.bfloat16),
        cost_estimate=lasting(6.5),
        compiler_params=kernel_params(),
        name="queries",
    )(normed, w_query.T)


def collect_kernel(*refs, places):
    buffer_ref, sems = refs[-2:]
    copy_pieces(refs[: len(places)], buffer_ref, places, sems)


def copy_pieces(piece_refs, buffer_ref, places, sems):
    copies = [
        pltpu.make_async_copy(piece, buffer_ref.at[pl.ds(at, piece.shape[0])], sems.at[n])
        for n, (piece, at) in enumerate(zip(piece_refs, places, strict=True))
    ]
    for copy in copies:
        copy.start()
    for copy in copies:
        copy.wait()


def collect(pieces, places, total):
    hbm = pl.BlockSpec(memory_space=pl.ANY)
    return pl.pallas_call(
        functools.partial(collect_kernel, places=places),
        in_specs=[hbm] * len(pieces),
        out_specs=hbm,
        out_shape=jax.ShapeDtypeStruct((total,) + pieces[0].shape[1:], pieces[0].dtype),
        scratch_shapes=[pltpu.SemaphoreType.DMA((len(pieces),))],
        cost_estimate=lasting(4),
        compiler_params=kernel_params(),
        name="collect_blocks",
    )(*pieces)


def attend_kernel(
    range_ref,
    order_ref,
    table_ref,
    query_ref,
    placed_ref,
    *rest,
    own_at,
    head_width,
    places,
):
    weight_refs, rest = rest[:4], rest[4:]
    piece_refs = rest[: len(places)]
    mixed_ref, buffer_ref, query_buf, member_buf, placed_buf = rest[-11:-6]
    attended_buf, before_buf, done_buf, in_sems, out_sems, piece_sems = rest[-6:]
    begin, count = range_ref[0], range_ref[1]
    pair_count = member_buf.shape[2] - 1
    copy_pieces(piece_refs, buffer_ref, places, piece_sems)

    def fetches(step, slot):
        for j in range(STEP):
            block = order_ref[step * STEP + j]
            sources = [(query_ref.at[block], query_buf.at[slot, j])]
            sources.append((placed_ref.at[block], placed_buf.at[slot, j]))
            sources.append((buffer_ref.at[own_at + block], member_buf.at[slot, j, 0]))
            for n in range(pair_count):
                listed = table_ref[block * pair_count + n]
                sources.append((buffer_ref.at[listed], member_buf.at[slot, j, 1 + n]))
            for n, (source_, target) in enumerate(sources):
                sem = in_sems.at[slot, j * (pair_count + 3) + n]
                yield pltpu.make_async_copy(source_, target, sem)

    def stores(step):
        for j in range(STEP):
            target = mixed_ref.at[order_ref[step * STEP + j]]
            yield pltpu.make_async_copy(done_buf.at[j], target, out_sems.at[j])

    def finish():
        return finish_step(before_buf[...], attended_buf[...], *weight_refs[2:])

    def one_step(i, carry):
        slot = i % 2
        for copy in fetches(begin + jnp.minimum(i + 1, count - 1), 1 - slot):
            copy.start()
        for copy in fetches(begin + i, slot):
            copy.wait()
        attended, mixed = attend_step(
            query_buf.at[slot], member_buf.at[slot], *weight_refs[:2], head_width, finish
        )

        @pl.when(i > 1)
        def _():
            for copy in stores(begin + i - 2):
                copy.wait()

        done_buf[...] = mixed.reshape(done_buf.shape)
        attended_buf[...] = attended
        before_buf[...] = placed_buf[slot].reshape(before_buf.shape)

        @pl.when(i > 0)
        def _():
            for copy in stores(begin + i - 1):
                copy.start()

        return carry

    @pl.when(count > 0)
    def _():
        for copy in fetches(begin, 0):
            copy.start()
        attended_buf[...] = jnp.zeros_like(attended_buf)
        before_buf[...] = jnp.zeros_like(before_buf)
        lax.fori_loop(0, count, one_step, 0)
        for copy in fetches(begin + count - 1, count % 2):
            copy.wait()
        mixed = finish()

        @pl.when(count > 1)
        def _():
            for copy in stores(begin + count - 2):
                copy.wait()

        done_buf[...] = mixed.reshape(done_buf.shape)
        for copy in stores(begin + count - 1):
            copy.start()
        for copy in stores(begin + count - 1):
            copy.wait()


def finish_step(placed, attended, out_w_ref, mix_ref):
    middle = placed.astype(jnp.float32) + jnp.dot(
        attended, out_w_ref[...], preferred_element_type=jnp.float32
    )
    middle = middle.astype(jnp.bfloat16).astype(jnp.float32)
    second = layer_norm(middle).astype(jnp.bfloat16)
    mixed = middle + jnp.tanh(jnp.dot(second, mix_ref[...], preferred_element_type=jnp.float32))
    return mixed.astype(jnp.bfloat16)


def attend_step(query_ref, member_ref, key_w_ref, value_w_ref, head_width, meanwhile):
    _, members_count, cluster, width = member_ref.shape
    span = GROUP * head_width
    tile = GROUP * cluster
    diagonal = head_mask((span, tile), head_width, cluster)
    fold_row = lax.broadcasted_iota(jnp.int32, (cluster, tile), 0)
    fold_lane = lax.broadcasted_iota(jnp.int32, (cluster, tile), 1) % cluster
    fold = jnp.where(fold_row == fold_lane, 1.0, 0.0).astype(jnp.bfloat16)
    zeros = jnp.zeros((span, tile), jnp.bfloat16)
    ones = jnp.ones((16, tile), jnp.bfloat16)
    tiles = HEADS // GROUP
    units = [(block, t) for block in range(STEP) for t in range(tiles)]
    keys, values = {}, {}

    def gather(block):
        members = member_ref[block].reshape(members_count * cluster, width)
        key = jnp.dot(members, key_w_ref[...], preferred_element_type=jnp.float32)
        keys[block] = key.astype(jnp.bfloat16)
        value = lax.dot_general(value_w_ref[...], members, NT, preferred_element_type=jnp.float32)
        values[block] = value.astype(jnp.bfloat16)

    def scores_of(block, t):
        if t == 0:
            gather(block)
        lo = t * span // 128 * 128
        picked = query_ref[block, t * span : (t + 1) * span, :]
        ahead, behind = t * span - lo, lo + 128 - (t + 1) * span
        stack = [zeros] * (ahead // span) + [picked] + [zeros] * (behind // span)
        return jnp.dot(
            keys[block][:, lo : lo + 128],
            jnp.concatenate(stack, axis=0),
            preferred_element_type=jnp.float32,
        )

    def weights_of(scores):
        top = jnp.max(scores, axis=0, keepdims=True)
        return jnp.exp2(scores - top).astype(jnp.bfloat16)

    def product_of(block, t, weights):
        lifted = jnp.concatenate([values[block][t * span : (t + 1) * span], ones], axis=0)
        return jnp.dot(lifted, weights, preferred_element_type=jnp.float32)

    def scaled(product):
        result = product[:span] * (1.0 / product[span : span + 1])
        return jnp.where(diagonal, result, 0.0).astype(jnp.bfloat16)

    count = len(units)
    scores, weights, products, pieces, attended = {}, {}, {}, [], []
    for at in range(-SCORES_AHEAD, count + 1):
        if at == 0:
            other = meanwhile()
        if at + SCORES_AHEAD < count:
            scores[at + SCORES_AHEAD] = scores_of(*units[at + SCORES_AHEAD])
        if 0 <= at + WEIGHTS_AHEAD < count:
            weights[at + WEIGHTS_AHEAD] = weights_of(scores.pop(at + WEIGHTS_AHEAD))
        if 0 <= at < count:
            products[at] = product_of(*units[at], weights.pop(at))
        if at > 0:
            pieces.append(scaled(products.pop(at - 1)))
            if len(pieces) == tiles:
                stacked = jnp.concatenate(pieces, axis=0)
                folded = lax.dot_general(fold, stacked, NT, preferred_element_type=jnp.float32)
                attended.append(folded.astype(jnp.bfloat16))
                pieces = []
    return jnp.concatenate(attended, axis=0), other


def attend(begin, count, order, table, queries, placed, weights, buffer, pieces, places, own_at, so_far):
    blocks, cluster, width = placed.shape
    pair_count = table.shape[0] // blocks
    smem = pl.BlockSpec(memory_space=pltpu.SMEM)
    vmem = pl.BlockSpec(memory_space=pltpu.VMEM)
    hbm = pl.BlockSpec(memory_space=pl.ANY)
    in_specs = [smem, smem, smem, hbm, hbm] + [vmem] * 4 + [hbm] * (len(pieces) + 1)
    aliases = {len(in_specs) - 1: 1}
    operands = [queries, placed, *weights, *pieces, buffer]
    if so_far is not None:
        aliases[len(in_specs)] = 0
        in_specs.append(hbm)
        operands.append(so_far)
    kernel = functools.partial(
        attend_kernel, own_at=own_at, head_width=width // HEADS, places=places
    )
    return pl.pallas_call(
        kernel,
        in_specs=in_specs,
        out_specs=[hbm, hbm],
        out_shape=[
            jax.ShapeDtypeStruct(placed.shape, jnp.bfloat16),
            jax.ShapeDtypeStruct(buffer.shape, jnp.bfloat16),
        ],
        scratch_shapes=[
            pltpu.VMEM((2, STEP) + queries.shape[1:], jnp.bfloat16),
            pltpu.VMEM((2, STEP, pair_count + 1, cluster, width), jnp.bfloat16),
            pltpu.VMEM((2, STEP, cluster, width), jnp.bfloat16),
            pltpu.VMEM((STEP * cluster, width), jnp.bfloat16),
            pltpu.VMEM((STEP * cluster, width), jnp.bfloat16),
            pltpu.VMEM((STEP, cluster, width), jnp.bfloat16),
            pltpu.SemaphoreType.DMA((2, STEP * (pair_count + 3))),
            pltpu.SemaphoreType.DMA((STEP,)),
            pltpu.SemaphoreType.DMA((len(pieces),)),
        ],
        input_output_aliases=aliases,
        cost_estimate=lasting(18),
        compiler_params=kernel_params(),
        name="attend_blocks",
    )(jnp.stack([begin, count]).astype(jnp.int32), order, table, *operands)


def slot_tables(owner, within, capacity):
    entries = owner.shape[0]
    alike = owner[:, None] == owner[None, :]
    earlier = jnp.arange(entries)[None, :] < jnp.arange(entries)[:, None]
    ranking = jnp.sum(jnp.where(alike & earlier, 1, 0), axis=1).astype(jnp.int32)
    slots = owner * capacity + ranking
    matches = slots[None, :] == jnp.arange(SPAN * capacity, dtype=jnp.int32)[:, None]
    return ranking, jnp.sum(jnp.where(matches, within[None, :], 0), axis=1).astype(jnp.int32)


def by_class(classes, count):
    blocks = jnp.arange(classes.shape[0], dtype=jnp.int32)
    before = (classes[None, :] < classes[:, None]) | (
        (classes[None, :] == classes[:, None]) & (blocks[None, :] < blocks[:, None])
    )
    rank = jnp.sum(jnp.where(before, 1, 0), axis=1)
    order = jnp.sum(jnp.where(rank[None, :] == blocks[:, None], blocks[None, :], 0), axis=1)
    ends = [jnp.sum(jnp.where(classes <= c, 1, 0)).astype(jnp.int32) for c in range(count)]
    return order.astype(jnp.int32), ends


OUT = (2, 0, 3, 1)
FROM = (1, 3, 0, 2)
LEVELS = 4


def position_at(z, y):
    return 2 * z + y


def partner(position):
    return position ^ 1


def onward(position):
    return position_at(choose(position // 2, OUT), position % 2)


def source(position):
    return position_at(choose(position // 2, FROM), position % 2)


def opposite(position):
    return position_at(LEVELS - 1 - position // 2, position % 2)


def itself(position):
    return position


def crossed(route):
    return lambda position: partner(route(position))


SECOND_PLAN = (((0, source, itself), (1, source, partner)),)
MIDDLE_PLAN = (((0, opposite, itself),),)
MIDDLE_CROSS_PLAN = (((0, opposite, partner),),)
ON_PLAN = (((0, crossed(onward), source),), ((0, onward, source),))
NEAR_PLAN = (((0, partner, source),),)


def body(features, assignment, pairs, w_query, w_key, w_value, w_out, w_mix):
    rows_dev, width = features.shape
    block_count, pair_count = pairs.shape
    cluster = rows_dev // block_count
    stride = lax.axis_size("elec") // SPAN
    groups = [[rest + place_ * stride for place_ in range(SPAN)] for rest in range(stride)]
    position = lax.axis_index("elec") // stride
    at_position = position.reshape(1)
    capacity = (block_count * pair_count + SPAN - 1) // SPAN + 1

    def moved(x, moves):
        pairs_of = [(s * stride + r, d * stride + r) for s, d in moves for r in range(stride)]
        return lax.ppermute(x, "elec", pairs_of)

    def across_z(pairs_of_z):
        return [(position_at(s, y), position_at(d, y)) for s, d in pairs_of_z for y in range(2)]

    swap = [(p, p ^ 1) for p in range(SPAN)]
    first_moves = across_z(enumerate(OUT))
    second_moves = across_z(enumerate(FROM))
    middle_moves = across_z([(1, 2), (2, 1)])
    outward_moves = across_z([(2, 3), (1, 0)])

    listed = pairs.reshape(-1)
    owner = listed // block_count // stride
    within = listed % block_count
    ranking, tables = slot_tables(owner, within, capacity)
    wanted = lax.all_to_all(
        jnp.broadcast_to(tables[None], (SPAN, SPAN * capacity)),
        "elec",
        split_axis=0,
        concat_axis=0,
        axis_index_groups=groups,
        tiled=True,
    )

    placed, normed = place(features, assignment.reshape(block_count // SUB, 1, SUB * cluster))
    blocks = normed.reshape(block_count, cluster, width)
    passed = moved(blocks, first_moves)
    beside = moved(blocks, swap)

    queries = project_queries(normed, w_query, cluster)
    own_at = 7 * capacity
    passed_at = own_at + block_count
    beside_at = passed_at + block_count
    total = beside_at + block_count

    (second,) = pick(at_position, wanted, (blocks, beside), SECOND_PLAN)
    second = moved(second, second_moves)
    on, outward = pick(at_position, wanted, (passed,), ON_PLAN)
    on = moved(on, swap)
    outward = moved(outward, outward_moves)
    (near,) = pick(at_position, wanted, (passed,), NEAR_PLAN, after=(on,))
    near = moved(near, swap)
    (middle,) = pick(at_position, wanted, (blocks,), MIDDLE_PLAN, after=(on,))
    middle = moved(middle, middle_moves)
    on = moved(on, outward_moves)
    (middle_cross,) = pick(
        at_position, wanted, (beside,), MIDDLE_CROSS_PLAN, after=(second,)
    )
    middle_cross = moved(middle_cross, middle_moves)

    buffer = collect((blocks, passed, beside), (own_at, passed_at, beside_at), total)

    z, y = position // 2, position % 2
    is_end = (z == 0) | (z == LEVELS - 1)
    z_owner, same = owner // 2, owner % 2 == y
    from_first = z_owner == choose(z, FROM)
    late = z_owner == LEVELS - 1 - z
    piece_of = jnp.where(
        from_first,
        0,
        jnp.where(
            late,
            jnp.where(is_end, jnp.where(same, 3, 4), jnp.where(same, 5, 6)),
            jnp.where(same, 1, 2),
        ),
    )
    whole_at = jnp.where(z_owner == z, jnp.where(same, own_at, beside_at), passed_at)
    whole = (z_owner == z) | (from_first & same)
    table = jnp.where(whole, whole_at + within, piece_of * capacity + ranking)

    arrival = jnp.where(late, jnp.where(same | is_end, 1, 2), 0)
    order, ends = by_class(jnp.max(arrival.reshape(block_count, pair_count), axis=1), 2)
    marks = [0, ends[0] // STEP, ends[1] // STEP, block_count // STEP]
    phases = [(marks[n], marks[n + 1] - marks[n]) for n in range(3)]
    weights = (w_key, w_value.T, w_out, w_mix)
    shared = (order, table, queries, placed.reshape(blocks.shape), weights)
    arrivals = (
        ((near, 0), (second, 1)),
        ((outward, 3), (on, 4), (middle, 5)),
        ((middle_cross, 6),),
    )
    mixed = None
    for phase, arrived in zip(phases, arrivals, strict=True):
        pieces = [piece for piece, _ in arrived]
        places = tuple(at * capacity for _, at in arrived)
        mixed, buffer = attend(*phase, *shared, buffer, pieces, places, own_at, mixed)
    return mixed.reshape(rows_dev, width)


def solution(mesh):
    placed = (
        P(("groups", "elec"), None),
        P(("groups", "elec")),
        P(("groups", "elec"), None),
        P(),
        P(),
        P(),
        P(),
        P(),
    )
    return jax.shard_map(
        body, mesh=mesh, in_specs=placed, out_specs=P(("groups", "elec"), None), check_vma=False
    )
```

```python
import functools
import math

import jax
import jax.numpy as jnp
from jax import lax
from jax.experimental import pallas as pl
from jax.experimental.pallas import tpu as pltpu
from jax.sharding import PartitionSpec as P

HEADS = 16
SPAN = 8
SUB = 8
GROUP = 4
STEP = 4
SCORES_AHEAD, WEIGHTS_AHEAD = 3, 1
VMEM_BYTES = 48 * 1024 * 1024

NT = (((1,), (1,)), ((), ()))


def lasting(us):
    return pl.CostEstimate(flops=int(us * 1.15e9), bytes_accessed=0, transcendentals=0)


def kernel_params():
    return pltpu.CompilerParams(vmem_limit_bytes=VMEM_BYTES)


def layer_norm(rows):
    mean = jnp.mean(rows, axis=-1, keepdims=True)
    centred = rows - mean
    variance = jnp.mean(centred * centred, axis=-1, keepdims=True)
    return centred * lax.rsqrt(variance + 1e-05)


def head_mask(shape, head_width, cluster):
    row_head = lax.broadcasted_iota(jnp.int32, shape, 0) // head_width % GROUP
    lane_head = lax.broadcasted_iota(jnp.int32, shape, 1) // cluster
    return row_head == lane_head


def place_kernel(features_ref, assignment_ref, placed_ref, normed_ref):
    rows = features_ref.shape[0]
    lane = 128
    features = features_ref[...]
    columns = lax.broadcasted_iota(jnp.int32, (lane, rows), 1)
    for part in range(rows // lane):
        chosen = assignment_ref[0, :, part * lane : (part + 1) * lane] & (rows - 1)
        chosen = jnp.broadcast_to(chosen, (lane, lane)).T
        chosen = jnp.concatenate([chosen] * (rows // lane), axis=1)
        one_hot = jnp.where(chosen == columns, 1.0, 0.0).astype(jnp.bfloat16)
        placed = jnp.dot(one_hot, features, preferred_element_type=jnp.float32)
        placed_ref[pl.ds(part * lane, lane), :] = placed.astype(jnp.bfloat16)
        normed_ref[pl.ds(part * lane, lane), :] = layer_norm(placed).astype(jnp.bfloat16)


def place(features, assignment):
    width = features.shape[1]
    walkers, _, rows = assignment.shape
    local = pl.BlockSpec((rows, width), lambda i: (i, 0))
    out = jax.ShapeDtypeStruct(features.shape, jnp.bfloat16)
    return pl.pallas_call(
        place_kernel,
        grid=(walkers,),
        in_specs=[local, pl.BlockSpec((1, 1, rows), lambda i: (i, 0, 0))],
        out_specs=[local] * 2,
        out_shape=[out, out],
        cost_estimate=lasting(7),
        compiler_params=kernel_params(),
        name="place_rows",
    )(features, assignment)


def choose(index, values):
    result = values[-1]
    for at in range(len(values) - 2, -1, -1):
        result = jnp.where(index == at, values[at], result)
    return result


def pick_kernel(position_ref, wanted_ref, *rest, plan, capacity):
    position = position_ref[0]
    for out_ref, pieces in zip(rest[len(rest) - len(plan) :], plan, strict=True):
        for at, (blocks, reader_of, owner_of) in enumerate(pieces):
            reader, first = reader_of(position), owner_of(position) * capacity

            def one_slot(slot, carry, out_ref=out_ref, at=at, blocks=blocks, reader=reader, first=first):
                out_ref[at * capacity + slot] = rest[blocks][wanted_ref[reader, first + slot]]
                return carry

            lax.fori_loop(0, capacity, one_slot, 0)


def pick(position, wanted, sources, plan, after=()):
    capacity = wanted.shape[1] // SPAN
    block = sources[0].shape[1:]
    outs = [
        jax.ShapeDtypeStruct((len(pieces) * capacity,) + block, sources[0].dtype)
        for pieces in plan
    ]
    smem = pl.BlockSpec(memory_space=pltpu.SMEM)
    vmem = pl.BlockSpec(memory_space=pltpu.VMEM)
    return pl.pallas_call(
        functools.partial(pick_kernel, plan=plan, capacity=capacity),
        in_specs=[smem, smem]
        + [vmem] * len(sources)
        + [pl.BlockSpec(memory_space=pl.ANY)] * len(after),
        out_specs=[vmem] * len(outs),
        out_shape=outs,
        cost_estimate=lasting(1.5),
        compiler_params=kernel_params(),
        name="pick_blocks",
    )(position, wanted, *sources, *after)


def query_kernel(normed_ref, query_w_ref, query_ref, *, cluster, head_width):
    width = normed_ref.shape[1]
    mask = head_mask((width, GROUP * cluster), head_width, cluster)
    for block in range(query_ref.shape[0]):
        own = normed_ref[pl.ds(block * cluster, cluster), :]
        own = jnp.concatenate([own] * GROUP, axis=0)
        query = lax.dot_general(query_w_ref[...], own, NT, preferred_element_type=jnp.float32)
        query = query * (math.log2(math.e) / head_width**0.5)
        query_ref[block] = jnp.where(mask, query, 0.0).astype(jnp.bfloat16)


def project_queries(normed, w_query, cluster):
    rows, width = normed.shape
    blocks = rows // cluster
    return pl.pallas_call(
        functools.partial(query_kernel, cluster=cluster, head_width=width // HEADS),
        grid=(blocks // SUB,),
        in_specs=[
            pl.BlockSpec((SUB * cluster, width), lambda i: (i, 0)),
            pl.BlockSpec((width, width), lambda i: (0, 0)),
        ],
        out_specs=pl.BlockSpec((SUB, width, GROUP * cluster), lambda i: (i, 0, 0)),
        out_shape=jax.ShapeDtypeStruct((blocks, width, GROUP * cluster), jnp.bfloat16),
        cost_estimate=lasting(6.5),
        compiler_params=kernel_params(),
        name="queries",
    )(normed, w_query.T)


def collect_kernel(*refs, places):
    buffer_ref, sems = refs[-2:]
    copy_pieces(refs[: len(places)], buffer_ref, places, sems)


def copy_pieces(piece_refs, buffer_ref, places, sems):
    copies = [
        pltpu.make_async_copy(piece, buffer_ref.at[pl.ds(at, piece.shape[0])], sems.at[n])
        for n, (piece, at) in enumerate(zip(piece_refs, places, strict=True))
    ]
    for copy in copies:
        copy.start()
    for copy in copies:
        copy.wait()


def collect(pieces, places, total):
    return pl.pallas_call(
        functools.partial(collect_kernel, places=places),
        in_specs=[pl.BlockSpec(memory_space=pltpu.VMEM)] * len(pieces),
        out_specs=pl.BlockSpec(memory_space=pl.ANY),
        out_shape=jax.ShapeDtypeStruct((total,) + pieces[0].shape[1:], pieces[0].dtype),
        scratch_shapes=[pltpu.SemaphoreType.DMA((len(pieces),))],
        cost_estimate=lasting(4),
        compiler_params=kernel_params(),
        name="collect_blocks",
    )(*pieces)


def attend_kernel(
    range_ref,
    order_ref,
    table_ref,
    query_ref,
    placed_ref,
    *rest,
    own_at,
    head_width,
    places,
):
    weight_refs, rest = rest[:4], rest[4:]
    piece_refs = rest[: len(places)]
    mixed_ref, buffer_ref, query_buf, member_buf, placed_buf = rest[-11:-6]
    attended_buf, before_buf, done_buf, in_sems, out_sems, piece_sems = rest[-6:]
    begin, count = range_ref[0], range_ref[1]
    pair_count = member_buf.shape[2] - 1
    copy_pieces(piece_refs, buffer_ref, places, piece_sems)

    def fetches(step, slot):
        for j in range(STEP):
            block = order_ref[step * STEP + j]
            sources = [(query_ref.at[block], query_buf.at[slot, j])]
            sources.append((placed_ref.at[block], placed_buf.at[slot, j]))
            sources.append((buffer_ref.at[own_at + block], member_buf.at[slot, j, 0]))
            for n in range(pair_count):
                listed = table_ref[block * pair_count + n]
                sources.append((buffer_ref.at[listed], member_buf.at[slot, j, 1 + n]))
            for n, (source_, target) in enumerate(sources):
                sem = in_sems.at[slot, j * (pair_count + 3) + n]
                yield pltpu.make_async_copy(source_, target, sem)

    def stores(step):
        for j in range(STEP):
            target = mixed_ref.at[order_ref[step * STEP + j]]
            yield pltpu.make_async_copy(done_buf.at[j], target, out_sems.at[j])

    def finish():
        return finish_step(before_buf[...], attended_buf[...], *weight_refs[2:])

    def one_step(i, carry):
        slot = i % 2
        for copy in fetches(begin + jnp.minimum(i + 1, count - 1), 1 - slot):
            copy.start()
        for copy in fetches(begin + i, slot):
            copy.wait()
        attended, mixed = attend_step(
            query_buf.at[slot], member_buf.at[slot], *weight_refs[:2], head_width, finish
        )

        @pl.when(i > 1)
        def _():
            for copy in stores(begin + i - 2):
                copy.wait()

        done_buf[...] = mixed.reshape(done_buf.shape)
        attended_buf[...] = attended
        before_buf[...] = placed_buf[slot].reshape(before_buf.shape)

        @pl.when(i > 0)
        def _():
            for copy in stores(begin + i - 1):
                copy.start()

        return carry

    @pl.when(count > 0)
    def _():
        for copy in fetches(begin, 0):
            copy.start()
        attended_buf[...] = jnp.zeros_like(attended_buf)
        before_buf[...] = jnp.zeros_like(before_buf)
        lax.fori_loop(0, count, one_step, 0)
        for copy in fetches(begin + count - 1, count % 2):
            copy.wait()
        mixed = finish()

        @pl.when(count > 1)
        def _():
            for copy in stores(begin + count - 2):
                copy.wait()

        done_buf[...] = mixed.reshape(done_buf.shape)
        for copy in stores(begin + count - 1):
            copy.start()
        for copy in stores(begin + count - 1):
            copy.wait()


def finish_step(placed, attended, out_w_ref, mix_ref):
    middle = placed.astype(jnp.float32) + jnp.dot(
        attended, out_w_ref[...], preferred_element_type=jnp.float32
    )
    middle = middle.astype(jnp.bfloat16).astype(jnp.float32)
    second = layer_norm(middle).astype(jnp.bfloat16)
    mixed = middle + jnp.tanh(jnp.dot(second, mix_ref[...], preferred_element_type=jnp.float32))
    return mixed.astype(jnp.bfloat16)


def attend_step(query_ref, member_ref, key_w_ref, value_w_ref, head_width, meanwhile):
    _, members_count, cluster, width = member_ref.shape
    span = GROUP * head_width
    tile = GROUP * cluster
    diagonal = head_mask((span, tile), head_width, cluster)
    fold_row = lax.broadcasted_iota(jnp.int32, (cluster, tile), 0)
    fold_lane = lax.broadcasted_iota(jnp.int32, (cluster, tile), 1) % cluster
    fold = jnp.where(fold_row == fold_lane, 1.0, 0.0).astype(jnp.bfloat16)
    zeros = jnp.zeros((span, tile), jnp.bfloat16)
    ones = jnp.ones((16, tile), jnp.bfloat16)
    tiles = HEADS // GROUP
    units = [(block, t) for block in range(STEP) for t in range(tiles)]
    keys, values = {}, {}

    def gather(block):
        members = member_ref[block].reshape(members_count * cluster, width)
        key = jnp.dot(members, key_w_ref[...], preferred_element_type=jnp.float32)
        keys[block] = key.astype(jnp.bfloat16)
        value = lax.dot_general(value_w_ref[...], members, NT, preferred_element_type=jnp.float32)
        values[block] = value.astype(jnp.bfloat16)

    def scores_of(block, t):
        if t == 0:
            gather(block)
        lo = t * span // 128 * 128
        picked = query_ref[block, t * span : (t + 1) * span, :]
        ahead, behind = t * span - lo, lo + 128 - (t + 1) * span
        stack = [zeros] * (ahead // span) + [picked] + [zeros] * (behind // span)
        return jnp.dot(
            keys[block][:, lo : lo + 128],
            jnp.concatenate(stack, axis=0),
            preferred_element_type=jnp.float32,
        )

    def weights_of(scores):
        top = jnp.max(scores, axis=0, keepdims=True)
        return jnp.exp2(scores - top).astype(jnp.bfloat16)

    def product_of(block, t, weights):
        lifted = jnp.concatenate([values[block][t * span : (t + 1) * span], ones], axis=0)
        return jnp.dot(lifted, weights, preferred_element_type=jnp.float32)

    def scaled(product):
        result = product[:span] * (1.0 / product[span : span + 1])
        return jnp.where(diagonal, result, 0.0).astype(jnp.bfloat16)

    count = len(units)
    scores, weights, products, pieces, attended = {}, {}, {}, [], []
    for at in range(-SCORES_AHEAD, count + 1):
        if at == 0:
            other = meanwhile()
        if at + SCORES_AHEAD < count:
            scores[at + SCORES_AHEAD] = scores_of(*units[at + SCORES_AHEAD])
        if 0 <= at + WEIGHTS_AHEAD < count:
            weights[at + WEIGHTS_AHEAD] = weights_of(scores.pop(at + WEIGHTS_AHEAD))
        if 0 <= at < count:
            products[at] = product_of(*units[at], weights.pop(at))
        if at > 0:
            pieces.append(scaled(products.pop(at - 1)))
            if len(pieces) == tiles:
                stacked = jnp.concatenate(pieces, axis=0)
                folded = lax.dot_general(fold, stacked, NT, preferred_element_type=jnp.float32)
                attended.append(folded.astype(jnp.bfloat16))
                pieces = []
    return jnp.concatenate(attended, axis=0), other


def attend(begin, count, order, table, queries, placed, weights, buffer, pieces, places, own_at, so_far):
    blocks, cluster, width = placed.shape
    pair_count = table.shape[0] // blocks
    smem = pl.BlockSpec(memory_space=pltpu.SMEM)
    vmem = pl.BlockSpec(memory_space=pltpu.VMEM)
    hbm = pl.BlockSpec(memory_space=pl.ANY)
    in_specs = [smem, smem, smem, hbm, hbm] + [vmem] * (4 + len(pieces)) + [hbm]
    aliases = {len(in_specs) - 1: 1}
    operands = [queries, placed, *weights, *pieces, buffer]
    if so_far is not None:
        aliases[len(in_specs)] = 0
        in_specs.append(hbm)
        operands.append(so_far)
    kernel = functools.partial(
        attend_kernel, own_at=own_at, head_width=width // HEADS, places=places
    )
    return pl.pallas_call(
        kernel,
        in_specs=in_specs,
        out_specs=[hbm, hbm],
        out_shape=[
            jax.ShapeDtypeStruct(placed.shape, jnp.bfloat16),
            jax.ShapeDtypeStruct(buffer.shape, jnp.bfloat16),
        ],
        scratch_shapes=[
            pltpu.VMEM((2, STEP) + queries.shape[1:], jnp.bfloat16),
            pltpu.VMEM((2, STEP, pair_count + 1, cluster, width), jnp.bfloat16),
            pltpu.VMEM((2, STEP, cluster, width), jnp.bfloat16),
            pltpu.VMEM((STEP * cluster, width), jnp.bfloat16),
            pltpu.VMEM((STEP * cluster, width), jnp.bfloat16),
            pltpu.VMEM((STEP, cluster, width), jnp.bfloat16),
            pltpu.SemaphoreType.DMA((2, STEP * (pair_count + 3))),
            pltpu.SemaphoreType.DMA((STEP,)),
            pltpu.SemaphoreType.DMA((len(pieces),)),
        ],
        input_output_aliases=aliases,
        cost_estimate=lasting(18),
        compiler_params=kernel_params(),
        name="attend_blocks",
    )(jnp.stack([begin, count]).astype(jnp.int32), order, table, *operands)


def slot_tables(owner, within, capacity):
    entries = owner.shape[0]
    alike = owner[:, None] == owner[None, :]
    earlier = jnp.arange(entries)[None, :] < jnp.arange(entries)[:, None]
    ranking = jnp.sum(jnp.where(alike & earlier, 1, 0), axis=1).astype(jnp.int32)
    slots = owner * capacity + ranking
    matches = slots[None, :] == jnp.arange(SPAN * capacity, dtype=jnp.int32)[:, None]
    return ranking, jnp.sum(jnp.where(matches, within[None, :], 0), axis=1).astype(jnp.int32)


def by_class(classes, count):
    blocks = jnp.arange(classes.shape[0], dtype=jnp.int32)
    before = (classes[None, :] < classes[:, None]) | (
        (classes[None, :] == classes[:, None]) & (blocks[None, :] < blocks[:, None])
    )
    rank = jnp.sum(jnp.where(before, 1, 0), axis=1)
    order = jnp.sum(jnp.where(rank[None, :] == blocks[:, None], blocks[None, :], 0), axis=1)
    ends = [jnp.sum(jnp.where(classes <= c, 1, 0)).astype(jnp.int32) for c in range(count)]
    return order.astype(jnp.int32), ends


OUT = (2, 0, 3, 1)
FROM = (1, 3, 0, 2)
LEVELS = 4


def position_at(z, y):
    return 2 * z + y


def partner(position):
    return position ^ 1


def onward(position):
    return position_at(choose(position // 2, OUT), position % 2)


def source(position):
    return position_at(choose(position // 2, FROM), position % 2)


def opposite(position):
    return position_at(LEVELS - 1 - position // 2, position % 2)


def itself(position):
    return position


def crossed(route):
    return lambda position: partner(route(position))


SECOND_PLAN = (((0, source, itself), (1, source, partner)),)
MIDDLE_PLAN = (((0, opposite, itself),),)
MIDDLE_CROSS_PLAN = (((0, opposite, partner),),)
ON_PLAN = (((0, crossed(onward), source),), ((0, onward, source),))
NEAR_PLAN = (((0, partner, source),),)


def body(features, assignment, pairs, w_query, w_key, w_value, w_out, w_mix):
    rows_dev, width = features.shape
    block_count, pair_count = pairs.shape
    cluster = rows_dev // block_count
    stride = lax.axis_size("elec") // SPAN
    groups = [[rest + place_ * stride for place_ in range(SPAN)] for rest in range(stride)]
    position = lax.axis_index("elec") // stride
    at_position = position.reshape(1)
    capacity = (block_count * pair_count + SPAN - 1) // SPAN + 1

    def moved(x, moves):
        pairs_of = [(s * stride + r, d * stride + r) for s, d in moves for r in range(stride)]
        return lax.ppermute(x, "elec", pairs_of)

    def across_z(pairs_of_z):
        return [(position_at(s, y), position_at(d, y)) for s, d in pairs_of_z for y in range(2)]

    swap = [(p, p ^ 1) for p in range(SPAN)]
    first_moves = across_z(enumerate(OUT))
    second_moves = across_z(enumerate(FROM))
    middle_moves = across_z([(1, 2), (2, 1)])
    outward_moves = across_z([(2, 3), (1, 0)])

    listed = pairs.reshape(-1)
    owner = listed // block_count // stride
    within = listed % block_count
    ranking, tables = slot_tables(owner, within, capacity)
    wanted = lax.all_to_all(
        jnp.broadcast_to(tables[None], (SPAN, SPAN * capacity)),
        "elec",
        split_axis=0,
        concat_axis=0,
        axis_index_groups=groups,
        tiled=True,
    )

    placed, normed = place(features, assignment.reshape(block_count // SUB, 1, SUB * cluster))
    blocks = normed.reshape(block_count, cluster, width)
    passed = moved(blocks, first_moves)
    beside = moved(blocks, swap)

    queries = project_queries(normed, w_query, cluster)
    own_at = 7 * capacity
    passed_at = own_at + block_count
    beside_at = passed_at + block_count
    total = beside_at + block_count

    (second,) = pick(at_position, wanted, (blocks, beside), SECOND_PLAN)
    second = moved(second, second_moves)
    on, outward = pick(at_position, wanted, (passed,), ON_PLAN)
    on = moved(on, swap)
    outward = moved(outward, outward_moves)
    (near,) = pick(at_position, wanted, (passed,), NEAR_PLAN, after=(on,))
    near = moved(near, swap)
    (middle,) = pick(at_position, wanted, (blocks,), MIDDLE_PLAN, after=(on,))
    middle = moved(middle, middle_moves)
    on = moved(on, outward_moves)
    (middle_cross,) = pick(
        at_position, wanted, (beside,), MIDDLE_CROSS_PLAN, after=(second,)
    )
    middle_cross = moved(middle_cross, middle_moves)

    buffer = collect((blocks, passed, beside), (own_at, passed_at, beside_at), total)

    z, y = position // 2, position % 2
    is_end = (z == 0) | (z == LEVELS - 1)
    z_owner, same = owner // 2, owner % 2 == y
    from_first = z_owner == choose(z, FROM)
    late = z_owner == LEVELS - 1 - z
    piece_of = jnp.where(
        from_first,
        0,
        jnp.where(
            late,
            jnp.where(is_end, jnp.where(same, 3, 4), jnp.where(same, 5, 6)),
            jnp.where(same, 1, 2),
        ),
    )
    whole_at = jnp.where(z_owner == z, jnp.where(same, own_at, beside_at), passed_at)
    whole = (z_owner == z) | (from_first & same)
    table = jnp.where(whole, whole_at + within, piece_of * capacity + ranking)

    arrival = jnp.where(late, jnp.where(same | is_end, 1, 2), 0)
    order, ends = by_class(jnp.max(arrival.reshape(block_count, pair_count), axis=1), 2)
    marks = [0, ends[0] // STEP, ends[1] // STEP, block_count // STEP]
    phases = [(marks[n], marks[n + 1] - marks[n]) for n in range(3)]
    weights = (w_key, w_value.T, w_out, w_mix)
    shared = (order, table, queries, placed.reshape(blocks.shape), weights)
    arrivals = (
        ((near, 0), (second, 1)),
        ((outward, 3), (on, 4), (middle, 5)),
        ((middle_cross, 6),),
    )
    mixed = None
    for phase, arrived in zip(phases, arrivals, strict=True):
        pieces = [piece for piece, _ in arrived]
        places = tuple(at * capacity for _, at in arrived)
        mixed, buffer = attend(*phase, *shared, buffer, pieces, places, own_at, mixed)
    return mixed.reshape(rows_dev, width)


def solution(mesh):
    placed = (
        P(("groups", "elec"), None),
        P(("groups", "elec")),
        P(("groups", "elec"), None),
        P(),
        P(),
        P(),
        P(),
        P(),
    )
    return jax.shard_map(
        body, mesh=mesh, in_specs=placed, out_specs=P(("groups", "elec"), None), check_vma=False
    )
```

```python
import functools
import math

import jax
import jax.numpy as jnp
from jax import lax
from jax.experimental import pallas as pl
from jax.experimental.pallas import tpu as pltpu
from jax.sharding import PartitionSpec as P

HEADS = 16
SPAN = 8
SUB = 8
GROUP = 4
STEP = 4
SCORES_AHEAD, WEIGHTS_AHEAD = 2, 1
VMEM_BYTES = 48 * 1024 * 1024

NT = (((1,), (1,)), ((), ()))


def lasting(us):
    return pl.CostEstimate(flops=int(us * 1.15e9), bytes_accessed=0, transcendentals=0)


def kernel_params():
    return pltpu.CompilerParams(vmem_limit_bytes=VMEM_BYTES)


def layer_norm(rows):
    mean = jnp.mean(rows, axis=-1, keepdims=True)
    centred = rows - mean
    variance = jnp.mean(centred * centred, axis=-1, keepdims=True)
    return centred * lax.rsqrt(variance + 1e-05)


def head_mask(shape, head_width, cluster):
    row_head = lax.broadcasted_iota(jnp.int32, shape, 0) // head_width % GROUP
    lane_head = lax.broadcasted_iota(jnp.int32, shape, 1) // cluster
    return row_head == lane_head


def place_kernel(features_ref, assignment_ref, *rest, outputs):
    normed_ref, *placed_ref = rest[len(rest) - outputs :]
    walkers, _, rows = assignment_ref.shape
    lane = 128
    columns = lax.broadcasted_iota(jnp.int32, (lane, rows), 1)
    for walker in range(walkers):
        features = features_ref[walker * rows : (walker + 1) * rows, :]
        for part in range(rows // lane):
            chosen = assignment_ref[walker, :, part * lane : (part + 1) * lane] & (rows - 1)
            chosen = jnp.broadcast_to(chosen, (lane, lane)).T
            chosen = jnp.concatenate([chosen] * (rows // lane), axis=1)
            one_hot = jnp.where(chosen == columns, 1.0, 0.0).astype(jnp.bfloat16)
            placed = jnp.dot(one_hot, features, preferred_element_type=jnp.float32)
            here = pl.ds(walker * rows + part * lane, lane)
            if placed_ref:
                placed_ref[0][here, :] = placed.astype(jnp.bfloat16)
            normed_ref[here, :] = layer_norm(placed).astype(jnp.bfloat16)


def place(features, assignment, outputs, after=()):
    width = features.shape[1]
    walkers, _, rows = assignment.shape
    local = pl.BlockSpec((2 * rows, width), lambda i: (i, 0))
    out = jax.ShapeDtypeStruct(features.shape, jnp.bfloat16)
    return pl.pallas_call(
        functools.partial(place_kernel, outputs=outputs),
        grid=(walkers // 2,),
        in_specs=[local, pl.BlockSpec((2, 1, rows), lambda i: (i, 0, 0))]
        + [pl.BlockSpec(memory_space=pl.ANY)] * len(after),
        out_specs=[local] * outputs,
        out_shape=[out] * outputs,
        cost_estimate=lasting(7),
        compiler_params=kernel_params(),
        name="place_rows",
    )(features, assignment, *after)


def choose(index, values):
    result = values[-1]
    for at in range(len(values) - 2, -1, -1):
        result = jnp.where(index == at, values[at], result)
    return result


def pick_kernel(position_ref, wanted_ref, *rest, plan, capacity):
    position = position_ref[0]
    for out_ref, pieces in zip(rest[len(rest) - len(plan) :], plan, strict=True):
        for at, (blocks, reader_of, owner_of) in enumerate(pieces):
            reader, first = reader_of(position), owner_of(position) * capacity

            def one_slot(slot, carry, out_ref=out_ref, at=at, blocks=blocks, reader=reader, first=first):
                out_ref[at * capacity + slot] = rest[blocks][wanted_ref[reader, first + slot]]
                return carry

            lax.fori_loop(0, capacity, one_slot, 0)


def pick(position, wanted, sources, plan, after=()):
    capacity = wanted.shape[1] // SPAN
    block = sources[0].shape[1:]
    outs = [
        jax.ShapeDtypeStruct((len(pieces) * capacity,) + block, sources[0].dtype)
        for pieces in plan
    ]
    smem = pl.BlockSpec(memory_space=pltpu.SMEM)
    vmem = pl.BlockSpec(memory_space=pltpu.VMEM)
    return pl.pallas_call(
        functools.partial(pick_kernel, plan=plan, capacity=capacity),
        in_specs=[smem, smem]
        + [vmem] * len(sources)
        + [pl.BlockSpec(memory_space=pl.ANY)] * len(after),
        out_specs=[vmem] * len(outs),
        out_shape=outs,
        cost_estimate=lasting(1.5),
        compiler_params=kernel_params(),
        name="pick_blocks",
    )(position, wanted, *sources, *after)


def query_kernel(normed_ref, query_w_ref, query_ref, *, cluster, head_width):
    width = normed_ref.shape[1]
    mask = head_mask((width, GROUP * cluster), head_width, cluster)
    for block in range(query_ref.shape[0]):
        own = normed_ref[pl.ds(block * cluster, cluster), :]
        own = jnp.concatenate([own] * GROUP, axis=0)
        query = lax.dot_general(query_w_ref[...], own, NT, preferred_element_type=jnp.float32)
        query = query * (math.log2(math.e) / head_width**0.5)
        query_ref[block] = jnp.where(mask, query, 0.0).astype(jnp.bfloat16)


def project_queries(normed, w_query, cluster):
    rows, width = normed.shape
    blocks = rows // cluster
    return pl.pallas_call(
        functools.partial(query_kernel, cluster=cluster, head_width=width // HEADS),
        grid=(blocks // SUB,),
        in_specs=[
            pl.BlockSpec((SUB * cluster, width), lambda i: (i, 0)),
            pl.BlockSpec((width, width), lambda i: (0, 0)),
        ],
        out_specs=pl.BlockSpec((SUB, width, GROUP * cluster), lambda i: (i, 0, 0)),
        out_shape=jax.ShapeDtypeStruct((blocks, width, GROUP * cluster), jnp.bfloat16),
        cost_estimate=lasting(6.5),
        compiler_params=kernel_params(),
        name="queries",
    )(normed, w_query.T)


def collect_kernel(*refs, places):
    buffer_ref, sems = refs[-2:]
    copy_pieces(refs[: len(places)], buffer_ref, places, sems)


def copy_pieces(piece_refs, buffer_ref, places, sems):
    copies = [
        pltpu.make_async_copy(piece, buffer_ref.at[pl.ds(at, piece.shape[0])], sems.at[n])
        for n, (piece, at) in enumerate(zip(piece_refs, places, strict=True))
    ]
    for copy in copies:
        copy.start()
    for copy in copies:
        copy.wait()


def collect(pieces, places, total):
    return pl.pallas_call(
        functools.partial(collect_kernel, places=places),
        in_specs=[pl.BlockSpec(memory_space=pltpu.VMEM)] * len(pieces),
        out_specs=pl.BlockSpec(memory_space=pl.ANY),
        out_shape=jax.ShapeDtypeStruct((total,) + pieces[0].shape[1:], pieces[0].dtype),
        scratch_shapes=[pltpu.SemaphoreType.DMA((len(pieces),))],
        cost_estimate=lasting(4),
        compiler_params=kernel_params(),
        name="collect_blocks",
    )(*pieces)


def attend_kernel(
    range_ref,
    order_ref,
    table_ref,
    query_ref,
    placed_ref,
    *rest,
    own_at,
    head_width,
    places,
):
    weight_refs, rest = rest[:4], rest[4:]
    piece_refs = rest[: len(places)]
    mixed_ref, buffer_ref, query_buf, member_buf, placed_buf = rest[-11:-6]
    attended_buf, before_buf, done_buf, in_sems, out_sems, piece_sems = rest[-6:]
    begin, count = range_ref[0], range_ref[1]
    pair_count = member_buf.shape[2] - 1
    copy_pieces(piece_refs, buffer_ref, places, piece_sems)

    def fetches(step, slot):
        for j in range(STEP):
            block = order_ref[step * STEP + j]
            sources = [(query_ref.at[block], query_buf.at[slot, j])]
            sources.append((placed_ref.at[block], placed_buf.at[slot, j]))
            sources.append((buffer_ref.at[own_at + block], member_buf.at[slot, j, 0]))
            for n in range(pair_count):
                listed = table_ref[block * pair_count + n]
                sources.append((buffer_ref.at[listed], member_buf.at[slot, j, 1 + n]))
            for n, (source_, target) in enumerate(sources):
                sem = in_sems.at[slot, j * (pair_count + 3) + n]
                yield pltpu.make_async_copy(source_, target, sem)

    def stores(step):
        for j in range(STEP):
            target = mixed_ref.at[order_ref[step * STEP + j]]
            yield pltpu.make_async_copy(done_buf.at[j], target, out_sems.at[j])

    def finish():
        return finish_step(before_buf[...], attended_buf[...], *weight_refs[2:])

    def one_step(i, carry):
        slot = i % 2
        for copy in fetches(begin + jnp.minimum(i + 1, count - 1), 1 - slot):
            copy.start()
        for copy in fetches(begin + i, slot):
            copy.wait()
        attended, mixed = attend_step(
            query_buf.at[slot], member_buf.at[slot], *weight_refs[:2], head_width, finish
        )

        @pl.when(i > 1)
        def _():
            for copy in stores(begin + i - 2):
                copy.wait()

        done_buf[...] = mixed.reshape(done_buf.shape)
        attended_buf[...] = attended
        before_buf[...] = placed_buf[slot].reshape(before_buf.shape)

        @pl.when(i > 0)
        def _():
            for copy in stores(begin + i - 1):
                copy.start()

        return carry

    @pl.when(count > 0)
    def _():
        for copy in fetches(begin, 0):
            copy.start()
        attended_buf[...] = jnp.zeros_like(attended_buf)
        before_buf[...] = jnp.zeros_like(before_buf)
        lax.fori_loop(0, count, one_step, 0)
        for copy in fetches(begin + count - 1, count % 2):
            copy.wait()
        mixed = finish()

        @pl.when(count > 1)
        def _():
            for copy in stores(begin + count - 2):
                copy.wait()

        done_buf[...] = mixed.reshape(done_buf.shape)
        for copy in stores(begin + count - 1):
            copy.start()
        for copy in stores(begin + count - 1):
            copy.wait()


def finish_step(placed, attended, out_w_ref, mix_ref):
    middle = placed.astype(jnp.float32) + jnp.dot(
        attended, out_w_ref[...], preferred_element_type=jnp.float32
    )
    middle = middle.astype(jnp.bfloat16).astype(jnp.float32)
    second = layer_norm(middle).astype(jnp.bfloat16)
    mixed = middle + jnp.tanh(jnp.dot(second, mix_ref[...], preferred_element_type=jnp.float32))
    return mixed.astype(jnp.bfloat16)


def attend_step(query_ref, member_ref, key_w_ref, value_w_ref, head_width, meanwhile):
    _, members_count, cluster, width = member_ref.shape
    span = GROUP * head_width
    tile = GROUP * cluster
    diagonal = head_mask((span, tile), head_width, cluster)
    fold_row = lax.broadcasted_iota(jnp.int32, (cluster, tile), 0)
    fold_lane = lax.broadcasted_iota(jnp.int32, (cluster, tile), 1) % cluster
    fold = jnp.where(fold_row == fold_lane, 1.0, 0.0).astype(jnp.bfloat16)
    zeros = jnp.zeros((span, tile), jnp.bfloat16)
    ones = jnp.ones((16, tile), jnp.bfloat16)
    units = [(block, pair) for block in range(STEP) for pair in range(HEADS // GROUP // 2)]
    keys, values = {}, {}

    def gather(block):
        members = member_ref[block].reshape(members_count * cluster, width)
        key = jnp.dot(members, key_w_ref[...], preferred_element_type=jnp.float32)
        keys[block] = key.astype(jnp.bfloat16)
        value = lax.dot_general(value_w_ref[...], members, NT, preferred_element_type=jnp.float32)
        values[block] = value.astype(jnp.bfloat16)

    def scores_of(block, pair):
        if pair == 0:
            gather(block)
        first = query_ref[block, pair * 2 * span : (pair * 2 + 1) * span, :]
        other = query_ref[block, (pair * 2 + 1) * span : (pair + 1) * 2 * span, :]
        both = jnp.concatenate(
            [
                jnp.concatenate([first, zeros], axis=1),
                jnp.concatenate([zeros, other], axis=1),
            ],
            axis=0,
        )
        return jnp.dot(
            keys[block][:, pair * 2 * span : (pair + 1) * 2 * span],
            both,
            preferred_element_type=jnp.float32,
        )

    def weights_of(scores):
        top = jnp.max(scores, axis=0, keepdims=True)
        return jnp.exp2((scores - top).astype(jnp.bfloat16))

    def products_of(block, pair, weights):
        for half in range(2):
            t = pair * 2 + half
            lifted = jnp.concatenate([values[block][t * span : (t + 1) * span], ones], axis=0)
            here = weights[:, half * tile : (half + 1) * tile]
            yield jnp.dot(lifted, here, preferred_element_type=jnp.float32)

    def scaled(product):
        result = product[:span] * (1.0 / product[span : span + 1])
        return jnp.where(diagonal, result, 0.0).astype(jnp.bfloat16)

    count = len(units)
    scores, weights, products, pieces, attended = {}, {}, {}, [], []
    for at in range(-SCORES_AHEAD, count + 1):
        if at == 0:
            finished = meanwhile()
        if at + SCORES_AHEAD < count:
            scores[at + SCORES_AHEAD] = scores_of(*units[at + SCORES_AHEAD])
        if 0 <= at + WEIGHTS_AHEAD < count:
            weights[at + WEIGHTS_AHEAD] = weights_of(scores.pop(at + WEIGHTS_AHEAD))
        if 0 <= at < count:
            products[at] = list(products_of(*units[at], weights.pop(at)))
        if at > 0:
            pieces += [scaled(product) for product in products.pop(at - 1)]
            if len(pieces) == HEADS // GROUP:
                stacked = jnp.concatenate(pieces, axis=0)
                folded = lax.dot_general(fold, stacked, NT, preferred_element_type=jnp.float32)
                attended.append(folded.astype(jnp.bfloat16))
                pieces = []
    return jnp.concatenate(attended, axis=0), finished


def attend(begin, count, order, table, queries, placed, weights, buffer, pieces, places, own_at, so_far):
    blocks, cluster, width = placed.shape
    pair_count = table.shape[0] // blocks
    smem = pl.BlockSpec(memory_space=pltpu.SMEM)
    vmem = pl.BlockSpec(memory_space=pltpu.VMEM)
    hbm = pl.BlockSpec(memory_space=pl.ANY)
    in_specs = [smem, smem, smem, hbm, hbm] + [vmem] * (4 + len(pieces)) + [hbm]
    aliases = {len(in_specs) - 1: 1}
    operands = [queries, placed, *weights, *pieces, buffer]
    if so_far is not None:
        aliases[len(in_specs)] = 0
        in_specs.append(hbm)
        operands.append(so_far)
    kernel = functools.partial(
        attend_kernel, own_at=own_at, head_width=width // HEADS, places=places
    )
    return pl.pallas_call(
        kernel,
        in_specs=in_specs,
        out_specs=[hbm, hbm],
        out_shape=[
            jax.ShapeDtypeStruct(placed.shape, jnp.bfloat16),
            jax.ShapeDtypeStruct(buffer.shape, jnp.bfloat16),
        ],
        scratch_shapes=[
            pltpu.VMEM((2, STEP) + queries.shape[1:], jnp.bfloat16),
            pltpu.VMEM((2, STEP, pair_count + 1, cluster, width), jnp.bfloat16),
            pltpu.VMEM((2, STEP, cluster, width), jnp.bfloat16),
            pltpu.VMEM((STEP * cluster, width), jnp.bfloat16),
            pltpu.VMEM((STEP * cluster, width), jnp.bfloat16),
            pltpu.VMEM((STEP, cluster, width), jnp.bfloat16),
            pltpu.SemaphoreType.DMA((2, STEP * (pair_count + 3))),
            pltpu.SemaphoreType.DMA((STEP,)),
            pltpu.SemaphoreType.DMA((len(pieces),)),
        ],
        input_output_aliases=aliases,
        cost_estimate=lasting(18),
        compiler_params=kernel_params(),
        name="attend_blocks",
    )(jnp.stack([begin, count]).astype(jnp.int32), order, table, *operands)


def slot_tables(owner, within, capacity):
    entries = owner.shape[0]
    alike = owner[:, None] == owner[None, :]
    earlier = jnp.arange(entries)[None, :] < jnp.arange(entries)[:, None]
    ranking = jnp.sum(jnp.where(alike & earlier, 1, 0), axis=1).astype(jnp.int32)
    slots = owner * capacity + ranking
    matches = slots[None, :] == jnp.arange(SPAN * capacity, dtype=jnp.int32)[:, None]
    return ranking, jnp.sum(jnp.where(matches, within[None, :], 0), axis=1).astype(jnp.int32)


def by_class(classes, count):
    blocks = jnp.arange(classes.shape[0], dtype=jnp.int32)
    before = (classes[None, :] < classes[:, None]) | (
        (classes[None, :] == classes[:, None]) & (blocks[None, :] < blocks[:, None])
    )
    rank = jnp.sum(jnp.where(before, 1, 0), axis=1)
    order = jnp.sum(jnp.where(rank[None, :] == blocks[:, None], blocks[None, :], 0), axis=1)
    ends = [jnp.sum(jnp.where(classes <= c, 1, 0)).astype(jnp.int32) for c in range(count)]
    return order.astype(jnp.int32), ends


OUT = (2, 0, 3, 1)
FROM = (1, 3, 0, 2)
LEVELS = 4


def position_at(z, y):
    return 2 * z + y


def partner(position):
    return position ^ 1


def onward(position):
    return position_at(choose(position // 2, OUT), position % 2)


def source(position):
    return position_at(choose(position // 2, FROM), position % 2)


def opposite(position):
    return position_at(LEVELS - 1 - position // 2, position % 2)


def itself(position):
    return position


def crossed(route):
    return lambda position: partner(route(position))


SECOND_PLAN = (((0, source, itself), (1, source, partner)),)
MIDDLE_PLAN = (((0, opposite, itself),),)
MIDDLE_CROSS_PLAN = (((0, opposite, partner),),)
ON_PLAN = (((0, crossed(onward), source),), ((0, onward, source),))
NEAR_PLAN = (((0, partner, source),),)


def body(features, assignment, pairs, w_query, w_key, w_value, w_out, w_mix):
    rows_dev, width = features.shape
    block_count, pair_count = pairs.shape
    cluster = rows_dev // block_count
    stride = lax.axis_size("elec") // SPAN
    groups = [[rest + place_ * stride for place_ in range(SPAN)] for rest in range(stride)]
    position = lax.axis_index("elec") // stride
    at_position = position.reshape(1)
    capacity = (block_count * pair_count + SPAN - 1) // SPAN + 1

    def moved(x, moves):
        pairs_of = [(s * stride + r, d * stride + r) for s, d in moves for r in range(stride)]
        return lax.ppermute(x, "elec", pairs_of)

    def across_z(pairs_of_z):
        return [(position_at(s, y), position_at(d, y)) for s, d in pairs_of_z for y in range(2)]

    swap = [(p, p ^ 1) for p in range(SPAN)]
    first_moves = across_z(enumerate(OUT))
    second_moves = across_z(enumerate(FROM))
    middle_moves = across_z([(1, 2), (2, 1)])
    outward_moves = across_z([(2, 3), (1, 0)])

    raw_passed, to_passed = moved(features, first_moves), moved(assignment, first_moves)

    listed = pairs.reshape(-1)
    owner = listed // block_count // stride
    within = listed % block_count
    ranking, tables = slot_tables(owner, within, capacity)
    wanted = lax.all_to_all(
        jnp.broadcast_to(tables[None], (SPAN, SPAN * capacity)),
        "elec",
        split_axis=0,
        concat_axis=0,
        axis_index_groups=groups,
        tiled=True,
    )

    shape = (block_count // SUB, 1, SUB * cluster)
    block_shape = (block_count, cluster, width)
    normed, placed = place(features, assignment.reshape(shape), 2)
    blocks = normed.reshape(block_shape)
    queries = project_queries(normed, w_query, cluster)
    own_at = 7 * capacity
    passed_at = own_at + block_count
    beside_at = passed_at + block_count
    total = beside_at + block_count

    beside = moved(blocks, swap)
    (passed,) = place(raw_passed, to_passed.reshape(shape), 1, after=(queries,))
    passed = passed.reshape(block_shape)
    (second,) = pick(at_position, wanted, (blocks, beside), SECOND_PLAN)
    second = moved(second, second_moves)
    on, outward = pick(at_position, wanted, (passed,), ON_PLAN)
    on = moved(on, swap)
    outward = moved(outward, outward_moves)
    (near,) = pick(at_position, wanted, (passed,), NEAR_PLAN, after=(on,))
    near = moved(near, swap)
    (middle,) = pick(at_position, wanted, (blocks,), MIDDLE_PLAN, after=(on,))
    middle = moved(middle, middle_moves)
    on = moved(on, outward_moves)
    (middle_cross,) = pick(
        at_position, wanted, (beside,), MIDDLE_CROSS_PLAN, after=(second,)
    )
    middle_cross = moved(middle_cross, middle_moves)

    buffer = collect((blocks, passed, beside), (own_at, passed_at, beside_at), total)

    z, y = position // 2, position % 2
    is_end = (z == 0) | (z == LEVELS - 1)
    z_owner, same = owner // 2, owner % 2 == y
    from_first = z_owner == choose(z, FROM)
    late = z_owner == LEVELS - 1 - z
    piece_of = jnp.where(
        from_first,
        0,
        jnp.where(
            late,
            jnp.where(is_end, jnp.where(same, 3, 4), jnp.where(same, 5, 6)),
            jnp.where(same, 1, 2),
        ),
    )
    whole_at = jnp.where(z_owner == z, jnp.where(same, own_at, beside_at), passed_at)
    whole = (z_owner == z) | (from_first & same)
    table = jnp.where(whole, whole_at + within, piece_of * capacity + ranking)

    arrival = jnp.where(late, jnp.where(same | is_end, 1, 2), 0)
    order, ends = by_class(jnp.max(arrival.reshape(block_count, pair_count), axis=1), 2)
    marks = [0, ends[0] // STEP, ends[1] // STEP, block_count // STEP]
    phases = [(marks[n], marks[n + 1] - marks[n]) for n in range(3)]
    weights = (w_key, w_value.T, w_out, w_mix)
    shared = (order, table, queries, placed.reshape(blocks.shape), weights)
    arrivals = (
        ((near, 0), (second, 1)),
        ((outward, 3), (on, 4), (middle, 5)),
        ((middle_cross, 6),),
    )
    mixed = None
    for phase, arrived in zip(phases, arrivals, strict=True):
        pieces = [piece for piece, _ in arrived]
        places = tuple(at * capacity for _, at in arrived)
        mixed, buffer = attend(*phase, *shared, buffer, pieces, places, own_at, mixed)
    return mixed.reshape(rows_dev, width)


def solution(mesh):
    placed = (
        P(("groups", "elec"), None),
        P(("groups", "elec")),
        P(("groups", "elec"), None),
        P(),
        P(),
        P(),
        P(),
        P(),
    )
    return jax.shard_map(
        body, mesh=mesh, in_specs=placed, out_specs=P(("groups", "elec"), None), check_vma=False
    )
```

```python
import functools
import math

import jax
import jax.numpy as jnp
from jax import lax
from jax.experimental import pallas as pl
from jax.experimental.pallas import tpu as pltpu
from jax.sharding import PartitionSpec as P

HEADS = 16
SPAN = 8
SUB = 8
GROUP = 4
STEP = 4
SCORES_AHEAD, WEIGHTS_AHEAD = 2, 1
VMEM_BYTES = 48 * 1024 * 1024

NT = (((1,), (1,)), ((), ()))


def lasting(us):
    return pl.CostEstimate(flops=int(us * 1.15e9), bytes_accessed=0, transcendentals=0)


def kernel_params():
    return pltpu.CompilerParams(vmem_limit_bytes=VMEM_BYTES)


def layer_norm(rows):
    mean = jnp.mean(rows, axis=-1, keepdims=True)
    centred = rows - mean
    variance = jnp.mean(centred * centred, axis=-1, keepdims=True)
    return centred * lax.rsqrt(variance + 1e-05)


def head_mask(shape, head_width, cluster):
    row_head = lax.broadcasted_iota(jnp.int32, shape, 0) // head_width % GROUP
    lane_head = lax.broadcasted_iota(jnp.int32, shape, 1) // cluster
    return row_head == lane_head


def place_kernel(features_ref, assignment_ref, placed_ref, normed_ref):
    walkers, _, rows = assignment_ref.shape
    lane = 128
    columns = lax.broadcasted_iota(jnp.int32, (lane, rows), 1)
    for walker in range(walkers):
        features = features_ref[walker * rows : (walker + 1) * rows, :]
        for part in range(rows // lane):
            chosen = assignment_ref[walker, :, part * lane : (part + 1) * lane] & (rows - 1)
            chosen = jnp.broadcast_to(chosen, (lane, lane)).T
            chosen = jnp.concatenate([chosen] * (rows // lane), axis=1)
            one_hot = jnp.where(chosen == columns, 1.0, 0.0).astype(jnp.bfloat16)
            placed = jnp.dot(one_hot, features, preferred_element_type=jnp.float32)
            here = pl.ds(walker * rows + part * lane, lane)
            placed_ref[here, :] = placed.astype(jnp.bfloat16)
            normed_ref[here, :] = layer_norm(placed).astype(jnp.bfloat16)


def place(features, assignment):
    width = features.shape[1]
    walkers, _, rows = assignment.shape
    local = pl.BlockSpec((2 * rows, width), lambda i: (i, 0))
    out = jax.ShapeDtypeStruct(features.shape, jnp.bfloat16)
    return pl.pallas_call(
        place_kernel,
        grid=(walkers // 2,),
        in_specs=[local, pl.BlockSpec((2, 1, rows), lambda i: (i, 0, 0))],
        out_specs=[local] * 2,
        out_shape=[out] * 2,
        cost_estimate=lasting(6),
        compiler_params=kernel_params(),
        name="place_rows",
    )(features, assignment)


def choose(index, values):
    result = values[-1]
    for at in range(len(values) - 2, -1, -1):
        result = jnp.where(index == at, values[at], result)
    return result


def pick_kernel(position_ref, wanted_ref, *rest, plan, capacity):
    position = position_ref[0]
    for out_ref, pieces in zip(rest[len(rest) - len(plan) :], plan, strict=True):
        for at, (blocks, reader_of, owner_of) in enumerate(pieces):
            reader, first = reader_of(position), owner_of(position) * capacity

            def one_slot(slot, carry, out_ref=out_ref, at=at, blocks=blocks, reader=reader, first=first):
                out_ref[at * capacity + slot] = rest[blocks][wanted_ref[reader, first + slot]]
                return carry

            lax.fori_loop(0, capacity, one_slot, 0)


def pick(position, wanted, sources, plan, after=()):
    capacity = wanted.shape[1] // SPAN
    block = sources[0].shape[1:]
    outs = [
        jax.ShapeDtypeStruct((len(pieces) * capacity,) + block, sources[0].dtype)
        for pieces in plan
    ]
    smem = pl.BlockSpec(memory_space=pltpu.SMEM)
    vmem = pl.BlockSpec(memory_space=pltpu.VMEM)
    return pl.pallas_call(
        functools.partial(pick_kernel, plan=plan, capacity=capacity),
        in_specs=[smem, smem]
        + [vmem] * len(sources)
        + [pl.BlockSpec(memory_space=pl.ANY)] * len(after),
        out_specs=[vmem] * len(outs),
        out_shape=outs,
        cost_estimate=lasting(1.5),
        compiler_params=kernel_params(),
        name="pick_blocks",
    )(position, wanted, *sources, *after)


def tiles_of(query, first, span):
    one = query[first : first + span]
    two = query[first + span : first + 2 * span]
    zeros = jnp.zeros_like(one)
    return jnp.concatenate(
        [jnp.concatenate([one, zeros], axis=1), jnp.concatenate([zeros, two], axis=1)], axis=0
    )


def own_kernel(
    normed_ref, query_w_ref, key_w_ref, value_w_ref, query_ref, own_ref, stats_ref, *, head_width
):
    blocks, width, tile = query_ref.shape
    cluster = tile // GROUP
    span = GROUP * head_width
    mask = head_mask((width, tile), head_width, cluster)
    scale = math.log2(math.e) / head_width**0.5
    ones = jnp.ones((16, cluster), jnp.bfloat16)
    rows = normed_ref[...]
    keys = jnp.dot(rows, key_w_ref[...], preferred_element_type=jnp.float32).astype(jnp.bfloat16)
    queries = []
    for block in range(blocks):
        own = rows[block * cluster : (block + 1) * cluster]
        tiled = jnp.concatenate([own] * GROUP, axis=0)
        query = lax.dot_general(query_w_ref[...], tiled, NT, preferred_element_type=jnp.float32)
        query = jnp.where(mask, query * scale, 0.0).astype(jnp.bfloat16)
        query_ref[block] = query
        queries.append(query)
    for block in range(blocks):
        own = rows[block * cluster : (block + 1) * cluster]
        value = lax.dot_general(value_w_ref[...], own, NT, preferred_element_type=jnp.float32)
        value = value.astype(jnp.bfloat16)
        tops, totals = [], []
        for pair in range(HEADS // GROUP // 2):
            first = pair * 2 * span
            scores = jnp.dot(
                keys[block * cluster : (block + 1) * cluster, first : first + 2 * span],
                tiles_of(queries[block], first, span),
                preferred_element_type=jnp.float32,
            )
            top = jnp.max(scores, axis=0, keepdims=True)
            weights = jnp.exp2(scores - top).astype(jnp.bfloat16)
            for half in range(2):
                at = first + half * span
                here = slice(half * tile, (half + 1) * tile)
                lifted = jnp.concatenate([value[at : at + span], ones], axis=0)
                product = jnp.dot(lifted, weights[:, here], preferred_element_type=jnp.float32)
                total = product[span : span + 1]
                result = jnp.where(mask[:span], product[:span] * (1.0 / total), 0.0)
                own_ref[block, at : at + span, :] = result.astype(jnp.bfloat16)
                tops.append(top[:, here])
                totals.append(total)
        stats_ref[block] = jnp.concatenate(tops + totals, axis=0)


def own_part(normed, w_query, w_key, w_value, cluster):
    rows, width = normed.shape
    blocks = rows // cluster
    tile = GROUP * cluster
    tiles = HEADS // GROUP
    whole = pl.BlockSpec((width, width), lambda i: (0, 0))
    square = pl.BlockSpec((STEP, width, tile), lambda i: (i, 0, 0))
    return pl.pallas_call(
        functools.partial(own_kernel, head_width=width // HEADS),
        grid=(blocks // STEP,),
        in_specs=[pl.BlockSpec((STEP * cluster, width), lambda i: (i, 0)), whole, whole, whole],
        out_specs=[
            square,
            square,
            pl.BlockSpec((STEP, 2 * tiles, tile), lambda i: (i, 0, 0)),
        ],
        out_shape=[
            jax.ShapeDtypeStruct((blocks, width, tile), jnp.bfloat16),
            jax.ShapeDtypeStruct((blocks, width, tile), jnp.bfloat16),
            jax.ShapeDtypeStruct((blocks, 2 * tiles, tile), jnp.float32),
        ],
        cost_estimate=lasting(20),
        compiler_params=kernel_params(),
        name="own_blocks",
    )(normed, w_query.T, w_key, w_value.T)


def collect_kernel(*refs, places):
    buffer_ref, sems = refs[-2:]
    copy_pieces(refs[: len(places)], buffer_ref, places, sems)


def copy_pieces(piece_refs, buffer_ref, places, sems):
    copies = [
        pltpu.make_async_copy(piece, buffer_ref.at[pl.ds(at, piece.shape[0])], sems.at[n])
        for n, (piece, at) in enumerate(zip(piece_refs, places, strict=True))
    ]
    for copy in copies:
        copy.start()
    for copy in copies:
        copy.wait()


def collect(pieces, places, total):
    return pl.pallas_call(
        functools.partial(collect_kernel, places=places),
        in_specs=[pl.BlockSpec(memory_space=pltpu.VMEM)] * len(pieces),
        out_specs=pl.BlockSpec(memory_space=pl.ANY),
        out_shape=jax.ShapeDtypeStruct((total,) + pieces[0].shape[1:], pieces[0].dtype),
        scratch_shapes=[pltpu.SemaphoreType.DMA((len(pieces),))],
        cost_estimate=lasting(4),
        compiler_params=kernel_params(),
        name="collect_blocks",
    )(*pieces)


def attend_kernel(
    range_ref,
    order_ref,
    table_ref,
    query_ref,
    own_ref,
    stats_ref,
    placed_ref,
    *rest,
    head_width,
    places,
):
    weight_refs, rest = rest[:4], rest[4:]
    piece_refs = rest[: len(places)]
    mixed_ref, buffer_ref, query_buf, own_buf, stats_buf, member_buf, placed_buf = rest[-13:-6]
    attended_buf, before_buf, done_buf, in_sems, out_sems, piece_sems = rest[-6:]
    begin, count = range_ref[0], range_ref[1]
    pair_count = member_buf.shape[2]
    copy_pieces(piece_refs, buffer_ref, places, piece_sems)

    def fetches(step, slot):
        for j in range(STEP):
            block = order_ref[step * STEP + j]
            sources = [(query_ref.at[block], query_buf.at[slot, j])]
            sources.append((own_ref.at[block], own_buf.at[slot, j]))
            sources.append((stats_ref.at[block], stats_buf.at[slot, j]))
            sources.append((placed_ref.at[block], placed_buf.at[slot, j]))
            for n in range(pair_count):
                listed = table_ref[block * pair_count + n]
                sources.append((buffer_ref.at[listed], member_buf.at[slot, j, n]))
            for n, (source_, target) in enumerate(sources):
                sem = in_sems.at[slot, j * (pair_count + 4) + n]
                yield pltpu.make_async_copy(source_, target, sem)

    def stores(step):
        for j in range(STEP):
            target = mixed_ref.at[order_ref[step * STEP + j]]
            yield pltpu.make_async_copy(done_buf.at[j], target, out_sems.at[j])

    def finish():
        return finish_step(before_buf[...], attended_buf[...], *weight_refs[2:])

    def one_step(i, carry):
        slot = i % 2
        for copy in fetches(begin + jnp.minimum(i + 1, count - 1), 1 - slot):
            copy.start()
        for copy in fetches(begin + i, slot):
            copy.wait()
        attended, mixed = attend_step(
            query_buf.at[slot],
            own_buf.at[slot],
            stats_buf.at[slot],
            member_buf.at[slot],
            *weight_refs[:2],
            head_width,
            finish,
        )

        @pl.when(i > 1)
        def _():
            for copy in stores(begin + i - 2):
                copy.wait()

        done_buf[...] = mixed.reshape(done_buf.shape)
        attended_buf[...] = attended
        before_buf[...] = placed_buf[slot].reshape(before_buf.shape)

        @pl.when(i > 0)
        def _():
            for copy in stores(begin + i - 1):
                copy.start()

        return carry

    @pl.when(count > 0)
    def _():
        for copy in fetches(begin, 0):
            copy.start()
        attended_buf[...] = jnp.zeros_like(attended_buf)
        before_buf[...] = jnp.zeros_like(before_buf)
        lax.fori_loop(0, count, one_step, 0)
        for copy in fetches(begin + count - 1, count % 2):
            copy.wait()
        mixed = finish()

        @pl.when(count > 1)
        def _():
            for copy in stores(begin + count - 2):
                copy.wait()

        done_buf[...] = mixed.reshape(done_buf.shape)
        for copy in stores(begin + count - 1):
            copy.start()
        for copy in stores(begin + count - 1):
            copy.wait()


def finish_step(placed, attended, out_w_ref, mix_ref):
    middle = placed.astype(jnp.float32) + jnp.dot(
        attended, out_w_ref[...], preferred_element_type=jnp.float32
    )
    middle = middle.astype(jnp.bfloat16).astype(jnp.float32)
    second = layer_norm(middle).astype(jnp.bfloat16)
    mixed = middle + jnp.tanh(jnp.dot(second, mix_ref[...], preferred_element_type=jnp.float32))
    return mixed.astype(jnp.bfloat16)


def attend_step(
    query_ref, own_ref, stats_ref, member_ref, key_w_ref, value_w_ref, head_width, meanwhile
):
    _, members_count, cluster, width = member_ref.shape
    span = GROUP * head_width
    tile = GROUP * cluster
    diagonal = head_mask((span, tile), head_width, cluster)
    fold_row = lax.broadcasted_iota(jnp.int32, (cluster, tile), 0)
    fold_lane = lax.broadcasted_iota(jnp.int32, (cluster, tile), 1) % cluster
    fold = jnp.where(fold_row == fold_lane, 1.0, 0.0).astype(jnp.bfloat16)
    ones = jnp.ones((16, members_count * cluster), jnp.bfloat16)
    tiles = HEADS // GROUP
    units = [(block, pair) for block in range(STEP) for pair in range(HEADS // GROUP // 2)]
    keys, values = {}, {}

    def gather(block):
        members = member_ref[block].reshape(members_count * cluster, width)
        key = jnp.dot(members, key_w_ref[...], preferred_element_type=jnp.float32)
        keys[block] = key.astype(jnp.bfloat16)
        value = lax.dot_general(value_w_ref[...], members, NT, preferred_element_type=jnp.float32)
        values[block] = value.astype(jnp.bfloat16)

    def scores_of(block, pair):
        if pair == 0:
            gather(block)
        first = pair * 2 * span
        return jnp.dot(
            keys[block][:, first : first + 2 * span],
            tiles_of(query_ref[block], first, span),
            preferred_element_type=jnp.float32,
        )

    def weights_of(block, pair, scores):
        own_top = jnp.concatenate(
            [stats_ref[block, t : t + 1, :] for t in (2 * pair, 2 * pair + 1)], axis=1
        )
        top = jnp.maximum(jnp.max(scores, axis=0, keepdims=True), own_top)
        weights = jnp.exp2((scores - top).astype(jnp.bfloat16))
        return weights, jnp.exp2(own_top - top)

    def products_of(block, pair, weights, own_factor):
        for half in range(2):
            t = pair * 2 + half
            here = slice(half * tile, (half + 1) * tile)
            lifted = jnp.concatenate([values[block][t * span : (t + 1) * span], ones], axis=0)
            product = jnp.dot(lifted, weights[:, here], preferred_element_type=jnp.float32)
            yield block, t, product, own_factor[:, here]

    def scaled(block, t, product, own_factor):
        own_total = stats_ref[block, tiles + t : tiles + t + 1, :] * own_factor
        inverse = 1.0 / (product[span : span + 1] + own_total)
        own = own_ref[block, t * span : (t + 1) * span, :].astype(jnp.float32)
        result = product[:span] * inverse + own * (own_total * inverse)
        return jnp.where(diagonal, result, 0.0).astype(jnp.bfloat16)

    count = len(units)
    scores, weights, products, pieces, attended = {}, {}, {}, [], []
    for at in range(-SCORES_AHEAD, count + 1):
        if at == 0:
            finished = meanwhile()
        if at + SCORES_AHEAD < count:
            scores[at + SCORES_AHEAD] = scores_of(*units[at + SCORES_AHEAD])
        if 0 <= at + WEIGHTS_AHEAD < count:
            ahead = at + WEIGHTS_AHEAD
            weights[ahead] = weights_of(*units[ahead], scores.pop(ahead))
        if 0 <= at < count:
            products[at] = list(products_of(*units[at], *weights.pop(at)))
        if at > 0:
            pieces += [scaled(*product) for product in products.pop(at - 1)]
            if len(pieces) == tiles:
                stacked = jnp.concatenate(pieces, axis=0)
                folded = lax.dot_general(fold, stacked, NT, preferred_element_type=jnp.float32)
                attended.append(folded.astype(jnp.bfloat16))
                pieces = []
    return jnp.concatenate(attended, axis=0), finished


def attend(begin, count, order, table, own, placed, weights, buffer, pieces, places, so_far):
    blocks, cluster, width = placed.shape
    pair_count = table.shape[0] // blocks
    smem = pl.BlockSpec(memory_space=pltpu.SMEM)
    vmem = pl.BlockSpec(memory_space=pltpu.VMEM)
    hbm = pl.BlockSpec(memory_space=pl.ANY)
    in_specs = [smem] * 3 + [hbm] * (len(own) + 1) + [vmem] * (4 + len(pieces)) + [hbm]
    aliases = {len(in_specs) - 1: 1}
    operands = [*own, placed, *weights, *pieces, buffer]
    if so_far is not None:
        aliases[len(in_specs)] = 0
        in_specs.append(hbm)
        operands.append(so_far)
    kernel = functools.partial(
        attend_kernel, head_width=width // HEADS, places=places
    )
    return pl.pallas_call(
        kernel,
        in_specs=in_specs,
        out_specs=[hbm, hbm],
        out_shape=[
            jax.ShapeDtypeStruct(placed.shape, jnp.bfloat16),
            jax.ShapeDtypeStruct(buffer.shape, jnp.bfloat16),
        ],
        scratch_shapes=[
            *[pltpu.VMEM((2, STEP) + x.shape[1:], x.dtype) for x in own],
            pltpu.VMEM((2, STEP, pair_count, cluster, width), jnp.bfloat16),
            pltpu.VMEM((2, STEP, cluster, width), jnp.bfloat16),
            pltpu.VMEM((STEP * cluster, width), jnp.bfloat16),
            pltpu.VMEM((STEP * cluster, width), jnp.bfloat16),
            pltpu.VMEM((STEP, cluster, width), jnp.bfloat16),
            pltpu.SemaphoreType.DMA((2, STEP * (pair_count + 4))),
            pltpu.SemaphoreType.DMA((STEP,)),
            pltpu.SemaphoreType.DMA((len(pieces),)),
        ],
        input_output_aliases=aliases,
        cost_estimate=lasting(18),
        compiler_params=kernel_params(),
        name="attend_blocks",
    )(jnp.stack([begin, count]).astype(jnp.int32), order, table, *operands)


def slot_tables(owner, within, capacity):
    entries = owner.shape[0]
    alike = owner[:, None] == owner[None, :]
    earlier = jnp.arange(entries)[None, :] < jnp.arange(entries)[:, None]
    ranking = jnp.sum(jnp.where(alike & earlier, 1, 0), axis=1).astype(jnp.int32)
    slots = owner * capacity + ranking
    matches = slots[None, :] == jnp.arange(SPAN * capacity, dtype=jnp.int32)[:, None]
    return ranking, jnp.sum(jnp.where(matches, within[None, :], 0), axis=1).astype(jnp.int32)


def by_class(classes, count):
    blocks = jnp.arange(classes.shape[0], dtype=jnp.int32)
    before = (classes[None, :] < classes[:, None]) | (
        (classes[None, :] == classes[:, None]) & (blocks[None, :] < blocks[:, None])
    )
    rank = jnp.sum(jnp.where(before, 1, 0), axis=1)
    order = jnp.sum(jnp.where(rank[None, :] == blocks[:, None], blocks[None, :], 0), axis=1)
    ends = [jnp.sum(jnp.where(classes <= c, 1, 0)).astype(jnp.int32) for c in range(count)]
    return order.astype(jnp.int32), ends


OUT = (2, 0, 3, 1)
FROM = (1, 3, 0, 2)
LEVELS = 4


def position_at(z, y):
    return 2 * z + y


def partner(position):
    return position ^ 1


def onward(position):
    return position_at(choose(position // 2, OUT), position % 2)


def source(position):
    return position_at(choose(position // 2, FROM), position % 2)


def opposite(position):
    return position_at(LEVELS - 1 - position // 2, position % 2)


def itself(position):
    return position


def crossed(route):
    return lambda position: partner(route(position))


SECOND_PLAN = (((0, source, itself), (1, source, partner)),)
MIDDLE_PLAN = (((0, opposite, itself),),)
MIDDLE_CROSS_PLAN = (((0, opposite, partner),),)
ON_PLAN = (((0, crossed(onward), source),), ((0, onward, source),))
NEAR_PLAN = (((0, partner, source),),)


def body(features, assignment, pairs, w_query, w_key, w_value, w_out, w_mix):
    rows_dev, width = features.shape
    block_count, pair_count = pairs.shape
    cluster = rows_dev // block_count
    stride = lax.axis_size("elec") // SPAN
    groups = [[rest + place_ * stride for place_ in range(SPAN)] for rest in range(stride)]
    position = lax.axis_index("elec") // stride
    at_position = position.reshape(1)
    capacity = (block_count * pair_count + SPAN - 1) // SPAN + 1

    def moved(x, moves):
        pairs_of = [(s * stride + r, d * stride + r) for s, d in moves for r in range(stride)]
        return lax.ppermute(x, "elec", pairs_of)

    def across_z(pairs_of_z):
        return [(position_at(s, y), position_at(d, y)) for s, d in pairs_of_z for y in range(2)]

    swap = [(p, p ^ 1) for p in range(SPAN)]
    first_moves = across_z(enumerate(OUT))
    second_moves = across_z(enumerate(FROM))
    middle_moves = across_z([(1, 2), (2, 1)])
    outward_moves = across_z([(2, 3), (1, 0)])

    listed = pairs.reshape(-1)
    owner = listed // block_count // stride
    within = listed % block_count
    ranking, tables = slot_tables(owner, within, capacity)
    wanted = lax.all_to_all(
        jnp.broadcast_to(tables[None], (SPAN, SPAN * capacity)),
        "elec",
        split_axis=0,
        concat_axis=0,
        axis_index_groups=groups,
        tiled=True,
    )

    shape = (block_count // SUB, 1, SUB * cluster)
    block_shape = (block_count, cluster, width)
    placed, normed = place(features, assignment.reshape(shape))
    blocks = normed.reshape(block_shape)
    own = own_part(normed, w_query, w_key, w_value, cluster)
    own_at = 7 * capacity
    passed_at = own_at + block_count
    beside_at = passed_at + block_count
    total = beside_at + block_count

    beside = moved(blocks, swap)
    passed = moved(blocks, first_moves)
    (second,) = pick(at_position, wanted, (blocks, beside), SECOND_PLAN, after=own[2:])
    second = moved(second, second_moves)
    on, outward = pick(at_position, wanted, (passed,), ON_PLAN, after=own[2:])
    on = moved(on, swap)
    outward = moved(outward, outward_moves)
    (near,) = pick(at_position, wanted, (passed,), NEAR_PLAN, after=(on,))
    near = moved(near, swap)
    (middle,) = pick(at_position, wanted, (blocks,), MIDDLE_PLAN, after=(on,))
    middle = moved(middle, middle_moves)
    on = moved(on, outward_moves)
    (middle_cross,) = pick(
        at_position, wanted, (beside,), MIDDLE_CROSS_PLAN, after=(second,)
    )
    middle_cross = moved(middle_cross, middle_moves)

    buffer = collect((blocks, passed, beside), (own_at, passed_at, beside_at), total)

    z, y = position // 2, position % 2
    is_end = (z == 0) | (z == LEVELS - 1)
    z_owner, same = owner // 2, owner % 2 == y
    from_first = z_owner == choose(z, FROM)
    late = z_owner == LEVELS - 1 - z
    piece_of = jnp.where(
        from_first,
        0,
        jnp.where(
            late,
            jnp.where(is_end, jnp.where(same, 3, 4), jnp.where(same, 5, 6)),
            jnp.where(same, 1, 2),
        ),
    )
    whole_at = jnp.where(z_owner == z, jnp.where(same, own_at, beside_at), passed_at)
    whole = (z_owner == z) | (from_first & same)
    table = jnp.where(whole, whole_at + within, piece_of * capacity + ranking)

    arrival = jnp.where(late, jnp.where(same | is_end, 1, 2), 0)
    order, ends = by_class(jnp.max(arrival.reshape(block_count, pair_count), axis=1), 2)
    marks = [0, ends[0] // STEP, ends[1] // STEP, block_count // STEP]
    phases = [(marks[n], marks[n + 1] - marks[n]) for n in range(3)]
    weights = (w_key, w_value.T, w_out, w_mix)
    shared = (order, table, own, placed.reshape(blocks.shape), weights)
    arrivals = (
        ((near, 0), (second, 1)),
        ((outward, 3), (on, 4), (middle, 5)),
        ((middle_cross, 6),),
    )
    mixed = None
    for phase, arrived in zip(phases, arrivals, strict=True):
        pieces = [piece for piece, _ in arrived]
        places = tuple(at * capacity for _, at in arrived)
        mixed, buffer = attend(*phase, *shared, buffer, pieces, places, mixed)
    return mixed.reshape(rows_dev, width)


def solution(mesh):
    placed = (
        P(("groups", "elec"), None),
        P(("groups", "elec")),
        P(("groups", "elec"), None),
        P(),
        P(),
        P(),
        P(),
        P(),
    )
    return jax.shard_map(
        body, mesh=mesh, in_specs=placed, out_specs=P(("groups", "elec"), None), check_vma=False
    )
```

```python
import functools
import math

import jax
import jax.numpy as jnp
from jax import lax
from jax.experimental import pallas as pl
from jax.experimental.pallas import tpu as pltpu
from jax.sharding import PartitionSpec as P

HEADS = 16
SPAN = 8
SUB = 8
GROUP = 4
STEP = 4
SCORES_AHEAD, WEIGHTS_AHEAD = 2, 1
VMEM_BYTES = 48 * 1024 * 1024

NT = (((1,), (1,)), ((), ()))


def lasting(us):
    return pl.CostEstimate(flops=int(us * 1.15e9), bytes_accessed=0, transcendentals=0)


def kernel_params():
    return pltpu.CompilerParams(vmem_limit_bytes=VMEM_BYTES)


def layer_norm(rows):
    mean = jnp.mean(rows, axis=-1, keepdims=True)
    centred = rows - mean
    variance = jnp.mean(centred * centred, axis=-1, keepdims=True)
    return centred * lax.rsqrt(variance + 1e-05)


def head_mask(shape, head_width, cluster):
    row_head = lax.broadcasted_iota(jnp.int32, shape, 0) // head_width % GROUP
    lane_head = lax.broadcasted_iota(jnp.int32, shape, 1) // cluster
    return row_head == lane_head


def place_kernel(features_ref, assignment_ref, placed_ref, normed_ref):
    walkers, _, rows = assignment_ref.shape
    lane = 128
    columns = lax.broadcasted_iota(jnp.int32, (lane, rows), 1)
    for walker in range(walkers):
        features = features_ref[walker * rows : (walker + 1) * rows, :]
        for part in range(rows // lane):
            chosen = assignment_ref[walker, :, part * lane : (part + 1) * lane] & (rows - 1)
            chosen = jnp.broadcast_to(chosen, (lane, lane)).T
            chosen = jnp.concatenate([chosen] * (rows // lane), axis=1)
            one_hot = jnp.where(chosen == columns, 1.0, 0.0).astype(jnp.bfloat16)
            placed = jnp.dot(one_hot, features, preferred_element_type=jnp.float32)
            here = pl.ds(walker * rows + part * lane, lane)
            placed_ref[here, :] = placed.astype(jnp.bfloat16)
            normed_ref[here, :] = layer_norm(placed).astype(jnp.bfloat16)


def place(features, assignment):
    width = features.shape[1]
    walkers, _, rows = assignment.shape
    local = pl.BlockSpec((2 * rows, width), lambda i: (i, 0))
    out = jax.ShapeDtypeStruct(features.shape, jnp.bfloat16)
    return pl.pallas_call(
        place_kernel,
        grid=(walkers // 2,),
        in_specs=[local, pl.BlockSpec((2, 1, rows), lambda i: (i, 0, 0))],
        out_specs=[local] * 2,
        out_shape=[out] * 2,
        cost_estimate=lasting(6),
        compiler_params=kernel_params(),
        name="place_rows",
    )(features, assignment)


def choose(index, values):
    result = values[-1]
    for at in range(len(values) - 2, -1, -1):
        result = jnp.where(index == at, values[at], result)
    return result


def pick_kernel(position_ref, wanted_ref, *rest, plan, capacity):
    position = position_ref[0]
    for out_ref, pieces in zip(rest[len(rest) - len(plan) :], plan, strict=True):
        for at, (blocks, reader_of, owner_of) in enumerate(pieces):
            reader, first = reader_of(position), owner_of(position) * capacity

            def one_slot(slot, carry, out_ref=out_ref, at=at, blocks=blocks, reader=reader, first=first):
                out_ref[at * capacity + slot] = rest[blocks][wanted_ref[reader, first + slot]]
                return carry

            lax.fori_loop(0, capacity, one_slot, 0)


def pick(position, wanted, sources, plan, after=()):
    capacity = wanted.shape[1] // SPAN
    block = sources[0].shape[1:]
    outs = [
        jax.ShapeDtypeStruct((len(pieces) * capacity,) + block, sources[0].dtype)
        for pieces in plan
    ]
    smem = pl.BlockSpec(memory_space=pltpu.SMEM)
    vmem = pl.BlockSpec(memory_space=pltpu.VMEM)
    return pl.pallas_call(
        functools.partial(pick_kernel, plan=plan, capacity=capacity),
        in_specs=[smem, smem]
        + [vmem] * len(sources)
        + [pl.BlockSpec(memory_space=pl.ANY)] * len(after),
        out_specs=[vmem] * len(outs),
        out_shape=outs,
        cost_estimate=lasting(1.5),
        compiler_params=kernel_params(),
        name="pick_blocks",
    )(position, wanted, *sources, *after)


def tiles_of(query, first, span):
    one = query[first : first + span]
    two = query[first + span : first + 2 * span]
    zeros = jnp.zeros_like(one)
    return jnp.concatenate(
        [jnp.concatenate([one, zeros], axis=1), jnp.concatenate([zeros, two], axis=1)], axis=0
    )


def own_kernel(normed_ref, query_w_ref, key_w_ref, value_w_ref, *rest, head_width):
    query_ref, own_ref, stats_ref = rest[-3:]
    blocks, width, tile = query_ref.shape
    cluster = tile // GROUP
    span = GROUP * head_width
    mask = head_mask((width, tile), head_width, cluster)
    scale = math.log2(math.e) / head_width**0.5
    ones = jnp.ones((16, cluster), jnp.bfloat16)
    rows = normed_ref[...]
    keys = jnp.dot(rows, key_w_ref[...], preferred_element_type=jnp.float32).astype(jnp.bfloat16)
    queries = []
    for block in range(blocks):
        own = rows[block * cluster : (block + 1) * cluster]
        tiled = jnp.concatenate([own] * GROUP, axis=0)
        query = lax.dot_general(query_w_ref[...], tiled, NT, preferred_element_type=jnp.float32)
        query = jnp.where(mask, query * scale, 0.0).astype(jnp.bfloat16)
        query_ref[block] = query
        queries.append(query)
    for block in range(blocks):
        own = rows[block * cluster : (block + 1) * cluster]
        value = lax.dot_general(value_w_ref[...], own, NT, preferred_element_type=jnp.float32)
        value = value.astype(jnp.bfloat16)
        tops, totals = [], []
        for pair in range(HEADS // GROUP // 2):
            first = pair * 2 * span
            scores = jnp.dot(
                keys[block * cluster : (block + 1) * cluster, first : first + 2 * span],
                tiles_of(queries[block], first, span),
                preferred_element_type=jnp.float32,
            )
            top = jnp.max(scores, axis=0, keepdims=True)
            weights = jnp.exp2(scores - top).astype(jnp.bfloat16)
            for half in range(2):
                at = first + half * span
                here = slice(half * tile, (half + 1) * tile)
                lifted = jnp.concatenate([value[at : at + span], ones], axis=0)
                product = jnp.dot(lifted, weights[:, here], preferred_element_type=jnp.float32)
                total = product[span : span + 1]
                result = jnp.where(mask[:span], product[:span] * (1.0 / total), 0.0)
                own_ref[block, at : at + span, :] = result.astype(jnp.bfloat16)
                tops.append(top[:, here])
                totals.append(total)
        stats_ref[block] = jnp.concatenate(tops + totals, axis=0)


def own_part(normed, w_query, w_key, w_value, cluster, half, so_far, after):
    rows, width = normed.shape
    blocks = rows // cluster
    tile = GROUP * cluster
    tiles = HEADS // GROUP
    steps = blocks // STEP // 2
    first = half * steps
    whole = pl.BlockSpec((width, width), lambda i: (0, 0))
    square = pl.BlockSpec((STEP, width, tile), lambda i: (first + i, 0, 0))
    extra = [*so_far, *after]
    return pl.pallas_call(
        functools.partial(own_kernel, head_width=width // HEADS),
        grid=(steps,),
        in_specs=[
            pl.BlockSpec((STEP * cluster, width), lambda i: (first + i, 0)),
            whole,
            whole,
            whole,
        ]
        + [pl.BlockSpec(memory_space=pl.ANY)] * len(extra),
        out_specs=[
            square,
            square,
            pl.BlockSpec((STEP, 2 * tiles, tile), lambda i: (first + i, 0, 0)),
        ],
        out_shape=[
            jax.ShapeDtypeStruct((blocks, width, tile), jnp.bfloat16),
            jax.ShapeDtypeStruct((blocks, width, tile), jnp.bfloat16),
            jax.ShapeDtypeStruct((blocks, 2 * tiles, tile), jnp.float32),
        ],
        input_output_aliases={4 + n: n for n in range(len(so_far))},
        cost_estimate=lasting(15),
        compiler_params=kernel_params(),
        name="own_blocks",
    )(normed, w_query.T, w_key, w_value.T, *extra)


def collect_kernel(*refs, places):
    buffer_ref, sems = refs[-2:]
    copy_pieces(refs[: len(places)], buffer_ref, places, sems)


def copy_pieces(piece_refs, buffer_ref, places, sems):
    copies = [
        pltpu.make_async_copy(piece, buffer_ref.at[pl.ds(at, piece.shape[0])], sems.at[n])
        for n, (piece, at) in enumerate(zip(piece_refs, places, strict=True))
    ]
    for copy in copies:
        copy.start()
    for copy in copies:
        copy.wait()


def collect(pieces, places, total):
    return pl.pallas_call(
        functools.partial(collect_kernel, places=places),
        in_specs=[pl.BlockSpec(memory_space=pltpu.VMEM)] * len(pieces),
        out_specs=pl.BlockSpec(memory_space=pl.ANY),
        out_shape=jax.ShapeDtypeStruct((total,) + pieces[0].shape[1:], pieces[0].dtype),
        scratch_shapes=[pltpu.SemaphoreType.DMA((len(pieces),))],
        cost_estimate=lasting(4),
        compiler_params=kernel_params(),
        name="collect_blocks",
    )(*pieces)


def attend_kernel(
    range_ref,
    order_ref,
    table_ref,
    query_ref,
    own_ref,
    stats_ref,
    placed_ref,
    *rest,
    head_width,
    places,
):
    weight_refs, rest = rest[:3], rest[3:]
    piece_refs = rest[: len(places)]
    mixed_ref, buffer_ref, query_buf, own_buf, stats_buf, member_buf, placed_buf = rest[-13:-6]
    attended_buf, before_buf, done_buf, in_sems, out_sems, piece_sems = rest[-6:]
    begin, count = range_ref[0], range_ref[1]
    pair_count = member_buf.shape[2]
    copy_pieces(piece_refs, buffer_ref, places, piece_sems)

    def fetches(step, slot):
        for j in range(STEP):
            block = order_ref[step * STEP + j]
            sources = [(query_ref.at[block], query_buf.at[slot, j])]
            sources.append((own_ref.at[block], own_buf.at[slot, j]))
            sources.append((stats_ref.at[block], stats_buf.at[slot, j]))
            sources.append((placed_ref.at[block], placed_buf.at[slot, j]))
            for n in range(pair_count):
                listed = table_ref[block * pair_count + n]
                sources.append((buffer_ref.at[listed], member_buf.at[slot, j, n]))
            for n, (source_, target) in enumerate(sources):
                sem = in_sems.at[slot, j * (pair_count + 4) + n]
                yield pltpu.make_async_copy(source_, target, sem)

    def stores(step):
        for j in range(STEP):
            target = mixed_ref.at[order_ref[step * STEP + j]]
            yield pltpu.make_async_copy(done_buf.at[j], target, out_sems.at[j])

    def finish():
        return finish_step(before_buf[...], attended_buf[...], *weight_refs[1:])

    def one_step(i, carry):
        slot = i % 2
        for copy in fetches(begin + jnp.minimum(i + 1, count - 1), 1 - slot):
            copy.start()
        for copy in fetches(begin + i, slot):
            copy.wait()
        attended, mixed = attend_step(
            query_buf.at[slot],
            own_buf.at[slot],
            stats_buf.at[slot],
            member_buf.at[slot],
            weight_refs[0],
            head_width,
            finish,
        )

        @pl.when(i > 1)
        def _():
            for copy in stores(begin + i - 2):
                copy.wait()

        done_buf[...] = mixed.reshape(done_buf.shape)
        attended_buf[...] = attended
        before_buf[...] = placed_buf[slot].reshape(before_buf.shape)

        @pl.when(i > 0)
        def _():
            for copy in stores(begin + i - 1):
                copy.start()

        return carry

    @pl.when(count > 0)
    def _():
        for copy in fetches(begin, 0):
            copy.start()
        attended_buf[...] = jnp.zeros_like(attended_buf)
        before_buf[...] = jnp.zeros_like(before_buf)
        lax.fori_loop(0, count, one_step, 0)
        for copy in fetches(begin + count - 1, count % 2):
            copy.wait()
        mixed = finish()

        @pl.when(count > 1)
        def _():
            for copy in stores(begin + count - 2):
                copy.wait()

        done_buf[...] = mixed.reshape(done_buf.shape)
        for copy in stores(begin + count - 1):
            copy.start()
        for copy in stores(begin + count - 1):
            copy.wait()


def finish_step(placed, attended, out_w_ref, mix_ref):
    middle = placed.astype(jnp.float32) + jnp.dot(
        attended, out_w_ref[...], preferred_element_type=jnp.float32
    )
    middle = middle.astype(jnp.bfloat16).astype(jnp.float32)
    second = layer_norm(middle).astype(jnp.bfloat16)
    mixed = middle + jnp.tanh(jnp.dot(second, mix_ref[...], preferred_element_type=jnp.float32))
    return mixed.astype(jnp.bfloat16)


def attend_step(
    query_ref, own_ref, stats_ref, member_ref, pair_w_ref, head_width, meanwhile
):
    _, members_count, cluster, width = member_ref.shape
    span = GROUP * head_width
    tile = GROUP * cluster
    diagonal = head_mask((span, tile), head_width, cluster)
    ones = jnp.ones((16, members_count * cluster), jnp.bfloat16)
    tiles = HEADS // GROUP
    units = [(block, pair) for block in range(STEP) for pair in range(HEADS // GROUP // 2)]
    listed = member_ref[...].reshape(STEP * members_count * cluster, width)
    both = jnp.dot(listed, pair_w_ref[...], preferred_element_type=jnp.float32)
    both = both.astype(jnp.bfloat16).reshape(STEP, members_count * cluster, 2 * width)
    finished = meanwhile()
    values = [both[block, :, width:].T for block in range(STEP)]

    def scores_of(block, pair):
        first = pair * 2 * span
        return jnp.dot(
            both[block, :, first : first + 2 * span],
            tiles_of(query_ref[block], first, span),
            preferred_element_type=jnp.float32,
        )

    def weights_of(block, pair, scores):
        own_top = jnp.concatenate(
            [stats_ref[block, t : t + 1, :] for t in (2 * pair, 2 * pair + 1)], axis=1
        )
        top = jnp.maximum(jnp.max(scores, axis=0, keepdims=True), own_top)
        weights = jnp.exp2((scores - top).astype(jnp.bfloat16))
        return weights, jnp.exp2(own_top - top)

    def products_of(block, pair, weights, own_factor):
        for half in range(2):
            t = pair * 2 + half
            here = slice(half * tile, (half + 1) * tile)
            lifted = jnp.concatenate([values[block][t * span : (t + 1) * span], ones], axis=0)
            product = jnp.dot(lifted, weights[:, here], preferred_element_type=jnp.float32)
            yield block, t, product, own_factor[:, here]

    def scaled(block, t, product, own_factor):
        own_total = stats_ref[block, tiles + t : tiles + t + 1, :] * own_factor
        inverse = 1.0 / (product[span : span + 1] + own_total)
        own = own_ref[block, t * span : (t + 1) * span, :].astype(jnp.float32)
        result = product[:span] * inverse + own * (own_total * inverse)
        result = jnp.where(diagonal, result, 0.0)
        return result[:, : tile // 2] + result[:, tile // 2 :]

    def rows_of(pieces):
        first, other = (jnp.concatenate(of, axis=0) for of in pieces)
        left = lax.broadcasted_iota(jnp.int32, first.shape, 1) < cluster
        first = first + pltpu.roll(first, cluster, 1)
        other = other + pltpu.roll(other, cluster, 1)
        return jnp.where(left, first, other).T.astype(jnp.bfloat16)

    count = len(units)
    scores, weights, products, pieces, attended = {}, {}, {}, [], []
    for at in range(-SCORES_AHEAD, count + 1):
        if at + SCORES_AHEAD < count:
            scores[at + SCORES_AHEAD] = scores_of(*units[at + SCORES_AHEAD])
        if 0 <= at + WEIGHTS_AHEAD < count:
            ahead = at + WEIGHTS_AHEAD
            weights[ahead] = weights_of(*units[ahead], scores.pop(ahead))
        if 0 <= at < count:
            products[at] = list(products_of(*units[at], *weights.pop(at)))
        if at > 0:
            pieces += [scaled(*product) for product in products.pop(at - 1)]
            if len(pieces) == 2 * tiles:
                attended.append(rows_of((pieces[:tiles], pieces[tiles:])))
                pieces = []
    return jnp.concatenate(attended, axis=0), finished


def attend(begin, count, order, table, own, placed, weights, buffer, pieces, places, so_far):
    blocks, cluster, width = placed.shape
    pair_count = table.shape[0] // blocks
    smem = pl.BlockSpec(memory_space=pltpu.SMEM)
    vmem = pl.BlockSpec(memory_space=pltpu.VMEM)
    hbm = pl.BlockSpec(memory_space=pl.ANY)
    in_specs = [smem] * 3 + [hbm] * (len(own) + 1) + [vmem] * (3 + len(pieces)) + [hbm]
    aliases = {len(in_specs) - 1: 1}
    operands = [*own, placed, *weights, *pieces, buffer]
    if so_far is not None:
        aliases[len(in_specs)] = 0
        in_specs.append(hbm)
        operands.append(so_far)
    kernel = functools.partial(
        attend_kernel, head_width=width // HEADS, places=places
    )
    return pl.pallas_call(
        kernel,
        in_specs=in_specs,
        out_specs=[hbm, hbm],
        out_shape=[
            jax.ShapeDtypeStruct(placed.shape, jnp.bfloat16),
            jax.ShapeDtypeStruct(buffer.shape, jnp.bfloat16),
        ],
        scratch_shapes=[
            *[pltpu.VMEM((2, STEP) + x.shape[1:], x.dtype) for x in own],
            pltpu.VMEM((2, STEP, pair_count, cluster, width), jnp.bfloat16),
            pltpu.VMEM((2, STEP, cluster, width), jnp.bfloat16),
            pltpu.VMEM((STEP * cluster, width), jnp.bfloat16),
            pltpu.VMEM((STEP * cluster, width), jnp.bfloat16),
            pltpu.VMEM((STEP, cluster, width), jnp.bfloat16),
            pltpu.SemaphoreType.DMA((2, STEP * (pair_count + 4))),
            pltpu.SemaphoreType.DMA((STEP,)),
            pltpu.SemaphoreType.DMA((len(pieces),)),
        ],
        input_output_aliases=aliases,
        cost_estimate=lasting(18),
        compiler_params=kernel_params(),
        name="attend_blocks",
    )(jnp.stack([begin, count]).astype(jnp.int32), order, table, *operands)


def slot_tables(owner, within, capacity):
    entries = owner.shape[0]
    alike = owner[:, None] == owner[None, :]
    earlier = jnp.arange(entries)[None, :] < jnp.arange(entries)[:, None]
    ranking = jnp.sum(jnp.where(alike & earlier, 1, 0), axis=1).astype(jnp.int32)
    slots = owner * capacity + ranking
    matches = slots[None, :] == jnp.arange(SPAN * capacity, dtype=jnp.int32)[:, None]
    return ranking, jnp.sum(jnp.where(matches, within[None, :], 0), axis=1).astype(jnp.int32)


def by_class(classes, count):
    blocks = jnp.arange(classes.shape[0], dtype=jnp.int32)
    before = (classes[None, :] < classes[:, None]) | (
        (classes[None, :] == classes[:, None]) & (blocks[None, :] < blocks[:, None])
    )
    rank = jnp.sum(jnp.where(before, 1, 0), axis=1)
    order = jnp.sum(jnp.where(rank[None, :] == blocks[:, None], blocks[None, :], 0), axis=1)
    ends = [jnp.sum(jnp.where(classes <= c, 1, 0)).astype(jnp.int32) for c in range(count)]
    return order.astype(jnp.int32), ends


OUT = (2, 0, 3, 1)
FROM = (1, 3, 0, 2)
LEVELS = 4


def position_at(z, y):
    return 2 * z + y


def partner(position):
    return position ^ 1


def onward(position):
    return position_at(choose(position // 2, OUT), position % 2)


def source(position):
    return position_at(choose(position // 2, FROM), position % 2)


def opposite(position):
    return position_at(LEVELS - 1 - position // 2, position % 2)


def itself(position):
    return position


def crossed(route):
    return lambda position: partner(route(position))


SECOND_PLAN = (((0, source, itself),),)
SECOND_CROSS_PLAN = (((0, source, partner),),)
MIDDLE_PLAN = (((0, opposite, itself),),)
MIDDLE_CROSS_PLAN = (((0, opposite, partner),),)
ON_PLAN = (((0, crossed(onward), source),), ((0, onward, source),))
NEAR_PLAN = (((0, partner, source),),)


def body(features, assignment, pairs, w_query, w_key, w_value, w_out, w_mix):
    rows_dev, width = features.shape
    block_count, pair_count = pairs.shape
    cluster = rows_dev // block_count
    stride = lax.axis_size("elec") // SPAN
    groups = [[rest + place_ * stride for place_ in range(SPAN)] for rest in range(stride)]
    position = lax.axis_index("elec") // stride
    at_position = position.reshape(1)
    capacity = (block_count * pair_count + SPAN - 1) // SPAN + 1

    def moved(x, moves):
        pairs_of = [(s * stride + r, d * stride + r) for s, d in moves for r in range(stride)]
        return lax.ppermute(x, "elec", pairs_of)

    def across_z(pairs_of_z):
        return [(position_at(s, y), position_at(d, y)) for s, d in pairs_of_z for y in range(2)]

    swap = [(p, p ^ 1) for p in range(SPAN)]
    first_moves = across_z(enumerate(OUT))
    second_moves = across_z(enumerate(FROM))
    middle_moves = across_z([(1, 2), (2, 1)])
    outward_moves = across_z([(2, 3), (1, 0)])

    listed = pairs.reshape(-1)
    owner = listed // block_count // stride
    within = listed % block_count
    ranking, tables = slot_tables(owner, within, capacity)
    wanted = lax.all_gather(tables, "elec", axis_index_groups=groups)

    shape = (block_count // SUB, 1, SUB * cluster)
    block_shape = (block_count, cluster, width)
    placed, normed = place(features, assignment.reshape(shape))
    blocks = normed.reshape(block_shape)
    own_operands = (normed, w_query, w_key, w_value, cluster)
    own = own_part(*own_operands, 0, (), (tables,))
    own = own_part(*own_operands, 1, own, (wanted,))
    own_at = 7 * capacity
    passed_at = own_at + block_count
    beside_at = passed_at + block_count
    total = beside_at + block_count

    beside = moved(blocks, swap)
    passed = moved(blocks, first_moves)
    (second,) = pick(at_position, wanted, (blocks,), SECOND_PLAN, after=own[2:])
    second = moved(second, second_moves)
    (second_cross,) = pick(at_position, wanted, (beside,), SECOND_CROSS_PLAN, after=own[2:])
    second_cross = moved(second_cross, second_moves)
    on, outward = pick(at_position, wanted, (passed,), ON_PLAN, after=own[2:])
    on = moved(on, swap)
    outward = moved(outward, outward_moves)
    (middle,) = pick(at_position, wanted, (blocks,), MIDDLE_PLAN, after=(second,))
    middle = moved(middle, middle_moves)
    (near,) = pick(at_position, wanted, (passed,), NEAR_PLAN, after=(on,))
    near = moved(near, swap)
    on = moved(on, outward_moves)
    (middle_cross,) = pick(
        at_position, wanted, (beside,), MIDDLE_CROSS_PLAN, after=(second_cross,)
    )
    middle_cross = moved(middle_cross, middle_moves)

    buffer = collect((blocks, passed, beside), (own_at, passed_at, beside_at), total)

    z, y = position // 2, position % 2
    is_end = (z == 0) | (z == LEVELS - 1)
    z_owner, same = owner // 2, owner % 2 == y
    from_first = z_owner == choose(z, FROM)
    late = z_owner == LEVELS - 1 - z
    piece_of = jnp.where(
        from_first,
        0,
        jnp.where(
            late,
            jnp.where(is_end, jnp.where(same, 3, 4), jnp.where(same, 5, 6)),
            jnp.where(same, 1, 2),
        ),
    )
    whole_at = jnp.where(z_owner == z, jnp.where(same, own_at, beside_at), passed_at)
    whole = (z_owner == z) | (from_first & same)
    table = jnp.where(whole, whole_at + within, piece_of * capacity + ranking)

    arrival = jnp.where(late, jnp.where(same | is_end, 1, 2), 0)
    order, ends = by_class(jnp.max(arrival.reshape(block_count, pair_count), axis=1), 2)
    marks = [0, ends[0] // STEP, ends[1] // STEP, block_count // STEP]
    phases = [(marks[n], marks[n + 1] - marks[n]) for n in range(3)]
    weights = (jnp.concatenate([w_key, w_value], axis=1), w_out, w_mix)
    shared = (order, table, own, placed.reshape(blocks.shape), weights)
    arrivals = (
        ((near, 0), (second, 1), (second_cross, 2)),
        ((outward, 3), (on, 4), (middle, 5)),
        ((middle_cross, 6),),
    )
    mixed = None
    for phase, arrived in zip(phases, arrivals, strict=True):
        pieces = [piece for piece, _ in arrived]
        places = tuple(at * capacity for _, at in arrived)
        mixed, buffer = attend(*phase, *shared, buffer, pieces, places, mixed)
    return mixed.reshape(rows_dev, width)


def solution(mesh):
    placed = (
        P(("groups", "elec"), None),
        P(("groups", "elec")),
        P(("groups", "elec"), None),
        P(),
        P(),
        P(),
        P(),
        P(),
    )
    return jax.shard_map(
        body, mesh=mesh, in_specs=placed, out_specs=P(("groups", "elec"), None), check_vma=False
    )
```

```python
import functools
import math

import jax
import jax.numpy as jnp
from jax import lax
from jax.experimental import pallas as pl
from jax.experimental.pallas import tpu as pltpu
from jax.sharding import PartitionSpec as P

HEADS = 16
SPAN = 8
SUB = 8
HEAD_WALKERS = 6
GROUP = 4
STEP = 4
SCORES_AHEAD, WEIGHTS_AHEAD = 2, 1
VMEM_BYTES = 48 * 1024 * 1024

NT = (((1,), (1,)), ((), ()))


def lasting(us):
    return pl.CostEstimate(flops=int(us * 1.15e9), bytes_accessed=0, transcendentals=0)


def kernel_params():
    return pltpu.CompilerParams(vmem_limit_bytes=VMEM_BYTES)


def layer_norm(rows):
    mean = jnp.mean(rows, axis=-1, keepdims=True)
    centred = rows - mean
    variance = jnp.mean(centred * centred, axis=-1, keepdims=True)
    return centred * lax.rsqrt(variance + 1e-05)


def head_mask(shape, head_width, cluster):
    row_head = lax.broadcasted_iota(jnp.int32, shape, 0) // head_width % GROUP
    lane_head = lax.broadcasted_iota(jnp.int32, shape, 1) // cluster
    return row_head == lane_head


def place_kernel(features_ref, assignment_ref, *rest):
    placed_ref, normed_ref = rest[-2:]
    walkers, _, rows = assignment_ref.shape
    lane = 128
    columns = lax.broadcasted_iota(jnp.int32, (lane, rows), 1)
    for walker in range(walkers):
        features = features_ref[walker * rows : (walker + 1) * rows, :]
        for part in range(rows // lane):
            chosen = assignment_ref[walker, :, part * lane : (part + 1) * lane] & (rows - 1)
            chosen = jnp.broadcast_to(chosen, (lane, lane)).T
            chosen = jnp.concatenate([chosen] * (rows // lane), axis=1)
            one_hot = jnp.where(chosen == columns, 1.0, 0.0).astype(jnp.bfloat16)
            placed = jnp.dot(one_hot, features, preferred_element_type=jnp.float32)
            here = pl.ds(walker * rows + part * lane, lane)
            placed_ref[here, :] = placed.astype(jnp.bfloat16)
            normed_ref[here, :] = layer_norm(placed).astype(jnp.bfloat16)


def place(features, assignment, first, count, so_far=None, after=()):
    total, width = features.shape
    _, _, rows = assignment.shape
    per = 2
    extra = ([] if so_far is None else [so_far]) + list(after)
    return pl.pallas_call(
        place_kernel,
        grid=(count // per,),
        in_specs=[
            pl.BlockSpec((per * rows, width), lambda i: (first // per + i, 0)),
            pl.BlockSpec((per, 1, rows), lambda i: (first // per + i, 0, 0)),
        ]
        + [pl.BlockSpec(memory_space=pl.ANY)] * len(extra),
        out_specs=[
            pl.BlockSpec((per * rows, width), lambda i: (first // per + i, 0)),
            pl.BlockSpec((per * rows, width), lambda i: (i, 0)),
        ],
        out_shape=[
            jax.ShapeDtypeStruct((total, width), jnp.bfloat16),
            jax.ShapeDtypeStruct((count * rows, width), jnp.bfloat16),
        ],
        input_output_aliases={} if so_far is None else {2: 0},
        cost_estimate=lasting(count * 0.7),
        compiler_params=kernel_params(),
        name="place_rows",
    )(features, assignment, *extra)


def choose(index, values):
    result = values[-1]
    for at in range(len(values) - 2, -1, -1):
        result = jnp.where(index == at, values[at], result)
    return result


def pick_kernel(position_ref, wanted_ref, head_ref, tail_ref, *rest, plan, capacity):
    position = position_ref[0]
    heads = head_ref.shape[0]
    for out_ref, (reader_of, owner_of) in zip(rest[len(rest) - len(plan) :], plan, strict=True):
        reader, first = reader_of(position), owner_of(position) * capacity

        def one_slot(slot, carry, out_ref=out_ref, reader=reader, first=first):
            block = wanted_ref[reader, first + slot]
            head = head_ref[jnp.minimum(block, heads - 1)]
            tail = tail_ref[jnp.maximum(block - heads, 0)]
            out_ref[slot] = jnp.where(block < heads, head, tail)
            return carry

        lax.fori_loop(0, capacity, one_slot, 0)


def pick(position, wanted, parts, plan, after=()):
    capacity = wanted.shape[1] // SPAN
    block = parts[0].shape[1:]
    outs = [jax.ShapeDtypeStruct((capacity,) + block, parts[0].dtype)] * len(plan)
    smem = pl.BlockSpec(memory_space=pltpu.SMEM)
    vmem = pl.BlockSpec(memory_space=pltpu.VMEM)
    return pl.pallas_call(
        functools.partial(pick_kernel, plan=plan, capacity=capacity),
        in_specs=[smem, smem, vmem, vmem] + [pl.BlockSpec(memory_space=pl.ANY)] * len(after),
        out_specs=[vmem] * len(outs),
        out_shape=outs,
        cost_estimate=lasting(1.5),
        compiler_params=kernel_params(),
        name="pick_blocks",
    )(position, wanted, *parts, *after)


def tiles_of(query, first, span):
    one = query[first : first + span]
    two = query[first + span : first + 2 * span]
    zeros = jnp.zeros_like(one)
    return jnp.concatenate(
        [jnp.concatenate([one, zeros], axis=1), jnp.concatenate([zeros, two], axis=1)], axis=0
    )


def own_kernel(normed_ref, query_w_ref, key_w_ref, value_w_ref, *rest, head_width):
    query_ref, own_ref, stats_ref = rest[-3:]
    blocks, width, tile = query_ref.shape
    cluster = tile // GROUP
    span = GROUP * head_width
    mask = head_mask((width, tile), head_width, cluster)
    scale = math.log2(math.e) / head_width**0.5
    ones = jnp.ones((16, cluster), jnp.bfloat16)
    rows = normed_ref[...]
    keys = jnp.dot(rows, key_w_ref[...], preferred_element_type=jnp.float32).astype(jnp.bfloat16)
    queries = []
    for block in range(blocks):
        own = rows[block * cluster : (block + 1) * cluster]
        tiled = jnp.concatenate([own] * GROUP, axis=0)
        query = lax.dot_general(query_w_ref[...], tiled, NT, preferred_element_type=jnp.float32)
        query = jnp.where(mask, query * scale, 0.0).astype(jnp.bfloat16)
        query_ref[block] = query
        queries.append(query)
    for block in range(blocks):
        own = rows[block * cluster : (block + 1) * cluster]
        value = lax.dot_general(value_w_ref[...], own, NT, preferred_element_type=jnp.float32)
        value = value.astype(jnp.bfloat16)
        tops, totals = [], []
        for pair in range(HEADS // GROUP // 2):
            first = pair * 2 * span
            scores = jnp.dot(
                keys[block * cluster : (block + 1) * cluster, first : first + 2 * span],
                tiles_of(queries[block], first, span),
                preferred_element_type=jnp.float32,
            )
            top = jnp.max(scores, axis=0, keepdims=True)
            weights = jnp.exp2(scores - top).astype(jnp.bfloat16)
            for half in range(2):
                at = first + half * span
                here = slice(half * tile, (half + 1) * tile)
                lifted = jnp.concatenate([value[at : at + span], ones], axis=0)
                product = jnp.dot(lifted, weights[:, here], preferred_element_type=jnp.float32)
                total = product[span : span + 1]
                result = jnp.where(mask[:span], product[:span] * (1.0 / total), 0.0)
                own_ref[block, at : at + span, :] = result.astype(jnp.bfloat16)
                tops.append(top[:, here])
                totals.append(total)
        stats_ref[block] = jnp.concatenate(tops + totals, axis=0)


def own_part(normed, weights, cluster, blocks, begin, at, count, so_far, after):
    width = normed.shape[1]
    tile = GROUP * cluster
    tiles = HEADS // GROUP
    begin, at = begin // STEP, at // STEP
    whole = pl.BlockSpec((width, width), lambda i: (0, 0))
    square = pl.BlockSpec((STEP, width, tile), lambda i: (at + i, 0, 0))
    extra = [*so_far, *after]
    return pl.pallas_call(
        functools.partial(own_kernel, head_width=width // HEADS),
        grid=(count // STEP,),
        in_specs=[
            pl.BlockSpec((STEP * cluster, width), lambda i: (begin + i, 0)),
            whole,
            whole,
            whole,
        ]
        + [pl.BlockSpec(memory_space=pl.ANY)] * len(extra),
        out_specs=[
            square,
            square,
            pl.BlockSpec((STEP, 2 * tiles, tile), lambda i: (at + i, 0, 0)),
        ],
        out_shape=[
            jax.ShapeDtypeStruct((blocks, width, tile), jnp.bfloat16),
            jax.ShapeDtypeStruct((blocks, width, tile), jnp.bfloat16),
            jax.ShapeDtypeStruct((blocks, 2 * tiles, tile), jnp.float32),
        ],
        input_output_aliases={4 + n: n for n in range(len(so_far))},
        cost_estimate=lasting(count / 2),
        compiler_params=kernel_params(),
        name="own_blocks",
    )(normed, *weights, *extra)


def collect_kernel(*refs, places):
    buffer_ref, sems = refs[-2:]
    copy_pieces(refs[: len(places)], buffer_ref, places, sems)


def copy_pieces(piece_refs, buffer_ref, places, sems):
    copies = [
        pltpu.make_async_copy(piece, buffer_ref.at[pl.ds(at, piece.shape[0])], sems.at[n])
        for n, (piece, at) in enumerate(zip(piece_refs, places, strict=True))
    ]
    for copy in copies:
        copy.start()
    for copy in copies:
        copy.wait()


def collect(pieces, places, total):
    return pl.pallas_call(
        functools.partial(collect_kernel, places=places),
        in_specs=[pl.BlockSpec(memory_space=pltpu.VMEM)] * len(pieces),
        out_specs=pl.BlockSpec(memory_space=pl.ANY),
        out_shape=jax.ShapeDtypeStruct((total,) + pieces[0].shape[1:], pieces[0].dtype),
        scratch_shapes=[pltpu.SemaphoreType.DMA((len(pieces),))],
        cost_estimate=lasting(4),
        compiler_params=kernel_params(),
        name="collect_blocks",
    )(*pieces)


def attend_kernel(
    range_ref,
    order_ref,
    table_ref,
    query_ref,
    own_ref,
    stats_ref,
    placed_ref,
    *rest,
    head_width,
    places,
):
    weight_refs, rest = rest[:3], rest[3:]
    piece_refs = rest[: len(places)]
    mixed_ref, buffer_ref, query_buf, own_buf, stats_buf, member_buf, placed_buf = rest[-13:-6]
    attended_buf, before_buf, done_buf, in_sems, out_sems, piece_sems = rest[-6:]
    begin, count = range_ref[0], range_ref[1]
    pair_count = member_buf.shape[2]
    copy_pieces(piece_refs, buffer_ref, places, piece_sems)

    def fetches(step, slot):
        for j in range(STEP):
            block = order_ref[step * STEP + j]
            sources = [(query_ref.at[block], query_buf.at[slot, j])]
            sources.append((own_ref.at[block], own_buf.at[slot, j]))
            sources.append((stats_ref.at[block], stats_buf.at[slot, j]))
            sources.append((placed_ref.at[block], placed_buf.at[slot, j]))
            for n in range(pair_count):
                listed = table_ref[block * pair_count + n]
                sources.append((buffer_ref.at[listed], member_buf.at[slot, j, n]))
            for n, (source_, target) in enumerate(sources):
                sem = in_sems.at[slot, j * (pair_count + 4) + n]
                yield pltpu.make_async_copy(source_, target, sem)

    def stores(step):
        for j in range(STEP):
            target = mixed_ref.at[order_ref[step * STEP + j]]
            yield pltpu.make_async_copy(done_buf.at[j], target, out_sems.at[j])

    def finish():
        return finish_step(before_buf[...], attended_buf[...], *weight_refs[1:])

    def one_step(i, carry):
        slot = i % 2
        for copy in fetches(begin + jnp.minimum(i + 1, count - 1), 1 - slot):
            copy.start()
        for copy in fetches(begin + i, slot):
            copy.wait()
        attended, mixed = attend_step(
            query_buf.at[slot],
            own_buf.at[slot],
            stats_buf.at[slot],
            member_buf.at[slot],
            weight_refs[0],
            head_width,
            finish,
        )

        @pl.when(i > 1)
        def _():
            for copy in stores(begin + i - 2):
                copy.wait()

        done_buf[...] = mixed.reshape(done_buf.shape)
        attended_buf[...] = attended
        before_buf[...] = placed_buf[slot].reshape(before_buf.shape)

        @pl.when(i > 0)
        def _():
            for copy in stores(begin + i - 1):
                copy.start()

        return carry

    @pl.when(count > 0)
    def _():
        for copy in fetches(begin, 0):
            copy.start()
        attended_buf[...] = jnp.zeros_like(attended_buf)
        before_buf[...] = jnp.zeros_like(before_buf)
        lax.fori_loop(0, count, one_step, 0)
        for copy in fetches(begin + count - 1, count % 2):
            copy.wait()
        mixed = finish()

        @pl.when(count > 1)
        def _():
            for copy in stores(begin + count - 2):
                copy.wait()

        done_buf[...] = mixed.reshape(done_buf.shape)
        for copy in stores(begin + count - 1):
            copy.start()
        for copy in stores(begin + count - 1):
            copy.wait()


def finish_step(placed, attended, out_w_ref, mix_ref):
    middle = placed.astype(jnp.float32) + jnp.dot(
        attended, out_w_ref[...], preferred_element_type=jnp.float32
    )
    middle = middle.astype(jnp.bfloat16).astype(jnp.float32)
    second = layer_norm(middle).astype(jnp.bfloat16)
    mixed = middle + jnp.tanh(jnp.dot(second, mix_ref[...], preferred_element_type=jnp.float32))
    return mixed.astype(jnp.bfloat16)


def attend_step(
    query_ref, own_ref, stats_ref, member_ref, pair_w_ref, head_width, meanwhile
):
    _, members_count, cluster, width = member_ref.shape
    span = GROUP * head_width
    tile = GROUP * cluster
    diagonal = head_mask((span, tile), head_width, cluster)
    ones = jnp.ones((16, members_count * cluster), jnp.bfloat16)
    tiles = HEADS // GROUP
    units = [(block, pair) for block in range(STEP) for pair in range(HEADS // GROUP // 2)]
    listed = member_ref[...].reshape(STEP * members_count * cluster, width)
    both = jnp.dot(listed, pair_w_ref[...], preferred_element_type=jnp.float32)
    both = both.astype(jnp.bfloat16).reshape(STEP, members_count * cluster, 2 * width)
    finished = meanwhile()
    values = [both[block, :, width:].T for block in range(STEP)]

    def scores_of(block, pair):
        first = pair * 2 * span
        return jnp.dot(
            both[block, :, first : first + 2 * span],
            tiles_of(query_ref[block], first, span),
            preferred_element_type=jnp.float32,
        )

    def weights_of(block, pair, scores):
        own_top = jnp.concatenate(
            [stats_ref[block, t : t + 1, :] for t in (2 * pair, 2 * pair + 1)], axis=1
        )
        top = jnp.maximum(jnp.max(scores, axis=0, keepdims=True), own_top)
        weights = jnp.exp2((scores - top).astype(jnp.bfloat16))
        return weights, jnp.exp2(own_top - top)

    def products_of(block, pair, weights, own_factor):
        for half in range(2):
            t = pair * 2 + half
            here = slice(half * tile, (half + 1) * tile)
            lifted = jnp.concatenate([values[block][t * span : (t + 1) * span], ones], axis=0)
            product = jnp.dot(lifted, weights[:, here], preferred_element_type=jnp.float32)
            yield block, t, product, own_factor[:, here]

    def scaled(block, t, product, own_factor):
        own_total = stats_ref[block, tiles + t : tiles + t + 1, :] * own_factor
        inverse = 1.0 / (product[span : span + 1] + own_total)
        own = own_ref[block, t * span : (t + 1) * span, :].astype(jnp.float32)
        result = product[:span] * inverse + own * (own_total * inverse)
        result = jnp.where(diagonal, result, 0.0)
        return result[:, : tile // 2] + result[:, tile // 2 :]

    def rows_of(pieces):
        first, other = (jnp.concatenate(of, axis=0) for of in pieces)
        left = lax.broadcasted_iota(jnp.int32, first.shape, 1) < cluster
        first = first + pltpu.roll(first, cluster, 1)
        other = other + pltpu.roll(other, cluster, 1)
        return jnp.where(left, first, other).T.astype(jnp.bfloat16)

    count = len(units)
    scores, weights, products, pieces, attended = {}, {}, {}, [], []
    for at in range(-SCORES_AHEAD, count + 1):
        if at + SCORES_AHEAD < count:
            scores[at + SCORES_AHEAD] = scores_of(*units[at + SCORES_AHEAD])
        if 0 <= at + WEIGHTS_AHEAD < count:
            ahead = at + WEIGHTS_AHEAD
            weights[ahead] = weights_of(*units[ahead], scores.pop(ahead))
        if 0 <= at < count:
            products[at] = list(products_of(*units[at], *weights.pop(at)))
        if at > 0:
            pieces += [scaled(*product) for product in products.pop(at - 1)]
            if len(pieces) == 2 * tiles:
                attended.append(rows_of((pieces[:tiles], pieces[tiles:])))
                pieces = []
    return jnp.concatenate(attended, axis=0), finished


def attend(begin, count, order, table, own, placed, weights, buffer, pieces, places, so_far):
    blocks, cluster, width = placed.shape
    pair_count = table.shape[0] // blocks
    smem = pl.BlockSpec(memory_space=pltpu.SMEM)
    vmem = pl.BlockSpec(memory_space=pltpu.VMEM)
    hbm = pl.BlockSpec(memory_space=pl.ANY)
    in_specs = [smem] * 3 + [hbm] * (len(own) + 1) + [vmem] * (3 + len(pieces)) + [hbm]
    aliases = {len(in_specs) - 1: 1}
    operands = [*own, placed, *weights, *pieces, buffer]
    if so_far is not None:
        aliases[len(in_specs)] = 0
        in_specs.append(hbm)
        operands.append(so_far)
    kernel = functools.partial(
        attend_kernel, head_width=width // HEADS, places=places
    )
    return pl.pallas_call(
        kernel,
        in_specs=in_specs,
        out_specs=[hbm, hbm],
        out_shape=[
            jax.ShapeDtypeStruct(placed.shape, jnp.bfloat16),
            jax.ShapeDtypeStruct(buffer.shape, jnp.bfloat16),
        ],
        scratch_shapes=[
            *[pltpu.VMEM((2, STEP) + x.shape[1:], x.dtype) for x in own],
            pltpu.VMEM((2, STEP, pair_count, cluster, width), jnp.bfloat16),
            pltpu.VMEM((2, STEP, cluster, width), jnp.bfloat16),
            pltpu.VMEM((STEP * cluster, width), jnp.bfloat16),
            pltpu.VMEM((STEP * cluster, width), jnp.bfloat16),
            pltpu.VMEM((STEP, cluster, width), jnp.bfloat16),
            pltpu.SemaphoreType.DMA((2, STEP * (pair_count + 4))),
            pltpu.SemaphoreType.DMA((STEP,)),
            pltpu.SemaphoreType.DMA((len(pieces),)),
        ],
        input_output_aliases=aliases,
        cost_estimate=lasting(18),
        compiler_params=kernel_params(),
        name="attend_blocks",
    )(jnp.stack([begin, count]).astype(jnp.int32), order, table, *operands)


def slot_tables(owner, within, capacity):
    readers, entries = owner.shape
    alike = owner[:, :, None] == owner[:, None, :]
    earlier = jnp.arange(entries)[None, :] < jnp.arange(entries)[:, None]
    ranking = jnp.sum(jnp.where(alike & earlier, 1, 0), axis=2).astype(jnp.int32)
    slots = owner * capacity + ranking
    every = jnp.arange(SPAN * capacity, dtype=jnp.int32)
    matches = slots[:, None, :] == every[None, :, None]
    return ranking, jnp.sum(jnp.where(matches, within[:, None, :], 0), axis=2).astype(jnp.int32)


def by_class(classes, count):
    blocks = jnp.arange(classes.shape[0], dtype=jnp.int32)
    before = (classes[None, :] < classes[:, None]) | (
        (classes[None, :] == classes[:, None]) & (blocks[None, :] < blocks[:, None])
    )
    rank = jnp.sum(jnp.where(before, 1, 0), axis=1)
    order = jnp.sum(jnp.where(rank[None, :] == blocks[:, None], blocks[None, :], 0), axis=1)
    ends = [jnp.sum(jnp.where(classes <= c, 1, 0)).astype(jnp.int32) for c in range(count)]
    return order.astype(jnp.int32), ends


OUT = (2, 0, 3, 1)
FROM = (1, 3, 0, 2)
LEVELS = 4


def position_at(z, y):
    return 2 * z + y


def partner(position):
    return position ^ 1


def onward(position):
    return position_at(choose(position // 2, OUT), position % 2)


def source(position):
    return position_at(choose(position // 2, FROM), position % 2)


def opposite(position):
    return position_at(LEVELS - 1 - position // 2, position % 2)


def itself(position):
    return position


def crossed(route):
    return lambda position: partner(route(position))


SECOND_PLAN = ((source, itself),)
MIDDLE_PLAN = ((opposite, itself),)
SECOND_CROSS_PLAN = ((source, partner),)
MIDDLE_CROSS_PLAN = ((opposite, partner),)
ON_PLAN = ((crossed(onward), source), (onward, source))
NEAR_PLAN = ((partner, source),)


def body(features, assignment, pairs, w_query, w_key, w_value, w_out, w_mix):
    rows_dev, width = features.shape
    block_count, pair_count = pairs.shape
    cluster = rows_dev // block_count
    stride = lax.axis_size("elec") // SPAN
    groups = [[rest + place_ * stride for place_ in range(SPAN)] for rest in range(stride)]
    position = lax.axis_index("elec") // stride
    at_position = position.reshape(1)
    capacity = (block_count * pair_count + SPAN - 1) // SPAN + 1

    def moved(x, moves):
        pairs_of = [(s * stride + r, d * stride + r) for s, d in moves for r in range(stride)]
        return lax.ppermute(x, "elec", pairs_of)

    def across_z(pairs_of_z):
        return [(position_at(s, y), position_at(d, y)) for s, d in pairs_of_z for y in range(2)]

    swap = [(p, p ^ 1) for p in range(SPAN)]
    first_moves = across_z(enumerate(OUT))
    second_moves = across_z(enumerate(FROM))
    middle_moves = across_z([(1, 2), (2, 1)])
    outward_moves = across_z([(2, 3), (1, 0)])

    all_pairs = lax.all_to_all(
        jnp.broadcast_to(pairs.reshape(1, -1), (SPAN, block_count * pair_count)),
        "elec",
        split_axis=0,
        concat_axis=0,
        axis_index_groups=groups,
        tiled=True,
    )
    _, wanted = slot_tables(all_pairs // block_count // stride, all_pairs % block_count, capacity)

    walkers = block_count // SUB
    heads = HEAD_WALKERS * SUB
    by_walker = assignment.reshape(walkers, 1, SUB * cluster)

    def in_blocks(rows):
        return rows.reshape(-1, cluster, width)

    own_weights = (w_query.T, w_key, w_value.T)
    own_shape = (own_weights, cluster, block_count)
    placed, head = place(features, by_walker, 0, HEAD_WALKERS, after=(all_pairs,))
    passed_head = moved(in_blocks(head), first_moves)
    beside_head = moved(in_blocks(head), swap)
    placed, tail = place(features, by_walker, HEAD_WALKERS, walkers - HEAD_WALKERS, placed)
    passed_tail = moved(in_blocks(tail), first_moves)
    beside_tail = moved(in_blocks(tail), swap)
    own = own_part(head, *own_shape, 0, 0, heads, (), (tail,))
    own = own_part(tail, *own_shape, 0, heads, block_count - heads, own, (wanted,))
    blocks = (in_blocks(head), in_blocks(tail))
    passed = (passed_head, passed_tail)
    beside = (beside_head, beside_tail)
    own_at = 7 * capacity
    passed_at = own_at + block_count
    beside_at = passed_at + block_count
    total = beside_at + block_count

    beside = moved(blocks, swap)
    passed = moved(blocks, first_moves)
    (second,) = pick(at_position, wanted, blocks, SECOND_PLAN, after=own[2:])
    second = moved(second, second_moves)
    (second_cross,) = pick(at_position, wanted, beside, SECOND_CROSS_PLAN, after=own[2:])
    second_cross = moved(second_cross, second_moves)
    on, outward = pick(at_position, wanted, passed, ON_PLAN, after=own[2:])
    on = moved(on, swap)
    outward = moved(outward, outward_moves)
    (middle,) = pick(at_position, wanted, blocks, MIDDLE_PLAN, after=(second,))
    middle = moved(middle, middle_moves)
    (near,) = pick(at_position, wanted, passed, NEAR_PLAN, after=(on,))
    near = moved(near, swap)
    on = moved(on, outward_moves)
    (middle_cross,) = pick(at_position, wanted, beside, MIDDLE_CROSS_PLAN, after=(second_cross,))
    middle_cross = moved(middle_cross, middle_moves)

    collected = (*blocks, *passed, *beside)
    places = [at + part for at in (own_at, passed_at, beside_at) for part in (0, heads)]
    buffer = collect(collected, places, total)

    listed = pairs.reshape(-1)
    owner, within = listed // block_count // stride, listed % block_count
    (ranking,), _ = slot_tables(owner[None], within[None], capacity)
    z, y = position // 2, position % 2
    is_end = (z == 0) | (z == LEVELS - 1)
    z_owner, same = owner // 2, owner % 2 == y
    from_first = z_owner == choose(z, FROM)
    late = z_owner == LEVELS - 1 - z
    piece_of = jnp.where(
        from_first,
        0,
        jnp.where(
            late,
            jnp.where(is_end, jnp.where(same, 3, 4), jnp.where(same, 5, 6)),
            jnp.where(same, 1, 2),
        ),
    )
    whole_at = jnp.where(z_owner == z, jnp.where(same, own_at, beside_at), passed_at)
    whole = (z_owner == z) | (from_first & same)
    table = jnp.where(whole, whole_at + within, piece_of * capacity + ranking)

    arrival = jnp.where(late, jnp.where(same | is_end, 1, 2), 0)
    order, ends = by_class(jnp.max(arrival.reshape(block_count, pair_count), axis=1), 2)
    marks = [0, ends[0] // STEP, ends[1] // STEP, block_count // STEP]
    phases = [(marks[n], marks[n + 1] - marks[n]) for n in range(3)]
    weights = (jnp.concatenate([w_key, w_value], axis=1), w_out, w_mix)
    shared = (order, table, own, in_blocks(placed), weights)
    arrivals = (
        ((near, 0), (second, 1), (second_cross, 2)),
        ((outward, 3), (on, 4), (middle, 5)),
        ((middle_cross, 6),),
    )
    mixed = None
    for phase, arrived in zip(phases, arrivals, strict=True):
        pieces = [piece for piece, _ in arrived]
        places = tuple(at * capacity for _, at in arrived)
        mixed, buffer = attend(*phase, *shared, buffer, pieces, places, mixed)
    return mixed.reshape(rows_dev, width)


def solution(mesh):
    placed = (
        P(("groups", "elec"), None),
        P(("groups", "elec")),
        P(("groups", "elec"), None),
        P(),
        P(),
        P(),
        P(),
        P(),
    )
    return jax.shard_map(
        body, mesh=mesh, in_specs=placed, out_specs=P(("groups", "elec"), None), check_vma=False
    )
```

```python
import functools
import math

import jax
import jax.numpy as jnp
from jax import lax
from jax.experimental import pallas as pl
from jax.experimental.pallas import tpu as pltpu
from jax.sharding import PartitionSpec as P

HEADS = 16
SPAN = 8
SUB = 8
GROUP = 4
STEP = 4
SCORES_AHEAD, WEIGHTS_AHEAD = 2, 1
VMEM_BYTES = 48 * 1024 * 1024

NT = (((1,), (1,)), ((), ()))


def lasting(us):
    return pl.CostEstimate(flops=int(us * 1.15e9), bytes_accessed=0, transcendentals=0)


def kernel_params():
    return pltpu.CompilerParams(vmem_limit_bytes=VMEM_BYTES)


def layer_norm(rows):
    mean = jnp.mean(rows, axis=-1, keepdims=True)
    centred = rows - mean
    variance = jnp.mean(centred * centred, axis=-1, keepdims=True)
    return centred * lax.rsqrt(variance + 1e-05)


def head_mask(shape, head_width, cluster):
    row_head = lax.broadcasted_iota(jnp.int32, shape, 0) // head_width % GROUP
    lane_head = lax.broadcasted_iota(jnp.int32, shape, 1) // cluster
    return row_head == lane_head


def place_kernel(features_ref, assignment_ref, placed_ref, normed_ref):
    walkers, _, rows = assignment_ref.shape
    lane = 128
    columns = lax.broadcasted_iota(jnp.int32, (lane, rows), 1)
    for walker in range(walkers):
        features = features_ref[walker * rows : (walker + 1) * rows, :]
        for part in range(rows // lane):
            chosen = assignment_ref[walker, :, part * lane : (part + 1) * lane] & (rows - 1)
            chosen = jnp.broadcast_to(chosen, (lane, lane)).T
            chosen = jnp.concatenate([chosen] * (rows // lane), axis=1)
            one_hot = jnp.where(chosen == columns, 1.0, 0.0).astype(jnp.bfloat16)
            placed = jnp.dot(one_hot, features, preferred_element_type=jnp.float32)
            here = pl.ds(walker * rows + part * lane, lane)
            placed_ref[here, :] = placed.astype(jnp.bfloat16)
            normed_ref[here, :] = layer_norm(placed).astype(jnp.bfloat16)


def place(features, assignment):
    width = features.shape[1]
    walkers, _, rows = assignment.shape
    local = pl.BlockSpec((2 * rows, width), lambda i: (i, 0))
    out = jax.ShapeDtypeStruct(features.shape, jnp.bfloat16)
    return pl.pallas_call(
        place_kernel,
        grid=(walkers // 2,),
        in_specs=[local, pl.BlockSpec((2, 1, rows), lambda i: (i, 0, 0))],
        out_specs=[local] * 2,
        out_shape=[out] * 2,
        cost_estimate=lasting(6),
        compiler_params=kernel_params(),
        name="place_rows",
    )(features, assignment)


def choose(index, values):
    result = values[-1]
    for at in range(len(values) - 2, -1, -1):
        result = jnp.where(index == at, values[at], result)
    return result


def pick_kernel(position_ref, wanted_ref, *rest, plan, capacity):
    position = position_ref[0]
    for out_ref, pieces in zip(rest[len(rest) - len(plan) :], plan, strict=True):
        for at, (blocks, reader_of, owner_of) in enumerate(pieces):
            reader, first = reader_of(position), owner_of(position) * capacity

            def one_slot(slot, carry, out_ref=out_ref, at=at, blocks=blocks, reader=reader, first=first):
                out_ref[at * capacity + slot] = rest[blocks][wanted_ref[reader, first + slot]]
                return carry

            lax.fori_loop(0, capacity, one_slot, 0)


def pick(position, wanted, sources, plan, after=()):
    capacity = wanted.shape[1] // SPAN
    block = sources[0].shape[1:]
    outs = [
        jax.ShapeDtypeStruct((len(pieces) * capacity,) + block, sources[0].dtype)
        for pieces in plan
    ]
    smem = pl.BlockSpec(memory_space=pltpu.SMEM)
    vmem = pl.BlockSpec(memory_space=pltpu.VMEM)
    return pl.pallas_call(
        functools.partial(pick_kernel, plan=plan, capacity=capacity),
        in_specs=[smem, smem]
        + [vmem] * len(sources)
        + [pl.BlockSpec(memory_space=pl.ANY)] * len(after),
        out_specs=[vmem] * len(outs),
        out_shape=outs,
        cost_estimate=lasting(1.5),
        compiler_params=kernel_params(),
        name="pick_blocks",
    )(position, wanted, *sources, *after)


def tiles_of(query, first, span):
    one = query[first : first + span]
    two = query[first + span : first + 2 * span]
    zeros = jnp.zeros_like(one)
    return jnp.concatenate(
        [jnp.concatenate([one, zeros], axis=1), jnp.concatenate([zeros, two], axis=1)], axis=0
    )


def own_kernel(
    normed_ref, query_w_ref, key_w_ref, value_w_ref, query_ref, own_ref, stats_ref, *, head_width
):
    blocks, width, tile = query_ref.shape
    cluster = tile // GROUP
    span = GROUP * head_width
    mask = head_mask((width, tile), head_width, cluster)
    scale = math.log2(math.e) / head_width**0.5
    ones = jnp.ones((16, cluster), jnp.bfloat16)
    rows = normed_ref[...]
    keys = jnp.dot(rows, key_w_ref[...], preferred_element_type=jnp.float32).astype(jnp.bfloat16)
    queries = []
    for block in range(blocks):
        own = rows[block * cluster : (block + 1) * cluster]
        tiled = jnp.concatenate([own] * GROUP, axis=0)
        query = lax.dot_general(query_w_ref[...], tiled, NT, preferred_element_type=jnp.float32)
        query = jnp.where(mask, query * scale, 0.0).astype(jnp.bfloat16)
        query_ref[block] = query
        queries.append(query)
    for block in range(blocks):
        own = rows[block * cluster : (block + 1) * cluster]
        value = lax.dot_general(value_w_ref[...], own, NT, preferred_element_type=jnp.float32)
        value = value.astype(jnp.bfloat16)
        tops, totals = [], []
        for pair in range(HEADS // GROUP // 2):
            first = pair * 2 * span
            scores = jnp.dot(
                keys[block * cluster : (block + 1) * cluster, first : first + 2 * span],
                tiles_of(queries[block], first, span),
                preferred_element_type=jnp.float32,
            )
            top = jnp.max(scores, axis=0, keepdims=True)
            weights = jnp.exp2(scores - top).astype(jnp.bfloat16)
            for half in range(2):
                at = first + half * span
                here = slice(half * tile, (half + 1) * tile)
                lifted = jnp.concatenate([value[at : at + span], ones], axis=0)
                product = jnp.dot(lifted, weights[:, here], preferred_element_type=jnp.float32)
                total = product[span : span + 1]
                result = jnp.where(mask[:span], product[:span] * (1.0 / total), 0.0)
                own_ref[block, at : at + span, :] = result.astype(jnp.bfloat16)
                tops.append(top[:, here])
                totals.append(total)
        stats_ref[block] = jnp.concatenate(tops + totals, axis=0)


def own_part(normed, w_query, w_key, w_value, cluster):
    rows, width = normed.shape
    blocks = rows // cluster
    tile = GROUP * cluster
    tiles = HEADS // GROUP
    whole = pl.BlockSpec((width, width), lambda i: (0, 0))
    square = pl.BlockSpec((STEP, width, tile), lambda i: (i, 0, 0))
    return pl.pallas_call(
        functools.partial(own_kernel, head_width=width // HEADS),
        grid=(blocks // STEP,),
        in_specs=[pl.BlockSpec((STEP * cluster, width), lambda i: (i, 0)), whole, whole, whole],
        out_specs=[
            square,
            square,
            pl.BlockSpec((STEP, 2 * tiles, tile), lambda i: (i, 0, 0)),
        ],
        out_shape=[
            jax.ShapeDtypeStruct((blocks, width, tile), jnp.bfloat16),
            jax.ShapeDtypeStruct((blocks, width, tile), jnp.bfloat16),
            jax.ShapeDtypeStruct((blocks, 2 * tiles, tile), jnp.float32),
        ],
        cost_estimate=lasting(20),
        compiler_params=kernel_params(),
        name="own_blocks",
    )(normed, w_query.T, w_key, w_value.T)


def collect_kernel(*refs, places):
    buffer_ref, sems = refs[-2:]
    copy_pieces(refs[: len(places)], buffer_ref, places, sems)


def copy_pieces(piece_refs, buffer_ref, places, sems):
    copies = [
        pltpu.make_async_copy(piece, buffer_ref.at[pl.ds(at, piece.shape[0])], sems.at[n])
        for n, (piece, at) in enumerate(zip(piece_refs, places, strict=True))
    ]
    for copy in copies:
        copy.start()
    for copy in copies:
        copy.wait()


def collect(pieces, places, total):
    return pl.pallas_call(
        functools.partial(collect_kernel, places=places),
        in_specs=[pl.BlockSpec(memory_space=pltpu.VMEM)] * len(pieces),
        out_specs=pl.BlockSpec(memory_space=pl.ANY),
        out_shape=jax.ShapeDtypeStruct((total,) + pieces[0].shape[1:], pieces[0].dtype),
        scratch_shapes=[pltpu.SemaphoreType.DMA((len(pieces),))],
        cost_estimate=lasting(4),
        compiler_params=kernel_params(),
        name="collect_blocks",
    )(*pieces)


def attend_kernel(
    range_ref,
    order_ref,
    table_ref,
    query_ref,
    own_ref,
    stats_ref,
    placed_ref,
    *rest,
    head_width,
    places,
):
    weight_refs, rest = rest[:3], rest[3:]
    piece_refs = rest[: len(places)]
    mixed_ref, buffer_ref, query_buf, own_buf, stats_buf, member_buf, placed_buf = rest[-13:-6]
    attended_buf, before_buf, done_buf, in_sems, out_sems, piece_sems = rest[-6:]
    begin, count = range_ref[0], range_ref[1]
    pair_count = member_buf.shape[2]
    copy_pieces(piece_refs, buffer_ref, places, piece_sems)

    def fetches(step, slot):
        for j in range(STEP):
            block = order_ref[step * STEP + j]
            sources = [(query_ref.at[block], query_buf.at[slot, j])]
            sources.append((own_ref.at[block], own_buf.at[slot, j]))
            sources.append((stats_ref.at[block], stats_buf.at[slot, j]))
            sources.append((placed_ref.at[block], placed_buf.at[slot, j]))
            for n in range(pair_count):
                listed = table_ref[block * pair_count + n]
                sources.append((buffer_ref.at[listed], member_buf.at[slot, j, n]))
            for n, (source_, target) in enumerate(sources):
                sem = in_sems.at[slot, j * (pair_count + 4) + n]
                yield pltpu.make_async_copy(source_, target, sem)

    def stores(step):
        for j in range(STEP):
            target = mixed_ref.at[order_ref[step * STEP + j]]
            yield pltpu.make_async_copy(done_buf.at[j], target, out_sems.at[j])

    def finish():
        return finish_step(before_buf[...], attended_buf[...], *weight_refs[1:])

    def one_step(i, carry):
        slot = i % 2
        for copy in fetches(begin + jnp.minimum(i + 1, count - 1), 1 - slot):
            copy.start()
        for copy in fetches(begin + i, slot):
            copy.wait()
        attended, mixed = attend_step(
            query_buf.at[slot],
            own_buf.at[slot],
            stats_buf.at[slot],
            member_buf.at[slot],
            weight_refs[0],
            head_width,
            finish,
        )

        @pl.when(i > 1)
        def _():
            for copy in stores(begin + i - 2):
                copy.wait()

        done_buf[...] = mixed.reshape(done_buf.shape)
        attended_buf[...] = attended
        before_buf[...] = placed_buf[slot].reshape(before_buf.shape)

        @pl.when(i > 0)
        def _():
            for copy in stores(begin + i - 1):
                copy.start()

        return carry

    @pl.when(count > 0)
    def _():
        for copy in fetches(begin, 0):
            copy.start()
        attended_buf[...] = jnp.zeros_like(attended_buf)
        before_buf[...] = jnp.zeros_like(before_buf)
        lax.fori_loop(0, count, one_step, 0)
        for copy in fetches(begin + count - 1, count % 2):
            copy.wait()
        mixed = finish()

        @pl.when(count > 1)
        def _():
            for copy in stores(begin + count - 2):
                copy.wait()

        done_buf[...] = mixed.reshape(done_buf.shape)
        for copy in stores(begin + count - 1):
            copy.start()
        for copy in stores(begin + count - 1):
            copy.wait()


def finish_step(placed, attended, out_w_ref, mix_ref):
    middle = placed.astype(jnp.float32) + jnp.dot(
        attended, out_w_ref[...], preferred_element_type=jnp.float32
    )
    middle = middle.astype(jnp.bfloat16).astype(jnp.float32)
    second = layer_norm(middle).astype(jnp.bfloat16)
    mixed = middle + jnp.tanh(jnp.dot(second, mix_ref[...], preferred_element_type=jnp.float32))
    return mixed.astype(jnp.bfloat16)


def attend_step(
    query_ref, own_ref, stats_ref, member_ref, pair_w_ref, head_width, meanwhile
):
    _, members_count, cluster, width = member_ref.shape
    span = GROUP * head_width
    tile = GROUP * cluster
    diagonal = head_mask((span, tile), head_width, cluster)
    ones = jnp.ones((16, members_count * cluster), jnp.bfloat16)
    tiles = HEADS // GROUP
    units = [(block, pair) for block in range(STEP) for pair in range(HEADS // GROUP // 2)]
    listed = member_ref[...].reshape(STEP * members_count * cluster, width)
    both = jnp.dot(listed, pair_w_ref[...], preferred_element_type=jnp.float32)
    both = both.astype(jnp.bfloat16).reshape(STEP, members_count * cluster, 2 * width)
    finished = meanwhile()
    values = [both[block, :, width:].T for block in range(STEP)]

    def scores_of(block, pair):
        first = pair * 2 * span
        return jnp.dot(
            both[block, :, first : first + 2 * span],
            tiles_of(query_ref[block], first, span),
            preferred_element_type=jnp.float32,
        )

    def weights_of(block, pair, scores):
        own_top = jnp.concatenate(
            [stats_ref[block, t : t + 1, :] for t in (2 * pair, 2 * pair + 1)], axis=1
        )
        top = jnp.maximum(jnp.max(scores, axis=0, keepdims=True), own_top)
        weights = jnp.exp2((scores - top).astype(jnp.bfloat16))
        return weights, jnp.exp2(own_top - top)

    def products_of(block, pair, weights, own_factor):
        for half in range(2):
            t = pair * 2 + half
            here = slice(half * tile, (half + 1) * tile)
            lifted = jnp.concatenate([values[block][t * span : (t + 1) * span], ones], axis=0)
            product = jnp.dot(lifted, weights[:, here], preferred_element_type=jnp.float32)
            yield block, t, product, own_factor[:, here]

    def scaled(block, t, product, own_factor):
        own_total = stats_ref[block, tiles + t : tiles + t + 1, :] * own_factor
        inverse = 1.0 / (product[span : span + 1] + own_total)
        own = own_ref[block, t * span : (t + 1) * span, :].astype(jnp.float32)
        result = product[:span] * inverse + own * (own_total * inverse)
        result = jnp.where(diagonal, result, 0.0)
        return result[:, : tile // 2] + result[:, tile // 2 :]

    def rows_of(pieces):
        first, other = (jnp.concatenate(of, axis=0) for of in pieces)
        left = lax.broadcasted_iota(jnp.int32, first.shape, 1) < cluster
        first = first + pltpu.roll(first, cluster, 1)
        other = other + pltpu.roll(other, cluster, 1)
        return jnp.where(left, first, other).T.astype(jnp.bfloat16)

    count = len(units)
    scores, weights, products, pieces, attended = {}, {}, {}, [], []
    for at in range(-SCORES_AHEAD, count + 1):
        if at + SCORES_AHEAD < count:
            scores[at + SCORES_AHEAD] = scores_of(*units[at + SCORES_AHEAD])
        if 0 <= at + WEIGHTS_AHEAD < count:
            ahead = at + WEIGHTS_AHEAD
            weights[ahead] = weights_of(*units[ahead], scores.pop(ahead))
        if 0 <= at < count:
            products[at] = list(products_of(*units[at], *weights.pop(at)))
        if at > 0:
            pieces += [scaled(*product) for product in products.pop(at - 1)]
            if len(pieces) == 2 * tiles:
                attended.append(rows_of((pieces[:tiles], pieces[tiles:])))
                pieces = []
    return jnp.concatenate(attended, axis=0), finished


def attend(begin, count, order, table, own, placed, weights, buffer, pieces, places, so_far):
    blocks, cluster, width = placed.shape
    pair_count = table.shape[0] // blocks
    smem = pl.BlockSpec(memory_space=pltpu.SMEM)
    vmem = pl.BlockSpec(memory_space=pltpu.VMEM)
    hbm = pl.BlockSpec(memory_space=pl.ANY)
    in_specs = [smem] * 3 + [hbm] * (len(own) + 1) + [vmem] * (3 + len(pieces)) + [hbm]
    aliases = {len(in_specs) - 1: 1}
    operands = [*own, placed, *weights, *pieces, buffer]
    if so_far is not None:
        aliases[len(in_specs)] = 0
        in_specs.append(hbm)
        operands.append(so_far)
    kernel = functools.partial(
        attend_kernel, head_width=width // HEADS, places=places
    )
    return pl.pallas_call(
        kernel,
        in_specs=in_specs,
        out_specs=[hbm, hbm],
        out_shape=[
            jax.ShapeDtypeStruct(placed.shape, jnp.bfloat16),
            jax.ShapeDtypeStruct(buffer.shape, jnp.bfloat16),
        ],
        scratch_shapes=[
            *[pltpu.VMEM((2, STEP) + x.shape[1:], x.dtype) for x in own],
            pltpu.VMEM((2, STEP, pair_count, cluster, width), jnp.bfloat16),
            pltpu.VMEM((2, STEP, cluster, width), jnp.bfloat16),
            pltpu.VMEM((STEP * cluster, width), jnp.bfloat16),
            pltpu.VMEM((STEP * cluster, width), jnp.bfloat16),
            pltpu.VMEM((STEP, cluster, width), jnp.bfloat16),
            pltpu.SemaphoreType.DMA((2, STEP * (pair_count + 4))),
            pltpu.SemaphoreType.DMA((STEP,)),
            pltpu.SemaphoreType.DMA((len(pieces),)),
        ],
        input_output_aliases=aliases,
        cost_estimate=lasting(18),
        compiler_params=kernel_params(),
        name="attend_blocks",
    )(jnp.stack([begin, count]).astype(jnp.int32), order, table, *operands)


def slot_tables(owner, within, capacity):
    entries = owner.shape[0]
    alike = owner[:, None] == owner[None, :]
    earlier = jnp.arange(entries)[None, :] < jnp.arange(entries)[:, None]
    ranking = jnp.sum(jnp.where(alike & earlier, 1, 0), axis=1).astype(jnp.int32)
    slots = owner * capacity + ranking
    matches = slots[None, :] == jnp.arange(SPAN * capacity, dtype=jnp.int32)[:, None]
    return ranking, jnp.sum(jnp.where(matches, within[None, :], 0), axis=1).astype(jnp.int32)


def by_class(classes, count):
    blocks = jnp.arange(classes.shape[0], dtype=jnp.int32)
    before = (classes[None, :] < classes[:, None]) | (
        (classes[None, :] == classes[:, None]) & (blocks[None, :] < blocks[:, None])
    )
    rank = jnp.sum(jnp.where(before, 1, 0), axis=1)
    order = jnp.sum(jnp.where(rank[None, :] == blocks[:, None], blocks[None, :], 0), axis=1)
    ends = [jnp.sum(jnp.where(classes <= c, 1, 0)).astype(jnp.int32) for c in range(count)]
    return order.astype(jnp.int32), ends


OUT = (2, 0, 3, 1)
FROM = (1, 3, 0, 2)
LEVELS = 4


def position_at(z, y):
    return 2 * z + y


def partner(position):
    return position ^ 1


def onward(position):
    return position_at(choose(position // 2, OUT), position % 2)


def source(position):
    return position_at(choose(position // 2, FROM), position % 2)


def opposite(position):
    return position_at(LEVELS - 1 - position // 2, position % 2)


def itself(position):
    return position


def crossed(route):
    return lambda position: partner(route(position))


SECOND_PLAN = (((0, source, itself),),)
SECOND_CROSS_PLAN = (((0, source, partner),),)
MIDDLE_PLAN = (((0, opposite, itself),),)
MIDDLE_CROSS_PLAN = (((0, opposite, partner),),)
ON_PLAN = (((0, crossed(onward), source),), ((0, onward, source),))
NEAR_PLAN = (((0, partner, source),),)


def body(features, assignment, pairs, w_query, w_key, w_value, w_out, w_mix):
    rows_dev, width = features.shape
    block_count, pair_count = pairs.shape
    cluster = rows_dev // block_count
    stride = lax.axis_size("elec") // SPAN
    groups = [[rest + place_ * stride for place_ in range(SPAN)] for rest in range(stride)]
    position = lax.axis_index("elec") // stride
    at_position = position.reshape(1)
    capacity = (block_count * pair_count + SPAN - 1) // SPAN + 1

    def moved(x, moves):
        pairs_of = [(s * stride + r, d * stride + r) for s, d in moves for r in range(stride)]
        return lax.ppermute(x, "elec", pairs_of)

    def across_z(pairs_of_z):
        return [(position_at(s, y), position_at(d, y)) for s, d in pairs_of_z for y in range(2)]

    swap = [(p, p ^ 1) for p in range(SPAN)]
    first_moves = across_z(enumerate(OUT))
    second_moves = across_z(enumerate(FROM))
    middle_moves = across_z([(1, 2), (2, 1)])
    outward_moves = across_z([(2, 3), (1, 0)])

    listed = pairs.reshape(-1)
    owner = listed // block_count // stride
    within = listed % block_count
    ranking, tables = slot_tables(owner, within, capacity)
    wanted = lax.all_to_all(
        jnp.broadcast_to(tables[None], (SPAN, SPAN * capacity)),
        "elec",
        split_axis=0,
        concat_axis=0,
        axis_index_groups=groups,
        tiled=True,
    )

    shape = (block_count // SUB, 1, SUB * cluster)
    block_shape = (block_count, cluster, width)
    placed, normed = place(features, assignment.reshape(shape))
    blocks = normed.reshape(block_shape)
    own = own_part(normed, w_query, w_key, w_value, cluster)
    own_at = 7 * capacity
    passed_at = own_at + block_count
    beside_at = passed_at + block_count
    total = beside_at + block_count

    beside = moved(blocks, swap)
    passed = moved(blocks, first_moves)
    (second_pick,) = pick(at_position, wanted, (blocks,), SECOND_PLAN, after=own[2:])
    second = moved(second_pick, second_moves)
    on, outward = pick(at_position, wanted, (passed,), ON_PLAN, after=(second_pick,))
    (second_cross,) = pick(at_position, wanted, (beside,), SECOND_CROSS_PLAN, after=(on,))
    second_cross = moved(second_cross, second_moves)
    on = moved(on, swap)
    outward = moved(outward, outward_moves)
    (middle,) = pick(at_position, wanted, (blocks,), MIDDLE_PLAN, after=(second,))
    middle = moved(middle, middle_moves)
    (near,) = pick(at_position, wanted, (passed,), NEAR_PLAN, after=(on,))
    near = moved(near, swap)
    on = moved(on, outward_moves)
    (middle_cross,) = pick(
        at_position, wanted, (beside,), MIDDLE_CROSS_PLAN, after=(second_cross,)
    )
    middle_cross = moved(middle_cross, middle_moves)

    buffer = collect((blocks, passed, beside), (own_at, passed_at, beside_at), total)

    z, y = position // 2, position % 2
    is_end = (z == 0) | (z == LEVELS - 1)
    z_owner, same = owner // 2, owner % 2 == y
    from_first = z_owner == choose(z, FROM)
    late = z_owner == LEVELS - 1 - z
    piece_of = jnp.where(
        from_first,
        0,
        jnp.where(
            late,
            jnp.where(is_end, jnp.where(same, 3, 4), jnp.where(same, 5, 6)),
            jnp.where(same, 1, 2),
        ),
    )
    whole_at = jnp.where(z_owner == z, jnp.where(same, own_at, beside_at), passed_at)
    whole = (z_owner == z) | (from_first & same)
    table = jnp.where(whole, whole_at + within, piece_of * capacity + ranking)

    arrival = jnp.where(late, jnp.where(same | is_end, 1, 2), 0)
    order, ends = by_class(jnp.max(arrival.reshape(block_count, pair_count), axis=1), 2)
    marks = [0, ends[0] // STEP, ends[1] // STEP, block_count // STEP]
    phases = [(marks[n], marks[n + 1] - marks[n]) for n in range(3)]
    weights = (jnp.concatenate([w_key, w_value], axis=1), w_out, w_mix)
    shared = (order, table, own, placed.reshape(blocks.shape), weights)
    arrivals = (
        ((near, 0), (second, 1), (second_cross, 2)),
        ((outward, 3), (on, 4), (middle, 5)),
        ((middle_cross, 6),),
    )
    mixed = None
    for phase, arrived in zip(phases, arrivals, strict=True):
        pieces = [piece for piece, _ in arrived]
        places = tuple(at * capacity for _, at in arrived)
        mixed, buffer = attend(*phase, *shared, buffer, pieces, places, mixed)
    return mixed.reshape(rows_dev, width)


def solution(mesh):
    placed = (
        P(("groups", "elec"), None),
        P(("groups", "elec")),
        P(("groups", "elec"), None),
        P(),
        P(),
        P(),
        P(),
        P(),
    )
    return jax.shard_map(
        body, mesh=mesh, in_specs=placed, out_specs=P(("groups", "elec"), None), check_vma=False
    )
```

```python
import functools
import math

import jax
import jax.numpy as jnp
from jax import lax
from jax.experimental import pallas as pl
from jax.experimental.pallas import tpu as pltpu
from jax.sharding import PartitionSpec as P

HEADS = 16
SPAN = 8
SUB = 8
GROUP = 4
STEP = 8
OWN_STEP = 4
SCORES_AHEAD, WEIGHTS_AHEAD = 2, 1
VMEM_BYTES = 48 * 1024 * 1024

NT = (((1,), (1,)), ((), ()))


def lasting(us):
    return pl.CostEstimate(flops=int(us * 1.15e9), bytes_accessed=0, transcendentals=0)


def kernel_params():
    return pltpu.CompilerParams(vmem_limit_bytes=VMEM_BYTES)


def layer_norm(rows):
    mean = jnp.mean(rows, axis=-1, keepdims=True)
    centred = rows - mean
    variance = jnp.mean(centred * centred, axis=-1, keepdims=True)
    return centred * lax.rsqrt(variance + 1e-05)


def head_mask(shape, head_width, cluster):
    row_head = lax.broadcasted_iota(jnp.int32, shape, 0) // head_width % GROUP
    lane_head = lax.broadcasted_iota(jnp.int32, shape, 1) // cluster
    return row_head == lane_head


def place_kernel(features_ref, assignment_ref, placed_ref, normed_ref):
    walkers, _, rows = assignment_ref.shape
    lane = 128
    columns = lax.broadcasted_iota(jnp.int32, (lane, rows), 1)
    for walker in range(walkers):
        features = features_ref[walker * rows : (walker + 1) * rows, :]
        for part in range(rows // lane):
            chosen = assignment_ref[walker, :, part * lane : (part + 1) * lane] & (rows - 1)
            chosen = jnp.broadcast_to(chosen, (lane, lane)).T
            chosen = jnp.concatenate([chosen] * (rows // lane), axis=1)
            one_hot = jnp.where(chosen == columns, 1.0, 0.0).astype(jnp.bfloat16)
            placed = jnp.dot(one_hot, features, preferred_element_type=jnp.float32)
            here = pl.ds(walker * rows + part * lane, lane)
            placed_ref[here, :] = placed.astype(jnp.bfloat16)
            normed_ref[here, :] = layer_norm(placed).astype(jnp.bfloat16)


def place(features, assignment):
    width = features.shape[1]
    walkers, _, rows = assignment.shape
    local = pl.BlockSpec((2 * rows, width), lambda i: (i, 0))
    out = jax.ShapeDtypeStruct(features.shape, jnp.bfloat16)
    return pl.pallas_call(
        place_kernel,
        grid=(walkers // 2,),
        in_specs=[local, pl.BlockSpec((2, 1, rows), lambda i: (i, 0, 0))],
        out_specs=[local] * 2,
        out_shape=[out] * 2,
        cost_estimate=lasting(6),
        compiler_params=kernel_params(),
        name="place_rows",
    )(features, assignment)


def choose(index, values):
    result = values[-1]
    for at in range(len(values) - 2, -1, -1):
        result = jnp.where(index == at, values[at], result)
    return result


def pick_kernel(position_ref, wanted_ref, blocks_ref, *rest, plan, capacity):
    sems = rest[-1]
    position = position_ref[0]

    def copies():
        for n, (reader_of, owner_of) in enumerate(plan):
            reader, first = reader_of(position), owner_of(position) * capacity
            for slot in range(capacity):
                block = wanted_ref[reader, first + slot]
                out_ref = rest[len(rest) - 1 - len(plan) + n]
                yield pltpu.make_async_copy(
                    blocks_ref.at[block], out_ref.at[slot], sems.at[n, slot]
                )

    for copy in copies():
        copy.start()
    for copy in copies():
        copy.wait()


def pick(position, wanted, blocks, plan, after=()):
    capacity = wanted.shape[1] // SPAN
    outs = [jax.ShapeDtypeStruct((capacity,) + blocks.shape[1:], blocks.dtype)] * len(plan)
    smem = pl.BlockSpec(memory_space=pltpu.SMEM)
    hbm = pl.BlockSpec(memory_space=pl.ANY)
    return pl.pallas_call(
        functools.partial(pick_kernel, plan=plan, capacity=capacity),
        in_specs=[smem, smem, hbm] + [hbm] * len(after),
        out_specs=[pl.BlockSpec(memory_space=pltpu.VMEM)] * len(outs),
        out_shape=outs,
        scratch_shapes=[pltpu.SemaphoreType.DMA((len(plan), capacity))],
        cost_estimate=lasting(1.5),
        compiler_params=kernel_params(),
        name="pick_blocks",
    )(position, wanted, blocks, *after)


def tiles_of(query, first, span):
    one = query[first : first + span]
    two = query[first + span : first + 2 * span]
    zeros = jnp.zeros_like(one)
    return jnp.concatenate(
        [jnp.concatenate([one, zeros], axis=1), jnp.concatenate([zeros, two], axis=1)], axis=0
    )


def own_kernel(
    normed_ref, query_w_ref, key_w_ref, value_w_ref, query_ref, own_ref, stats_ref, *, head_width
):
    blocks, width, tile = query_ref.shape
    cluster = tile // GROUP
    span = GROUP * head_width
    mask = head_mask((width, tile), head_width, cluster)
    scale = math.log2(math.e) / head_width**0.5
    ones = jnp.ones((16, cluster), jnp.bfloat16)
    rows = normed_ref[...]
    keys = jnp.dot(rows, key_w_ref[...], preferred_element_type=jnp.float32).astype(jnp.bfloat16)
    queries = []
    for block in range(blocks):
        own = rows[block * cluster : (block + 1) * cluster]
        tiled = jnp.concatenate([own] * GROUP, axis=0)
        query = lax.dot_general(query_w_ref[...], tiled, NT, preferred_element_type=jnp.float32)
        query = jnp.where(mask, query * scale, 0.0).astype(jnp.bfloat16)
        query_ref[block] = query
        queries.append(query)
    for block in range(blocks):
        own = rows[block * cluster : (block + 1) * cluster]
        value = lax.dot_general(value_w_ref[...], own, NT, preferred_element_type=jnp.float32)
        value = value.astype(jnp.bfloat16)
        tops, totals = [], []
        for pair in range(HEADS // GROUP // 2):
            first = pair * 2 * span
            scores = jnp.dot(
                keys[block * cluster : (block + 1) * cluster, first : first + 2 * span],
                tiles_of(queries[block], first, span),
                preferred_element_type=jnp.float32,
            )
            top = jnp.max(scores, axis=0, keepdims=True)
            weights = jnp.exp2(scores - top).astype(jnp.bfloat16)
            for half in range(2):
                at = first + half * span
                here = slice(half * tile, (half + 1) * tile)
                lifted = jnp.concatenate([value[at : at + span], ones], axis=0)
                product = jnp.dot(lifted, weights[:, here], preferred_element_type=jnp.float32)
                total = product[span : span + 1]
                result = jnp.where(mask[:span], product[:span] * (1.0 / total), 0.0)
                own_ref[block, at : at + span, :] = result.astype(jnp.bfloat16)
                tops.append(top[:, here])
                totals.append(total)
        stats_ref[block] = jnp.concatenate(tops + totals, axis=0)


def own_part(normed, w_query, w_key, w_value, cluster):
    rows, width = normed.shape
    blocks = rows // cluster
    tile = GROUP * cluster
    tiles = HEADS // GROUP
    whole = pl.BlockSpec((width, width), lambda i: (0, 0))
    square = pl.BlockSpec((OWN_STEP, width, tile), lambda i: (i, 0, 0))
    return pl.pallas_call(
        functools.partial(own_kernel, head_width=width // HEADS),
        grid=(blocks // OWN_STEP,),
        in_specs=[pl.BlockSpec((OWN_STEP * cluster, width), lambda i: (i, 0)), whole, whole, whole],
        out_specs=[
            square,
            square,
            pl.BlockSpec((OWN_STEP, 2 * tiles, tile), lambda i: (i, 0, 0)),
        ],
        out_shape=[
            jax.ShapeDtypeStruct((blocks, width, tile), jnp.bfloat16),
            jax.ShapeDtypeStruct((blocks, width, tile), jnp.bfloat16),
            jax.ShapeDtypeStruct((blocks, 2 * tiles, tile), jnp.float32),
        ],
        cost_estimate=lasting(20),
        compiler_params=kernel_params(),
        name="own_blocks",
    )(normed, w_query.T, w_key, w_value.T)


def collect_kernel(*refs, places):
    buffer_ref, sems = refs[-2:]
    copies = copy_pieces(refs[: len(places)], buffer_ref, places, sems)
    for copy in copies:
        copy.start()
    for copy in copies:
        copy.wait()


def copy_pieces(piece_refs, buffer_ref, places, sems):
    return [
        pltpu.make_async_copy(piece, buffer_ref.at[pl.ds(at, piece.shape[0])], sems.at[n])
        for n, (piece, at) in enumerate(zip(piece_refs, places, strict=True))
    ]


def collect(pieces, places, total):
    return pl.pallas_call(
        functools.partial(collect_kernel, places=places),
        in_specs=[pl.BlockSpec(memory_space=pltpu.VMEM)] * len(pieces),
        out_specs=pl.BlockSpec(memory_space=pl.ANY),
        out_shape=jax.ShapeDtypeStruct((total,) + pieces[0].shape[1:], pieces[0].dtype),
        scratch_shapes=[pltpu.SemaphoreType.DMA((len(pieces),))],
        cost_estimate=lasting(4),
        compiler_params=kernel_params(),
        name="collect_blocks",
    )(*pieces)


def attend_kernel(
    range_ref,
    order_ref,
    table_ref,
    query_ref,
    own_ref,
    stats_ref,
    placed_ref,
    *rest,
    head_width,
    places,
):
    weight_refs, rest = rest[:3], rest[3:]
    piece_refs = rest[: len(places)]
    mixed_ref, buffer_ref, query_buf, own_buf, stats_buf, member_buf, placed_buf = rest[-13:-6]
    attended_buf, before_buf, done_buf, in_sems, out_sems, piece_sems = rest[-6:]
    begin, count = range_ref[0], range_ref[1]
    pair_count = member_buf.shape[2]
    copies = copy_pieces(piece_refs, buffer_ref, places, piece_sems)
    for copy in copies:
        copy.start()

    def fetches(step, slot, known=True, listed=True):
        for j in range(STEP):
            block = order_ref[step * STEP + j]
            sources = [
                (query_ref.at[block], query_buf.at[slot, j]),
                (own_ref.at[block], own_buf.at[slot, j]),
                (stats_ref.at[block], stats_buf.at[slot, j]),
                (placed_ref.at[block], placed_buf.at[slot, j]),
            ]
            for n in range(pair_count):
                member = table_ref[block * pair_count + n]
                sources.append((buffer_ref.at[member], member_buf.at[slot, j, n]))
            for n, (source_, target) in enumerate(sources):
                if listed if n >= 4 else known:
                    sem = in_sems.at[slot, j * (pair_count + 4) + n]
                    yield pltpu.make_async_copy(source_, target, sem)

    def stores(step):
        for j in range(STEP):
            target = mixed_ref.at[order_ref[step * STEP + j]]
            yield pltpu.make_async_copy(done_buf.at[j], target, out_sems.at[j])

    def finish():
        return finish_step(before_buf[...], attended_buf[...], *weight_refs[1:])

    def one_step(i, carry):
        slot = i % 2
        for copy in fetches(begin + jnp.minimum(i + 1, count - 1), 1 - slot):
            copy.start()
        for copy in fetches(begin + i, slot):
            copy.wait()
        attended, mixed = attend_step(
            query_buf.at[slot],
            own_buf.at[slot],
            stats_buf.at[slot],
            member_buf.at[slot],
            weight_refs[0],
            head_width,
            finish,
        )

        @pl.when(i > 1)
        def _():
            for copy in stores(begin + i - 2):
                copy.wait()

        done_buf[...] = mixed.reshape(done_buf.shape)
        attended_buf[...] = attended
        before_buf[...] = placed_buf[slot].reshape(before_buf.shape)

        @pl.when(i > 0)
        def _():
            for copy in stores(begin + i - 1):
                copy.start()

        return carry

    @pl.when(count > 0)
    def _():
        for copy in fetches(begin, 0, listed=False):
            copy.start()

    for copy in copies:
        copy.wait()

    @pl.when(count > 0)
    def _():
        for copy in fetches(begin, 0, known=False):
            copy.start()
        attended_buf[...] = jnp.zeros_like(attended_buf)
        before_buf[...] = jnp.zeros_like(before_buf)
        lax.fori_loop(0, count, one_step, 0)
        for copy in fetches(begin + count - 1, count % 2):
            copy.wait()
        mixed = finish()

        @pl.when(count > 1)
        def _():
            for copy in stores(begin + count - 2):
                copy.wait()

        done_buf[...] = mixed.reshape(done_buf.shape)
        for copy in stores(begin + count - 1):
            copy.start()
        for copy in stores(begin + count - 1):
            copy.wait()


def finish_step(placed, attended, out_w_ref, mix_ref):
    middle = placed.astype(jnp.float32) + jnp.dot(
        attended, out_w_ref[...], preferred_element_type=jnp.float32
    )
    middle = middle.astype(jnp.bfloat16).astype(jnp.float32)
    second = layer_norm(middle).astype(jnp.bfloat16)
    mixed = middle + jnp.tanh(jnp.dot(second, mix_ref[...], preferred_element_type=jnp.float32))
    return mixed.astype(jnp.bfloat16)


def attend_step(
    query_ref, own_ref, stats_ref, member_ref, pair_w_ref, head_width, meanwhile
):
    _, members_count, cluster, width = member_ref.shape
    span = GROUP * head_width
    tile = GROUP * cluster
    diagonal = head_mask((span, tile), head_width, cluster)
    ones = jnp.ones((16, members_count * cluster), jnp.bfloat16)
    tiles = HEADS // GROUP
    units = [(block, pair) for block in range(STEP) for pair in range(HEADS // GROUP // 2)]
    listed = member_ref[...].reshape(STEP * members_count * cluster, width)
    both = jnp.dot(listed, pair_w_ref[...], preferred_element_type=jnp.float32)
    both = both.astype(jnp.bfloat16).reshape(STEP, members_count * cluster, 2 * width)
    finished = meanwhile()
    values = [both[block, :, width:].T for block in range(STEP)]

    def scores_of(block, pair):
        first = pair * 2 * span
        return jnp.dot(
            both[block, :, first : first + 2 * span],
            tiles_of(query_ref[block], first, span),
            preferred_element_type=jnp.float32,
        )

    def weights_of(block, pair, scores):
        own_top = jnp.concatenate(
            [stats_ref[block, t : t + 1, :] for t in (2 * pair, 2 * pair + 1)], axis=1
        )
        top = jnp.maximum(jnp.max(scores, axis=0, keepdims=True), own_top)
        weights = jnp.exp2((scores - top).astype(jnp.bfloat16))
        return weights, jnp.exp2(own_top - top)

    def products_of(block, pair, weights, own_factor):
        for half in range(2):
            t = pair * 2 + half
            here = slice(half * tile, (half + 1) * tile)
            lifted = jnp.concatenate([values[block][t * span : (t + 1) * span], ones], axis=0)
            product = jnp.dot(lifted, weights[:, here], preferred_element_type=jnp.float32)
            yield block, t, product, own_factor[:, here]

    def scaled(block, t, product, own_factor):
        own_total = stats_ref[block, tiles + t : tiles + t + 1, :] * own_factor
        inverse = 1.0 / (product[span : span + 1] + own_total)
        own = own_ref[block, t * span : (t + 1) * span, :].astype(jnp.float32)
        result = product[:span] * inverse + own * (own_total * inverse)
        result = jnp.where(diagonal, result, 0.0)
        return result[:, : tile // 2] + result[:, tile // 2 :]

    def rows_of(pieces):
        first, other = (jnp.concatenate(of, axis=0) for of in pieces)
        left = lax.broadcasted_iota(jnp.int32, first.shape, 1) < cluster
        first = first + pltpu.roll(first, cluster, 1)
        other = other + pltpu.roll(other, cluster, 1)
        return jnp.where(left, first, other).T.astype(jnp.bfloat16)

    count = len(units)
    scores, weights, products, pieces, attended = {}, {}, {}, [], []
    for at in range(-SCORES_AHEAD, count + 1):
        if at + SCORES_AHEAD < count:
            scores[at + SCORES_AHEAD] = scores_of(*units[at + SCORES_AHEAD])
        if 0 <= at + WEIGHTS_AHEAD < count:
            ahead = at + WEIGHTS_AHEAD
            weights[ahead] = weights_of(*units[ahead], scores.pop(ahead))
        if 0 <= at < count:
            products[at] = list(products_of(*units[at], *weights.pop(at)))
        if at > 0:
            pieces += [scaled(*product) for product in products.pop(at - 1)]
            if len(pieces) == 2 * tiles:
                attended.append(rows_of((pieces[:tiles], pieces[tiles:])))
                pieces = []
    return jnp.concatenate(attended, axis=0), finished


def attend(begin, count, order, table, own, placed, weights, buffer, pieces, places, so_far):
    blocks, cluster, width = placed.shape
    pair_count = table.shape[0] // blocks
    smem = pl.BlockSpec(memory_space=pltpu.SMEM)
    vmem = pl.BlockSpec(memory_space=pltpu.VMEM)
    hbm = pl.BlockSpec(memory_space=pl.ANY)
    in_specs = [smem] * 3 + [hbm] * (len(own) + 1) + [vmem] * (3 + len(pieces)) + [hbm]
    aliases = {len(in_specs) - 1: 1}
    operands = [*own, placed, *weights, *pieces, buffer]
    if so_far is not None:
        aliases[len(in_specs)] = 0
        in_specs.append(hbm)
        operands.append(so_far)
    kernel = functools.partial(
        attend_kernel, head_width=width // HEADS, places=places
    )
    return pl.pallas_call(
        kernel,
        in_specs=in_specs,
        out_specs=[hbm, hbm],
        out_shape=[
            jax.ShapeDtypeStruct(placed.shape, jnp.bfloat16),
            jax.ShapeDtypeStruct(buffer.shape, jnp.bfloat16),
        ],
        scratch_shapes=[
            *[pltpu.VMEM((2, STEP) + x.shape[1:], x.dtype) for x in own],
            pltpu.VMEM((2, STEP, pair_count, cluster, width), jnp.bfloat16),
            pltpu.VMEM((2, STEP, cluster, width), jnp.bfloat16),
            pltpu.VMEM((STEP * cluster, width), jnp.bfloat16),
            pltpu.VMEM((STEP * cluster, width), jnp.bfloat16),
            pltpu.VMEM((STEP, cluster, width), jnp.bfloat16),
            pltpu.SemaphoreType.DMA((2, STEP * (pair_count + 4))),
            pltpu.SemaphoreType.DMA((STEP,)),
            pltpu.SemaphoreType.DMA((len(pieces),)),
        ],
        input_output_aliases=aliases,
        cost_estimate=lasting(18),
        compiler_params=kernel_params(),
        name="attend_blocks",
    )(jnp.stack([begin, count]).astype(jnp.int32), order, table, *operands)


def slot_tables(owner, within, capacity):
    entries = owner.shape[0]
    alike = owner[:, None] == owner[None, :]
    earlier = jnp.arange(entries)[None, :] < jnp.arange(entries)[:, None]
    ranking = jnp.sum(jnp.where(alike & earlier, 1, 0), axis=1).astype(jnp.int32)
    slots = owner * capacity + ranking
    matches = slots[None, :] == jnp.arange(SPAN * capacity, dtype=jnp.int32)[:, None]
    return ranking, jnp.sum(jnp.where(matches, within[None, :], 0), axis=1).astype(jnp.int32)


def by_class(classes, count):
    blocks = jnp.arange(classes.shape[0], dtype=jnp.int32)
    before = (classes[None, :] < classes[:, None]) | (
        (classes[None, :] == classes[:, None]) & (blocks[None, :] < blocks[:, None])
    )
    rank = jnp.sum(jnp.where(before, 1, 0), axis=1)
    order = jnp.sum(jnp.where(rank[None, :] == blocks[:, None], blocks[None, :], 0), axis=1)
    ends = [jnp.sum(jnp.where(classes <= c, 1, 0)).astype(jnp.int32) for c in range(count)]
    return order.astype(jnp.int32), ends


OUT = (2, 0, 3, 1)
FROM = (1, 3, 0, 2)
LEVELS = 4


def position_at(z, y):
    return 2 * z + y


def partner(position):
    return position ^ 1


def onward(position):
    return position_at(choose(position // 2, OUT), position % 2)


def source(position):
    return position_at(choose(position // 2, FROM), position % 2)


def opposite(position):
    return position_at(LEVELS - 1 - position // 2, position % 2)


def itself(position):
    return position


def crossed(route):
    return lambda position: partner(route(position))


SECOND_PLAN = ((source, itself),)
MIDDLE_PLAN = ((opposite, itself),)
SECOND_CROSS_PLAN = ((source, partner),)
MIDDLE_CROSS_PLAN = ((opposite, partner),)
ON_PLAN = ((crossed(onward), source), (onward, source))
NEAR_PLAN = ((partner, source),)


def body(features, assignment, pairs, w_query, w_key, w_value, w_out, w_mix):
    rows_dev, width = features.shape
    block_count, pair_count = pairs.shape
    cluster = rows_dev // block_count
    stride = lax.axis_size("elec") // SPAN
    groups = [[rest + place_ * stride for place_ in range(SPAN)] for rest in range(stride)]
    position = lax.axis_index("elec") // stride
    at_position = position.reshape(1)
    capacity = (block_count * pair_count + SPAN - 1) // SPAN + 1

    def moved(x, moves):
        pairs_of = [(s * stride + r, d * stride + r) for s, d in moves for r in range(stride)]
        return lax.ppermute(x, "elec", pairs_of)

    def across_z(pairs_of_z):
        return [(position_at(s, y), position_at(d, y)) for s, d in pairs_of_z for y in range(2)]

    swap = [(p, p ^ 1) for p in range(SPAN)]
    first_moves = across_z(enumerate(OUT))
    second_moves = across_z(enumerate(FROM))
    middle_moves = across_z([(1, 2), (2, 1)])
    outward_moves = across_z([(2, 3), (1, 0)])

    listed = pairs.reshape(-1)
    owner = listed // block_count // stride
    within = listed % block_count
    ranking, tables = slot_tables(owner, within, capacity)
    wanted = lax.all_to_all(
        jnp.broadcast_to(tables[None], (SPAN, SPAN * capacity)),
        "elec",
        split_axis=0,
        concat_axis=0,
        axis_index_groups=groups,
        tiled=True,
    )

    shape = (block_count // SUB, 1, SUB * cluster)
    block_shape = (block_count, cluster, width)
    placed, normed = place(features, assignment.reshape(shape))
    blocks = normed.reshape(block_shape)
    own = own_part(normed, w_query, w_key, w_value, cluster)
    own_at = 7 * capacity
    passed_at = own_at + block_count
    beside_at = passed_at + block_count
    total = beside_at + block_count

    beside = moved(blocks, swap)
    passed = moved(blocks, first_moves)
    (second_pick,) = pick(at_position, wanted, blocks, SECOND_PLAN, after=own[2:])
    second = moved(second_pick, second_moves)
    on, outward = pick(at_position, wanted, passed, ON_PLAN, after=(second_pick,))
    (second_cross,) = pick(at_position, wanted, beside, SECOND_CROSS_PLAN, after=(on,))
    second_cross = moved(second_cross, second_moves)
    on = moved(on, swap)
    outward = moved(outward, outward_moves)
    (middle,) = pick(at_position, wanted, blocks, MIDDLE_PLAN, after=(second,))
    middle = moved(middle, middle_moves)
    (near,) = pick(at_position, wanted, passed, NEAR_PLAN, after=(on,))
    near = moved(near, swap)
    on = moved(on, outward_moves)
    (middle_cross,) = pick(
        at_position, wanted, beside, MIDDLE_CROSS_PLAN, after=(second_cross,)
    )
    middle_cross = moved(middle_cross, middle_moves)

    buffer = collect((blocks, passed, beside), (own_at, passed_at, beside_at), total)

    z, y = position // 2, position % 2
    is_end = (z == 0) | (z == LEVELS - 1)
    z_owner, same = owner // 2, owner % 2 == y
    from_first = z_owner == choose(z, FROM)
    late = z_owner == LEVELS - 1 - z
    piece_of = jnp.where(
        from_first,
        0,
        jnp.where(
            late,
            jnp.where(is_end, jnp.where(same, 3, 4), jnp.where(same, 5, 6)),
            jnp.where(same, 1, 2),
        ),
    )
    whole_at = jnp.where(z_owner == z, jnp.where(same, own_at, beside_at), passed_at)
    whole = (z_owner == z) | (from_first & same)
    table = jnp.where(whole, whole_at + within, piece_of * capacity + ranking)

    arrival = jnp.where(late & ~is_end, jnp.where(same, 1, 2), 0)
    order, ends = by_class(jnp.max(arrival.reshape(block_count, pair_count), axis=1), 2)
    marks = [0, ends[0] // STEP, ends[1] // STEP, block_count // STEP]
    phases = [(marks[n], marks[n + 1] - marks[n]) for n in range(3)]
    weights = (jnp.concatenate([w_key, w_value], axis=1), w_out, w_mix)
    shared = (order, table, own, placed.reshape(blocks.shape), weights)
    arrivals = (
        ((near, 0), (second, 1), (second_cross, 2), (outward, 3), (on, 4)),
        ((middle, 5),),
        ((middle_cross, 6),),
    )
    mixed = None
    for phase, arrived in zip(phases, arrivals, strict=True):
        pieces = [piece for piece, _ in arrived]
        places = tuple(at * capacity for _, at in arrived)
        mixed, buffer = attend(*phase, *shared, buffer, pieces, places, mixed)
    return mixed.reshape(rows_dev, width)


def solution(mesh):
    placed = (
        P(("groups", "elec"), None),
        P(("groups", "elec")),
        P(("groups", "elec"), None),
        P(),
        P(),
        P(),
        P(),
        P(),
    )
    return jax.shard_map(
        body, mesh=mesh, in_specs=placed, out_specs=P(("groups", "elec"), None), check_vma=False
    )
```

```python
import functools
import math

import jax
import jax.numpy as jnp
from jax import lax
from jax.experimental import pallas as pl
from jax.experimental.pallas import tpu as pltpu
from jax.sharding import PartitionSpec as P

HEADS = 16
SPAN = 8
SUB = 8
GROUP = 4
STEP = 8
OWN_STEP = 4
SCORES_AHEAD, WEIGHTS_AHEAD = 2, 1
VMEM_BYTES = 48 * 1024 * 1024

NT = (((1,), (1,)), ((), ()))


def lasting(us):
    return pl.CostEstimate(flops=int(us * 1.15e9), bytes_accessed=0, transcendentals=0)


def kernel_params():
    return pltpu.CompilerParams(vmem_limit_bytes=VMEM_BYTES)


def layer_norm(rows):
    mean = jnp.mean(rows, axis=-1, keepdims=True)
    centred = rows - mean
    variance = jnp.mean(centred * centred, axis=-1, keepdims=True)
    return centred * lax.rsqrt(variance + 1e-05)


def head_mask(shape, head_width, cluster):
    row_head = lax.broadcasted_iota(jnp.int32, shape, 0) // head_width % GROUP
    lane_head = lax.broadcasted_iota(jnp.int32, shape, 1) // cluster
    return row_head == lane_head


def place_kernel(features_ref, assignment_ref, placed_ref, normed_ref):
    walkers, _, rows = assignment_ref.shape
    lane = 128
    columns = lax.broadcasted_iota(jnp.int32, (lane, rows), 1)
    for walker in range(walkers):
        features = features_ref[walker * rows : (walker + 1) * rows, :]
        for part in range(rows // lane):
            chosen = assignment_ref[walker, :, part * lane : (part + 1) * lane] & (rows - 1)
            chosen = jnp.broadcast_to(chosen, (lane, lane)).T
            chosen = jnp.concatenate([chosen] * (rows // lane), axis=1)
            one_hot = jnp.where(chosen == columns, 1.0, 0.0).astype(jnp.bfloat16)
            placed = jnp.dot(one_hot, features, preferred_element_type=jnp.float32)
            here = pl.ds(walker * rows + part * lane, lane)
            placed_ref[here, :] = placed.astype(jnp.bfloat16)
            normed_ref[here, :] = layer_norm(placed).astype(jnp.bfloat16)


def place(features, assignment):
    width = features.shape[1]
    walkers, _, rows = assignment.shape
    local = pl.BlockSpec((2 * rows, width), lambda i: (i, 0))
    out = jax.ShapeDtypeStruct(features.shape, jnp.bfloat16)
    return pl.pallas_call(
        place_kernel,
        grid=(walkers // 2,),
        in_specs=[local, pl.BlockSpec((2, 1, rows), lambda i: (i, 0, 0))],
        out_specs=[local] * 2,
        out_shape=[out] * 2,
        cost_estimate=lasting(6),
        compiler_params=kernel_params(),
        name="place_rows",
    )(features, assignment)


def choose(index, values):
    result = values[-1]
    for at in range(len(values) - 2, -1, -1):
        result = jnp.where(index == at, values[at], result)
    return result


def pick_kernel(position_ref, wanted_ref, *rest, plan, capacity):
    position = position_ref[0]
    for out_ref, (at, reader_of, owner_of) in zip(rest[len(rest) - len(plan) :], plan, strict=True):
        reader, first = reader_of(position), owner_of(position) * capacity

        def one_slot(slot, carry, out_ref=out_ref, at=at, reader=reader, first=first):
            out_ref[slot] = rest[at][wanted_ref[reader, first + slot]]
            return carry

        lax.fori_loop(0, capacity, one_slot, 0)


def pick(position, wanted, sources, plan, after=()):
    capacity = wanted.shape[1] // SPAN
    block = sources[0].shape[1:]
    outs = [jax.ShapeDtypeStruct((capacity,) + block, sources[0].dtype)] * len(plan)
    smem = pl.BlockSpec(memory_space=pltpu.SMEM)
    vmem = pl.BlockSpec(memory_space=pltpu.VMEM)
    return pl.pallas_call(
        functools.partial(pick_kernel, plan=plan, capacity=capacity),
        in_specs=[smem, smem]
        + [vmem] * len(sources)
        + [pl.BlockSpec(memory_space=pl.ANY)] * len(after),
        out_specs=[vmem] * len(outs),
        out_shape=outs,
        cost_estimate=lasting(1.5),
        compiler_params=kernel_params(),
        name="pick_blocks",
    )(position, wanted, *sources, *after)


def tiles_of(query, first, span):
    one = query[first : first + span]
    two = query[first + span : first + 2 * span]
    zeros = jnp.zeros_like(one)
    return jnp.concatenate(
        [jnp.concatenate([one, zeros], axis=1), jnp.concatenate([zeros, two], axis=1)], axis=0
    )


def own_kernel(normed_ref, query_w_ref, key_w_ref, value_w_ref, *rest, head_width):
    query_ref, own_ref, stats_ref = rest[-3:]
    blocks, width, tile = query_ref.shape
    cluster = tile // GROUP
    span = GROUP * head_width
    mask = head_mask((width, tile), head_width, cluster)
    scale = math.log2(math.e) / head_width**0.5
    ones = jnp.ones((16, cluster), jnp.bfloat16)
    rows = normed_ref[...]
    keys = jnp.dot(rows, key_w_ref[...], preferred_element_type=jnp.float32).astype(jnp.bfloat16)
    queries = []
    for block in range(blocks):
        own = rows[block * cluster : (block + 1) * cluster]
        tiled = jnp.concatenate([own] * GROUP, axis=0)
        query = lax.dot_general(query_w_ref[...], tiled, NT, preferred_element_type=jnp.float32)
        query = jnp.where(mask, query * scale, 0.0).astype(jnp.bfloat16)
        query_ref[block] = query
        queries.append(query)
    for block in range(blocks):
        own = rows[block * cluster : (block + 1) * cluster]
        value = lax.dot_general(value_w_ref[...], own, NT, preferred_element_type=jnp.float32)
        value = value.astype(jnp.bfloat16)
        tops, totals = [], []
        for pair in range(HEADS // GROUP // 2):
            first = pair * 2 * span
            scores = jnp.dot(
                keys[block * cluster : (block + 1) * cluster, first : first + 2 * span],
                tiles_of(queries[block], first, span),
                preferred_element_type=jnp.float32,
            )
            top = jnp.max(scores, axis=0, keepdims=True)
            weights = jnp.exp2(scores - top).astype(jnp.bfloat16)
            for half in range(2):
                at = first + half * span
                here = slice(half * tile, (half + 1) * tile)
                lifted = jnp.concatenate([value[at : at + span], ones], axis=0)
                product = jnp.dot(lifted, weights[:, here], preferred_element_type=jnp.float32)
                total = product[span : span + 1]
                result = jnp.where(mask[:span], product[:span] * (1.0 / total), 0.0)
                own_ref[block, at : at + span, :] = result.astype(jnp.bfloat16)
                tops.append(top[:, here])
                totals.append(total)
        stats_ref[block] = jnp.concatenate(tops + totals, axis=0)


def own_part(normed, w_query, w_key, w_value, cluster, after):
    rows, width = normed.shape
    blocks = rows // cluster
    tile = GROUP * cluster
    tiles = HEADS // GROUP
    whole = pl.BlockSpec((width, width), lambda i: (0, 0))
    square = pl.BlockSpec((OWN_STEP, width, tile), lambda i: (i, 0, 0))
    return pl.pallas_call(
        functools.partial(own_kernel, head_width=width // HEADS),
        grid=(blocks // OWN_STEP,),
        in_specs=[pl.BlockSpec((OWN_STEP * cluster, width), lambda i: (i, 0)), whole, whole, whole]
        + [pl.BlockSpec(memory_space=pl.ANY)] * len(after),
        out_specs=[
            square,
            square,
            pl.BlockSpec((OWN_STEP, 2 * tiles, tile), lambda i: (i, 0, 0)),
        ],
        out_shape=[
            jax.ShapeDtypeStruct((blocks, width, tile), jnp.bfloat16),
            jax.ShapeDtypeStruct((blocks, width, tile), jnp.bfloat16),
            jax.ShapeDtypeStruct((blocks, 2 * tiles, tile), jnp.float32),
        ],
        cost_estimate=lasting(20),
        compiler_params=kernel_params(),
        name="own_blocks",
    )(normed, w_query.T, w_key, w_value.T, *after)


def collect_kernel(*refs, places):
    buffer_ref, sems = refs[-2:]
    copies = copy_pieces(refs[: len(places)], buffer_ref, places, sems)
    for copy in copies:
        copy.start()
    for copy in copies:
        copy.wait()


def copy_pieces(piece_refs, buffer_ref, places, sems):
    return [
        pltpu.make_async_copy(piece, buffer_ref.at[pl.ds(at, piece.shape[0])], sems.at[n])
        for n, (piece, at) in enumerate(zip(piece_refs, places, strict=True))
    ]


def collect(pieces, places, total):
    return pl.pallas_call(
        functools.partial(collect_kernel, places=places),
        in_specs=[pl.BlockSpec(memory_space=pltpu.VMEM)] * len(pieces),
        out_specs=pl.BlockSpec(memory_space=pl.ANY),
        out_shape=jax.ShapeDtypeStruct((total,) + pieces[0].shape[1:], pieces[0].dtype),
        scratch_shapes=[pltpu.SemaphoreType.DMA((len(pieces),))],
        cost_estimate=lasting(4),
        compiler_params=kernel_params(),
        name="collect_blocks",
    )(*pieces)


def attend_kernel(
    range_ref,
    order_ref,
    table_ref,
    query_ref,
    own_ref,
    stats_ref,
    placed_ref,
    *rest,
    head_width,
    places,
):
    weight_refs, rest = rest[:3], rest[3:]
    piece_refs = rest[: len(places)]
    mixed_ref, buffer_ref, query_buf, own_buf, stats_buf, member_buf, placed_buf = rest[-13:-6]
    attended_buf, before_buf, done_buf, in_sems, out_sems, piece_sems = rest[-6:]
    begin, count = range_ref[0], range_ref[1]
    pair_count = member_buf.shape[2]
    copies = copy_pieces(piece_refs, buffer_ref, places, piece_sems)
    for copy in copies:
        copy.start()

    def fetches(step, slot, known=True, listed=True):
        for j in range(STEP):
            block = order_ref[step * STEP + j]
            sources = [
                (query_ref.at[block], query_buf.at[slot, j]),
                (own_ref.at[block], own_buf.at[slot, j]),
                (stats_ref.at[block], stats_buf.at[slot, j]),
                (placed_ref.at[block], placed_buf.at[slot, j]),
            ]
            for n in range(pair_count):
                member = table_ref[block * pair_count + n]
                sources.append((buffer_ref.at[member], member_buf.at[slot, j, n]))
            for n, (source_, target) in enumerate(sources):
                if listed if n >= 4 else known:
                    sem = in_sems.at[slot, j * (pair_count + 4) + n]
                    yield pltpu.make_async_copy(source_, target, sem)

    def stores(step):
        for j in range(STEP):
            target = mixed_ref.at[order_ref[step * STEP + j]]
            yield pltpu.make_async_copy(done_buf.at[j], target, out_sems.at[j])

    def finish():
        return finish_step(before_buf[...], attended_buf[...], *weight_refs[1:])

    def one_step(i, carry):
        slot = i % 2
        for copy in fetches(begin + jnp.minimum(i + 1, count - 1), 1 - slot):
            copy.start()
        for copy in fetches(begin + i, slot):
            copy.wait()
        attended, mixed = attend_step(
            query_buf.at[slot],
            own_buf.at[slot],
            stats_buf.at[slot],
            member_buf.at[slot],
            weight_refs[0],
            head_width,
            finish,
        )

        @pl.when(i > 1)
        def _():
            for copy in stores(begin + i - 2):
                copy.wait()

        done_buf[...] = mixed.reshape(done_buf.shape)
        attended_buf[...] = attended
        before_buf[...] = placed_buf[slot].reshape(before_buf.shape)

        @pl.when(i > 0)
        def _():
            for copy in stores(begin + i - 1):
                copy.start()

        return carry

    @pl.when(count > 0)
    def _():
        for copy in fetches(begin, 0, listed=False):
            copy.start()

    for copy in copies:
        copy.wait()

    @pl.when(count > 0)
    def _():
        for copy in fetches(begin, 0, known=False):
            copy.start()
        attended_buf[...] = jnp.zeros_like(attended_buf)
        before_buf[...] = jnp.zeros_like(before_buf)
        lax.fori_loop(0, count, one_step, 0)
        for copy in fetches(begin + count - 1, count % 2):
            copy.wait()
        mixed = finish()

        @pl.when(count > 1)
        def _():
            for copy in stores(begin + count - 2):
                copy.wait()

        done_buf[...] = mixed.reshape(done_buf.shape)
        for copy in stores(begin + count - 1):
            copy.start()
        for copy in stores(begin + count - 1):
            copy.wait()


def finish_step(placed, attended, out_w_ref, mix_ref):
    middle = placed.astype(jnp.float32) + jnp.dot(
        attended, out_w_ref[...], preferred_element_type=jnp.float32
    )
    middle = middle.astype(jnp.bfloat16).astype(jnp.float32)
    second = layer_norm(middle).astype(jnp.bfloat16)
    mixed = middle + jnp.tanh(jnp.dot(second, mix_ref[...], preferred_element_type=jnp.float32))
    return mixed.astype(jnp.bfloat16)


def attend_step(
    query_ref, own_ref, stats_ref, member_ref, pair_w_ref, head_width, meanwhile
):
    _, members_count, cluster, width = member_ref.shape
    span = GROUP * head_width
    tile = GROUP * cluster
    diagonal = head_mask((span, tile), head_width, cluster)
    ones = jnp.ones((16, members_count * cluster), jnp.bfloat16)
    tiles = HEADS // GROUP
    units = [(block, pair) for block in range(STEP) for pair in range(HEADS // GROUP // 2)]
    listed = member_ref[...].reshape(STEP * members_count * cluster, width)
    both = jnp.dot(listed, pair_w_ref[...], preferred_element_type=jnp.float32)
    both = both.astype(jnp.bfloat16).reshape(STEP, members_count * cluster, 2 * width)
    finished = meanwhile()
    values = [both[block, :, width:].T for block in range(STEP)]

    def scores_of(block, pair):
        first = pair * 2 * span
        return jnp.dot(
            both[block, :, first : first + 2 * span],
            tiles_of(query_ref[block], first, span),
            preferred_element_type=jnp.float32,
        )

    def weights_of(block, pair, scores):
        own_top = jnp.concatenate(
            [stats_ref[block, t : t + 1, :] for t in (2 * pair, 2 * pair + 1)], axis=1
        )
        top = jnp.maximum(jnp.max(scores, axis=0, keepdims=True), own_top)
        weights = jnp.exp2((scores - top).astype(jnp.bfloat16))
        return weights, jnp.exp2(own_top - top)

    def products_of(block, pair, weights, own_factor):
        for half in range(2):
            t = pair * 2 + half
            here = slice(half * tile, (half + 1) * tile)
            lifted = jnp.concatenate([values[block][t * span : (t + 1) * span], ones], axis=0)
            product = jnp.dot(lifted, weights[:, here], preferred_element_type=jnp.float32)
            yield block, t, product, own_factor[:, here]

    def scaled(block, t, product, own_factor):
        own_total = stats_ref[block, tiles + t : tiles + t + 1, :] * own_factor
        inverse = 1.0 / (product[span : span + 1] + own_total)
        own = own_ref[block, t * span : (t + 1) * span, :].astype(jnp.float32)
        result = product[:span] * inverse + own * (own_total * inverse)
        result = jnp.where(diagonal, result, 0.0)
        return result[:, : tile // 2] + result[:, tile // 2 :]

    def rows_of(pieces):
        first, other = (jnp.concatenate(of, axis=0) for of in pieces)
        left = lax.broadcasted_iota(jnp.int32, first.shape, 1) < cluster
        first = first + pltpu.roll(first, cluster, 1)
        other = other + pltpu.roll(other, cluster, 1)
        return jnp.where(left, first, other).T.astype(jnp.bfloat16)

    count = len(units)
    scores, weights, products, pieces, attended = {}, {}, {}, [], []
    for at in range(-SCORES_AHEAD, count + 1):
        if at + SCORES_AHEAD < count:
            scores[at + SCORES_AHEAD] = scores_of(*units[at + SCORES_AHEAD])
        if 0 <= at + WEIGHTS_AHEAD < count:
            ahead = at + WEIGHTS_AHEAD
            weights[ahead] = weights_of(*units[ahead], scores.pop(ahead))
        if 0 <= at < count:
            products[at] = list(products_of(*units[at], *weights.pop(at)))
        if at > 0:
            pieces += [scaled(*product) for product in products.pop(at - 1)]
            if len(pieces) == 2 * tiles:
                attended.append(rows_of((pieces[:tiles], pieces[tiles:])))
                pieces = []
    return jnp.concatenate(attended, axis=0), finished


def attend(steps, order, table, own, placed, weights, buffer, pieces, places, so_far):
    blocks, cluster, width = placed.shape
    pair_count = table.shape[0] // blocks
    smem = pl.BlockSpec(memory_space=pltpu.SMEM)
    vmem = pl.BlockSpec(memory_space=pltpu.VMEM)
    hbm = pl.BlockSpec(memory_space=pl.ANY)
    in_specs = [smem] * 3 + [hbm] * (len(own) + 1) + [vmem] * (3 + len(pieces)) + [hbm]
    aliases = {len(in_specs) - 1: 1}
    operands = [*own, placed, *weights, *pieces, buffer]
    if so_far is not None:
        aliases[len(in_specs)] = 0
        in_specs.append(hbm)
        operands.append(so_far)
    kernel = functools.partial(
        attend_kernel, head_width=width // HEADS, places=places
    )
    return pl.pallas_call(
        kernel,
        in_specs=in_specs,
        out_specs=[hbm, hbm],
        out_shape=[
            jax.ShapeDtypeStruct(placed.shape, jnp.bfloat16),
            jax.ShapeDtypeStruct(buffer.shape, jnp.bfloat16),
        ],
        scratch_shapes=[
            *[pltpu.VMEM((2, STEP) + x.shape[1:], x.dtype) for x in own],
            pltpu.VMEM((2, STEP, pair_count, cluster, width), jnp.bfloat16),
            pltpu.VMEM((2, STEP, cluster, width), jnp.bfloat16),
            pltpu.VMEM((STEP * cluster, width), jnp.bfloat16),
            pltpu.VMEM((STEP * cluster, width), jnp.bfloat16),
            pltpu.VMEM((STEP, cluster, width), jnp.bfloat16),
            pltpu.SemaphoreType.DMA((2, STEP * (pair_count + 4))),
            pltpu.SemaphoreType.DMA((STEP,)),
            pltpu.SemaphoreType.DMA((len(pieces),)),
        ],
        input_output_aliases=aliases,
        cost_estimate=lasting(18),
        compiler_params=kernel_params(),
        name="attend_blocks",
    )(steps, order, table, *operands)


def slot_tables(owner, within, capacity):
    entries = owner.shape[0]
    alike = owner[:, None] == owner[None, :]
    earlier = jnp.arange(entries)[None, :] < jnp.arange(entries)[:, None]
    ranking = jnp.sum(jnp.where(alike & earlier, 1, 0), axis=1).astype(jnp.int32)
    slots = owner * capacity + ranking
    matches = slots[None, :] == jnp.arange(SPAN * capacity, dtype=jnp.int32)[:, None]
    return ranking, jnp.sum(jnp.where(matches, within[None, :], 0), axis=1).astype(jnp.int32)


def by_class(classes, count):
    blocks = jnp.arange(classes.shape[0], dtype=jnp.int32)
    before = (classes[None, :] < classes[:, None]) | (
        (classes[None, :] == classes[:, None]) & (blocks[None, :] < blocks[:, None])
    )
    rank = jnp.sum(jnp.where(before, 1, 0), axis=1)
    order = jnp.sum(jnp.where(rank[None, :] == blocks[:, None], blocks[None, :], 0), axis=1)
    ends = [jnp.sum(jnp.where(classes <= c, 1, 0)).astype(jnp.int32) for c in range(count)]
    return order.astype(jnp.int32), ends


OUT = (2, 0, 3, 1)
FROM = (1, 3, 0, 2)
LEVELS = 4


def position_at(z, y):
    return 2 * z + y


def partner(position):
    return position ^ 1


def onward(position):
    return position_at(choose(position // 2, OUT), position % 2)


def source(position):
    return position_at(choose(position // 2, FROM), position % 2)


def opposite(position):
    return position_at(LEVELS - 1 - position // 2, position % 2)


def itself(position):
    return position


def crossed(route):
    return lambda position: partner(route(position))


SECOND_PLAN = ((0, source, itself), (1, source, partner))
MIDDLE_PLAN = ((0, opposite, itself),)
MIDDLE_CROSS_PLAN = ((0, opposite, partner),)
ON_PLAN = ((0, crossed(onward), source),)
NEAR_PLAN = ((0, partner, source), (0, onward, source))


def body(features, assignment, pairs, w_query, w_key, w_value, w_out, w_mix):
    rows_dev, width = features.shape
    block_count, pair_count = pairs.shape
    cluster = rows_dev // block_count
    stride = lax.axis_size("elec") // SPAN
    groups = [[rest + place_ * stride for place_ in range(SPAN)] for rest in range(stride)]
    position = lax.axis_index("elec") // stride
    at_position = position.reshape(1)
    capacity = (block_count * pair_count + SPAN - 1) // SPAN + 1

    def moved(x, moves):
        pairs_of = [(s * stride + r, d * stride + r) for s, d in moves for r in range(stride)]
        return lax.ppermute(x, "elec", pairs_of)

    def across_z(pairs_of_z):
        return [(position_at(s, y), position_at(d, y)) for s, d in pairs_of_z for y in range(2)]

    swap = [(p, p ^ 1) for p in range(SPAN)]
    first_moves = across_z(enumerate(OUT))
    second_moves = across_z(enumerate(FROM))
    middle_moves = across_z([(1, 2), (2, 1)])
    outward_moves = across_z([(2, 3), (1, 0)])

    listed = pairs.reshape(-1)
    owner = listed // block_count // stride
    within = listed % block_count
    ranking, tables = slot_tables(owner, within, capacity)
    wanted = lax.all_to_all(
        jnp.broadcast_to(tables[None], (SPAN, SPAN * capacity)),
        "elec",
        split_axis=0,
        concat_axis=0,
        axis_index_groups=groups,
        tiled=True,
    )

    shape = (block_count // SUB, 1, SUB * cluster)
    block_shape = (block_count, cluster, width)
    placed, normed = place(features, assignment.reshape(shape))
    blocks = normed.reshape(block_shape)
    own_at = 7 * capacity
    passed_at = own_at + block_count
    beside_at = passed_at + block_count
    total = beside_at + block_count

    z, y = position // 2, position % 2
    is_end = (z == 0) | (z == LEVELS - 1)
    z_owner, same = owner // 2, owner % 2 == y
    from_first = z_owner == choose(z, FROM)
    late = z_owner == LEVELS - 1 - z
    piece_of = jnp.where(
        from_first,
        0,
        jnp.where(
            late,
            jnp.where(is_end, jnp.where(same, 3, 4), jnp.where(same, 5, 6)),
            jnp.where(same, 1, 2),
        ),
    )
    whole_at = jnp.where(z_owner == z, jnp.where(same, own_at, beside_at), passed_at)
    whole = (z_owner == z) | (from_first & same)
    table = jnp.where(whole, whole_at + within, piece_of * capacity + ranking)

    arrival = jnp.where(late, jnp.where(same, 1, 2), 0)
    order, ends = by_class(jnp.max(arrival.reshape(block_count, pair_count), axis=1), 2)
    marks = [0, ends[0] // STEP, ends[1] // STEP, block_count // STEP]
    phases = [
        jnp.stack([marks[n], marks[n + 1] - marks[n]]).astype(jnp.int32) for n in range(3)
    ]
    weights = (jnp.concatenate([w_key, w_value], axis=1), w_out, w_mix)

    own = own_part(normed, w_query, w_key, w_value, cluster, (order, table, *phases, weights[0]))
    beside = moved(blocks, swap)
    passed = moved(blocks, first_moves)
    second_pick, cross_pick = pick(
        at_position, wanted, (blocks, beside), SECOND_PLAN, after=own[2:]
    )
    second = moved(second_pick, second_moves)
    second_cross = moved(cross_pick, second_moves)
    (on,) = pick(at_position, wanted, (passed,), ON_PLAN, after=(cross_pick,))
    on = moved(on, swap)
    (middle,) = pick(at_position, wanted, (blocks,), MIDDLE_PLAN, after=(second,))
    middle = moved(middle, middle_moves)
    near, outward = pick(at_position, wanted, (passed,), NEAR_PLAN, after=(on,))
    near = moved(near, swap)
    outward = moved(outward, outward_moves)
    on = moved(on, outward_moves)
    (middle_cross,) = pick(
        at_position, wanted, (beside,), MIDDLE_CROSS_PLAN, after=(second_cross,)
    )
    middle_cross = moved(middle_cross, middle_moves)

    buffer = collect((blocks, passed, beside), (own_at, passed_at, beside_at), total)

    shared = (order, table, own, placed.reshape(blocks.shape), weights)
    arrivals = (
        ((near, 0), (second, 1), (second_cross, 2)),
        ((outward, 3), (middle, 5)),
        ((on, 4), (middle_cross, 6)),
    )
    mixed = None
    for phase, arrived in zip(phases, arrivals, strict=True):
        pieces = [piece for piece, _ in arrived]
        places = tuple(at * capacity for _, at in arrived)
        mixed, buffer = attend(phase, *shared, buffer, pieces, places, mixed)
    return mixed.reshape(rows_dev, width)


def solution(mesh):
    placed = (
        P(("groups", "elec"), None),
        P(("groups", "elec")),
        P(("groups", "elec"), None),
        P(),
        P(),
        P(),
        P(),
        P(),
    )
    return jax.shard_map(
        body, mesh=mesh, in_specs=placed, out_specs=P(("groups", "elec"), None), check_vma=False
    )
```

```python
import functools
import math

import jax
import jax.numpy as jnp
from jax import lax
from jax.experimental import pallas as pl
from jax.experimental.pallas import tpu as pltpu
from jax.sharding import PartitionSpec as P

HEADS = 16
SPAN = 8
SUB = 8
GROUP = 4
STEP = 8
OWN_STEP = 4
SCORES_AHEAD, WEIGHTS_AHEAD = 2, 1
VMEM_BYTES = 48 * 1024 * 1024

NT = (((1,), (1,)), ((), ()))


def lasting(us):
    return pl.CostEstimate(flops=int(us * 1.15e9), bytes_accessed=0, transcendentals=0)


def kernel_params(share=1):
    return pltpu.CompilerParams(vmem_limit_bytes=VMEM_BYTES // share)


def layer_norm(rows):
    mean = jnp.mean(rows, axis=-1, keepdims=True)
    centred = rows - mean
    variance = jnp.mean(centred * centred, axis=-1, keepdims=True)
    return centred * lax.rsqrt(variance + 1e-05)


def head_mask(shape, head_width, cluster):
    row_head = lax.broadcasted_iota(jnp.int32, shape, 0) // head_width % GROUP
    lane_head = lax.broadcasted_iota(jnp.int32, shape, 1) // cluster
    return row_head == lane_head


def place_kernel(features_ref, assignment_ref, placed_ref, normed_ref):
    walkers, _, rows = assignment_ref.shape
    lane = 128
    columns = lax.broadcasted_iota(jnp.int32, (lane, rows), 1)
    for walker in range(walkers):
        features = features_ref[walker * rows : (walker + 1) * rows, :]
        for part in range(rows // lane):
            chosen = assignment_ref[walker, :, part * lane : (part + 1) * lane] & (rows - 1)
            chosen = jnp.broadcast_to(chosen, (lane, lane)).T
            chosen = jnp.concatenate([chosen] * (rows // lane), axis=1)
            one_hot = jnp.where(chosen == columns, 1.0, 0.0).astype(jnp.bfloat16)
            placed = jnp.dot(one_hot, features, preferred_element_type=jnp.float32)
            here = pl.ds(walker * rows + part * lane, lane)
            placed_ref[here, :] = placed.astype(jnp.bfloat16)
            normed_ref[here, :] = layer_norm(placed).astype(jnp.bfloat16)


def place(features, assignment):
    width = features.shape[1]
    walkers, _, rows = assignment.shape
    local = pl.BlockSpec((2 * rows, width), lambda i: (i, 0))
    out = jax.ShapeDtypeStruct(features.shape, jnp.bfloat16)
    return pl.pallas_call(
        place_kernel,
        grid=(walkers // 2,),
        in_specs=[local, pl.BlockSpec((2, 1, rows), lambda i: (i, 0, 0))],
        out_specs=[local] * 2,
        out_shape=[pltpu.HBM(out.shape, out.dtype), out],
        cost_estimate=lasting(6),
        compiler_params=kernel_params(),
        name="place_rows",
    )(features, assignment)


def choose(index, values):
    result = values[-1]
    for at in range(len(values) - 2, -1, -1):
        result = jnp.where(index == at, values[at], result)
    return result


def pick_kernel(position_ref, wanted_ref, *rest, plan, capacity):
    position = position_ref[0]
    for out_ref, (at, reader_of, owner_of) in zip(rest[len(rest) - len(plan) :], plan, strict=True):
        reader, first = reader_of(position), owner_of(position) * capacity

        def one_slot(slot, carry, out_ref=out_ref, at=at, reader=reader, first=first):
            out_ref[slot] = rest[at][wanted_ref[reader, first + slot]]
            return carry

        lax.fori_loop(0, capacity, one_slot, 0)


def pick(position, wanted, sources, plan, after=()):
    capacity = wanted.shape[1] // SPAN
    block = sources[0].shape[1:]
    outs = [jax.ShapeDtypeStruct((capacity,) + block, sources[0].dtype)] * len(plan)
    smem = pl.BlockSpec(memory_space=pltpu.SMEM)
    vmem = pl.BlockSpec(memory_space=pltpu.VMEM)
    return pl.pallas_call(
        functools.partial(pick_kernel, plan=plan, capacity=capacity),
        in_specs=[smem, smem]
        + [vmem] * len(sources)
        + [pl.BlockSpec(memory_space=pl.ANY)] * len(after),
        out_specs=[vmem] * len(outs),
        out_shape=outs,
        cost_estimate=lasting(1.5),
        compiler_params=kernel_params(3),
        name="pick_blocks",
    )(position, wanted, *sources, *after)


def tiles_of(query, first, span):
    one = query[first : first + span]
    two = query[first + span : first + 2 * span]
    zeros = jnp.zeros_like(one)
    return jnp.concatenate(
        [jnp.concatenate([one, zeros], axis=1), jnp.concatenate([zeros, two], axis=1)], axis=0
    )


def own_kernel(normed_ref, query_w_ref, key_w_ref, value_w_ref, *rest, head_width):
    query_ref, own_ref, stats_ref = rest[-3:]
    blocks, width, tile = query_ref.shape
    cluster = tile // GROUP
    span = GROUP * head_width
    mask = head_mask((width, tile), head_width, cluster)
    scale = math.log2(math.e) / head_width**0.5
    ones = jnp.ones((16, cluster), jnp.bfloat16)
    rows = normed_ref[...]
    keys = jnp.dot(rows, key_w_ref[...], preferred_element_type=jnp.float32).astype(jnp.bfloat16)
    queries = []
    for block in range(blocks):
        own = rows[block * cluster : (block + 1) * cluster]
        tiled = jnp.concatenate([own] * GROUP, axis=0)
        query = lax.dot_general(query_w_ref[...], tiled, NT, preferred_element_type=jnp.float32)
        query = jnp.where(mask, query * scale, 0.0).astype(jnp.bfloat16)
        query_ref[block] = query
        queries.append(query)
    for block in range(blocks):
        own = rows[block * cluster : (block + 1) * cluster]
        value = lax.dot_general(value_w_ref[...], own, NT, preferred_element_type=jnp.float32)
        value = value.astype(jnp.bfloat16)
        tops, totals = [], []
        for pair in range(HEADS // GROUP // 2):
            first = pair * 2 * span
            scores = jnp.dot(
                keys[block * cluster : (block + 1) * cluster, first : first + 2 * span],
                tiles_of(queries[block], first, span),
                preferred_element_type=jnp.float32,
            )
            top = jnp.max(scores, axis=0, keepdims=True)
            weights = jnp.exp2(scores - top).astype(jnp.bfloat16)
            for half in range(2):
                at = first + half * span
                here = slice(half * tile, (half + 1) * tile)
                lifted = jnp.concatenate([value[at : at + span], ones], axis=0)
                product = jnp.dot(lifted, weights[:, here], preferred_element_type=jnp.float32)
                total = product[span : span + 1]
                result = jnp.where(mask[:span], product[:span] * (1.0 / total), 0.0)
                own_ref[block, at : at + span, :] = result.astype(jnp.bfloat16)
                tops.append(top[:, here])
                totals.append(total)
        stats_ref[block] = jnp.concatenate(tops + totals, axis=0)


def own_part(normed, w_query, w_key, w_value, cluster, after):
    rows, width = normed.shape
    blocks = rows // cluster
    tile = GROUP * cluster
    tiles = HEADS // GROUP
    whole = pl.BlockSpec((width, width), lambda i: (0, 0))
    square = pl.BlockSpec((OWN_STEP, width, tile), lambda i: (i, 0, 0))
    return pl.pallas_call(
        functools.partial(own_kernel, head_width=width // HEADS),
        grid=(blocks // OWN_STEP,),
        in_specs=[pl.BlockSpec((OWN_STEP * cluster, width), lambda i: (i, 0)), whole, whole, whole]
        + [pl.BlockSpec(memory_space=pl.ANY)] * len(after),
        out_specs=[
            square,
            square,
            pl.BlockSpec((OWN_STEP, 2 * tiles, tile), lambda i: (i, 0, 0)),
        ],
        out_shape=[
            jax.ShapeDtypeStruct((blocks, width, tile), jnp.bfloat16),
            jax.ShapeDtypeStruct((blocks, width, tile), jnp.bfloat16),
            jax.ShapeDtypeStruct((blocks, 2 * tiles, tile), jnp.float32),
        ],
        cost_estimate=lasting(20),
        compiler_params=kernel_params(),
        name="own_blocks",
    )(normed, w_query.T, w_key, w_value.T, *after)


def collect_kernel(*refs, places):
    buffer_ref, sems = refs[-2:]
    copies = copy_pieces(refs[: len(places)], buffer_ref, places, sems)
    for copy in copies:
        copy.start()
    for copy in copies:
        copy.wait()


def parts_of(blocks):
    return 5 if blocks % 5 == 0 else 4


def copy_pieces(piece_refs, buffer_ref, places, sems):
    copies = []
    for n, (piece, at) in enumerate(zip(piece_refs, places, strict=True)):
        parts = parts_of(piece.shape[0])
        per = piece.shape[0] // parts
        for part in range(parts):
            target = buffer_ref.at[pl.ds(at + part * per, per)]
            copies.append(
                pltpu.make_async_copy(piece.at[pl.ds(part * per, per)], target, sems.at[n, part])
            )
    return copies


def collect(pieces, places, total):
    return pl.pallas_call(
        functools.partial(collect_kernel, places=places),
        in_specs=[pl.BlockSpec(memory_space=pltpu.VMEM)] * len(pieces),
        out_specs=pl.BlockSpec(memory_space=pl.ANY),
        out_shape=pltpu.HBM((total,) + pieces[0].shape[1:], pieces[0].dtype),
        scratch_shapes=[pltpu.SemaphoreType.DMA((len(pieces), 5))],
        cost_estimate=lasting(4),
        compiler_params=kernel_params(3),
        name="collect_blocks",
    )(*pieces)


def attend_kernel(
    range_ref,
    order_ref,
    table_ref,
    query_ref,
    own_ref,
    stats_ref,
    placed_ref,
    *rest,
    head_width,
    places,
):
    weight_refs, rest = rest[:3], rest[3:]
    piece_refs = rest[: len(places)]
    mixed_ref, buffer_ref, query_buf, own_buf, stats_buf, member_buf, placed_buf = rest[-13:-6]
    attended_buf, before_buf, done_buf, in_sems, out_sems, piece_sems = rest[-6:]
    begin, count = range_ref[0], range_ref[1]
    pair_count = member_buf.shape[2]
    copies = copy_pieces(piece_refs, buffer_ref, places, piece_sems)
    for copy in copies:
        copy.start()

    def fetches(step, slot, known=True, listed=True):
        for j in range(STEP):
            block = order_ref[step * STEP + j]
            sources = [
                (query_ref.at[block], query_buf.at[slot, j]),
                (own_ref.at[block], own_buf.at[slot, j]),
                (stats_ref.at[block], stats_buf.at[slot, j]),
                (placed_ref.at[block], placed_buf.at[slot, j]),
            ]
            for n in range(pair_count):
                member = table_ref[block * pair_count + n]
                sources.append((buffer_ref.at[member], member_buf.at[slot, j, n]))
            for n, (source_, target) in enumerate(sources):
                if listed if n >= 4 else known:
                    sem = in_sems.at[slot, j * (pair_count + 4) + n]
                    yield pltpu.make_async_copy(source_, target, sem)

    def stores(step):
        for j in range(STEP):
            target = mixed_ref.at[order_ref[step * STEP + j]]
            yield pltpu.make_async_copy(done_buf.at[j], target, out_sems.at[j])

    def finish():
        return finish_step(before_buf[...], attended_buf[...], *weight_refs[1:])

    def one_step(i, carry):
        slot = i % 2
        for copy in fetches(begin + jnp.minimum(i + 1, count - 1), 1 - slot):
            copy.start()
        for copy in fetches(begin + i, slot):
            copy.wait()
        attended, mixed = attend_step(
            query_buf.at[slot],
            own_buf.at[slot],
            stats_buf.at[slot],
            member_buf.at[slot],
            weight_refs[0],
            head_width,
            finish,
        )

        @pl.when(i > 1)
        def _():
            for copy in stores(begin + i - 2):
                copy.wait()

        done_buf[...] = mixed.reshape(done_buf.shape)
        attended_buf[...] = attended
        before_buf[...] = placed_buf[slot].reshape(before_buf.shape)

        @pl.when(i > 0)
        def _():
            for copy in stores(begin + i - 1):
                copy.start()

        return carry

    @pl.when(count > 0)
    def _():
        for copy in fetches(begin, 0, listed=False):
            copy.start()

    for copy in copies:
        copy.wait()

    @pl.when(count > 0)
    def _():
        for copy in fetches(begin, 0, known=False):
            copy.start()
        attended_buf[...] = jnp.zeros_like(attended_buf)
        before_buf[...] = jnp.zeros_like(before_buf)
        lax.fori_loop(0, count, one_step, 0)
        for copy in fetches(begin + count - 1, count % 2):
            copy.wait()
        mixed = finish()

        @pl.when(count > 1)
        def _():
            for copy in stores(begin + count - 2):
                copy.wait()

        done_buf[...] = mixed.reshape(done_buf.shape)
        for copy in stores(begin + count - 1):
            copy.start()
        for copy in stores(begin + count - 1):
            copy.wait()


def finish_step(placed, attended, out_w_ref, mix_ref):
    middle = placed.astype(jnp.float32) + jnp.dot(
        attended, out_w_ref[...], preferred_element_type=jnp.float32
    )
    middle = middle.astype(jnp.bfloat16).astype(jnp.float32)
    second = layer_norm(middle).astype(jnp.bfloat16)
    mixed = middle + jnp.tanh(jnp.dot(second, mix_ref[...], preferred_element_type=jnp.float32))
    return mixed.astype(jnp.bfloat16)


def attend_step(
    query_ref, own_ref, stats_ref, member_ref, pair_w_ref, head_width, meanwhile
):
    _, members_count, cluster, width = member_ref.shape
    span = GROUP * head_width
    tile = GROUP * cluster
    diagonal = head_mask((span, tile), head_width, cluster)
    ones = jnp.ones((16, members_count * cluster), jnp.bfloat16)
    tiles = HEADS // GROUP
    units = [(block, pair) for block in range(STEP) for pair in range(HEADS // GROUP // 2)]
    listed = member_ref[...].reshape(STEP * members_count * cluster, width)
    both = jnp.dot(listed, pair_w_ref[...], preferred_element_type=jnp.float32)
    both = both.astype(jnp.bfloat16).reshape(STEP, members_count * cluster, 2 * width)
    finished = meanwhile()
    values = [both[block, :, width:].T for block in range(STEP)]

    def scores_of(block, pair):
        first = pair * 2 * span
        return jnp.dot(
            both[block, :, first : first + 2 * span],
            tiles_of(query_ref[block], first, span),
            preferred_element_type=jnp.float32,
        )

    def weights_of(block, pair, scores):
        own_top = jnp.concatenate(
            [stats_ref[block, t : t + 1, :] for t in (2 * pair, 2 * pair + 1)], axis=1
        )
        top = jnp.maximum(jnp.max(scores, axis=0, keepdims=True), own_top)
        weights = jnp.exp2((scores - top).astype(jnp.bfloat16))
        return weights, jnp.exp2(own_top - top)

    def products_of(block, pair, weights, own_factor):
        for half in range(2):
            t = pair * 2 + half
            here = slice(half * tile, (half + 1) * tile)
            lifted = jnp.concatenate([values[block][t * span : (t + 1) * span], ones], axis=0)
            product = jnp.dot(lifted, weights[:, here], preferred_element_type=jnp.float32)
            yield block, t, product, own_factor[:, here]

    def scaled(block, t, product, own_factor):
        own_total = stats_ref[block, tiles + t : tiles + t + 1, :] * own_factor
        inverse = 1.0 / (product[span : span + 1] + own_total)
        own = own_ref[block, t * span : (t + 1) * span, :].astype(jnp.float32)
        result = product[:span] * inverse + own * (own_total * inverse)
        result = jnp.where(diagonal, result, 0.0)
        return result[:, : tile // 2] + result[:, tile // 2 :]

    def rows_of(pieces):
        first, other = (jnp.concatenate(of, axis=0) for of in pieces)
        left = lax.broadcasted_iota(jnp.int32, first.shape, 1) < cluster
        first = first + pltpu.roll(first, cluster, 1)
        other = other + pltpu.roll(other, cluster, 1)
        return jnp.where(left, first, other).T.astype(jnp.bfloat16)

    count = len(units)
    scores, weights, products, pieces, attended = {}, {}, {}, [], []
    for at in range(-SCORES_AHEAD, count + 1):
        if at + SCORES_AHEAD < count:
            scores[at + SCORES_AHEAD] = scores_of(*units[at + SCORES_AHEAD])
        if 0 <= at + WEIGHTS_AHEAD < count:
            ahead = at + WEIGHTS_AHEAD
            weights[ahead] = weights_of(*units[ahead], scores.pop(ahead))
        if 0 <= at < count:
            products[at] = list(products_of(*units[at], *weights.pop(at)))
        if at > 0:
            pieces += [scaled(*product) for product in products.pop(at - 1)]
            if len(pieces) == 2 * tiles:
                attended.append(rows_of((pieces[:tiles], pieces[tiles:])))
                pieces = []
    return jnp.concatenate(attended, axis=0), finished


def attend(steps, order, table, own, placed, weights, buffer, pieces, places, so_far):
    blocks, cluster, width = placed.shape
    pair_count = table.shape[0] // blocks
    smem = pl.BlockSpec(memory_space=pltpu.SMEM)
    vmem = pl.BlockSpec(memory_space=pltpu.VMEM)
    hbm = pl.BlockSpec(memory_space=pl.ANY)
    in_specs = [smem] * 3 + [hbm] * len(own) + [pl.BlockSpec(memory_space=pltpu.HBM)] + [vmem] * (3 + len(pieces)) + [hbm]
    aliases = {len(in_specs) - 1: 1}
    operands = [*own, placed, *weights, *pieces, buffer]
    if so_far is not None:
        aliases[len(in_specs)] = 0
        in_specs.append(hbm)
        operands.append(so_far)
    kernel = functools.partial(
        attend_kernel, head_width=width // HEADS, places=places
    )
    return pl.pallas_call(
        kernel,
        in_specs=in_specs,
        out_specs=[hbm, hbm],
        out_shape=[
            jax.ShapeDtypeStruct(placed.shape, jnp.bfloat16),
            jax.ShapeDtypeStruct(buffer.shape, jnp.bfloat16),
        ],
        scratch_shapes=[
            *[pltpu.VMEM((2, STEP) + x.shape[1:], x.dtype) for x in own],
            pltpu.VMEM((2, STEP, pair_count, cluster, width), jnp.bfloat16),
            pltpu.VMEM((2, STEP, cluster, width), jnp.bfloat16),
            pltpu.VMEM((STEP * cluster, width), jnp.bfloat16),
            pltpu.VMEM((STEP * cluster, width), jnp.bfloat16),
            pltpu.VMEM((STEP, cluster, width), jnp.bfloat16),
            pltpu.SemaphoreType.DMA((2, STEP * (pair_count + 4))),
            pltpu.SemaphoreType.DMA((STEP,)),
            pltpu.SemaphoreType.DMA((len(pieces), 5)),
        ],
        input_output_aliases=aliases,
        cost_estimate=lasting(18),
        compiler_params=kernel_params(),
        name="attend_blocks",
    )(steps, order, table, *operands)


def slot_tables(owner, within, capacity):
    entries = owner.shape[0]
    alike = owner[:, None] == owner[None, :]
    earlier = jnp.arange(entries)[None, :] < jnp.arange(entries)[:, None]
    ranking = jnp.sum(jnp.where(alike & earlier, 1, 0), axis=1).astype(jnp.int32)
    slots = owner * capacity + ranking
    matches = slots[None, :] == jnp.arange(SPAN * capacity, dtype=jnp.int32)[:, None]
    return ranking, jnp.sum(jnp.where(matches, within[None, :], 0), axis=1).astype(jnp.int32)


def by_class(classes, count):
    blocks = jnp.arange(classes.shape[0], dtype=jnp.int32)
    before = (classes[None, :] < classes[:, None]) | (
        (classes[None, :] == classes[:, None]) & (blocks[None, :] < blocks[:, None])
    )
    rank = jnp.sum(jnp.where(before, 1, 0), axis=1)
    order = jnp.sum(jnp.where(rank[None, :] == blocks[:, None], blocks[None, :], 0), axis=1)
    ends = [jnp.sum(jnp.where(classes <= c, 1, 0)).astype(jnp.int32) for c in range(count)]
    return order.astype(jnp.int32), ends


OUT = (2, 0, 3, 1)
FROM = (1, 3, 0, 2)
LEVELS = 4


def position_at(z, y):
    return 2 * z + y


def partner(position):
    return position ^ 1


def onward(position):
    return position_at(choose(position // 2, OUT), position % 2)


def source(position):
    return position_at(choose(position // 2, FROM), position % 2)


def opposite(position):
    return position_at(LEVELS - 1 - position // 2, position % 2)


def itself(position):
    return position


def crossed(route):
    return lambda position: partner(route(position))


SECOND_PLAN = ((0, source, itself), (1, source, partner))
MIDDLE_PLAN = ((0, opposite, itself),)
MIDDLE_CROSS_PLAN = ((0, opposite, partner),)
ON_PLAN = ((0, crossed(onward), source),)
NEAR_PLAN = ((0, partner, source), (0, onward, source))


def body(features, assignment, pairs, w_query, w_key, w_value, w_out, w_mix):
    rows_dev, width = features.shape
    block_count, pair_count = pairs.shape
    cluster = rows_dev // block_count
    stride = lax.axis_size("elec") // SPAN
    groups = [[rest + place_ * stride for place_ in range(SPAN)] for rest in range(stride)]
    position = lax.axis_index("elec") // stride
    at_position = position.reshape(1)
    capacity = (block_count * pair_count + SPAN - 1) // SPAN + 1

    def moved(x, moves):
        pairs_of = [(s * stride + r, d * stride + r) for s, d in moves for r in range(stride)]
        return lax.ppermute(x, "elec", pairs_of)

    def across_z(pairs_of_z):
        return [(position_at(s, y), position_at(d, y)) for s, d in pairs_of_z for y in range(2)]

    swap = [(p, p ^ 1) for p in range(SPAN)]
    first_moves = across_z(enumerate(OUT))
    second_moves = across_z(enumerate(FROM))
    middle_moves = across_z([(1, 2), (2, 1)])
    outward_moves = across_z([(2, 3), (1, 0)])

    listed = pairs.reshape(-1)
    owner = listed // block_count // stride
    within = listed % block_count
    ranking, tables = slot_tables(owner, within, capacity)
    wanted = lax.all_to_all(
        jnp.broadcast_to(tables[None], (SPAN, SPAN * capacity)),
        "elec",
        split_axis=0,
        concat_axis=0,
        axis_index_groups=groups,
        tiled=True,
    )

    shape = (block_count // SUB, 1, SUB * cluster)
    block_shape = (block_count, cluster, width)
    placed, normed = place(features, assignment.reshape(shape))
    blocks = normed.reshape(block_shape)
    own_at = 7 * capacity
    passed_at = own_at + block_count
    beside_at = passed_at + block_count
    total = beside_at + block_count

    z, y = position // 2, position % 2
    is_end = (z == 0) | (z == LEVELS - 1)
    z_owner, same = owner // 2, owner % 2 == y
    from_first = z_owner == choose(z, FROM)
    late = z_owner == LEVELS - 1 - z
    piece_of = jnp.where(
        from_first,
        0,
        jnp.where(
            late,
            jnp.where(is_end, jnp.where(same, 3, 4), jnp.where(same, 5, 6)),
            jnp.where(same, 1, 2),
        ),
    )
    whole_at = jnp.where(z_owner == z, jnp.where(same, own_at, beside_at), passed_at)
    whole = (z_owner == z) | (from_first & same)
    table = jnp.where(whole, whole_at + within, piece_of * capacity + ranking)

    arrival = jnp.where(late, jnp.where(same, 1, 2), 0)
    order, ends = by_class(jnp.max(arrival.reshape(block_count, pair_count), axis=1), 2)
    marks = [0, ends[0] // STEP, ends[1] // STEP, block_count // STEP]
    phases = [
        jnp.stack([marks[n], marks[n + 1] - marks[n]]).astype(jnp.int32) for n in range(3)
    ]
    weights = (jnp.concatenate([w_key, w_value], axis=1), w_out, w_mix)

    own = own_part(normed, w_query, w_key, w_value, cluster, (order, table, *phases, weights[0]))
    beside = moved(blocks, swap)
    passed = moved(blocks, first_moves)
    second_pick, cross_pick = pick(
        at_position, wanted, (blocks, beside), SECOND_PLAN, after=own[2:]
    )
    second = moved(second_pick, second_moves)
    second_cross = moved(cross_pick, second_moves)
    (on,) = pick(at_position, wanted, (passed,), ON_PLAN, after=(cross_pick,))
    on = moved(on, swap)
    (middle,) = pick(at_position, wanted, (blocks,), MIDDLE_PLAN, after=(second,))
    middle = moved(middle, middle_moves)
    near, outward = pick(at_position, wanted, (passed,), NEAR_PLAN, after=(on,))
    near = moved(near, swap)
    outward = moved(outward, outward_moves)
    on = moved(on, outward_moves)
    (middle_cross,) = pick(
        at_position, wanted, (beside,), MIDDLE_CROSS_PLAN, after=(second_cross,)
    )
    middle_cross = moved(middle_cross, middle_moves)

    buffer = collect((blocks, passed, beside), (own_at, passed_at, beside_at), total)

    placed = pltpu.with_memory_space_constraint(placed.reshape(blocks.shape), pltpu.HBM)
    shared = (order, table, own, placed, weights)
    arrivals = (
        ((near, 0), (second, 1), (second_cross, 2)),
        ((outward, 3), (middle, 5)),
        ((on, 4), (middle_cross, 6)),
    )
    mixed = None
    for phase, arrived in zip(phases, arrivals, strict=True):
        pieces = [piece for piece, _ in arrived]
        places = tuple(at * capacity for _, at in arrived)
        mixed, buffer = attend(phase, *shared, buffer, pieces, places, mixed)
    return mixed.reshape(rows_dev, width)


def solution(mesh):
    placed = (
        P(("groups", "elec"), None),
        P(("groups", "elec")),
        P(("groups", "elec"), None),
        P(),
        P(),
        P(),
        P(),
        P(),
    )
    return jax.shard_map(
        body, mesh=mesh, in_specs=placed, out_specs=P(("groups", "elec"), None), check_vma=False
    )
```

```python
import functools
import math

import jax
import jax.numpy as jnp
from jax import lax
from jax.experimental import pallas as pl
from jax.experimental.pallas import tpu as pltpu
from jax.sharding import PartitionSpec as P

HEADS = 16
SPAN = 8
SUB = 8
GROUP = 4
STEP = 8
OWN_STEP = 4
SCORES_AHEAD, WEIGHTS_AHEAD = 2, 1
VMEM_BYTES = 48 * 1024 * 1024

NT = (((1,), (1,)), ((), ()))


def lasting(us):
    return pl.CostEstimate(flops=int(us * 1.15e9), bytes_accessed=0, transcendentals=0)


def kernel_params(share=1):
    return pltpu.CompilerParams(vmem_limit_bytes=VMEM_BYTES // share)


def layer_norm(rows):
    mean = jnp.mean(rows, axis=-1, keepdims=True)
    centred = rows - mean
    variance = jnp.mean(centred * centred, axis=-1, keepdims=True)
    return centred * lax.rsqrt(variance + 1e-05)


def head_mask(shape, head_width, cluster):
    row_head = lax.broadcasted_iota(jnp.int32, shape, 0) // head_width % GROUP
    lane_head = lax.broadcasted_iota(jnp.int32, shape, 1) // cluster
    return row_head == lane_head


def place_kernel(features_ref, assignment_ref, placed_ref, normed_ref):
    walkers, _, rows = assignment_ref.shape
    lane = 128
    columns = lax.broadcasted_iota(jnp.int32, (lane, rows), 1)
    for walker in range(walkers):
        here = pl.ds(walker * rows, rows)
        one_hots = []
        for part in range(rows // lane):
            chosen = assignment_ref[walker, :, part * lane : (part + 1) * lane] & (rows - 1)
            chosen = jnp.broadcast_to(chosen, (lane, lane)).T
            chosen = jnp.concatenate([chosen] * (rows // lane), axis=1)
            one_hots.append(jnp.where(chosen == columns, 1.0, 0.0).astype(jnp.bfloat16))
        one_hot = jnp.concatenate(one_hots, axis=0)
        placed = jnp.dot(one_hot, features_ref[here, :], preferred_element_type=jnp.float32)
        placed_ref[here, :] = placed.astype(jnp.bfloat16)
        normed_ref[here, :] = layer_norm(placed).astype(jnp.bfloat16)


def place(features, assignment):
    width = features.shape[1]
    walkers, _, rows = assignment.shape
    local = pl.BlockSpec((2 * rows, width), lambda i: (i, 0))
    out = jax.ShapeDtypeStruct(features.shape, jnp.bfloat16)
    return pl.pallas_call(
        place_kernel,
        grid=(walkers // 2,),
        in_specs=[local, pl.BlockSpec((2, 1, rows), lambda i: (i, 0, 0))],
        out_specs=[local] * 2,
        out_shape=[pltpu.HBM(out.shape, out.dtype), out],
        cost_estimate=lasting(6),
        compiler_params=kernel_params(),
        name="place_rows",
    )(features, assignment)


def choose(index, values):
    result = values[-1]
    for at in range(len(values) - 2, -1, -1):
        result = jnp.where(index == at, values[at], result)
    return result


def pick_kernel(position_ref, wanted_ref, *rest, plan, capacity):
    position = position_ref[0]
    for out_ref, (at, reader_of, owner_of) in zip(rest[len(rest) - len(plan) :], plan, strict=True):
        reader, first = reader_of(position), owner_of(position) * capacity

        def one_slot(slot, carry, out_ref=out_ref, at=at, reader=reader, first=first):
            out_ref[slot] = rest[at][wanted_ref[reader, first + slot]]
            return carry

        lax.fori_loop(0, capacity, one_slot, 0)


def pick(position, wanted, sources, plan, after=()):
    capacity = wanted.shape[1] // SPAN
    block = sources[0].shape[1:]
    outs = [jax.ShapeDtypeStruct((capacity,) + block, sources[0].dtype)] * len(plan)
    smem = pl.BlockSpec(memory_space=pltpu.SMEM)
    vmem = pl.BlockSpec(memory_space=pltpu.VMEM)
    return pl.pallas_call(
        functools.partial(pick_kernel, plan=plan, capacity=capacity),
        in_specs=[smem, smem]
        + [vmem] * len(sources)
        + [pl.BlockSpec(memory_space=pl.ANY)] * len(after),
        out_specs=[vmem] * len(outs),
        out_shape=outs,
        cost_estimate=lasting(1.5),
        compiler_params=kernel_params(3),
        name="pick_blocks",
    )(position, wanted, *sources, *after)


def tiles_of(query, first, span):
    one = query[first : first + span]
    two = query[first + span : first + 2 * span]
    zeros = jnp.zeros_like(one)
    return jnp.concatenate(
        [jnp.concatenate([one, zeros], axis=1), jnp.concatenate([zeros, two], axis=1)], axis=0
    )


def own_kernel(normed_ref, query_w_ref, key_w_ref, value_w_ref, *rest, head_width):
    query_ref, own_ref, stats_ref = rest[-3:]
    blocks, width, tile = query_ref.shape
    cluster = tile // GROUP
    span = GROUP * head_width
    mask = head_mask((width, tile), head_width, cluster)
    scale = math.log2(math.e) / head_width**0.5
    ones = jnp.ones((16, cluster), jnp.bfloat16)
    rows = normed_ref[...]
    keys = jnp.dot(rows, key_w_ref[...], preferred_element_type=jnp.float32).astype(jnp.bfloat16)
    queries = []
    for block in range(blocks):
        own = rows[block * cluster : (block + 1) * cluster]
        tiled = jnp.concatenate([own] * GROUP, axis=0)
        query = lax.dot_general(query_w_ref[...], tiled, NT, preferred_element_type=jnp.float32)
        query = jnp.where(mask, query * scale, 0.0).astype(jnp.bfloat16)
        query_ref[block] = query
        queries.append(query)
    for block in range(blocks):
        own = rows[block * cluster : (block + 1) * cluster]
        value = lax.dot_general(value_w_ref[...], own, NT, preferred_element_type=jnp.float32)
        value = value.astype(jnp.bfloat16)
        tops, totals = [], []
        for pair in range(HEADS // GROUP // 2):
            first = pair * 2 * span
            scores = jnp.dot(
                keys[block * cluster : (block + 1) * cluster, first : first + 2 * span],
                tiles_of(queries[block], first, span),
                preferred_element_type=jnp.float32,
            )
            top = jnp.max(scores, axis=0, keepdims=True)
            weights = jnp.exp2(scores - top).astype(jnp.bfloat16)
            for half in range(2):
                at = first + half * span
                here = slice(half * tile, (half + 1) * tile)
                lifted = jnp.concatenate([value[at : at + span], ones], axis=0)
                product = jnp.dot(lifted, weights[:, here], preferred_element_type=jnp.float32)
                total = product[span : span + 1]
                result = jnp.where(mask[:span], product[:span] * (1.0 / total), 0.0)
                own_ref[block, at : at + span, :] = result.astype(jnp.bfloat16)
                tops.append(top[:, here])
                totals.append(total)
        stats_ref[block] = jnp.concatenate(tops + totals, axis=0)


def own_part(normed, w_query, w_key, w_value, cluster, after):
    rows, width = normed.shape
    blocks = rows // cluster
    tile = GROUP * cluster
    tiles = HEADS // GROUP
    whole = pl.BlockSpec((width, width), lambda i: (0, 0))
    square = pl.BlockSpec((OWN_STEP, width, tile), lambda i: (i, 0, 0))
    return pl.pallas_call(
        functools.partial(own_kernel, head_width=width // HEADS),
        grid=(blocks // OWN_STEP,),
        in_specs=[pl.BlockSpec((OWN_STEP * cluster, width), lambda i: (i, 0)), whole, whole, whole]
        + [pl.BlockSpec(memory_space=pl.ANY)] * len(after),
        out_specs=[
            square,
            square,
            pl.BlockSpec((OWN_STEP, 2 * tiles, tile), lambda i: (i, 0, 0)),
        ],
        out_shape=[
            jax.ShapeDtypeStruct((blocks, width, tile), jnp.bfloat16),
            jax.ShapeDtypeStruct((blocks, width, tile), jnp.bfloat16),
            jax.ShapeDtypeStruct((blocks, 2 * tiles, tile), jnp.float32),
        ],
        cost_estimate=lasting(20),
        compiler_params=kernel_params(),
        name="own_blocks",
    )(normed, w_query.T, w_key, w_value.T, *after)


def collect_kernel(*refs, places):
    buffer_ref, sems = refs[-2:]
    copies = copy_pieces(refs[: len(places)], buffer_ref, places, sems)
    for copy in copies:
        copy.start()
    for copy in copies:
        copy.wait()


def parts_of(blocks):
    return 5 if blocks % 5 == 0 else 4


def copy_pieces(piece_refs, buffer_ref, places, sems):
    copies = []
    for n, (piece, at) in enumerate(zip(piece_refs, places, strict=True)):
        parts = parts_of(piece.shape[0])
        per = piece.shape[0] // parts
        for part in range(parts):
            target = buffer_ref.at[pl.ds(at + part * per, per)]
            copies.append(
                pltpu.make_async_copy(piece.at[pl.ds(part * per, per)], target, sems.at[n, part])
            )
    return copies


def collect(pieces, places, total):
    return pl.pallas_call(
        functools.partial(collect_kernel, places=places),
        in_specs=[pl.BlockSpec(memory_space=pltpu.VMEM)] * len(pieces),
        out_specs=pl.BlockSpec(memory_space=pl.ANY),
        out_shape=pltpu.HBM((total,) + pieces[0].shape[1:], pieces[0].dtype),
        scratch_shapes=[pltpu.SemaphoreType.DMA((len(pieces), 5))],
        cost_estimate=lasting(4),
        compiler_params=kernel_params(3),
        name="collect_blocks",
    )(*pieces)


def attend_kernel(
    range_ref,
    order_ref,
    table_ref,
    query_ref,
    own_ref,
    stats_ref,
    placed_ref,
    *rest,
    head_width,
    places,
):
    weight_refs, rest = rest[:3], rest[3:]
    piece_refs = rest[: len(places)]
    mixed_ref, buffer_ref, query_buf, own_buf, stats_buf, member_buf, placed_buf = rest[-13:-6]
    attended_buf, before_buf, done_buf, in_sems, out_sems, piece_sems = rest[-6:]
    begin, count = range_ref[0], range_ref[1]
    pair_count = member_buf.shape[2]
    copies = copy_pieces(piece_refs, buffer_ref, places, piece_sems)
    for copy in copies:
        copy.start()

    def fetches(step, slot, known=True, listed=True):
        for j in range(STEP):
            block = order_ref[step * STEP + j]
            sources = [
                (query_ref.at[block], query_buf.at[slot, j]),
                (own_ref.at[block], own_buf.at[slot, j]),
                (stats_ref.at[block], stats_buf.at[slot, j]),
                (placed_ref.at[block], placed_buf.at[slot, j]),
            ]
            for n in range(pair_count):
                member = table_ref[block * pair_count + n]
                sources.append((buffer_ref.at[member], member_buf.at[slot, j, n]))
            for n, (source_, target) in enumerate(sources):
                if listed if n >= 4 else known:
                    sem = in_sems.at[slot, j * (pair_count + 4) + n]
                    yield pltpu.make_async_copy(source_, target, sem)

    def stores(step):
        for j in range(STEP):
            target = mixed_ref.at[order_ref[step * STEP + j]]
            yield pltpu.make_async_copy(done_buf.at[j], target, out_sems.at[j])

    def finish():
        return finish_step(before_buf[...], attended_buf[...], *weight_refs[1:])

    def one_step(i, carry):
        slot = i % 2
        for copy in fetches(begin + jnp.minimum(i + 1, count - 1), 1 - slot):
            copy.start()
        for copy in fetches(begin + i, slot):
            copy.wait()
        attended, mixed = attend_step(
            query_buf.at[slot],
            own_buf.at[slot],
            stats_buf.at[slot],
            member_buf.at[slot],
            weight_refs[0],
            head_width,
            finish,
        )

        @pl.when(i > 1)
        def _():
            for copy in stores(begin + i - 2):
                copy.wait()

        done_buf[...] = mixed.reshape(done_buf.shape)
        attended_buf[...] = attended
        before_buf[...] = placed_buf[slot].reshape(before_buf.shape)

        @pl.when(i > 0)
        def _():
            for copy in stores(begin + i - 1):
                copy.start()

        return carry

    @pl.when(count > 0)
    def _():
        for copy in fetches(begin, 0, listed=False):
            copy.start()

    for copy in copies:
        copy.wait()

    @pl.when(count > 0)
    def _():
        for copy in fetches(begin, 0, known=False):
            copy.start()
        attended_buf[...] = jnp.zeros_like(attended_buf)
        before_buf[...] = jnp.zeros_like(before_buf)
        lax.fori_loop(0, count, one_step, 0)
        for copy in fetches(begin + count - 1, count % 2):
            copy.wait()
        mixed = finish()

        @pl.when(count > 1)
        def _():
            for copy in stores(begin + count - 2):
                copy.wait()

        done_buf[...] = mixed.reshape(done_buf.shape)
        for copy in stores(begin + count - 1):
            copy.start()
        for copy in stores(begin + count - 1):
            copy.wait()


def finish_step(placed, attended, out_w_ref, mix_ref):
    middle = placed.astype(jnp.float32) + jnp.dot(
        attended, out_w_ref[...], preferred_element_type=jnp.float32
    )
    middle = middle.astype(jnp.bfloat16).astype(jnp.float32)
    second = layer_norm(middle).astype(jnp.bfloat16)
    mixed = middle + jnp.tanh(jnp.dot(second, mix_ref[...], preferred_element_type=jnp.float32))
    return mixed.astype(jnp.bfloat16)


def attend_step(
    query_ref, own_ref, stats_ref, member_ref, pair_w_ref, head_width, meanwhile
):
    _, members_count, cluster, width = member_ref.shape
    span = GROUP * head_width
    tile = GROUP * cluster
    diagonal = head_mask((span, tile), head_width, cluster)
    ones = jnp.ones((16, members_count * cluster), jnp.bfloat16)
    tiles = HEADS // GROUP
    units = [(block, pair) for block in range(STEP) for pair in range(HEADS // GROUP // 2)]
    listed = member_ref[...].reshape(STEP * members_count * cluster, width)
    both = jnp.dot(listed, pair_w_ref[...], preferred_element_type=jnp.float32)
    both = both.astype(jnp.bfloat16).reshape(STEP, members_count * cluster, 2 * width)
    finished = meanwhile()
    values = [both[block, :, width:].T for block in range(STEP)]

    def scores_of(block, pair):
        return [
            jnp.dot(
                both[block, :, t * span : (t + 1) * span],
                query_ref[block, t * span : (t + 1) * span, :],
                preferred_element_type=jnp.float32,
            )
            for t in (2 * pair, 2 * pair + 1)
        ]

    def weights_of(block, pair, scores):
        weights, factors = [], []
        for t, score in zip((2 * pair, 2 * pair + 1), scores, strict=True):
            own_top = stats_ref[block, t : t + 1, :]
            top = jnp.maximum(jnp.max(score, axis=0, keepdims=True), own_top)
            weights.append(jnp.exp2((score - top).astype(jnp.bfloat16)))
            factors.append(jnp.exp2(own_top - top))
        return weights, factors

    def products_of(block, pair, weights, own_factor):
        for half in range(2):
            t = pair * 2 + half
            lifted = jnp.concatenate([values[block][t * span : (t + 1) * span], ones], axis=0)
            product = jnp.dot(lifted, weights[half], preferred_element_type=jnp.float32)
            yield block, t, product, own_factor[half]

    def scaled(block, t, product, own_factor):
        own_total = stats_ref[block, tiles + t : tiles + t + 1, :] * own_factor
        inverse = 1.0 / (product[span : span + 1] + own_total)
        own = own_ref[block, t * span : (t + 1) * span, :].astype(jnp.float32)
        result = product[:span] * inverse + own * (own_total * inverse)
        result = jnp.where(diagonal, result, 0.0)
        return result[:, : tile // 2] + result[:, tile // 2 :]

    def rows_of(pieces):
        first, other = (jnp.concatenate(of, axis=0) for of in pieces)
        left = lax.broadcasted_iota(jnp.int32, first.shape, 1) < cluster
        first = first + pltpu.roll(first, cluster, 1)
        other = other + pltpu.roll(other, cluster, 1)
        return jnp.where(left, first, other).T.astype(jnp.bfloat16)

    count = len(units)
    scores, weights, products, pieces, attended = {}, {}, {}, [], []
    for at in range(-SCORES_AHEAD, count + 1):
        if at + SCORES_AHEAD < count:
            scores[at + SCORES_AHEAD] = scores_of(*units[at + SCORES_AHEAD])
        if 0 <= at + WEIGHTS_AHEAD < count:
            ahead = at + WEIGHTS_AHEAD
            weights[ahead] = weights_of(*units[ahead], scores.pop(ahead))
        if 0 <= at < count:
            products[at] = list(products_of(*units[at], *weights.pop(at)))
        if at > 0:
            pieces += [scaled(*product) for product in products.pop(at - 1)]
            if len(pieces) == 2 * tiles:
                attended.append(rows_of((pieces[:tiles], pieces[tiles:])))
                pieces = []
    return jnp.concatenate(attended, axis=0), finished


def attend(steps, order, table, own, placed, weights, buffer, pieces, places, so_far):
    blocks, cluster, width = placed.shape
    pair_count = table.shape[0] // blocks
    smem = pl.BlockSpec(memory_space=pltpu.SMEM)
    vmem = pl.BlockSpec(memory_space=pltpu.VMEM)
    hbm = pl.BlockSpec(memory_space=pl.ANY)
    in_specs = [smem] * 3 + [hbm] * len(own) + [pl.BlockSpec(memory_space=pltpu.HBM)] + [vmem] * (3 + len(pieces)) + [hbm]
    aliases = {len(in_specs) - 1: 1}
    operands = [*own, placed, *weights, *pieces, buffer]
    if so_far is not None:
        aliases[len(in_specs)] = 0
        in_specs.append(hbm)
        operands.append(so_far)
    kernel = functools.partial(
        attend_kernel, head_width=width // HEADS, places=places
    )
    return pl.pallas_call(
        kernel,
        in_specs=in_specs,
        out_specs=[hbm, hbm],
        out_shape=[
            jax.ShapeDtypeStruct(placed.shape, jnp.bfloat16),
            jax.ShapeDtypeStruct(buffer.shape, jnp.bfloat16),
        ],
        scratch_shapes=[
            *[pltpu.VMEM((2, STEP) + x.shape[1:], x.dtype) for x in own],
            pltpu.VMEM((2, STEP, pair_count, cluster, width), jnp.bfloat16),
            pltpu.VMEM((2, STEP, cluster, width), jnp.bfloat16),
            pltpu.VMEM((STEP * cluster, width), jnp.bfloat16),
            pltpu.VMEM((STEP * cluster, width), jnp.bfloat16),
            pltpu.VMEM((STEP, cluster, width), jnp.bfloat16),
            pltpu.SemaphoreType.DMA((2, STEP * (pair_count + 4))),
            pltpu.SemaphoreType.DMA((STEP,)),
            pltpu.SemaphoreType.DMA((len(pieces), 5)),
        ],
        input_output_aliases=aliases,
        cost_estimate=lasting(18),
        compiler_params=kernel_params(),
        name="attend_blocks",
    )(steps, order, table, *operands)


def slot_tables(owner, within, capacity):
    entries = owner.shape[0]
    alike = owner[:, None] == owner[None, :]
    earlier = jnp.arange(entries)[None, :] < jnp.arange(entries)[:, None]
    ranking = jnp.sum(jnp.where(alike & earlier, 1, 0), axis=1).astype(jnp.int32)
    slots = owner * capacity + ranking
    matches = slots[None, :] == jnp.arange(SPAN * capacity, dtype=jnp.int32)[:, None]
    return ranking, jnp.sum(jnp.where(matches, within[None, :], 0), axis=1).astype(jnp.int32)


def by_class(classes, count):
    blocks = jnp.arange(classes.shape[0], dtype=jnp.int32)
    before = (classes[None, :] < classes[:, None]) | (
        (classes[None, :] == classes[:, None]) & (blocks[None, :] < blocks[:, None])
    )
    rank = jnp.sum(jnp.where(before, 1, 0), axis=1)
    order = jnp.sum(jnp.where(rank[None, :] == blocks[:, None], blocks[None, :], 0), axis=1)
    ends = [jnp.sum(jnp.where(classes <= c, 1, 0)).astype(jnp.int32) for c in range(count)]
    return order.astype(jnp.int32), ends


OUT = (2, 0, 3, 1)
FROM = (1, 3, 0, 2)
LEVELS = 4


def position_at(z, y):
    return 2 * z + y


def partner(position):
    return position ^ 1


def onward(position):
    return position_at(choose(position // 2, OUT), position % 2)


def source(position):
    return position_at(choose(position // 2, FROM), position % 2)


def opposite(position):
    return position_at(LEVELS - 1 - position // 2, position % 2)


def itself(position):
    return position


def crossed(route):
    return lambda position: partner(route(position))


FIRST_PLAN = ((0, source, itself), (1, source, partner), (2, crossed(onward), source))
MIDDLE_PLAN = ((0, opposite, itself),)
MIDDLE_CROSS_PLAN = ((0, opposite, partner),)
NEAR_PLAN = ((0, partner, source), (0, onward, source))


def body(features, assignment, pairs, w_query, w_key, w_value, w_out, w_mix):
    rows_dev, width = features.shape
    block_count, pair_count = pairs.shape
    cluster = rows_dev // block_count
    stride = lax.axis_size("elec") // SPAN
    groups = [[rest + place_ * stride for place_ in range(SPAN)] for rest in range(stride)]
    position = lax.axis_index("elec") // stride
    at_position = position.reshape(1)
    capacity = (block_count * pair_count + SPAN - 1) // SPAN + 1

    def moved(x, moves):
        pairs_of = [(s * stride + r, d * stride + r) for s, d in moves for r in range(stride)]
        return lax.ppermute(x, "elec", pairs_of)

    def across_z(pairs_of_z):
        return [(position_at(s, y), position_at(d, y)) for s, d in pairs_of_z for y in range(2)]

    swap = [(p, p ^ 1) for p in range(SPAN)]
    first_moves = across_z(enumerate(OUT))
    second_moves = across_z(enumerate(FROM))
    middle_moves = across_z([(1, 2), (2, 1)])
    outward_moves = across_z([(2, 3), (1, 0)])

    listed = pairs.reshape(-1)
    owner = listed // block_count // stride
    within = listed % block_count
    ranking, tables = slot_tables(owner, within, capacity)
    wanted = lax.all_to_all(
        jnp.broadcast_to(tables[None], (SPAN, SPAN * capacity)),
        "elec",
        split_axis=0,
        concat_axis=0,
        axis_index_groups=groups,
        tiled=True,
    )

    shape = (block_count // SUB, 1, SUB * cluster)
    block_shape = (block_count, cluster, width)
    placed, normed = place(features, assignment.reshape(shape))
    blocks = normed.reshape(block_shape)
    own_at = 7 * capacity
    passed_at = own_at + block_count
    beside_at = passed_at + block_count
    total = beside_at + block_count

    z, y = position // 2, position % 2
    is_end = (z == 0) | (z == LEVELS - 1)
    z_owner, same = owner // 2, owner % 2 == y
    from_first = z_owner == choose(z, FROM)
    late = z_owner == LEVELS - 1 - z
    piece_of = jnp.where(
        from_first,
        0,
        jnp.where(
            late,
            jnp.where(is_end, jnp.where(same, 3, 4), jnp.where(same, 5, 6)),
            jnp.where(same, 1, 2),
        ),
    )
    whole_at = jnp.where(z_owner == z, jnp.where(same, own_at, beside_at), passed_at)
    whole = (z_owner == z) | (from_first & same)
    table = jnp.where(whole, whole_at + within, piece_of * capacity + ranking)

    arrival = jnp.where(late, jnp.where(same, 1, 2), 0)
    order, ends = by_class(jnp.max(arrival.reshape(block_count, pair_count), axis=1), 2)
    marks = [0, ends[0] // STEP, ends[1] // STEP, block_count // STEP]
    phases = [
        jnp.stack([marks[n], marks[n + 1] - marks[n]]).astype(jnp.int32) for n in range(3)
    ]
    weights = (jnp.concatenate([w_key, w_value], axis=1), w_out, w_mix)

    own = own_part(normed, w_query, w_key, w_value, cluster, (order, table, *phases, weights[0]))
    beside = moved(blocks, swap)
    passed = moved(blocks, first_moves)
    second, second_cross, on = pick(
        at_position, wanted, (blocks, beside, passed), FIRST_PLAN, after=own[2:]
    )
    second = moved(second, second_moves)
    second_cross = moved(second_cross, second_moves)
    on = moved(on, swap)
    (middle_pick,) = pick(at_position, wanted, (blocks,), MIDDLE_PLAN, after=(second,))
    middle = moved(middle_pick, middle_moves)
    near, outward = pick(at_position, wanted, (passed,), NEAR_PLAN, after=(on,))
    near = moved(near, swap)
    outward = moved(outward, outward_moves)
    on = moved(on, outward_moves)
    (middle_cross,) = pick(
        at_position, wanted, (beside,), MIDDLE_CROSS_PLAN, after=(second_cross, middle_pick)
    )
    middle_cross = moved(middle_cross, middle_moves)

    buffer = collect((blocks, passed, beside), (own_at, passed_at, beside_at), total)

    placed = pltpu.with_memory_space_constraint(placed.reshape(blocks.shape), pltpu.HBM)
    shared = (order, table, own, placed, weights)
    arrivals = (
        ((near, 0), (second, 1), (second_cross, 2)),
        ((outward, 3), (middle, 5)),
        ((on, 4), (middle_cross, 6)),
    )
    mixed = None
    for phase, arrived in zip(phases, arrivals, strict=True):
        pieces = [piece for piece, _ in arrived]
        places = tuple(at * capacity for _, at in arrived)
        mixed, buffer = attend(phase, *shared, buffer, pieces, places, mixed)
    return mixed.reshape(rows_dev, width)


def solution(mesh):
    placed = (
        P(("groups", "elec"), None),
        P(("groups", "elec")),
        P(("groups", "elec"), None),
        P(),
        P(),
        P(),
        P(),
        P(),
    )
    return jax.shard_map(
        body, mesh=mesh, in_specs=placed, out_specs=P(("groups", "elec"), None), check_vma=False
    )
```

```python
import functools
import math

import jax
import jax.numpy as jnp
from jax import lax
from jax.experimental import pallas as pl
from jax.experimental.pallas import tpu as pltpu
from jax.sharding import PartitionSpec as P

HEADS = 16
SPAN = 8
SUB = 8
GROUP = 4
STEP = 8
OWN_STEP = 4
SCORES_AHEAD, WEIGHTS_AHEAD = 2, 1
VMEM_BYTES = 48 * 1024 * 1024

NT = (((1,), (1,)), ((), ()))


def lasting(us):
    return pl.CostEstimate(flops=int(us * 1.15e9), bytes_accessed=0, transcendentals=0)


def kernel_params(share=1):
    return pltpu.CompilerParams(vmem_limit_bytes=VMEM_BYTES // share)


def layer_norm(rows):
    mean = jnp.mean(rows, axis=-1, keepdims=True)
    centred = rows - mean
    variance = jnp.mean(centred * centred, axis=-1, keepdims=True)
    return centred * lax.rsqrt(variance + 1e-05)


def head_mask(shape, head_width, cluster):
    row_head = lax.broadcasted_iota(jnp.int32, shape, 0) // head_width % GROUP
    lane_head = lax.broadcasted_iota(jnp.int32, shape, 1) // cluster
    return row_head == lane_head


def place_kernel(features_ref, assignment_ref, placed_ref, normed_ref):
    walkers, _, rows = assignment_ref.shape
    lane = 128
    columns = lax.broadcasted_iota(jnp.int32, (lane, rows), 1)
    for walker in range(walkers):
        here = pl.ds(walker * rows, rows)
        one_hots = []
        for part in range(rows // lane):
            chosen = assignment_ref[walker, :, part * lane : (part + 1) * lane] & (rows - 1)
            chosen = jnp.broadcast_to(chosen, (lane, lane)).T
            chosen = jnp.concatenate([chosen] * (rows // lane), axis=1)
            one_hots.append(jnp.where(chosen == columns, 1.0, 0.0).astype(jnp.bfloat16))
        one_hot = jnp.concatenate(one_hots, axis=0)
        placed = jnp.dot(one_hot, features_ref[here, :], preferred_element_type=jnp.float32)
        placed_ref[here, :] = placed.astype(jnp.bfloat16)
        normed_ref[here, :] = layer_norm(placed).astype(jnp.bfloat16)


def place(features, assignment):
    width = features.shape[1]
    walkers, _, rows = assignment.shape
    local = pl.BlockSpec((2 * rows, width), lambda i: (i, 0))
    out = jax.ShapeDtypeStruct(features.shape, jnp.bfloat16)
    return pl.pallas_call(
        place_kernel,
        grid=(walkers // 2,),
        in_specs=[local, pl.BlockSpec((2, 1, rows), lambda i: (i, 0, 0))],
        out_specs=[local] * 2,
        out_shape=[pltpu.HBM(out.shape, out.dtype), out],
        cost_estimate=lasting(6),
        compiler_params=kernel_params(),
        name="place_rows",
    )(features, assignment)


def choose(index, values):
    result = values[-1]
    for at in range(len(values) - 2, -1, -1):
        result = jnp.where(index == at, values[at], result)
    return result


def pick_kernel(position_ref, wanted_ref, *rest, plan, capacity):
    position = position_ref[0]
    for out_ref, (at, reader_of, owner_of) in zip(rest[len(rest) - len(plan) :], plan, strict=True):
        reader, first = reader_of(position), owner_of(position) * capacity

        def one_slot(slot, carry, out_ref=out_ref, at=at, reader=reader, first=first):
            out_ref[slot] = rest[at][wanted_ref[reader, first + slot]]
            return carry

        lax.fori_loop(0, capacity, one_slot, 0)


def pick(position, wanted, sources, plan, after=()):
    capacity = wanted.shape[1] // SPAN
    block = sources[0].shape[1:]
    outs = [jax.ShapeDtypeStruct((capacity,) + block, sources[0].dtype)] * len(plan)
    smem = pl.BlockSpec(memory_space=pltpu.SMEM)
    vmem = pl.BlockSpec(memory_space=pltpu.VMEM)
    return pl.pallas_call(
        functools.partial(pick_kernel, plan=plan, capacity=capacity),
        in_specs=[smem, smem]
        + [vmem] * len(sources)
        + [pl.BlockSpec(memory_space=pl.ANY)] * len(after),
        out_specs=[vmem] * len(outs),
        out_shape=outs,
        cost_estimate=lasting(1.5),
        compiler_params=kernel_params(3),
        name="pick_blocks",
    )(position, wanted, *sources, *after)


def tiles_of(query, first, span):
    one = query[first : first + span]
    two = query[first + span : first + 2 * span]
    zeros = jnp.zeros_like(one)
    return jnp.concatenate(
        [jnp.concatenate([one, zeros], axis=1), jnp.concatenate([zeros, two], axis=1)], axis=0
    )


def own_kernel(normed_ref, query_w_ref, key_w_ref, value_w_ref, *rest, head_width):
    query_ref, own_ref, stats_ref = rest[-3:]
    blocks, width, tile = query_ref.shape
    cluster = tile // GROUP
    span = GROUP * head_width
    mask = head_mask((width, tile), head_width, cluster)
    scale = math.log2(math.e) / head_width**0.5
    ones = jnp.ones((16, cluster), jnp.bfloat16)
    rows = normed_ref[...]
    keys = jnp.dot(rows, key_w_ref[...], preferred_element_type=jnp.float32).astype(jnp.bfloat16)
    queries = []
    for block in range(blocks):
        own = rows[block * cluster : (block + 1) * cluster]
        tiled = jnp.concatenate([own] * GROUP, axis=0)
        query = lax.dot_general(query_w_ref[...], tiled, NT, preferred_element_type=jnp.float32)
        query = jnp.where(mask, query * scale, 0.0).astype(jnp.bfloat16)
        query_ref[block] = query
        queries.append(query)
    for block in range(blocks):
        own = rows[block * cluster : (block + 1) * cluster]
        value = lax.dot_general(value_w_ref[...], own, NT, preferred_element_type=jnp.float32)
        value = value.astype(jnp.bfloat16)
        tops, totals = [], []
        for pair in range(HEADS // GROUP // 2):
            first = pair * 2 * span
            scores = jnp.dot(
                keys[block * cluster : (block + 1) * cluster, first : first + 2 * span],
                tiles_of(queries[block], first, span),
                preferred_element_type=jnp.float32,
            )
            top = jnp.max(scores, axis=0, keepdims=True)
            weights = jnp.exp2(scores - top).astype(jnp.bfloat16)
            for half in range(2):
                at = first + half * span
                here = slice(half * tile, (half + 1) * tile)
                lifted = jnp.concatenate([value[at : at + span], ones], axis=0)
                product = jnp.dot(lifted, weights[:, here], preferred_element_type=jnp.float32)
                total = product[span : span + 1]
                result = jnp.where(mask[:span], product[:span] * (1.0 / total), 0.0)
                own_ref[block, at : at + span, :] = result.astype(jnp.bfloat16)
                tops.append(top[:, here])
                totals.append(total)
        stats_ref[block] = jnp.concatenate(tops + totals, axis=0)


def own_part(normed, w_query, w_key, w_value, cluster, after):
    rows, width = normed.shape
    blocks = rows // cluster
    tile = GROUP * cluster
    tiles = HEADS // GROUP
    whole = pl.BlockSpec((width, width), lambda i: (0, 0))
    square = pl.BlockSpec((OWN_STEP, width, tile), lambda i: (i, 0, 0))
    return pl.pallas_call(
        functools.partial(own_kernel, head_width=width // HEADS),
        grid=(blocks // OWN_STEP,),
        in_specs=[pl.BlockSpec((OWN_STEP * cluster, width), lambda i: (i, 0)), whole, whole, whole]
        + [pl.BlockSpec(memory_space=pl.ANY)] * len(after),
        out_specs=[
            square,
            square,
            pl.BlockSpec((OWN_STEP, 2 * tiles, tile), lambda i: (i, 0, 0)),
        ],
        out_shape=[
            jax.ShapeDtypeStruct((blocks, width, tile), jnp.bfloat16),
            jax.ShapeDtypeStruct((blocks, width, tile), jnp.bfloat16),
            jax.ShapeDtypeStruct((blocks, 2 * tiles, tile), jnp.float32),
        ],
        cost_estimate=lasting(20),
        compiler_params=kernel_params(),
        name="own_blocks",
    )(normed, w_query.T, w_key, w_value.T, *after)


def collect_kernel(*refs, places):
    buffer_ref, sems = refs[-2:]
    copies = copy_pieces(refs[: len(places)], buffer_ref, places, sems)
    for copy in copies:
        copy.start()
    for copy in copies:
        copy.wait()


def parts_of(blocks):
    return 5 if blocks % 5 == 0 else 4


def copy_pieces(piece_refs, buffer_ref, places, sems):
    copies = []
    for n, (piece, at) in enumerate(zip(piece_refs, places, strict=True)):
        parts = parts_of(piece.shape[0])
        per = piece.shape[0] // parts
        for part in range(parts):
            target = buffer_ref.at[pl.ds(at + part * per, per)]
            copies.append(
                pltpu.make_async_copy(piece.at[pl.ds(part * per, per)], target, sems.at[n, part])
            )
    return copies


def collect(pieces, places, total):
    return pl.pallas_call(
        functools.partial(collect_kernel, places=places),
        in_specs=[pl.BlockSpec(memory_space=pltpu.VMEM)] * len(pieces),
        out_specs=pl.BlockSpec(memory_space=pl.ANY),
        out_shape=pltpu.HBM((total,) + pieces[0].shape[1:], pieces[0].dtype),
        scratch_shapes=[pltpu.SemaphoreType.DMA((len(pieces), 5))],
        cost_estimate=lasting(4),
        compiler_params=kernel_params(3),
        name="collect_blocks",
    )(*pieces)


def attend_kernel(
    range_ref,
    order_ref,
    table_ref,
    query_ref,
    own_ref,
    stats_ref,
    placed_ref,
    *rest,
    head_width,
    places,
    first,
    last,
):
    weight_refs, rest = rest[:3], rest[3:]
    piece_refs = rest[: len(places)]
    mixed_ref, buffer_ref, *states = rest[-16:-12]
    query_buf, own_buf, stats_buf, member_buf, placed_buf = rest[-12:-7]
    attended_buf, before_buf, done_buf, in_sems, out_sems, piece_sems, state_sems = rest[-7:]
    begin, count = range_ref[0], range_ref[1]
    pair_count = member_buf.shape[2]
    copies = copy_pieces(piece_refs, buffer_ref, places, piece_sems)
    for copy in copies:
        copy.start()

    def fetches(step, slot, known=True, listed=True):
        for j in range(STEP):
            block = order_ref[step * STEP + j]
            sources = [
                (query_ref.at[block], query_buf.at[slot, j]),
                (own_ref.at[block], own_buf.at[slot, j]),
                (stats_ref.at[block], stats_buf.at[slot, j]),
                (placed_ref.at[block], placed_buf.at[slot, j]),
            ]
            for n in range(pair_count):
                member = table_ref[block * pair_count + n]
                sources.append((buffer_ref.at[member], member_buf.at[slot, j, n]))
            for n, (source_, target) in enumerate(sources):
                if listed if n >= 4 else known:
                    sem = in_sems.at[slot, j * (pair_count + 4) + n]
                    yield pltpu.make_async_copy(source_, target, sem)

    def stores(step):
        for j in range(STEP):
            target = mixed_ref.at[order_ref[step * STEP + j]]
            yield pltpu.make_async_copy(done_buf.at[j], target, out_sems.at[j])

    def finish():
        return finish_step(before_buf[...], attended_buf[...], *weight_refs[1:])

    def one_step(i, carry):
        slot = i % 2
        for copy in fetches(begin + jnp.minimum(i + 1, count - 1), 1 - slot):
            copy.start()
        for copy in fetches(begin + i, slot):
            copy.wait()
        attended, mixed = attend_step(
            query_buf.at[slot],
            own_buf.at[slot],
            stats_buf.at[slot],
            member_buf.at[slot],
            weight_refs[0],
            head_width,
            finish,
        )

        @pl.when((i > 0) & (begin + i > 1))
        def _():
            for copy in stores(begin + i - 2):
                copy.wait()

        done_buf[...] = mixed.reshape(done_buf.shape)
        attended_buf[...] = attended
        before_buf[...] = placed_buf[slot].reshape(before_buf.shape)

        @pl.when(begin + i > 0)
        def _():
            for copy in stores(begin + i - 1):
                copy.start()

        return carry

    held = (attended_buf, before_buf)
    if first:
        for buf in held:
            buf[...] = jnp.zeros_like(buf)
    else:
        loads = [
            pltpu.make_async_copy(state, buf, state_sems.at[n])
            for n, (state, buf) in enumerate(zip(states, held, strict=True))
        ]
        for copy in loads:
            copy.start()

    @pl.when(count > 0)
    def _():
        for copy in fetches(begin, 0, listed=False):
            copy.start()

    for copy in copies:
        copy.wait()

    @pl.when(count > 0)
    def _():
        for copy in fetches(begin, 0, known=False):
            copy.start()

    if not first:
        for copy in loads:
            copy.wait()

    @pl.when(count > 0)
    def _():
        lax.fori_loop(0, count, one_step, 0)
        for copy in fetches(begin + count - 1, count % 2):
            copy.wait()

    @pl.when((count > 0) & (begin + count > 1))
    def _():
        for copy in stores(begin + count - 2):
            copy.wait()

    if last:
        done_buf[...] = finish().reshape(done_buf.shape)
        for copy in stores(begin + count - 1):
            copy.start()
        for copy in stores(begin + count - 1):
            copy.wait()
    else:
        saves = [
            pltpu.make_async_copy(buf, state, state_sems.at[n])
            for n, (state, buf) in enumerate(zip(states, held, strict=True))
        ]
        for copy in saves:
            copy.start()
        for copy in saves:
            copy.wait()


def finish_step(placed, attended, out_w_ref, mix_ref):
    middle = placed.astype(jnp.float32) + jnp.dot(
        attended, out_w_ref[...], preferred_element_type=jnp.float32
    )
    middle = middle.astype(jnp.bfloat16).astype(jnp.float32)
    second = layer_norm(middle).astype(jnp.bfloat16)
    mixed = middle + jnp.tanh(jnp.dot(second, mix_ref[...], preferred_element_type=jnp.float32))
    return mixed.astype(jnp.bfloat16)


def attend_step(
    query_ref, own_ref, stats_ref, member_ref, pair_w_ref, head_width, meanwhile
):
    _, members_count, cluster, width = member_ref.shape
    span = GROUP * head_width
    tile = GROUP * cluster
    diagonal = head_mask((span, tile), head_width, cluster)
    ones = jnp.ones((16, members_count * cluster), jnp.bfloat16)
    tiles = HEADS // GROUP
    units = [(block, pair) for block in range(STEP) for pair in range(HEADS // GROUP // 2)]
    listed = member_ref[...].reshape(STEP * members_count * cluster, width)
    both = jnp.dot(listed, pair_w_ref[...], preferred_element_type=jnp.float32)
    both = both.astype(jnp.bfloat16).reshape(STEP, members_count * cluster, 2 * width)
    finished = meanwhile()
    values = [both[block, :, width:].T for block in range(STEP)]

    def scores_of(block, pair):
        return [
            jnp.dot(
                both[block, :, t * span : (t + 1) * span],
                query_ref[block, t * span : (t + 1) * span, :],
                preferred_element_type=jnp.float32,
            )
            for t in (2 * pair, 2 * pair + 1)
        ]

    def weights_of(block, pair, scores):
        weights, factors = [], []
        for t, score in zip((2 * pair, 2 * pair + 1), scores, strict=True):
            own_top = stats_ref[block, t : t + 1, :]
            top = jnp.maximum(jnp.max(score, axis=0, keepdims=True), own_top)
            weights.append(jnp.exp2((score - top).astype(jnp.bfloat16)))
            factors.append(jnp.exp2(own_top - top))
        return weights, factors

    def products_of(block, pair, weights, own_factor):
        for half in range(2):
            t = pair * 2 + half
            lifted = jnp.concatenate([values[block][t * span : (t + 1) * span], ones], axis=0)
            product = jnp.dot(lifted, weights[half], preferred_element_type=jnp.float32)
            yield block, t, product, own_factor[half]

    def scaled(block, t, product, own_factor):
        own_total = stats_ref[block, tiles + t : tiles + t + 1, :] * own_factor
        inverse = 1.0 / (product[span : span + 1] + own_total)
        own = own_ref[block, t * span : (t + 1) * span, :].astype(jnp.float32)
        result = product[:span] * inverse + own * (own_total * inverse)
        result = jnp.where(diagonal, result, 0.0)
        return result[:, : tile // 2] + result[:, tile // 2 :]

    def rows_of(pieces):
        first, other = (jnp.concatenate(of, axis=0) for of in pieces)
        left = lax.broadcasted_iota(jnp.int32, first.shape, 1) < cluster
        first = first + pltpu.roll(first, cluster, 1)
        other = other + pltpu.roll(other, cluster, 1)
        return jnp.where(left, first, other).T.astype(jnp.bfloat16)

    count = len(units)
    scores, weights, products, pieces, attended = {}, {}, {}, [], []
    for at in range(-SCORES_AHEAD, count + 1):
        if at + SCORES_AHEAD < count:
            scores[at + SCORES_AHEAD] = scores_of(*units[at + SCORES_AHEAD])
        if 0 <= at + WEIGHTS_AHEAD < count:
            ahead = at + WEIGHTS_AHEAD
            weights[ahead] = weights_of(*units[ahead], scores.pop(ahead))
        if 0 <= at < count:
            products[at] = list(products_of(*units[at], *weights.pop(at)))
        if at > 0:
            pieces += [scaled(*product) for product in products.pop(at - 1)]
            if len(pieces) == 2 * tiles:
                attended.append(rows_of((pieces[:tiles], pieces[tiles:])))
                pieces = []
    return jnp.concatenate(attended, axis=0), finished


def attend(steps, order, table, own, placed, weights, buffer, pieces, places, so_far, last):
    blocks, cluster, width = placed.shape
    pair_count = table.shape[0] // blocks
    smem = pl.BlockSpec(memory_space=pltpu.SMEM)
    vmem = pl.BlockSpec(memory_space=pltpu.VMEM)
    hbm = pl.BlockSpec(memory_space=pl.ANY)
    in_specs = [smem] * 3 + [hbm] * len(own) + [pl.BlockSpec(memory_space=pltpu.HBM)] + [vmem] * (3 + len(pieces)) + [hbm]
    aliases = {len(in_specs) - 1: 1}
    operands = [*own, placed, *weights, *pieces, buffer]
    for at, x in zip((0, 2, 3), so_far):
        aliases[len(in_specs)] = at
        in_specs.append(hbm)
        operands.append(x)
    kernel = functools.partial(
        attend_kernel,
        head_width=width // HEADS,
        places=places,
        first=not so_far,
        last=last,
    )
    state = jax.ShapeDtypeStruct((STEP * cluster, width), jnp.bfloat16)
    return pl.pallas_call(
        kernel,
        in_specs=in_specs,
        out_specs=[hbm] * 4,
        out_shape=[
            jax.ShapeDtypeStruct(placed.shape, jnp.bfloat16),
            jax.ShapeDtypeStruct(buffer.shape, jnp.bfloat16),
            state,
            state,
        ],
        scratch_shapes=[
            *[pltpu.VMEM((2, STEP) + x.shape[1:], x.dtype) for x in own],
            pltpu.VMEM((2, STEP, pair_count, cluster, width), jnp.bfloat16),
            pltpu.VMEM((2, STEP, cluster, width), jnp.bfloat16),
            pltpu.VMEM((STEP * cluster, width), jnp.bfloat16),
            pltpu.VMEM((STEP * cluster, width), jnp.bfloat16),
            pltpu.VMEM((STEP, cluster, width), jnp.bfloat16),
            pltpu.SemaphoreType.DMA((2, STEP * (pair_count + 4))),
            pltpu.SemaphoreType.DMA((STEP,)),
            pltpu.SemaphoreType.DMA((len(pieces), 5)),
            pltpu.SemaphoreType.DMA((2,)),
        ],
        input_output_aliases=aliases,
        cost_estimate=lasting(18),
        compiler_params=kernel_params(),
        name="attend_blocks",
    )(steps, order, table, *operands)


def slot_tables(owner, within, capacity):
    entries = owner.shape[0]
    alike = owner[:, None] == owner[None, :]
    earlier = jnp.arange(entries)[None, :] < jnp.arange(entries)[:, None]
    ranking = jnp.sum(jnp.where(alike & earlier, 1, 0), axis=1).astype(jnp.int32)
    slots = owner * capacity + ranking
    matches = slots[None, :] == jnp.arange(SPAN * capacity, dtype=jnp.int32)[:, None]
    return ranking, jnp.sum(jnp.where(matches, within[None, :], 0), axis=1).astype(jnp.int32)


def by_class(classes, count):
    blocks = jnp.arange(classes.shape[0], dtype=jnp.int32)
    before = (classes[None, :] < classes[:, None]) | (
        (classes[None, :] == classes[:, None]) & (blocks[None, :] < blocks[:, None])
    )
    rank = jnp.sum(jnp.where(before, 1, 0), axis=1)
    order = jnp.sum(jnp.where(rank[None, :] == blocks[:, None], blocks[None, :], 0), axis=1)
    ends = [jnp.sum(jnp.where(classes <= c, 1, 0)).astype(jnp.int32) for c in range(count)]
    return order.astype(jnp.int32), ends


OUT = (2, 0, 3, 1)
FROM = (1, 3, 0, 2)
LEVELS = 4


def position_at(z, y):
    return 2 * z + y


def partner(position):
    return position ^ 1


def onward(position):
    return position_at(choose(position // 2, OUT), position % 2)


def source(position):
    return position_at(choose(position // 2, FROM), position % 2)


def opposite(position):
    return position_at(LEVELS - 1 - position // 2, position % 2)


def itself(position):
    return position


def crossed(route):
    return lambda position: partner(route(position))


FIRST_PLAN = ((0, source, itself), (1, source, partner), (2, crossed(onward), source))
MIDDLE_PLAN = ((0, opposite, itself),)
MIDDLE_CROSS_PLAN = ((0, opposite, partner),)
NEAR_PLAN = ((0, partner, source), (0, onward, source))


def body(features, assignment, pairs, w_query, w_key, w_value, w_out, w_mix):
    rows_dev, width = features.shape
    block_count, pair_count = pairs.shape
    cluster = rows_dev // block_count
    stride = lax.axis_size("elec") // SPAN
    groups = [[rest + place_ * stride for place_ in range(SPAN)] for rest in range(stride)]
    position = lax.axis_index("elec") // stride
    at_position = position.reshape(1)
    capacity = (block_count * pair_count + SPAN - 1) // SPAN + 1

    def moved(x, moves):
        pairs_of = [(s * stride + r, d * stride + r) for s, d in moves for r in range(stride)]
        return lax.ppermute(x, "elec", pairs_of)

    def across_z(pairs_of_z):
        return [(position_at(s, y), position_at(d, y)) for s, d in pairs_of_z for y in range(2)]

    swap = [(p, p ^ 1) for p in range(SPAN)]
    first_moves = across_z(enumerate(OUT))
    second_moves = across_z(enumerate(FROM))
    middle_moves = across_z([(1, 2), (2, 1)])
    outward_moves = across_z([(2, 3), (1, 0)])

    listed = pairs.reshape(-1)
    owner = listed // block_count // stride
    within = listed % block_count
    ranking, tables = slot_tables(owner, within, capacity)
    wanted = lax.all_to_all(
        jnp.broadcast_to(tables[None], (SPAN, SPAN * capacity)),
        "elec",
        split_axis=0,
        concat_axis=0,
        axis_index_groups=groups,
        tiled=True,
    )

    shape = (block_count // SUB, 1, SUB * cluster)
    block_shape = (block_count, cluster, width)
    placed, normed = place(features, assignment.reshape(shape))
    blocks = normed.reshape(block_shape)
    own_at = 7 * capacity
    passed_at = own_at + block_count
    beside_at = passed_at + block_count
    total = beside_at + block_count

    z, y = position // 2, position % 2
    is_end = (z == 0) | (z == LEVELS - 1)
    z_owner, same = owner // 2, owner % 2 == y
    from_first = z_owner == choose(z, FROM)
    late = z_owner == LEVELS - 1 - z
    piece_of = jnp.where(
        from_first,
        0,
        jnp.where(
            late,
            jnp.where(is_end, jnp.where(same, 3, 4), jnp.where(same, 5, 6)),
            jnp.where(same, 1, 2),
        ),
    )
    whole_at = jnp.where(z_owner == z, jnp.where(same, own_at, beside_at), passed_at)
    whole = (z_owner == z) | (from_first & same)
    table = jnp.where(whole, whole_at + within, piece_of * capacity + ranking)

    arrival = jnp.where(late, jnp.where(same, 1, 2), 0)
    order, ends = by_class(jnp.max(arrival.reshape(block_count, pair_count), axis=1), 2)
    marks = [0, ends[0] // STEP, ends[1] // STEP, block_count // STEP]
    phases = [
        jnp.stack([marks[n], marks[n + 1] - marks[n]]).astype(jnp.int32) for n in range(3)
    ]
    weights = (jnp.concatenate([w_key, w_value], axis=1), w_out, w_mix)

    own = own_part(normed, w_query, w_key, w_value, cluster, (order, table, *phases, weights[0]))
    beside = moved(blocks, swap)
    passed = moved(blocks, first_moves)
    second, second_cross, on = pick(
        at_position, wanted, (blocks, beside, passed), FIRST_PLAN, after=own[2:]
    )
    second = moved(second, second_moves)
    second_cross = moved(second_cross, second_moves)
    on = moved(on, swap)
    (middle_pick,) = pick(at_position, wanted, (blocks,), MIDDLE_PLAN, after=(second,))
    middle = moved(middle_pick, middle_moves)
    near, outward = pick(at_position, wanted, (passed,), NEAR_PLAN, after=(on,))
    near = moved(near, swap)
    outward = moved(outward, outward_moves)
    on = moved(on, outward_moves)
    (middle_cross,) = pick(
        at_position, wanted, (beside,), MIDDLE_CROSS_PLAN, after=(second_cross, middle_pick)
    )
    middle_cross = moved(middle_cross, middle_moves)

    buffer = collect((blocks, passed, beside), (own_at, passed_at, beside_at), total)

    placed = pltpu.with_memory_space_constraint(placed.reshape(blocks.shape), pltpu.HBM)
    shared = (order, table, own, placed, weights)
    arrivals = (
        ((near, 0), (second, 1), (second_cross, 2)),
        ((outward, 3), (middle, 5)),
        ((on, 4), (middle_cross, 6)),
    )
    so_far = ()
    for phase, arrived in zip(phases, arrivals, strict=True):
        pieces = [piece for piece, _ in arrived]
        places = tuple(at * capacity for _, at in arrived)
        last = arrived is arrivals[-1]
        mixed, buffer, *states = attend(phase, *shared, buffer, pieces, places, so_far, last)
        so_far = (mixed, *states)
    return mixed.reshape(rows_dev, width)


def solution(mesh):
    placed = (
        P(("groups", "elec"), None),
        P(("groups", "elec")),
        P(("groups", "elec"), None),
        P(),
        P(),
        P(),
        P(),
        P(),
    )
    return jax.shard_map(
        body, mesh=mesh, in_specs=placed, out_specs=P(("groups", "elec"), None), check_vma=False
    )
```

```python
import functools
import math

import jax
import jax.numpy as jnp
from jax import lax
from jax.experimental import pallas as pl
from jax.experimental.pallas import tpu as pltpu
from jax.sharding import PartitionSpec as P

HEADS = 16
SPAN = 8
SUB = 8
GROUP = 4
STEP = 8
OWN_STEP = 4
SCORES_AHEAD, WEIGHTS_AHEAD = 3, 1
VMEM_BYTES = 48 * 1024 * 1024

NT = (((1,), (1,)), ((), ()))


def lasting(us):
    return pl.CostEstimate(flops=int(us * 1.15e9), bytes_accessed=0, transcendentals=0)


def kernel_params(share=1):
    return pltpu.CompilerParams(vmem_limit_bytes=VMEM_BYTES // share)


def layer_norm(rows):
    mean = jnp.mean(rows, axis=-1, keepdims=True)
    centred = rows - mean
    variance = jnp.mean(centred * centred, axis=-1, keepdims=True)
    return centred * lax.rsqrt(variance + 1e-05)


def head_mask(shape, head_width, cluster):
    row_head = lax.broadcasted_iota(jnp.int32, shape, 0) // head_width % GROUP
    lane_head = lax.broadcasted_iota(jnp.int32, shape, 1) // cluster
    return row_head == lane_head


def place_kernel(features_ref, assignment_ref, placed_ref, normed_ref):
    walkers, _, rows = assignment_ref.shape
    lane = 128
    columns = lax.broadcasted_iota(jnp.int32, (lane, rows), 1)
    for walker in range(walkers):
        here = pl.ds(walker * rows, rows)
        one_hots = []
        for part in range(rows // lane):
            chosen = assignment_ref[walker, :, part * lane : (part + 1) * lane] & (rows - 1)
            chosen = jnp.broadcast_to(chosen, (lane, lane)).T
            chosen = jnp.concatenate([chosen] * (rows // lane), axis=1)
            one_hots.append(jnp.where(chosen == columns, 1.0, 0.0).astype(jnp.bfloat16))
        one_hot = jnp.concatenate(one_hots, axis=0)
        placed = jnp.dot(one_hot, features_ref[here, :], preferred_element_type=jnp.float32)
        placed_ref[here, :] = placed.astype(jnp.bfloat16)
        normed_ref[here, :] = layer_norm(placed).astype(jnp.bfloat16)


def place(features, assignment):
    width = features.shape[1]
    walkers, _, rows = assignment.shape
    local = pl.BlockSpec((2 * rows, width), lambda i: (i, 0))
    out = jax.ShapeDtypeStruct(features.shape, jnp.bfloat16)
    return pl.pallas_call(
        place_kernel,
        grid=(walkers // 2,),
        in_specs=[local, pl.BlockSpec((2, 1, rows), lambda i: (i, 0, 0))],
        out_specs=[local] * 2,
        out_shape=[pltpu.HBM(out.shape, out.dtype), out],
        cost_estimate=lasting(6),
        compiler_params=kernel_params(),
        name="place_rows",
    )(features, assignment)


def choose(index, values):
    result = values[-1]
    for at in range(len(values) - 2, -1, -1):
        result = jnp.where(index == at, values[at], result)
    return result


def pick_kernel(position_ref, wanted_ref, *rest, plan, capacity):
    position = position_ref[0]
    for out_ref, (at, reader_of, owner_of) in zip(rest[len(rest) - len(plan) :], plan, strict=True):
        reader, first = reader_of(position), owner_of(position) * capacity

        def one_slot(slot, carry, out_ref=out_ref, at=at, reader=reader, first=first):
            out_ref[slot] = rest[at][wanted_ref[reader, first + slot]]
            return carry

        lax.fori_loop(0, capacity, one_slot, 0)


def pick(position, wanted, sources, plan, after=()):
    capacity = wanted.shape[1] // SPAN
    block = sources[0].shape[1:]
    outs = [jax.ShapeDtypeStruct((capacity,) + block, sources[0].dtype)] * len(plan)
    smem = pl.BlockSpec(memory_space=pltpu.SMEM)
    vmem = pl.BlockSpec(memory_space=pltpu.VMEM)
    return pl.pallas_call(
        functools.partial(pick_kernel, plan=plan, capacity=capacity),
        in_specs=[smem, smem]
        + [vmem] * len(sources)
        + [pl.BlockSpec(memory_space=pl.ANY)] * len(after),
        out_specs=[vmem] * len(outs),
        out_shape=outs,
        cost_estimate=lasting(1.5),
        compiler_params=kernel_params(3),
        name="pick_blocks",
    )(position, wanted, *sources, *after)


def tiles_of(query, first, span):
    one = query[first : first + span]
    two = query[first + span : first + 2 * span]
    zeros = jnp.zeros_like(one)
    return jnp.concatenate(
        [jnp.concatenate([one, zeros], axis=1), jnp.concatenate([zeros, two], axis=1)], axis=0
    )


def own_kernel(normed_ref, query_w_ref, key_w_ref, value_w_ref, *rest, head_width):
    query_ref, own_ref, stats_ref = rest[-3:]
    blocks, width, tile = query_ref.shape
    cluster = tile // GROUP
    span = GROUP * head_width
    mask = head_mask((width, tile), head_width, cluster)
    scale = math.log2(math.e) / head_width**0.5
    ones = jnp.ones((16, cluster), jnp.bfloat16)
    rows = normed_ref[...]
    keys = jnp.dot(rows, key_w_ref[...], preferred_element_type=jnp.float32).astype(jnp.bfloat16)
    queries = []
    for block in range(blocks):
        own = rows[block * cluster : (block + 1) * cluster]
        tiled = jnp.concatenate([own] * GROUP, axis=0)
        query = lax.dot_general(query_w_ref[...], tiled, NT, preferred_element_type=jnp.float32)
        query = jnp.where(mask, query * scale, 0.0).astype(jnp.bfloat16)
        query_ref[block] = query
        queries.append(query)
    for block in range(blocks):
        own = rows[block * cluster : (block + 1) * cluster]
        value = lax.dot_general(value_w_ref[...], own, NT, preferred_element_type=jnp.float32)
        value = value.astype(jnp.bfloat16)
        tops, totals = [], []
        for pair in range(HEADS // GROUP // 2):
            first = pair * 2 * span
            scores = jnp.dot(
                keys[block * cluster : (block + 1) * cluster, first : first + 2 * span],
                tiles_of(queries[block], first, span),
                preferred_element_type=jnp.float32,
            )
            top = jnp.max(scores, axis=0, keepdims=True)
            weights = jnp.exp2(scores - top).astype(jnp.bfloat16)
            for half in range(2):
                at = first + half * span
                here = slice(half * tile, (half + 1) * tile)
                lifted = jnp.concatenate([value[at : at + span], ones], axis=0)
                product = jnp.dot(lifted, weights[:, here], preferred_element_type=jnp.float32)
                total = product[span : span + 1]
                result = jnp.where(mask[:span], product[:span] * (1.0 / total), 0.0)
                own_ref[block, at : at + span, :] = result.astype(jnp.bfloat16)
                tops.append(top[:, here])
                totals.append(total)
        stats_ref[block] = jnp.concatenate(tops + totals, axis=0)


def own_part(normed, w_query, w_key, w_value, cluster, after):
    rows, width = normed.shape
    blocks = rows // cluster
    tile = GROUP * cluster
    tiles = HEADS // GROUP
    whole = pl.BlockSpec((width, width), lambda i: (0, 0))
    square = pl.BlockSpec((OWN_STEP, width, tile), lambda i: (i, 0, 0))
    return pl.pallas_call(
        functools.partial(own_kernel, head_width=width // HEADS),
        grid=(blocks // OWN_STEP,),
        in_specs=[pl.BlockSpec((OWN_STEP * cluster, width), lambda i: (i, 0)), whole, whole, whole]
        + [pl.BlockSpec(memory_space=pl.ANY)] * len(after),
        out_specs=[
            square,
            square,
            pl.BlockSpec((OWN_STEP, 2 * tiles, tile), lambda i: (i, 0, 0)),
        ],
        out_shape=[
            jax.ShapeDtypeStruct((blocks, width, tile), jnp.bfloat16),
            jax.ShapeDtypeStruct((blocks, width, tile), jnp.bfloat16),
            jax.ShapeDtypeStruct((blocks, 2 * tiles, tile), jnp.float32),
        ],
        cost_estimate=lasting(20),
        compiler_params=kernel_params(),
        name="own_blocks",
    )(normed, w_query.T, w_key, w_value.T, *after)


def collect_kernel(*refs, places):
    buffer_ref, sems = refs[-2:]
    copies = copy_pieces(refs[: len(places)], buffer_ref, places, sems)
    for copy in copies:
        copy.start()
    for copy in copies:
        copy.wait()


def parts_of(blocks):
    return 5 if blocks % 5 == 0 else 4


def copy_pieces(piece_refs, buffer_ref, places, sems):
    copies = []
    for n, (piece, at) in enumerate(zip(piece_refs, places, strict=True)):
        parts = parts_of(piece.shape[0])
        per = piece.shape[0] // parts
        for part in range(parts):
            target = buffer_ref.at[pl.ds(at + part * per, per)]
            copies.append(
                pltpu.make_async_copy(piece.at[pl.ds(part * per, per)], target, sems.at[n, part])
            )
    return copies


def collect(pieces, places, total):
    return pl.pallas_call(
        functools.partial(collect_kernel, places=places),
        in_specs=[pl.BlockSpec(memory_space=pltpu.VMEM)] * len(pieces),
        out_specs=pl.BlockSpec(memory_space=pl.ANY),
        out_shape=pltpu.HBM((total,) + pieces[0].shape[1:], pieces[0].dtype),
        scratch_shapes=[pltpu.SemaphoreType.DMA((len(pieces), 5))],
        cost_estimate=lasting(4),
        compiler_params=kernel_params(3),
        name="collect_blocks",
    )(*pieces)


def attend_kernel(
    range_ref,
    order_ref,
    table_ref,
    query_ref,
    own_ref,
    stats_ref,
    placed_ref,
    *rest,
    head_width,
    places,
    first,
    last,
):
    weight_refs, rest = rest[:3], rest[3:]
    piece_refs = rest[: len(places)]
    mixed_ref, buffer_ref, *states = rest[-16:-12]
    query_buf, own_buf, stats_buf, member_buf, placed_buf = rest[-12:-7]
    attended_buf, before_buf, done_buf, in_sems, out_sems, piece_sems, state_sems = rest[-7:]
    begin, count = range_ref[0], range_ref[1]
    pair_count = member_buf.shape[2]
    copies = copy_pieces(piece_refs, buffer_ref, places, piece_sems)
    for copy in copies:
        copy.start()

    def fetches(step, slot, known=True, listed=True):
        for j in range(STEP):
            block = order_ref[step * STEP + j]
            sources = [
                (query_ref.at[block], query_buf.at[slot, j]),
                (own_ref.at[block], own_buf.at[slot, j]),
                (stats_ref.at[block], stats_buf.at[slot, j]),
                (placed_ref.at[block], placed_buf.at[slot, j]),
            ]
            for n in range(pair_count):
                member = table_ref[block * pair_count + n]
                sources.append((buffer_ref.at[member], member_buf.at[slot, j, n]))
            for n, (source_, target) in enumerate(sources):
                if listed if n >= 4 else known:
                    sem = in_sems.at[slot, j * (pair_count + 4) + n]
                    yield pltpu.make_async_copy(source_, target, sem)

    def stores(step):
        for j in range(STEP):
            target = mixed_ref.at[order_ref[step * STEP + j]]
            yield pltpu.make_async_copy(done_buf.at[j], target, out_sems.at[j])

    def finish():
        return finish_step(before_buf[...], attended_buf[...], *weight_refs[1:])

    def one_step(i, carry):
        slot = i % 2
        for copy in fetches(begin + jnp.minimum(i + 1, count - 1), 1 - slot):
            copy.start()
        for copy in fetches(begin + i, slot):
            copy.wait()
        attended, mixed = attend_step(
            query_buf.at[slot],
            own_buf.at[slot],
            stats_buf.at[slot],
            member_buf.at[slot],
            weight_refs[0],
            head_width,
            finish,
        )

        @pl.when((i > 0) & (begin + i > 1))
        def _():
            for copy in stores(begin + i - 2):
                copy.wait()

        done_buf[...] = mixed.reshape(done_buf.shape)
        attended_buf[...] = attended
        before_buf[...] = placed_buf[slot].reshape(before_buf.shape)

        @pl.when(begin + i > 0)
        def _():
            for copy in stores(begin + i - 1):
                copy.start()

        return carry

    held = (attended_buf, before_buf)
    if first:
        for buf in held:
            buf[...] = jnp.zeros_like(buf)
    else:
        loads = [
            pltpu.make_async_copy(state, buf, state_sems.at[n])
            for n, (state, buf) in enumerate(zip(states, held, strict=True))
        ]
        for copy in loads:
            copy.start()

    @pl.when(count > 0)
    def _():
        for copy in fetches(begin, 0, listed=False):
            copy.start()

    for copy in copies:
        copy.wait()

    @pl.when(count > 0)
    def _():
        for copy in fetches(begin, 0, known=False):
            copy.start()

    if not first:
        for copy in loads:
            copy.wait()

    @pl.when(count > 0)
    def _():
        lax.fori_loop(0, count, one_step, 0)
        for copy in fetches(begin + count - 1, count % 2):
            copy.wait()

    @pl.when((count > 0) & (begin + count > 1))
    def _():
        for copy in stores(begin + count - 2):
            copy.wait()

    if last:
        done_buf[...] = finish().reshape(done_buf.shape)
        for copy in stores(begin + count - 1):
            copy.start()
        for copy in stores(begin + count - 1):
            copy.wait()
    else:
        saves = [
            pltpu.make_async_copy(buf, state, state_sems.at[n])
            for n, (state, buf) in enumerate(zip(states, held, strict=True))
        ]
        for copy in saves:
            copy.start()
        for copy in saves:
            copy.wait()


def finish_step(placed, attended, out_w_ref, mix_ref):
    middle = placed.astype(jnp.float32) + jnp.dot(
        attended, out_w_ref[...], preferred_element_type=jnp.float32
    )
    middle = middle.astype(jnp.bfloat16).astype(jnp.float32)
    second = layer_norm(middle).astype(jnp.bfloat16)
    mixed = middle + jnp.tanh(jnp.dot(second, mix_ref[...], preferred_element_type=jnp.float32))
    return mixed.astype(jnp.bfloat16)


def attend_step(
    query_ref, own_ref, stats_ref, member_ref, pair_w_ref, head_width, meanwhile
):
    _, members_count, cluster, width = member_ref.shape
    span = GROUP * head_width
    tile = GROUP * cluster
    diagonal = head_mask((span, tile), head_width, cluster)
    ones = jnp.ones((16, members_count * cluster), jnp.bfloat16)
    tiles = HEADS // GROUP
    units = [(block, pair) for block in range(STEP) for pair in range(HEADS // GROUP // 2)]
    listed = member_ref[...].reshape(STEP * members_count * cluster, width)
    both = jnp.dot(listed, pair_w_ref[...], preferred_element_type=jnp.float32)
    both = both.astype(jnp.bfloat16).reshape(STEP, members_count * cluster, 2 * width)
    finished = meanwhile()
    values = [both[block, :, width:].T for block in range(STEP)]

    def scores_of(block, pair):
        return [
            jnp.dot(
                both[block, :, t * span : (t + 1) * span],
                query_ref[block, t * span : (t + 1) * span, :],
                preferred_element_type=jnp.float32,
            )
            for t in (2 * pair, 2 * pair + 1)
        ]

    def weights_of(block, pair, scores):
        weights, factors = [], []
        for t, score in zip((2 * pair, 2 * pair + 1), scores, strict=True):
            own_top = stats_ref[block, t : t + 1, :]
            top = jnp.maximum(jnp.max(score, axis=0, keepdims=True), own_top)
            weights.append(jnp.exp2((score - top).astype(jnp.bfloat16)))
            factors.append(jnp.exp2(own_top - top))
        return weights, factors

    def products_of(block, pair, weights, own_factor):
        for half in range(2):
            t = pair * 2 + half
            lifted = jnp.concatenate([values[block][t * span : (t + 1) * span], ones], axis=0)
            product = jnp.dot(lifted, weights[half], preferred_element_type=jnp.float32)
            yield block, t, product, own_factor[half]

    def scaled(block, t, product, own_factor):
        own_total = stats_ref[block, tiles + t : tiles + t + 1, :] * own_factor
        inverse = 1.0 / (product[span : span + 1] + own_total)
        own = own_ref[block, t * span : (t + 1) * span, :].astype(jnp.float32)
        result = product[:span] * inverse + own * (own_total * inverse)
        result = jnp.where(diagonal, result, 0.0)
        return result[:, : tile // 2] + result[:, tile // 2 :]

    def rows_of(pieces):
        first, other = (jnp.concatenate(of, axis=0) for of in pieces)
        left = lax.broadcasted_iota(jnp.int32, first.shape, 1) < cluster
        first = first + pltpu.roll(first, cluster, 1)
        other = other + pltpu.roll(other, cluster, 1)
        return jnp.where(left, first, other).T.astype(jnp.bfloat16)

    count = len(units)
    scores, weights, products, pieces, attended = {}, {}, {}, [], []
    for at in range(-SCORES_AHEAD, count + 1):
        if at + SCORES_AHEAD < count:
            scores[at + SCORES_AHEAD] = scores_of(*units[at + SCORES_AHEAD])
        if 0 <= at + WEIGHTS_AHEAD < count:
            ahead = at + WEIGHTS_AHEAD
            weights[ahead] = weights_of(*units[ahead], scores.pop(ahead))
        if 0 <= at < count:
            products[at] = list(products_of(*units[at], *weights.pop(at)))
        if at > 0:
            pieces += [scaled(*product) for product in products.pop(at - 1)]
            if len(pieces) == 2 * tiles:
                attended.append(rows_of((pieces[:tiles], pieces[tiles:])))
                pieces = []
    return jnp.concatenate(attended, axis=0), finished


def attend(steps, order, table, own, placed, weights, buffer, pieces, places, so_far, last):
    blocks, cluster, width = placed.shape
    pair_count = table.shape[0] // blocks
    smem = pl.BlockSpec(memory_space=pltpu.SMEM)
    vmem = pl.BlockSpec(memory_space=pltpu.VMEM)
    hbm = pl.BlockSpec(memory_space=pl.ANY)
    in_specs = [smem] * 3 + [hbm] * len(own) + [pl.BlockSpec(memory_space=pltpu.HBM)] + [vmem] * (3 + len(pieces)) + [hbm]
    aliases = {len(in_specs) - 1: 1}
    operands = [*own, placed, *weights, *pieces, buffer]
    for at, x in zip((0, 2, 3), so_far):
        aliases[len(in_specs)] = at
        in_specs.append(hbm)
        operands.append(x)
    kernel = functools.partial(
        attend_kernel,
        head_width=width // HEADS,
        places=places,
        first=not so_far,
        last=last,
    )
    state = jax.ShapeDtypeStruct((STEP * cluster, width), jnp.bfloat16)
    return pl.pallas_call(
        kernel,
        in_specs=in_specs,
        out_specs=[hbm] * 4,
        out_shape=[
            jax.ShapeDtypeStruct(placed.shape, jnp.bfloat16),
            jax.ShapeDtypeStruct(buffer.shape, jnp.bfloat16),
            state,
            state,
        ],
        scratch_shapes=[
            *[pltpu.VMEM((2, STEP) + x.shape[1:], x.dtype) for x in own],
            pltpu.VMEM((2, STEP, pair_count, cluster, width), jnp.bfloat16),
            pltpu.VMEM((2, STEP, cluster, width), jnp.bfloat16),
            pltpu.VMEM((STEP * cluster, width), jnp.bfloat16),
            pltpu.VMEM((STEP * cluster, width), jnp.bfloat16),
            pltpu.VMEM((STEP, cluster, width), jnp.bfloat16),
            pltpu.SemaphoreType.DMA((2, STEP * (pair_count + 4))),
            pltpu.SemaphoreType.DMA((STEP,)),
            pltpu.SemaphoreType.DMA((len(pieces), 5)),
            pltpu.SemaphoreType.DMA((2,)),
        ],
        input_output_aliases=aliases,
        cost_estimate=lasting(18),
        compiler_params=kernel_params(),
        name="attend_blocks",
    )(steps, order, table, *operands)


def slot_tables(owner, within, capacity):
    entries = owner.shape[0]
    alike = owner[:, None] == owner[None, :]
    earlier = jnp.arange(entries)[None, :] < jnp.arange(entries)[:, None]
    ranking = jnp.sum(jnp.where(alike & earlier, 1, 0), axis=1).astype(jnp.int32)
    slots = owner * capacity + ranking
    matches = slots[None, :] == jnp.arange(SPAN * capacity, dtype=jnp.int32)[:, None]
    return ranking, jnp.sum(jnp.where(matches, within[None, :], 0), axis=1).astype(jnp.int32)


def by_class(classes, count):
    blocks = jnp.arange(classes.shape[0], dtype=jnp.int32)
    before = (classes[None, :] < classes[:, None]) | (
        (classes[None, :] == classes[:, None]) & (blocks[None, :] < blocks[:, None])
    )
    rank = jnp.sum(jnp.where(before, 1, 0), axis=1)
    order = jnp.sum(jnp.where(rank[None, :] == blocks[:, None], blocks[None, :], 0), axis=1)
    ends = [jnp.sum(jnp.where(classes <= c, 1, 0)).astype(jnp.int32) for c in range(count)]
    return order.astype(jnp.int32), ends


OUT = (2, 0, 3, 1)
FROM = (1, 3, 0, 2)
LEVELS = 4


def position_at(z, y):
    return 2 * z + y


def partner(position):
    return position ^ 1


def onward(position):
    return position_at(choose(position // 2, OUT), position % 2)


def source(position):
    return position_at(choose(position // 2, FROM), position % 2)


def opposite(position):
    return position_at(LEVELS - 1 - position // 2, position % 2)


def itself(position):
    return position


def crossed(route):
    return lambda position: partner(route(position))


FIRST_PLAN = ((0, source, itself), (1, source, partner), (2, crossed(onward), source))
MIDDLE_PLAN = ((0, opposite, itself),)
MIDDLE_CROSS_PLAN = ((0, opposite, partner),)
NEAR_PLAN = ((0, partner, source), (0, onward, source))


def body(features, assignment, pairs, w_query, w_key, w_value, w_out, w_mix):
    rows_dev, width = features.shape
    block_count, pair_count = pairs.shape
    cluster = rows_dev // block_count
    stride = lax.axis_size("elec") // SPAN
    groups = [[rest + place_ * stride for place_ in range(SPAN)] for rest in range(stride)]
    position = lax.axis_index("elec") // stride
    at_position = position.reshape(1)
    capacity = (block_count * pair_count + SPAN - 1) // SPAN + 1

    def moved(x, moves):
        pairs_of = [(s * stride + r, d * stride + r) for s, d in moves for r in range(stride)]
        return lax.ppermute(x, "elec", pairs_of)

    def across_z(pairs_of_z):
        return [(position_at(s, y), position_at(d, y)) for s, d in pairs_of_z for y in range(2)]

    swap = [(p, p ^ 1) for p in range(SPAN)]
    first_moves = across_z(enumerate(OUT))
    second_moves = across_z(enumerate(FROM))
    middle_moves = across_z([(1, 2), (2, 1)])
    outward_moves = across_z([(2, 3), (1, 0)])

    listed = pairs.reshape(-1)
    owner = listed // block_count // stride
    within = listed % block_count
    ranking, tables = slot_tables(owner, within, capacity)
    wanted = lax.all_to_all(
        jnp.broadcast_to(tables[None], (SPAN, SPAN * capacity)),
        "elec",
        split_axis=0,
        concat_axis=0,
        axis_index_groups=groups,
        tiled=True,
    )

    shape = (block_count // SUB, 1, SUB * cluster)
    block_shape = (block_count, cluster, width)
    features = pltpu.with_memory_space_constraint(features, pltpu.HBM)
    placed, normed = place(features, assignment.reshape(shape))
    blocks = normed.reshape(block_shape)
    own_at = 7 * capacity
    passed_at = own_at + block_count
    beside_at = passed_at + block_count
    total = beside_at + block_count

    z, y = position // 2, position % 2
    is_end = (z == 0) | (z == LEVELS - 1)
    z_owner, same = owner // 2, owner % 2 == y
    from_first = z_owner == choose(z, FROM)
    late = z_owner == LEVELS - 1 - z
    piece_of = jnp.where(
        from_first,
        0,
        jnp.where(
            late,
            jnp.where(is_end, jnp.where(same, 3, 4), jnp.where(same, 5, 6)),
            jnp.where(same, 1, 2),
        ),
    )
    whole_at = jnp.where(z_owner == z, jnp.where(same, own_at, beside_at), passed_at)
    whole = (z_owner == z) | (from_first & same)
    table = jnp.where(whole, whole_at + within, piece_of * capacity + ranking)

    arrival = jnp.where(late, jnp.where(same, 1, 2), 0)
    order, ends = by_class(jnp.max(arrival.reshape(block_count, pair_count), axis=1), 2)
    marks = [0, ends[0] // STEP, ends[1] // STEP, block_count // STEP]
    phases = [
        jnp.stack([marks[n], marks[n + 1] - marks[n]]).astype(jnp.int32) for n in range(3)
    ]
    weights = (jnp.concatenate([w_key, w_value], axis=1), w_out, w_mix)

    own = own_part(normed, w_query, w_key, w_value, cluster, (order, table, *phases, weights[0]))
    beside = moved(blocks, swap)
    passed = moved(blocks, first_moves)
    second, second_cross, on = pick(
        at_position, wanted, (blocks, beside, passed), FIRST_PLAN, after=own[2:]
    )
    second = moved(second, second_moves)
    second_cross = moved(second_cross, second_moves)
    on = moved(on, swap)
    (middle_pick,) = pick(at_position, wanted, (blocks,), MIDDLE_PLAN, after=(second,))
    middle = moved(middle_pick, middle_moves)
    near, outward = pick(at_position, wanted, (passed,), NEAR_PLAN, after=(on,))
    near = moved(near, swap)
    outward = moved(outward, outward_moves)
    on = moved(on, outward_moves)
    (middle_cross,) = pick(
        at_position, wanted, (beside,), MIDDLE_CROSS_PLAN, after=(second_cross, middle_pick)
    )
    middle_cross = moved(middle_cross, middle_moves)

    buffer = collect((blocks, passed, beside), (own_at, passed_at, beside_at), total)

    placed = pltpu.with_memory_space_constraint(placed.reshape(blocks.shape), pltpu.HBM)
    shared = (order, table, own, placed, weights)
    arrivals = (
        ((near, 0), (second, 1), (second_cross, 2)),
        ((outward, 3), (middle, 5)),
        ((on, 4), (middle_cross, 6)),
    )
    so_far = ()
    for phase, arrived in zip(phases, arrivals, strict=True):
        pieces = [piece for piece, _ in arrived]
        places = tuple(at * capacity for _, at in arrived)
        last = arrived is arrivals[-1]
        mixed, buffer, *states = attend(phase, *shared, buffer, pieces, places, so_far, last)
        so_far = (mixed, *states)
    return mixed.reshape(rows_dev, width)


def solution(mesh):
    placed = (
        P(("groups", "elec"), None),
        P(("groups", "elec")),
        P(("groups", "elec"), None),
        P(),
        P(),
        P(),
        P(),
        P(),
    )
    return jax.shard_map(
        body, mesh=mesh, in_specs=placed, out_specs=P(("groups", "elec"), None), check_vma=False
    )
```

```python
import functools
import math

import jax
import jax.numpy as jnp
from jax import lax
from jax.experimental import pallas as pl
from jax.experimental.pallas import tpu as pltpu
from jax.sharding import PartitionSpec as P

HEADS = 16
SPAN = 8
SUB = 8
GROUP = 4
STEP = 8
OWN_STEP = 4
SCORES_AHEAD, WEIGHTS_AHEAD = 3, 1
VMEM_BYTES = 48 * 1024 * 1024

NT = (((1,), (1,)), ((), ()))


def lasting(us):
    return pl.CostEstimate(flops=int(us * 1.15e9), bytes_accessed=0, transcendentals=0)


def kernel_params(share=1):
    return pltpu.CompilerParams(vmem_limit_bytes=VMEM_BYTES // share)


def layer_norm(rows):
    mean = jnp.mean(rows, axis=-1, keepdims=True)
    centred = rows - mean
    variance = jnp.mean(centred * centred, axis=-1, keepdims=True)
    return centred * lax.rsqrt(variance + 1e-05)


def head_mask(shape, head_width, cluster):
    row_head = lax.broadcasted_iota(jnp.int32, shape, 0) // head_width % GROUP
    lane_head = lax.broadcasted_iota(jnp.int32, shape, 1) // cluster
    return row_head == lane_head


def place_kernel(features_ref, assignment_ref, placed_ref, normed_ref):
    walkers, _, rows = assignment_ref.shape
    lane = 128
    columns = lax.broadcasted_iota(jnp.int32, (lane, rows), 1)
    for walker in range(walkers):
        here = pl.ds(walker * rows, rows)
        one_hots = []
        for part in range(rows // lane):
            chosen = assignment_ref[walker, :, part * lane : (part + 1) * lane] & (rows - 1)
            chosen = jnp.broadcast_to(chosen, (lane, lane)).T
            chosen = jnp.concatenate([chosen] * (rows // lane), axis=1)
            one_hots.append(jnp.where(chosen == columns, 1.0, 0.0).astype(jnp.bfloat16))
        one_hot = jnp.concatenate(one_hots, axis=0)
        placed = jnp.dot(one_hot, features_ref[here, :], preferred_element_type=jnp.float32)
        placed_ref[here, :] = placed.astype(jnp.bfloat16)
        normed_ref[here, :] = layer_norm(placed).astype(jnp.bfloat16)


def place(features, assignment):
    width = features.shape[1]
    walkers, _, rows = assignment.shape
    local = pl.BlockSpec((2 * rows, width), lambda i: (i, 0))
    out = jax.ShapeDtypeStruct(features.shape, jnp.bfloat16)
    return pl.pallas_call(
        place_kernel,
        grid=(walkers // 2,),
        in_specs=[local, pl.BlockSpec((2, 1, rows), lambda i: (i, 0, 0))],
        out_specs=[local] * 2,
        out_shape=[pltpu.HBM(out.shape, out.dtype), out],
        cost_estimate=lasting(6),
        compiler_params=kernel_params(),
        name="place_rows",
    )(features, assignment)


def choose(index, values):
    result = values[-1]
    for at in range(len(values) - 2, -1, -1):
        result = jnp.where(index == at, values[at], result)
    return result


def pick_kernel(position_ref, wanted_ref, *rest, plan, capacity):
    position = position_ref[0]
    for out_ref, (at, reader_of, owner_of) in zip(rest[len(rest) - len(plan) :], plan, strict=True):
        reader, first = reader_of(position), owner_of(position) * capacity

        def one_slot(slot, carry, out_ref=out_ref, at=at, reader=reader, first=first):
            out_ref[slot] = rest[at][wanted_ref[reader, first + slot]]
            return carry

        lax.fori_loop(0, capacity, one_slot, 0)


def pick(position, wanted, sources, plan, after=()):
    capacity = wanted.shape[1] // SPAN
    block = sources[0].shape[1:]
    outs = [jax.ShapeDtypeStruct((capacity,) + block, sources[0].dtype)] * len(plan)
    smem = pl.BlockSpec(memory_space=pltpu.SMEM)
    vmem = pl.BlockSpec(memory_space=pltpu.VMEM)
    return pl.pallas_call(
        functools.partial(pick_kernel, plan=plan, capacity=capacity),
        in_specs=[smem, smem]
        + [vmem] * len(sources)
        + [pl.BlockSpec(memory_space=pl.ANY)] * len(after),
        out_specs=[vmem] * len(outs),
        out_shape=outs,
        cost_estimate=lasting(1.5),
        compiler_params=kernel_params(3),
        name="pick_blocks",
    )(position, wanted, *sources, *after)


def held_kernel(piece_ref, *rest):
    rest[-1][...] = piece_ref[...]


def held_until(piece, after):
    vmem = pl.BlockSpec(memory_space=pltpu.VMEM)
    return pl.pallas_call(
        held_kernel,
        in_specs=[vmem] + [pl.BlockSpec(memory_space=pl.ANY)] * len(after),
        out_specs=vmem,
        out_shape=jax.ShapeDtypeStruct(piece.shape, piece.dtype),
        cost_estimate=lasting(0.5),
        compiler_params=kernel_params(3),
        name="held_piece",
    )(piece, *after)


def tiles_of(query, first, span):
    one = query[first : first + span]
    two = query[first + span : first + 2 * span]
    zeros = jnp.zeros_like(one)
    return jnp.concatenate(
        [jnp.concatenate([one, zeros], axis=1), jnp.concatenate([zeros, two], axis=1)], axis=0
    )


def own_kernel(normed_ref, query_w_ref, key_w_ref, value_w_ref, *rest, head_width):
    query_ref, own_ref, stats_ref = rest[-3:]
    blocks, width, tile = query_ref.shape
    cluster = tile // GROUP
    span = GROUP * head_width
    mask = head_mask((width, tile), head_width, cluster)
    scale = math.log2(math.e) / head_width**0.5
    ones = jnp.ones((16, cluster), jnp.bfloat16)
    rows = normed_ref[...]
    keys = jnp.dot(rows, key_w_ref[...], preferred_element_type=jnp.float32).astype(jnp.bfloat16)
    queries = []
    for block in range(blocks):
        own = rows[block * cluster : (block + 1) * cluster]
        tiled = jnp.concatenate([own] * GROUP, axis=0)
        query = lax.dot_general(query_w_ref[...], tiled, NT, preferred_element_type=jnp.float32)
        query = jnp.where(mask, query * scale, 0.0).astype(jnp.bfloat16)
        query_ref[block] = query
        queries.append(query)
    for block in range(blocks):
        own = rows[block * cluster : (block + 1) * cluster]
        value = lax.dot_general(value_w_ref[...], own, NT, preferred_element_type=jnp.float32)
        value = value.astype(jnp.bfloat16)
        tops, totals = [], []
        for pair in range(HEADS // GROUP // 2):
            first = pair * 2 * span
            scores = jnp.dot(
                keys[block * cluster : (block + 1) * cluster, first : first + 2 * span],
                tiles_of(queries[block], first, span),
                preferred_element_type=jnp.float32,
            )
            top = jnp.max(scores, axis=0, keepdims=True)
            weights = jnp.exp2(scores - top).astype(jnp.bfloat16)
            for half in range(2):
                at = first + half * span
                here = slice(half * tile, (half + 1) * tile)
                lifted = jnp.concatenate([value[at : at + span], ones], axis=0)
                product = jnp.dot(lifted, weights[:, here], preferred_element_type=jnp.float32)
                total = product[span : span + 1]
                result = jnp.where(mask[:span], product[:span] * (1.0 / total), 0.0)
                own_ref[block, at : at + span, :] = result.astype(jnp.bfloat16)
                tops.append(top[:, here])
                totals.append(total)
        stats_ref[block] = jnp.concatenate(tops + totals, axis=0)


def own_part(normed, w_query, w_key, w_value, cluster, after):
    rows, width = normed.shape
    blocks = rows // cluster
    tile = GROUP * cluster
    tiles = HEADS // GROUP
    whole = pl.BlockSpec((width, width), lambda i: (0, 0))
    square = pl.BlockSpec((OWN_STEP, width, tile), lambda i: (i, 0, 0))
    return pl.pallas_call(
        functools.partial(own_kernel, head_width=width // HEADS),
        grid=(blocks // OWN_STEP,),
        in_specs=[pl.BlockSpec((OWN_STEP * cluster, width), lambda i: (i, 0)), whole, whole, whole]
        + [pl.BlockSpec(memory_space=pl.ANY)] * len(after),
        out_specs=[
            square,
            square,
            pl.BlockSpec((OWN_STEP, 2 * tiles, tile), lambda i: (i, 0, 0)),
        ],
        out_shape=[
            jax.ShapeDtypeStruct((blocks, width, tile), jnp.bfloat16),
            jax.ShapeDtypeStruct((blocks, width, tile), jnp.bfloat16),
            jax.ShapeDtypeStruct((blocks, 2 * tiles, tile), jnp.float32),
        ],
        cost_estimate=lasting(20),
        compiler_params=kernel_params(),
        name="own_blocks",
    )(normed, w_query.T, w_key, w_value.T, *after)


def collect_kernel(*refs, places):
    buffer_ref, sems = refs[-2:]
    copies = copy_pieces(refs[: len(places)], buffer_ref, places, sems)
    for copy in copies:
        copy.start()
    for copy in copies:
        copy.wait()


def parts_of(blocks):
    return 5 if blocks % 5 == 0 else 4


def copy_pieces(piece_refs, buffer_ref, places, sems):
    copies = []
    for n, (piece, at) in enumerate(zip(piece_refs, places, strict=True)):
        parts = parts_of(piece.shape[0])
        per = piece.shape[0] // parts
        for part in range(parts):
            target = buffer_ref.at[pl.ds(at + part * per, per)]
            copies.append(
                pltpu.make_async_copy(piece.at[pl.ds(part * per, per)], target, sems.at[n, part])
            )
    return copies


def collect(pieces, places, total):
    return pl.pallas_call(
        functools.partial(collect_kernel, places=places),
        in_specs=[pl.BlockSpec(memory_space=pltpu.VMEM)] * len(pieces),
        out_specs=pl.BlockSpec(memory_space=pl.ANY),
        out_shape=pltpu.HBM((total,) + pieces[0].shape[1:], pieces[0].dtype),
        scratch_shapes=[pltpu.SemaphoreType.DMA((len(pieces), 5))],
        cost_estimate=lasting(4),
        compiler_params=kernel_params(3),
        name="collect_blocks",
    )(*pieces)


def attend_kernel(
    range_ref,
    order_ref,
    table_ref,
    query_ref,
    own_ref,
    stats_ref,
    placed_ref,
    *rest,
    head_width,
    places,
    first,
    last,
):
    weight_refs, rest = rest[:3], rest[3:]
    piece_refs = rest[: len(places)]
    mixed_ref, buffer_ref, *states = rest[-16:-12]
    query_buf, own_buf, stats_buf, member_buf, placed_buf = rest[-12:-7]
    attended_buf, before_buf, done_buf, in_sems, out_sems, piece_sems, state_sems = rest[-7:]
    begin, count = range_ref[0], range_ref[1]
    pair_count = member_buf.shape[2]
    copies = copy_pieces(piece_refs, buffer_ref, places, piece_sems)
    for copy in copies:
        copy.start()

    def fetches(step, slot, known=True, listed=True):
        for j in range(STEP):
            block = order_ref[step * STEP + j]
            sources = [
                (query_ref.at[block], query_buf.at[slot, j]),
                (own_ref.at[block], own_buf.at[slot, j]),
                (stats_ref.at[block], stats_buf.at[slot, j]),
                (placed_ref.at[block], placed_buf.at[slot, j]),
            ]
            for n in range(pair_count):
                member = table_ref[block * pair_count + n]
                sources.append((buffer_ref.at[member], member_buf.at[slot, j, n]))
            for n, (source_, target) in enumerate(sources):
                if listed if n >= 4 else known:
                    sem = in_sems.at[slot, j * (pair_count + 4) + n]
                    yield pltpu.make_async_copy(source_, target, sem)

    def stores(step):
        for j in range(STEP):
            target = mixed_ref.at[order_ref[step * STEP + j]]
            yield pltpu.make_async_copy(done_buf.at[j], target, out_sems.at[j])

    def finish():
        return finish_step(before_buf[...], attended_buf[...], *weight_refs[1:])

    def one_step(i, carry):
        slot = i % 2
        for copy in fetches(begin + jnp.minimum(i + 1, count - 1), 1 - slot):
            copy.start()
        for copy in fetches(begin + i, slot):
            copy.wait()
        attended, mixed = attend_step(
            query_buf.at[slot],
            own_buf.at[slot],
            stats_buf.at[slot],
            member_buf.at[slot],
            weight_refs[0],
            head_width,
            finish,
        )

        @pl.when((i > 0) & (begin + i > 1))
        def _():
            for copy in stores(begin + i - 2):
                copy.wait()

        done_buf[...] = mixed.reshape(done_buf.shape)
        attended_buf[...] = attended
        before_buf[...] = placed_buf[slot].reshape(before_buf.shape)

        @pl.when(begin + i > 0)
        def _():
            for copy in stores(begin + i - 1):
                copy.start()

        return carry

    held = (attended_buf, before_buf)
    if first:
        for buf in held:
            buf[...] = jnp.zeros_like(buf)
    else:
        loads = [
            pltpu.make_async_copy(state, buf, state_sems.at[n])
            for n, (state, buf) in enumerate(zip(states, held, strict=True))
        ]
        for copy in loads:
            copy.start()

    @pl.when(count > 0)
    def _():
        for copy in fetches(begin, 0, listed=False):
            copy.start()

    for copy in copies:
        copy.wait()

    @pl.when(count > 0)
    def _():
        for copy in fetches(begin, 0, known=False):
            copy.start()

    if not first:
        for copy in loads:
            copy.wait()

    @pl.when(count > 0)
    def _():
        lax.fori_loop(0, count, one_step, 0)
        for copy in fetches(begin + count - 1, count % 2):
            copy.wait()

    @pl.when((count > 0) & (begin + count > 1))
    def _():
        for copy in stores(begin + count - 2):
            copy.wait()

    if last:
        done_buf[...] = finish().reshape(done_buf.shape)
        for copy in stores(begin + count - 1):
            copy.start()
        for copy in stores(begin + count - 1):
            copy.wait()
    else:
        saves = [
            pltpu.make_async_copy(buf, state, state_sems.at[n])
            for n, (state, buf) in enumerate(zip(states, held, strict=True))
        ]
        for copy in saves:
            copy.start()
        for copy in saves:
            copy.wait()


def finish_step(placed, attended, out_w_ref, mix_ref):
    middle = placed.astype(jnp.float32) + jnp.dot(
        attended, out_w_ref[...], preferred_element_type=jnp.float32
    )
    middle = middle.astype(jnp.bfloat16).astype(jnp.float32)
    second = layer_norm(middle).astype(jnp.bfloat16)
    mixed = middle + jnp.tanh(jnp.dot(second, mix_ref[...], preferred_element_type=jnp.float32))
    return mixed.astype(jnp.bfloat16)


def attend_step(
    query_ref, own_ref, stats_ref, member_ref, pair_w_ref, head_width, meanwhile
):
    _, members_count, cluster, width = member_ref.shape
    span = GROUP * head_width
    tile = GROUP * cluster
    diagonal = head_mask((span, tile), head_width, cluster)
    ones = jnp.ones((16, members_count * cluster), jnp.bfloat16)
    tiles = HEADS // GROUP
    units = [(block, pair) for block in range(STEP) for pair in range(HEADS // GROUP // 2)]
    listed = member_ref[...].reshape(STEP * members_count * cluster, width)
    both = jnp.dot(listed, pair_w_ref[...], preferred_element_type=jnp.float32)
    both = both.astype(jnp.bfloat16).reshape(STEP, members_count * cluster, 2 * width)
    finished = meanwhile()
    values = [both[block, :, width:].T for block in range(STEP)]

    def scores_of(block, pair):
        return [
            jnp.dot(
                both[block, :, t * span : (t + 1) * span],
                query_ref[block, t * span : (t + 1) * span, :],
                preferred_element_type=jnp.float32,
            )
            for t in (2 * pair, 2 * pair + 1)
        ]

    def weights_of(block, pair, scores):
        weights, factors = [], []
        for t, score in zip((2 * pair, 2 * pair + 1), scores, strict=True):
            own_top = stats_ref[block, t : t + 1, :]
            top = jnp.maximum(jnp.max(score, axis=0, keepdims=True), own_top)
            weights.append(jnp.exp2((score - top).astype(jnp.bfloat16)))
            factors.append(jnp.exp2(own_top - top))
        return weights, factors

    def products_of(block, pair, weights, own_factor):
        for half in range(2):
            t = pair * 2 + half
            lifted = jnp.concatenate([values[block][t * span : (t + 1) * span], ones], axis=0)
            product = jnp.dot(lifted, weights[half], preferred_element_type=jnp.float32)
            yield block, t, product, own_factor[half]

    def scaled(block, t, product, own_factor):
        own_total = stats_ref[block, tiles + t : tiles + t + 1, :] * own_factor
        inverse = 1.0 / (product[span : span + 1] + own_total)
        own = own_ref[block, t * span : (t + 1) * span, :].astype(jnp.float32)
        result = product[:span] * inverse + own * (own_total * inverse)
        result = jnp.where(diagonal, result, 0.0)
        return result[:, : tile // 2] + result[:, tile // 2 :]

    def rows_of(pieces):
        first, other = (jnp.concatenate(of, axis=0) for of in pieces)
        left = lax.broadcasted_iota(jnp.int32, first.shape, 1) < cluster
        first = first + pltpu.roll(first, cluster, 1)
        other = other + pltpu.roll(other, cluster, 1)
        return jnp.where(left, first, other).T.astype(jnp.bfloat16)

    count = len(units)
    scores, weights, products, pieces, attended = {}, {}, {}, [], []
    for at in range(-SCORES_AHEAD, count + 1):
        if at + SCORES_AHEAD < count:
            scores[at + SCORES_AHEAD] = scores_of(*units[at + SCORES_AHEAD])
        if 0 <= at + WEIGHTS_AHEAD < count:
            ahead = at + WEIGHTS_AHEAD
            weights[ahead] = weights_of(*units[ahead], scores.pop(ahead))
        if 0 <= at < count:
            products[at] = list(products_of(*units[at], *weights.pop(at)))
        if at > 0:
            pieces += [scaled(*product) for product in products.pop(at - 1)]
            if len(pieces) == 2 * tiles:
                attended.append(rows_of((pieces[:tiles], pieces[tiles:])))
                pieces = []
    return jnp.concatenate(attended, axis=0), finished


def attend(steps, order, table, own, placed, weights, buffer, pieces, places, so_far, last):
    blocks, cluster, width = placed.shape
    pair_count = table.shape[0] // blocks
    smem = pl.BlockSpec(memory_space=pltpu.SMEM)
    vmem = pl.BlockSpec(memory_space=pltpu.VMEM)
    hbm = pl.BlockSpec(memory_space=pl.ANY)
    in_specs = [smem] * 3 + [hbm] * len(own) + [pl.BlockSpec(memory_space=pltpu.HBM)] + [vmem] * (3 + len(pieces)) + [hbm]
    aliases = {len(in_specs) - 1: 1}
    operands = [*own, placed, *weights, *pieces, buffer]
    for at, x in zip((0, 2, 3), so_far):
        aliases[len(in_specs)] = at
        in_specs.append(hbm)
        operands.append(x)
    kernel = functools.partial(
        attend_kernel,
        head_width=width // HEADS,
        places=places,
        first=not so_far,
        last=last,
    )
    state = jax.ShapeDtypeStruct((STEP * cluster, width), jnp.bfloat16)
    return pl.pallas_call(
        kernel,
        in_specs=in_specs,
        out_specs=[hbm] * 4,
        out_shape=[
            jax.ShapeDtypeStruct(placed.shape, jnp.bfloat16),
            jax.ShapeDtypeStruct(buffer.shape, jnp.bfloat16),
            state,
            state,
        ],
        scratch_shapes=[
            *[pltpu.VMEM((2, STEP) + x.shape[1:], x.dtype) for x in own],
            pltpu.VMEM((2, STEP, pair_count, cluster, width), jnp.bfloat16),
            pltpu.VMEM((2, STEP, cluster, width), jnp.bfloat16),
            pltpu.VMEM((STEP * cluster, width), jnp.bfloat16),
            pltpu.VMEM((STEP * cluster, width), jnp.bfloat16),
            pltpu.VMEM((STEP, cluster, width), jnp.bfloat16),
            pltpu.SemaphoreType.DMA((2, STEP * (pair_count + 4))),
            pltpu.SemaphoreType.DMA((STEP,)),
            pltpu.SemaphoreType.DMA((len(pieces), 5)),
            pltpu.SemaphoreType.DMA((2,)),
        ],
        input_output_aliases=aliases,
        cost_estimate=lasting(18),
        compiler_params=kernel_params(),
        name="attend_blocks",
    )(steps, order, table, *operands)


def slot_tables(owner, within, capacity):
    entries = owner.shape[0]
    alike = owner[:, None] == owner[None, :]
    earlier = jnp.arange(entries)[None, :] < jnp.arange(entries)[:, None]
    ranking = jnp.sum(jnp.where(alike & earlier, 1, 0), axis=1).astype(jnp.int32)
    slots = owner * capacity + ranking
    matches = slots[None, :] == jnp.arange(SPAN * capacity, dtype=jnp.int32)[:, None]
    return ranking, jnp.sum(jnp.where(matches, within[None, :], 0), axis=1).astype(jnp.int32)


def by_class(classes, count):
    blocks = jnp.arange(classes.shape[0], dtype=jnp.int32)
    before = (classes[None, :] < classes[:, None]) | (
        (classes[None, :] == classes[:, None]) & (blocks[None, :] < blocks[:, None])
    )
    rank = jnp.sum(jnp.where(before, 1, 0), axis=1)
    order = jnp.sum(jnp.where(rank[None, :] == blocks[:, None], blocks[None, :], 0), axis=1)
    ends = [jnp.sum(jnp.where(classes <= c, 1, 0)).astype(jnp.int32) for c in range(count)]
    return order.astype(jnp.int32), ends


OUT = (2, 0, 3, 1)
FROM = (1, 3, 0, 2)
LEVELS = 4


def position_at(z, y):
    return 2 * z + y


def partner(position):
    return position ^ 1


def onward(position):
    return position_at(choose(position // 2, OUT), position % 2)


def source(position):
    return position_at(choose(position // 2, FROM), position % 2)


def opposite(position):
    return position_at(LEVELS - 1 - position // 2, position % 2)


def itself(position):
    return position


def crossed(route):
    return lambda position: partner(route(position))


FIRST_PLAN = ((0, source, itself), (1, source, partner), (2, crossed(onward), source))
MIDDLE_PLAN = ((0, opposite, itself),)
NEAR_PLAN = ((0, partner, source), (0, onward, source), (1, opposite, partner))


def body(features, assignment, pairs, w_query, w_key, w_value, w_out, w_mix):
    rows_dev, width = features.shape
    block_count, pair_count = pairs.shape
    cluster = rows_dev // block_count
    stride = lax.axis_size("elec") // SPAN
    groups = [[rest + place_ * stride for place_ in range(SPAN)] for rest in range(stride)]
    position = lax.axis_index("elec") // stride
    at_position = position.reshape(1)
    capacity = (block_count * pair_count + SPAN - 1) // SPAN + 1

    def moved(x, moves):
        pairs_of = [(s * stride + r, d * stride + r) for s, d in moves for r in range(stride)]
        return lax.ppermute(x, "elec", pairs_of)

    def across_z(pairs_of_z):
        return [(position_at(s, y), position_at(d, y)) for s, d in pairs_of_z for y in range(2)]

    swap = [(p, p ^ 1) for p in range(SPAN)]
    first_moves = across_z(enumerate(OUT))
    second_moves = across_z(enumerate(FROM))
    middle_moves = across_z([(1, 2), (2, 1)])
    outward_moves = across_z([(2, 3), (1, 0)])

    listed = pairs.reshape(-1)
    owner = listed // block_count // stride
    within = listed % block_count
    ranking, tables = slot_tables(owner, within, capacity)
    wanted = lax.all_to_all(
        jnp.broadcast_to(tables[None], (SPAN, SPAN * capacity)),
        "elec",
        split_axis=0,
        concat_axis=0,
        axis_index_groups=groups,
        tiled=True,
    )

    shape = (block_count // SUB, 1, SUB * cluster)
    block_shape = (block_count, cluster, width)
    placed, normed = place(features, assignment.reshape(shape))
    blocks = normed.reshape(block_shape)
    own_at = 7 * capacity
    passed_at = own_at + block_count
    beside_at = passed_at + block_count
    total = beside_at + block_count

    z, y = position // 2, position % 2
    is_end = (z == 0) | (z == LEVELS - 1)
    z_owner, same = owner // 2, owner % 2 == y
    from_first = z_owner == choose(z, FROM)
    late = z_owner == LEVELS - 1 - z
    piece_of = jnp.where(
        from_first,
        0,
        jnp.where(
            late,
            jnp.where(is_end, jnp.where(same, 3, 4), jnp.where(same, 5, 6)),
            jnp.where(same, 1, 2),
        ),
    )
    whole_at = jnp.where(z_owner == z, jnp.where(same, own_at, beside_at), passed_at)
    whole = (z_owner == z) | (from_first & same)
    table = jnp.where(whole, whole_at + within, piece_of * capacity + ranking)

    arrival = jnp.where(late, jnp.where(same, 1, 2), 0)
    order, ends = by_class(jnp.max(arrival.reshape(block_count, pair_count), axis=1), 2)
    marks = [0, ends[0] // STEP, ends[1] // STEP, block_count // STEP]
    phases = [
        jnp.stack([marks[n], marks[n + 1] - marks[n]]).astype(jnp.int32) for n in range(3)
    ]
    weights = (jnp.concatenate([w_key, w_value], axis=1), w_out, w_mix)

    own = own_part(normed, w_query, w_key, w_value, cluster, (order, table, *phases, weights[0]))
    beside = moved(blocks, swap)
    passed = moved(blocks, first_moves)
    second, second_cross, on = pick(
        at_position, wanted, (blocks, beside, passed), FIRST_PLAN, after=own[2:]
    )
    second = moved(second, second_moves)
    second_cross = moved(second_cross, second_moves)
    on = moved(on, swap)
    (middle_pick,) = pick(at_position, wanted, (blocks,), MIDDLE_PLAN, after=(second,))
    middle = moved(middle_pick, middle_moves)
    near, outward, middle_cross = pick(
        at_position, wanted, (passed, beside), NEAR_PLAN, after=(on,)
    )
    near = moved(near, swap)
    outward = moved(outward, outward_moves)
    on = moved(on, outward_moves)
    middle_cross = held_until(middle_cross, (second_cross, middle_pick))
    middle_cross = moved(middle_cross, middle_moves)

    buffer = collect((blocks, passed, beside), (own_at, passed_at, beside_at), total)

    placed = pltpu.with_memory_space_constraint(placed.reshape(blocks.shape), pltpu.HBM)
    shared = (order, table, own, placed, weights)
    arrivals = (
        ((near, 0), (second, 1), (second_cross, 2)),
        ((outward, 3), (middle, 5)),
        ((on, 4), (middle_cross, 6)),
    )
    so_far = ()
    for phase, arrived in zip(phases, arrivals, strict=True):
        pieces = [piece for piece, _ in arrived]
        places = tuple(at * capacity for _, at in arrived)
        last = arrived is arrivals[-1]
        mixed, buffer, *states = attend(phase, *shared, buffer, pieces, places, so_far, last)
        so_far = (mixed, *states)
    return mixed.reshape(rows_dev, width)


def solution(mesh):
    placed = (
        P(("groups", "elec"), None),
        P(("groups", "elec")),
        P(("groups", "elec"), None),
        P(),
        P(),
        P(),
        P(),
        P(),
    )
    return jax.shard_map(
        body, mesh=mesh, in_specs=placed, out_specs=P(("groups", "elec"), None), check_vma=False
    )
```
